32 devices in a mesh: groups: 2 (over y), blk: 4 (over z), sub: 2 (over x), inner: 2 (over core).
Axes of the slice: x: 2, y: 2, z: 4, core: 2. Of those that a mesh axis runs over, the one named last changes fastest.
Arguments:
- mass_profile_vectors: bfloat16 [10240, 1024], P(('groups', 'blk', 'sub', 'inner')), parts along dimension 0, may hold values from -6 to 6
- sugar_tree_vectors: bfloat16 [10240, 1024], P(('groups', 'blk', 'sub', 'inner')), parts along dimension 0, may hold values from -6 to 6
- matching_glycan_rows: int32 [10240], P(('groups', 'blk', 'sub', 'inner')), parts along dimension 0, may hold values from 0 to 5119, as said below
- sharpness_factor: float32 [1], replicated, may hold values from 0.03 to 0.08
- offset_shift_term: float32 [1], replicated, may hold values from -2 to 0
Outputs:
- grad_spectra: bfloat16 [10240, 1024], P(('groups', 'blk', 'sub', 'inner')), parts along dimension 0
- grad_structures: bfloat16 [10240, 1024], P(('groups', 'blk', 'sub', 'inner')), parts along dimension 0
The draws below stay inside these ranges and needn't reach their ends.
There are 2 independent parts, one for each index of `groups`. The reference program is written for one: setup_inputs(seed, part) draws one part's arguments, and reference() takes and returns one part's arrays. A program takes and returns all parts, laid end to end along the dimension named above; an argument that names none is the same for every part. Nothing has to cross between parts.
Inputs may be any that keep to these rules, and one draw needn't show every extreme that they name: `matching_glycan_rows`: labels_i names a glycan row in node w(n, s) for some s in 0 .. 3, where n is the node of spectrum row i; several spectra may share one glycan.
All inputs are finite; a program needn't handle non-finite values.
Results may differ from the reference program's by a relative error of at most 0.0095.
Values may be sent and summed in bfloat16 or wider, within the bound.
No kernel may reach another device: no remote copies, remote signals or barrier semaphores. Data moves between devices by JAX's collectives and lax.ppermute only.
A program may use at most 64 MiB of HBM per device.

```python
import math
import jax
import jax.numpy as jnp
from jax import lax

D = 1024
ROWS_DEV = 320
STEPS = 4
NODE = 640
B = 5120
N_BLK = 4
N_SUB = 2
N_INNER = 2


def draw_matching_glycan_rows(key, part):
    key = jax.random.fold_in(key, 7)
    key_step, key_row = jax.random.split(key)
    rows = jnp.arange(B, dtype=jnp.int32)
    node = rows // NODE
    position = node // N_SUB
    lane = node % N_SUB
    offset = jax.random.randint(key_step, (B,), 0, STEPS, dtype=jnp.int32)
    ends = (rows == 0) | (rows == B - 1)
    offset = jnp.where(ends, 0, offset).astype(jnp.int32)
    target_sign = (position - offset) % N_BLK * N_SUB + lane
    within = jax.random.randint(key_row, (B,), 0, NODE, dtype=jnp.int32)
    within = jnp.where(rows == 0, 0, jnp.where(rows == B - 1, NODE - 1, within)).astype(jnp.int32)
    return (target_sign * NODE + within).astype(jnp.int32)


def block_levels(own_key, extent, cuts, least, high):
    loudness, own = 1.0, jax.random.fold_in(own_key, 6)
    for axis_at, blocks in cuts:
        draws = jnp.exp(jax.random.uniform(jax.random.fold_in(own, axis_at), (blocks,), jnp.float32, least / len(cuts), high / len(cuts)))
        loudness = loudness * jnp.repeat(draws, extent[axis_at] // blocks).reshape([-1 if axis == axis_at else 1 for axis in range(len(extent))])
    return loudness


def normal_values(key, shape, spread, limit, pieces=(), kind=jnp.bfloat16):
    drawn = spread * jax.random.normal(key, shape, jnp.float32)
    if pieces:
        drawn = drawn * block_levels(key, shape, pieces, -0.22, 0.18)
    return jnp.clip(drawn, -limit, limit).astype(kind)


def setup_inputs(seed: int = 0, part: int = 0) -> dict:
    key_of = jax.random.split(jax.random.key(seed), 6)
    part_splits = jax.random.split(jax.random.fold_in(key_of[5], part), 6)
    return {
        "mass_profile_vectors": normal_values(part_splits[0], (B, D), 1.0, 6.0, ((0, 16),)),
        "sugar_tree_vectors": normal_values(part_splits[1], (B, D), 1.0, 6.0, ((0, 16),)),
        "matching_glycan_rows": draw_matching_glycan_rows(jax.random.fold_in(jax.random.fold_in(key_of[5], part), 71), part),
        "sharpness_factor": jnp.clip(jnp.exp(jax.random.uniform(key_of[3], (1,), jnp.float32, math.log(0.03), math.log(0.08))), 0.03, 0.08),
        "offset_shift_term": jnp.clip(jax.random.uniform(key_of[4], (1,), jnp.float32, -2.0, 0.0), -2.0, 0.0),
    }


def reference(mass_profile_vectors, sugar_tree_vectors, matching_glycan_rows, sharpness_factor, offset_shift_term):
    similarity_multiplier = sharpness_factor[0]
    shift_b = offset_shift_term[0]
    spec_nodes = mass_profile_vectors.reshape(N_BLK, N_SUB, NODE, D)
    glyc_nodes = sugar_tree_vectors.reshape(N_BLK, N_SUB, NODE, D)
    node_label_table = matching_glycan_rows.reshape(N_BLK, N_SUB, NODE)
    worker_identifiers = (jnp.arange(N_BLK, dtype=jnp.int32)[:, None] * N_SUB + jnp.arange(N_SUB, dtype=jnp.int32)[None, :]).astype(jnp.int32)
    grad_s = jnp.zeros((N_BLK, N_SUB, NODE, D), jnp.float32)
    grad_g = jnp.zeros((N_BLK, N_SUB, NODE, D), jnp.float32)
    for step in range(STEPS):
        held = jnp.roll(glyc_nodes, step, axis=0)
        held_ids = jnp.roll(worker_identifiers, step, axis=0)

        def one_node(items):
            spec, glyc, lab, ids = items
            spec_f = spec.astype(jnp.float32)
            glyc_f = glyc.astype(jnp.float32)
            logits = similarity_multiplier * jnp.einsum('pid,pjd->pij', spec_f, glyc_f) + shift_b
            targets = (ids[:, None] * NODE + jnp.arange(NODE, dtype=jnp.int32)[None, :]).astype(jnp.int32)
            positive = (lab[:, :, None] == targets[:, None, :]).astype(jnp.float32)
            coef = (jax.nn.sigmoid(logits) - positive).astype(jnp.bfloat16)
            coef_f = coef.astype(jnp.float32)
            spec_part = jnp.einsum('pij,pjd->pid', coef_f, glyc_f)
            coef_dev = coef_f.reshape(N_SUB, N_INNER, ROWS_DEV, NODE)
            spec_dev = spec_f.reshape(N_SUB, N_INNER, ROWS_DEV, D)
            partial_value = (similarity_multiplier * jnp.einsum('pcij,pcid->pcjd', coef_dev, spec_dev)).astype(jnp.bfloat16)
            return spec_part, jnp.sum(partial_value.astype(jnp.float32), axis=1)

        spec_part, glyc_part = lax.map(one_node, (spec_nodes, held, node_label_table, held_ids))
        grad_s = grad_s + spec_part
        grad_g = grad_g + jnp.roll(glyc_part, -step, axis=0)
    grad_spectra = (similarity_multiplier * grad_s).astype(jnp.bfloat16).reshape(B, D)
    grad_structures = grad_g.astype(jnp.bfloat16).reshape(B, D)
    return grad_spectra, grad_structures
```

```python
import jax
import jax.numpy as jnp
from jax import lax
from jax.sharding import PartitionSpec as P

STEPS = 4
LINE = 4


def from_behind(block, axis, distance):
    devices = range(lax.axis_size(axis))
    route = [((i - distance) % len(devices), i) for i in devices]
    return lax.ppermute(block, axis, route)


def swap_inner(block):
    return from_behind(block, "inner", 1)


def coefficients(spectra, glycans, labels, first_target, scale, shift):
    logits = (
        scale
        * lax.dot_general(
            spectra, glycans, (((1,), (1,)), ((), ())), preferred_element_type=jnp.float32
        )
        + shift
    )
    targets = first_target + jnp.arange(glycans.shape[0], dtype=jnp.int32)
    positive = (labels[:, None] == targets[None, :]).astype(jnp.float32)
    return (jax.nn.sigmoid(logits) - positive).astype(jnp.bfloat16)


def toward_spectra(coef, glycans):
    return jnp.dot(coef, glycans, preferred_element_type=jnp.float32)


def toward_glycans(coef, spectra):
    return lax.dot_general(
        coef, spectra, (((0,), (0,)), ((), ())), preferred_element_type=jnp.float32
    )


def merge_spectra(total, rows_here, scale):
    other = swap_inner((scale * total[rows_here:]).astype(jnp.bfloat16))
    return (scale * total[:rows_here] + other.astype(jnp.float32)).astype(jnp.bfloat16)


def around_ring(spectra, glycans, labels, scale, shift):
    rows_here = spectra.shape[0]
    node_rows = rows_here * lax.axis_size("inner")
    loop_count = lax.axis_size("blk")
    position = lax.axis_index("blk")
    core_first = lax.axis_index("sub") * node_rows + lax.axis_index("inner") * rows_here
    lane_rows = lax.axis_size("sub") * node_rows
    node_spectra = jnp.concatenate([spectra, swap_inner(spectra)])
    node_labels = jnp.concatenate([labels, swap_inner(labels)])
    spectrum_total = 0.0
    glycan_total = 0.0
    held = glycans
    for step in range(STEPS):
        if step > 0:
            held = from_behind(held, "blk", 1)
        first_target = (position - step) % loop_count * lane_rows + core_first
        coef = coefficients(node_spectra, held, node_labels, first_target, scale, shift)
        spectrum_total += toward_spectra(coef, held)
        partial_value = scale * toward_glycans(coef, node_spectra)
        if step > 0:
            back = from_behind(partial_value.astype(jnp.bfloat16), "blk", -step)
            partial_value = back.astype(jnp.float32)
        glycan_total += partial_value
    return (
        merge_spectra(spectrum_total, rows_here, scale),
        glycan_total.astype(jnp.bfloat16),
    )


def along_line(spectra, glycans, labels, scale, shift):
    rows_here = spectra.shape[0]
    node_rows = rows_here * lax.axis_size("inner")
    position = lax.axis_index("blk")
    outer = (position == 0) | (position == LINE - 1)
    core_first = lax.axis_index("sub") * node_rows + lax.axis_index("inner") * rows_here
    lane_rows = lax.axis_size("sub") * node_rows

    def permute(block, pairs):
        return lax.ppermute(block, "blk", pairs)

    def first_of(block_position):
        return block_position * lane_rows + core_first

    sides = [(0, 1), (1, 0), (2, 3), (3, 2)]
    middle = [(1, 2), (2, 1)]
    inward = [(0, 1), (3, 2)]
    outward = [(1, 0), (2, 3)]

    side = permute(glycans, sides)
    across = permute(glycans, middle)
    node_spectra = jnp.concatenate([spectra, swap_inner(spectra)])
    node_labels = jnp.concatenate([labels, swap_inner(labels)])
    end_labels = permute(node_labels, inward)

    far = permute(side, middle)
    next_out = permute(across, outward)
    end_half = permute(spectra, inward)
    last_out = permute(far, outward)
    end_spectra = jnp.concatenate([end_half, swap_inner(end_half)])

    here_at = first_of(position)
    side_at = first_of(position ^ 1)
    across_at = first_of(LINE - 1 - position)
    far_at = first_of((LINE - 1 - position) ^ 1)

    def own(block, at):
        coef = coefficients(node_spectra, block, node_labels, at, scale, shift)
        return toward_spectra(coef, block), toward_glycans(coef, node_spectra)

    def ends(block, at):
        coef = coefficients(end_spectra, block, end_labels, at, scale, shift)
        return toward_glycans(coef, end_spectra)

    here_s, here_g = own(glycans, here_at)
    side_s, side_g = own(side, side_at)
    across_s, across_g = own(across, across_at)
    far_s, far_g = own(far, far_at)

    far_back = permute((scale * (far_g + ends(far, far_at))).astype(jnp.bfloat16), middle)
    across_back = permute(
        (scale * (across_g + ends(across, across_at))).astype(jnp.bfloat16), middle
    )
    side_total = scale * (side_g + ends(side, side_at)) + far_back.astype(jnp.float32)
    from_inside = permute(side_total.astype(jnp.bfloat16), outward)
    here_total = scale * (here_g + ends(glycans, here_at)) + across_back.astype(jnp.float32)
    grad_structures = jnp.where(outer, from_inside, here_total.astype(jnp.bfloat16))

    next_s, _ = own(next_out, far_at)
    last_s, _ = own(last_out, across_at)
    spectrum_total = here_s + side_s + across_s + far_s + next_s + last_s
    return merge_spectra(spectrum_total, rows_here, scale), grad_structures


def local(
    mass_profile_vectors,
    sugar_tree_vectors,
    matching_glycan_rows,
    sharpness_factor,
    offset_shift_term,
):
    work = along_line if lax.axis_size("blk") == STEPS == LINE else around_ring
    return work(
        mass_profile_vectors,
        sugar_tree_vectors,
        matching_glycan_rows,
        sharpness_factor[0],
        offset_shift_term[0],
    )


def solution(mesh):
    placed = (
        P(("groups", "blk", "sub", "inner"), None),
        P(("groups", "blk", "sub", "inner"), None),
        P(("groups", "blk", "sub", "inner")),
        P(),
        P(),
    )
    return jax.shard_map(
        local,
        mesh=mesh,
        in_specs=placed,
        out_specs=(
            P(("groups", "blk", "sub", "inner"), None),
            P(("groups", "blk", "sub", "inner"), None),
        ),
        check_vma=False,
    )
```

```python
import functools

import jax
import jax.numpy as jnp
from jax import lax
from jax.experimental import pallas as pl
from jax.experimental.pallas import tpu as pltpu
from jax.sharding import PartitionSpec as P

STEPS = 4
LINE = 4
VMEM_BYTES = 32 * 1024 * 1024


def from_behind(block, axis, distance):
    devices = range(lax.axis_size(axis))
    route = [((i - distance) % len(devices), i) for i in devices]
    return lax.ppermute(block, axis, route)


def swap_inner(block):
    return from_behind(block, "inner", 1)


def after(value, *earlier):
    return lax.optimization_barrier((value,) + earlier)[0]


def coefficients(spectra, glycans, labels, first_target, scale, shift):
    logits = (
        scale
        * lax.dot_general(
            spectra, glycans, (((1,), (1,)), ((), ())), preferred_element_type=jnp.float32
        )
        + shift
    )
    targets = first_target + jnp.arange(glycans.shape[0], dtype=jnp.int32)
    positive = (labels[:, None] == targets[None, :]).astype(jnp.float32)
    return (jax.nn.sigmoid(logits) - positive).astype(jnp.bfloat16)


def around_ring(spectra, glycans, labels, scale, shift):
    rows_here = spectra.shape[0]
    node_rows = rows_here * lax.axis_size("inner")
    loop_count = lax.axis_size("blk")
    position = lax.axis_index("blk")
    core_first = lax.axis_index("sub") * node_rows + lax.axis_index("inner") * rows_here
    lane_rows = lax.axis_size("sub") * node_rows
    node_spectra = jnp.concatenate([spectra, swap_inner(spectra)])
    node_labels = jnp.concatenate([labels, swap_inner(labels)])
    spectrum_total = 0.0
    glycan_total = 0.0
    held = glycans
    for step in range(STEPS):
        if step > 0:
            held = from_behind(held, "blk", 1)
        first_target = (position - step) % loop_count * lane_rows + core_first
        coef = coefficients(node_spectra, held, node_labels, first_target, scale, shift)
        spectrum_total += jnp.dot(coef, held, preferred_element_type=jnp.float32)
        partial_value = scale * lax.dot_general(
            coef, node_spectra, (((0,), (0,)), ((), ())), preferred_element_type=jnp.float32
        )
        if step > 0:
            back = from_behind(partial_value.astype(jnp.bfloat16), "blk", -step)
            partial_value = back.astype(jnp.float32)
        glycan_total += partial_value
    other = swap_inner((scale * spectrum_total[rows_here:]).astype(jnp.bfloat16))
    spectrum_total = scale * spectrum_total[:rows_here] + other.astype(jnp.float32)
    return spectrum_total.astype(jnp.bfloat16), glycan_total.astype(jnp.bfloat16)


def pair_body(plan, *refs):
    n_spectra, blocks, with_spectra, prior_spectra, round_glycans, half = plan
    refs = list(refs)
    factors, ints, labels = refs[:3]
    refs = refs[3:]
    spectra_in, refs = refs[:n_spectra], refs[n_spectra:]
    blocks_in, refs = refs[: len(blocks)], refs[len(blocks) :]
    priors_in = []
    for _, _, has_prior, _ in blocks:
        priors_in.append(refs.pop(0) if has_prior else None)
    prior_s_in = refs.pop(0) if prior_spectra else None
    glycans_out = []
    for _, _, _, wants in blocks:
        glycans_out.append(refs.pop(0) if wants else None)
    if with_spectra == "final":
        mine_out, other_out = refs.pop(0), refs.pop(0)
    elif with_spectra:
        spectra_out = refs.pop(0)
    spectra = refs.pop(0)
    held = [refs.pop(0) for _ in blocks]
    priors = [refs.pop(0) if b[2] else None for b in blocks]
    if with_spectra == "final":
        spectra_out = refs.pop(0)
    sems = refs.pop(0)

    scale, shift = factors[0], factors[1]
    rows = spectra.shape[0] // n_spectra
    at = 0
    moves = []

    def move(source, target):
        nonlocal at
        copy = pltpu.make_async_copy(source, target, sems.at[at])
        copy.start()
        at += 1
        return copy

    for i, ref in enumerate(spectra_in):
        moves.append(move(ref, spectra.at[pl.ds(i * rows, rows)]))
    block_moves = [
        move(ref.at[pl.ds(b[0], b[1])], held[i]) for i, (ref, b) in enumerate(zip(blocks_in, blocks))
    ]
    prior_moves = [
        move(ref.at[pl.ds(b[0], b[1])], priors[i]) if b[2] else None
        for i, (ref, b) in enumerate(zip(priors_in, blocks))
    ]
    prior_s_move = move(prior_s_in, spectra_out) if prior_spectra else None
    for copy in moves:
        copy.wait()
    waited = False
    for i, block in enumerate(blocks):
        block_moves[i].wait()
        if block[2]:
            prior_moves[i].wait()
        if with_spectra and prior_spectra and not waited:
            prior_s_move.wait()
            waited = True

        def work(i=i, block=block):
            glycans = held[i][...]
            logits = scale * lax.dot_general(
                glycans, spectra[...], (((1,), (1,)), ((), ())), preferred_element_type=jnp.float32
            )
            logits = logits + shift
            targets = ints[2 * i] + block[0] + lax.broadcasted_iota(jnp.int32, logits.shape, 0)
            positive = jnp.where(targets == labels[...], 1.0, 0.0)
            coef = (jax.nn.sigmoid(logits) - positive).astype(jnp.bfloat16)
            if block[3]:
                total = jnp.dot(coef, spectra[...], preferred_element_type=jnp.float32)
                if block[2]:
                    total = total + priors[i][...]
                if round_glycans:
                    glycans_out[i][...] = (scale * total).astype(jnp.bfloat16)
                else:
                    glycans_out[i][...] = total
            if with_spectra:
                part = lax.dot_general(
                    coef, glycans, (((0,), (0,)), ((), ())), preferred_element_type=jnp.float32
                )
                if prior_spectra or i > 0:
                    spectra_out[...] += part
                else:
                    spectra_out[...] = part

        if with_spectra == "final":
            pl.when(ints[2 * i + 1] != 0)(work)
        else:
            work()
    if with_spectra == "final":
        mine_out[...] = scale * spectra_out[pl.ds(0, half)]
        other_out[...] = (scale * spectra_out[pl.ds(half, half)]).astype(jnp.bfloat16)


def pair_work(
    factors, spectra, labels, blocks, with_spectra=False, prior_s=None, round_glycans=False
):
    rows, width = spectra[0].shape
    all_rows = rows * len(spectra)
    ints = []
    for b in blocks:
        ints += [jnp.int32(b[1]), jnp.int32(b[2])]
    shapes = tuple((b[3], b[4], b[5] is not None, b[6]) for b in blocks)
    plan = (len(spectra), shapes, with_spectra, prior_s is not None, round_glycans, rows)
    anywhere = pl.BlockSpec(memory_space=pl.ANY)
    in_vmem = pl.BlockSpec(memory_space=pltpu.VMEM)
    in_smem = pl.BlockSpec(memory_space=pltpu.SMEM)
    operands = [factors, jnp.stack(ints), labels] + list(spectra) + [b[0] for b in blocks]
    operands += [b[5] for b in blocks if b[5] is not None]
    if prior_s is not None:
        operands.append(prior_s)
    in_specs = [in_smem, in_smem, in_vmem] + [anywhere] * (len(operands) - 3)
    glycan_type = jnp.bfloat16 if round_glycans else jnp.float32
    outs = [jax.ShapeDtypeStruct((b[4], width), glycan_type) for b in blocks if b[6]]
    if with_spectra == "final":
        outs.append(jax.ShapeDtypeStruct((rows, width), jnp.float32))
        outs.append(jax.ShapeDtypeStruct((rows, width), jnp.bfloat16))
    elif with_spectra:
        outs.append(jax.ShapeDtypeStruct((all_rows, width), jnp.float32))
    scratch = [pltpu.VMEM((all_rows, width), jnp.bfloat16)]
    scratch += [pltpu.VMEM((b[4], width), jnp.bfloat16) for b in blocks]
    scratch += [pltpu.VMEM((b[4], width), jnp.float32) for b in blocks if b[5] is not None]
    if with_spectra == "final":
        scratch.append(pltpu.VMEM((all_rows, width), jnp.float32))
    scratch.append(pltpu.SemaphoreType.DMA((len(operands),)))
    return pl.pallas_call(
        functools.partial(pair_body, plan),
        out_shape=outs,
        in_specs=in_specs,
        out_specs=[in_vmem] * len(outs),
        scratch_shapes=scratch,
        cost_estimate=pl.CostEstimate(flops=1024, bytes_accessed=1024, transcendentals=0),
        compiler_params=pltpu.CompilerParams(vmem_limit_bytes=VMEM_BYTES),
    )(*operands)


def along_line(spectra, glycans, labels, scale, shift):
    rows = spectra.shape[0]
    half = rows // 2
    first_part = 3 * rows // 5
    node_rows = rows * lax.axis_size("inner")
    position = lax.axis_index("blk")
    outer = (position == 0) | (position == LINE - 1)
    core_first = lax.axis_index("sub") * node_rows + lax.axis_index("inner") * rows
    lane_rows = lax.axis_size("sub") * node_rows
    factors = jnp.stack([scale, shift])

    def permute(block, pairs):
        return lax.ppermute(block, "blk", pairs)

    def first_of(block_position):
        return block_position * lane_rows + core_first

    sides = [(0, 1), (1, 0), (2, 3), (3, 2)]
    middle = [(1, 2), (2, 1)]
    inward = [(0, 1), (3, 2)]
    outward = [(1, 0), (2, 3)]
    here_at = first_of(position)
    side_at = first_of(position ^ 1)
    across_at = first_of(LINE - 1 - position)
    far_at = first_of((LINE - 1 - position) ^ 1)

    side = permute(glycans, sides)
    across = permute(glycans, middle)
    partner = swap_inner(spectra)
    own_labels = labels.reshape(1, rows)
    node_labels = jnp.concatenate([own_labels, swap_inner(own_labels)], axis=1)
    end_labels = permute(node_labels, inward)
    node = [spectra, partner]
    here_g, own_s = pair_work(
        factors, node, node_labels, [(glycans, here_at, 1, 0, rows, None, True)], with_spectra=True
    )

    side, across, late_spectra, end_labels = lax.optimization_barrier(
        (side, across, spectra, end_labels, here_g)
    )[:4]
    far = permute(side, middle)
    end_mine = permute(late_spectra, inward)
    next_out = permute(across, outward)
    side_g, across_g, own_s = pair_work(
        factors,
        node,
        node_labels,
        [(side, side_at, 1, 0, rows, None, True), (across, across_at, 1, 0, rows, None, True)],
        with_spectra=True,
        prior_s=own_s,
    )

    end_mine, far, next_out = lax.optimization_barrier((end_mine, far, next_out, own_s))[:3]
    end_other = swap_inner(end_mine)
    last_out = permute(far, outward)
    three_labels = jnp.concatenate([node_labels, end_labels[:, :rows]], axis=1)
    (far_g,) = pair_work(
        factors,
        node + [end_mine],
        three_labels,
        [(far, far_at, 1, 0, rows, None, True)],
    )

    def far_part(first, count, *earlier):
        (out,) = pair_work(
            factors,
            [end_other],
            end_labels[:, rows:],
            [(after(far, far_g, *earlier), far_at, 1, first, count, far_g, True)],
            round_glycans=True,
        )
        return out

    ends = [end_mine, end_other]
    far_a = far_part(0, first_part)
    back_a = permute(far_a, middle)
    side_g, here_g = pair_work(
        factors,
        ends,
        end_labels,
        [
            (after(side, far_a), side_at, 1, 0, rows, side_g, True),
            (glycans, here_at, 1, 0, rows, here_g, True),
        ],
    )
    far_b = far_part(first_part, rows - first_part, side_g)
    back_b = permute(far_b, middle)
    (across_out,) = pair_work(
        factors,
        ends,
        end_labels,
        [(after(across, far_b), across_at, 1, 0, rows, across_g, True)],
        round_glycans=True,
    )
    across_back = permute(across_out, middle)

    total_a = (scale * side_g[:first_part] + back_a.astype(jnp.float32)).astype(jnp.bfloat16)
    inside_a = permute(total_a, outward)
    mine_s, other_s = pair_work(
        factors,
        node,
        node_labels,
        [
            (after(far, total_a), far_at, ~outer, 0, rows, None, False),
            (next_out, far_at, outer, 0, rows, None, False),
            (last_out, across_at, outer, 0, rows, None, False),
        ],
        with_spectra="final",
        prior_s=own_s,
    )
    other_back = jnp.concatenate([swap_inner(other_s[:half]), swap_inner(other_s[half:])])
    back_b = after(back_b, mine_s)
    total_b = (scale * side_g[first_part:] + back_b.astype(jnp.float32)).astype(jnp.bfloat16)
    inside_b = permute(total_b, outward)

    grad_spectra = (mine_s + other_back.astype(jnp.float32)).astype(jnp.bfloat16)
    here_total = (scale * here_g + across_back.astype(jnp.float32)).astype(jnp.bfloat16)
    grad_structures = jnp.where(outer, jnp.concatenate([inside_a, inside_b]), here_total)
    return grad_spectra, grad_structures


def local(
    mass_profile_vectors,
    sugar_tree_vectors,
    matching_glycan_rows,
    sharpness_factor,
    offset_shift_term,
):
    work = along_line if lax.axis_size("blk") == STEPS == LINE else around_ring
    return work(
        mass_profile_vectors,
        sugar_tree_vectors,
        matching_glycan_rows,
        sharpness_factor[0],
        offset_shift_term[0],
    )


def solution(mesh):
    placed = (
        P(("groups", "blk", "sub", "inner"), None),
        P(("groups", "blk", "sub", "inner"), None),
        P(("groups", "blk", "sub", "inner")),
        P(),
        P(),
    )
    return jax.shard_map(
        local,
        mesh=mesh,
        in_specs=placed,
        out_specs=(
            P(("groups", "blk", "sub", "inner"), None),
            P(("groups", "blk", "sub", "inner"), None),
        ),
        check_vma=False,
    )
```

```python
import dataclasses
import functools

import jax
import jax.numpy as jnp
from jax import lax
from jax.experimental import pallas as pl
from jax.experimental.pallas import tpu as pltpu
from jax.sharding import PartitionSpec as P

STEPS = 4
LINE = 4
LABEL_ROWS = 16
VMEM_BYTES = 24 * 1024 * 1024


def from_behind(block, axis, distance):
    devices = range(lax.axis_size(axis))
    route = [((i - distance) % len(devices), i) for i in devices]
    return lax.ppermute(block, axis, route)


def swap_inner(block):
    return from_behind(block, "inner", 1)


def after(value, *earlier):
    return lax.optimization_barrier((value,) + earlier)[0]


def coefficients(spectra, glycans, labels, first_target, scale, shift):
    logits = (
        scale
        * lax.dot_general(
            spectra, glycans, (((1,), (1,)), ((), ())), preferred_element_type=jnp.float32
        )
        + shift
    )
    targets = first_target + jnp.arange(glycans.shape[0], dtype=jnp.int32)
    positive = (labels[:, None] == targets[None, :]).astype(jnp.float32)
    return (jax.nn.sigmoid(logits) - positive).astype(jnp.bfloat16)


def around_ring(spectra, glycans, labels, scale, shift):
    rows_here = spectra.shape[0]
    node_rows = rows_here * lax.axis_size("inner")
    loop_count = lax.axis_size("blk")
    position = lax.axis_index("blk")
    core_first = lax.axis_index("sub") * node_rows + lax.axis_index("inner") * rows_here
    lane_rows = lax.axis_size("sub") * node_rows
    node_spectra = jnp.concatenate([spectra, swap_inner(spectra)])
    node_labels = jnp.concatenate([labels, swap_inner(labels)])
    spectrum_total = 0.0
    glycan_total = 0.0
    held = glycans
    for step in range(STEPS):
        if step > 0:
            held = from_behind(held, "blk", 1)
        first_target = (position - step) % loop_count * lane_rows + core_first
        coef = coefficients(node_spectra, held, node_labels, first_target, scale, shift)
        spectrum_total += jnp.dot(coef, held, preferred_element_type=jnp.float32)
        partial_value = scale * lax.dot_general(
            coef, node_spectra, (((0,), (0,)), ((), ())), preferred_element_type=jnp.float32
        )
        if step > 0:
            back = from_behind(partial_value.astype(jnp.bfloat16), "blk", -step)
            partial_value = back.astype(jnp.float32)
        glycan_total += partial_value
    other = swap_inner((scale * spectrum_total[rows_here:]).astype(jnp.bfloat16))
    spectrum_total = scale * spectrum_total[:rows_here] + other.astype(jnp.float32)
    return spectrum_total.astype(jnp.bfloat16), glycan_total.astype(jnp.bfloat16)


def pair_body(plan, *refs):
    n_spectra, blocks, with_spectra, has_prior_s, rows = plan
    refs = list(refs)

    def take(count):
        taken = refs[:count]
        del refs[:count]
        return taken

    factors, ints, labels = take(3)
    spectra = take(n_spectra)
    held = take(len(blocks))
    priors = [take(1)[0] if b.has_prior else None for b in blocks]
    prior_s = take(1)[0] if has_prior_s else None
    glycans_out = [take(1)[0] if b.out else None for b in blocks]
    if with_spectra == "final":
        mine_out, other_out, spectra_out = take(3)
    elif with_spectra:
        (spectra_out,) = take(1)

    scale, shift = factors[0], factors[1]
    row_labels = []
    for j in range(n_spectra):
        if spectra[j].shape[0] > rows:
            digits = spectra[j][pl.ds(rows, LABEL_ROWS), pl.ds(0, rows)].astype(jnp.float32)
            label = digits[0:1] * 16384.0 + digits[1:2] * 128.0 + digits[2:3]
            row_labels.append(label.astype(jnp.int32))
        else:
            row_labels.append(labels[:, pl.ds(j * rows, rows)])
    if with_spectra == "final":
        spectra_out[...] = prior_s[...]
    for i, block in enumerate(blocks):

        def work(i=i, block=block):
            where = pl.ds(block.first, block.count)
            glycans = held[i][where]
            total = priors[i][where] if block.has_prior else None
            for j in range(block.first_spectra, n_spectra):
                here = spectra[j][pl.ds(0, rows)]
                logits = scale * lax.dot_general(
                    glycans, here, (((1,), (1,)), ((), ())), preferred_element_type=jnp.float32
                )
                logits = logits + shift
                targets = ints[2 * i] + block.first
                targets = targets + lax.broadcasted_iota(jnp.int32, logits.shape, 0)
                positive = jnp.where(targets == row_labels[j], 1.0, 0.0)
                coef = (jax.nn.sigmoid(logits) - positive).astype(jnp.bfloat16)
                if block.out:
                    part = jnp.dot(coef, here, preferred_element_type=jnp.float32)
                    total = part if total is None else total + part
                if with_spectra:
                    part = lax.dot_general(
                        coef, glycans, (((0,), (0,)), ((), ())), preferred_element_type=jnp.float32
                    )
                    at = pl.ds(j * rows, rows)
                    if i > 0 or block.optional:
                        spectra_out[at] += part
                    elif has_prior_s:
                        spectra_out[at] = prior_s[at] + part
                    else:
                        spectra_out[at] = part
            if block.out == "rounded":
                glycans_out[i][...] = (scale * total).astype(jnp.bfloat16)
            elif block.out:
                glycans_out[i][...] = total

        if block.optional:
            pl.when(ints[2 * i + 1] != 0)(work)
        else:
            work()
    if with_spectra == "final":
        mine_out[...] = scale * spectra_out[pl.ds(0, rows)]
        other_out[...] = (scale * spectra_out[pl.ds(rows, rows)]).astype(jnp.bfloat16)


@dataclasses.dataclass(frozen=True)
class Block:
    first: int
    count: int
    out: str = "total"
    has_prior: bool = False
    optional: bool = False
    first_spectra: int = 0


def in_vmem(array):
    return pltpu.with_memory_space_constraint(array, pltpu.VMEM)


def vmem_out(shape, kind):
    return pltpu.VMEM(shape, kind)


def pair_work(factors, spectra, labels, blocks, rows, with_spectra=False, prior_s=None):
    width = spectra[0].shape[1]
    all_rows = rows * len(spectra)
    ints = []
    for _, _, first_target, active, _ in blocks:
        ints += [jnp.int32(first_target), jnp.int32(active)]
    shapes = tuple(b[0] for b in blocks)
    plan = (len(spectra), shapes, with_spectra, prior_s is not None, rows)
    vmem = pl.BlockSpec(memory_space=pltpu.VMEM)
    smem = pl.BlockSpec(memory_space=pltpu.SMEM)
    arrays = list(spectra) + [b[1] for b in blocks]
    arrays += [b[4] for b in blocks if b[0].has_prior]
    if prior_s is not None:
        arrays.append(prior_s)
    outs = []
    for shape in shapes:
        if shape.out:
            kind = jnp.bfloat16 if shape.out == "rounded" else jnp.float32
            outs.append(vmem_out((shape.count, width), kind))
    scratch = []
    if with_spectra == "final":
        outs.append(vmem_out((rows, width), jnp.float32))
        outs.append(vmem_out((rows, width), jnp.bfloat16))
        scratch.append(pltpu.VMEM((all_rows, width), jnp.float32))
    elif with_spectra:
        outs.append(vmem_out((all_rows, width), jnp.float32))
    return pl.pallas_call(
        functools.partial(pair_body, plan),
        out_shape=outs,
        in_specs=[smem, smem] + [vmem] * (len(arrays) + 1),
        out_specs=[vmem] * len(outs),
        scratch_shapes=scratch,
        cost_estimate=pl.CostEstimate(flops=1024, bytes_accessed=1024, transcendentals=0),
        compiler_params=pltpu.CompilerParams(vmem_limit_bytes=VMEM_BYTES),
    )(factors, jnp.stack(ints), labels, *[in_vmem(a) for a in arrays])


def code_labels(labels, row_count, width):
    digits = jnp.stack([labels // 16384, labels // 128 % 128, labels % 128])
    spare = ((0, row_count - 3), (0, width - labels.shape[0]))
    return jnp.pad(digits.astype(jnp.bfloat16), spare)


def choose_body(flag, if_true, if_false, tail, out):
    rows = if_true.shape[0]

    @pl.when(flag[0] != 0)
    def _():
        out[pl.ds(0, rows)] = if_true[...]

    @pl.when(flag[0] == 0)
    def _():
        out[pl.ds(0, rows)] = if_false[...]

    out[pl.ds(rows, tail.shape[0])] = tail[...]


def choose(flag, if_true, if_false, tail):
    rows, width = if_true.shape
    vmem = pl.BlockSpec(memory_space=pltpu.VMEM)
    return pl.pallas_call(
        choose_body,
        out_shape=vmem_out((rows + tail.shape[0], width), if_true.dtype),
        in_specs=[pl.BlockSpec(memory_space=pltpu.SMEM)] + [vmem] * 3,
        out_specs=vmem,
        cost_estimate=pl.CostEstimate(flops=1024, bytes_accessed=1024, transcendentals=0),
        compiler_params=pltpu.CompilerParams(vmem_limit_bytes=VMEM_BYTES),
    )(jnp.int32(flag).reshape(1), in_vmem(if_true), in_vmem(if_false), in_vmem(tail))


def finish_body(flag, factors, mine_s, here_g, across_back, inside_a, inside_b, *rest):
    others, (spectra_out, glycans_out) = rest[:-2], rest[-2:]
    half = inside_a.shape[0]
    at = 0
    for other in others:
        where = pl.ds(at, other.shape[0])
        spectra_out[where] = (mine_s[where] + other[...].astype(jnp.float32)).astype(jnp.bfloat16)
        at += other.shape[0]

    @pl.when(flag[0] != 0)
    def _():
        glycans_out[pl.ds(0, half)] = inside_a[...]
        glycans_out[pl.ds(half, half)] = inside_b[...]

    @pl.when(flag[0] == 0)
    def _():
        total = factors[0] * here_g[...] + across_back[...].astype(jnp.float32)
        glycans_out[...] = total.astype(jnp.bfloat16)


def finish(flag, factors, mine_s, here_g, across_back, inside_a, inside_b, others):
    vmem = pl.BlockSpec(memory_space=pltpu.VMEM)
    smem = pl.BlockSpec(memory_space=pltpu.SMEM)
    arrays = [mine_s, here_g, across_back, inside_a, inside_b] + others
    out = jax.ShapeDtypeStruct(mine_s.shape, jnp.bfloat16)
    return pl.pallas_call(
        finish_body,
        out_shape=[out, out],
        in_specs=[smem, smem] + [vmem] * len(arrays),
        out_specs=[vmem, vmem],
        cost_estimate=pl.CostEstimate(flops=1024, bytes_accessed=1024, transcendentals=0),
        compiler_params=pltpu.CompilerParams(vmem_limit_bytes=VMEM_BYTES),
    )(jnp.int32(flag).reshape(1), factors, *[in_vmem(a) for a in arrays])


def along_line(spectra, glycans, labels, scale, shift):
    rows, width = spectra.shape
    half = rows // 2
    node_rows = rows * lax.axis_size("inner")
    position = lax.axis_index("blk")
    outer = (position == 0) | (position == LINE - 1)
    core_first = lax.axis_index("sub") * node_rows + lax.axis_index("inner") * rows
    lane_rows = lax.axis_size("sub") * node_rows
    factors = jnp.stack([scale, shift])

    def permute(block, pairs):
        return lax.ppermute(block, "blk", pairs)

    def first_of(block_position):
        return block_position * lane_rows + core_first

    sides = [(0, 1), (1, 0), (2, 3), (3, 2)]
    middle = [(1, 2), (2, 1)]
    outward = [(1, 0), (2, 3)]
    here_at = first_of(position)
    side_at = first_of(position ^ 1)
    across_at = first_of(LINE - 1 - position)
    far_at = first_of((LINE - 1 - position) ^ 1)
    whole = Block(0, rows)
    more = Block(0, rows, has_prior=True)

    side = permute(glycans, sides)
    across = permute(glycans, middle)
    partner = swap_inner(spectra)
    own_labels = labels.reshape(1, rows)
    node_labels = jnp.concatenate([own_labels, swap_inner(own_labels)], axis=1)
    node = [spectra, partner]
    here_g, own_s = pair_work(
        factors, node, node_labels, [(whole, glycans, here_at, 1, None)], rows, with_spectra=True
    )

    coded = code_labels(labels, LABEL_ROWS, width)
    side, across = lax.optimization_barrier((side, across, here_g))[:2]
    far = permute(side, middle)
    mixed = permute(choose(outer, spectra, across, coded), sides)
    side_g, across_g, own_s = pair_work(
        factors,
        node,
        node_labels,
        [(whole, side, side_at, 1, None), (whole, across, across_at, 1, None)],
        rows,
        with_spectra=True,
        prior_s=own_s,
    )

    mixed, far = lax.optimization_barrier((mixed, far, own_s))[:2]
    mixed_other = swap_inner(mixed)
    last_out = permute(far, outward)
    (far_g,) = pair_work(
        factors,
        node + [mixed],
        node_labels,
        [(whole, far, far_at, 1, None)],
        rows,
    )
    (far_a,) = pair_work(
        factors,
        [mixed_other],
        node_labels,
        [(Block(0, half, "rounded", True), far, far_at, 1, far_g)],
        rows,
    )
    back_a = permute(far_a, middle)
    far_b, across_out, side_g, here_g = pair_work(
        factors,
        [mixed, mixed_other],
        node_labels,
        [
            (Block(half, rows - half, "rounded", True, False, 1), far, far_at, 1, far_g),
            (Block(0, rows, "rounded", True), across, across_at, 1, across_g),
            (more, after(side, far_a), side_at, 1, side_g),
            (more, glycans, here_at, 1, here_g),
        ],
        rows,
    )
    back_b = permute(far_b, middle)
    total_a = (scale * side_g[:half] + back_a.astype(jnp.float32)).astype(jnp.bfloat16)
    inside_a = permute(total_a, outward)
    across_back = permute(after(across_out, total_a), middle)
    back_b = after(back_b, total_a)
    total_b = (scale * side_g[half:] + back_b.astype(jnp.float32)).astype(jnp.bfloat16)
    inside_b = permute(total_b, outward)

    only_s = Block(0, rows, "", False, True)
    mine_s, other_s = pair_work(
        factors,
        node,
        node_labels,
        [
            (only_s, after(far, total_b), far_at, ~outer, None),
            (only_s, mixed, far_at, outer, None),
            (only_s, last_out, across_at, outer, None),
        ],
        rows,
        with_spectra="final",
        prior_s=own_s,
    )
    piece = -(-rows // 48) * 16
    others = [swap_inner(other_s[at : at + piece]) for at in range(0, rows, piece)]
    return finish(outer, factors, mine_s, here_g, across_back, inside_a, inside_b, others)


def local(
    mass_profile_vectors,
    sugar_tree_vectors,
    matching_glycan_rows,
    sharpness_factor,
    offset_shift_term,
):
    work = along_line if lax.axis_size("blk") == STEPS == LINE else around_ring
    return work(
        mass_profile_vectors,
        sugar_tree_vectors,
        matching_glycan_rows,
        sharpness_factor[0],
        offset_shift_term[0],
    )


def solution(mesh):
    placed = (
        P(("groups", "blk", "sub", "inner"), None),
        P(("groups", "blk", "sub", "inner"), None),
        P(("groups", "blk", "sub", "inner")),
        P(),
        P(),
    )
    return jax.shard_map(
        local,
        mesh=mesh,
        in_specs=placed,
        out_specs=(
            P(("groups", "blk", "sub", "inner"), None),
            P(("groups", "blk", "sub", "inner"), None),
        ),
        check_vma=False,
    )
```

```python
import dataclasses
import functools

import jax
import jax.numpy as jnp
from jax import lax
from jax.experimental import pallas as pl
from jax.experimental.pallas import tpu as pltpu
from jax.sharding import PartitionSpec as P

STEPS = 4
LINE = 4
LABEL_ROWS = 16
KEEP_ROW = 6
VMEM_BYTES = 20 * 1024 * 1024


def from_behind(block, axis, distance):
    devices = range(lax.axis_size(axis))
    route = [((i - distance) % len(devices), i) for i in devices]
    return lax.ppermute(block, axis, route)


def swap_inner(block):
    return from_behind(block, "inner", 1)


def after(value, *earlier):
    return lax.optimization_barrier((value,) + earlier)[0]


def coefficients(spectra, glycans, labels, first_target, scale, shift):
    logits = (
        scale
        * lax.dot_general(
            spectra, glycans, (((1,), (1,)), ((), ())), preferred_element_type=jnp.float32
        )
        + shift
    )
    targets = first_target + jnp.arange(glycans.shape[0], dtype=jnp.int32)
    positive = (labels[:, None] == targets[None, :]).astype(jnp.float32)
    return (jax.nn.sigmoid(logits) - positive).astype(jnp.bfloat16)


def around_ring(spectra, glycans, labels, scale, shift):
    rows_here = spectra.shape[0]
    node_rows = rows_here * lax.axis_size("inner")
    loop_count = lax.axis_size("blk")
    position = lax.axis_index("blk")
    core_first = lax.axis_index("sub") * node_rows + lax.axis_index("inner") * rows_here
    lane_rows = lax.axis_size("sub") * node_rows
    node_spectra = jnp.concatenate([spectra, swap_inner(spectra)])
    node_labels = jnp.concatenate([labels, swap_inner(labels)])
    spectrum_total = 0.0
    glycan_total = 0.0
    held = glycans
    for step in range(STEPS):
        if step > 0:
            held = from_behind(held, "blk", 1)
        first_target = (position - step) % loop_count * lane_rows + core_first
        coef = coefficients(node_spectra, held, node_labels, first_target, scale, shift)
        spectrum_total += jnp.dot(coef, held, preferred_element_type=jnp.float32)
        partial_value = scale * lax.dot_general(
            coef, node_spectra, (((0,), (0,)), ((), ())), preferred_element_type=jnp.float32
        )
        if step > 0:
            back = from_behind(partial_value.astype(jnp.bfloat16), "blk", -step)
            partial_value = back.astype(jnp.float32)
        glycan_total += partial_value
    other = swap_inner((scale * spectrum_total[rows_here:]).astype(jnp.bfloat16))
    spectrum_total = scale * spectrum_total[:rows_here] + other.astype(jnp.float32)
    return spectrum_total.astype(jnp.bfloat16), glycan_total.astype(jnp.bfloat16)


@dataclasses.dataclass(frozen=True)
class Block:
    first: int
    count: int
    out: str
    prior: str = ""
    optional: str = ""
    first_spectra: int = 0


def pair_body(plan, *refs):
    n_spectra, blocks, with_spectra, has_prior_s, rows, row_of = plan
    refs = list(refs)

    def take(count):
        taken = refs[:count]
        del refs[:count]
        return taken

    def take_if(condition):
        return take(1)[0] if condition else None

    consts, labels = take(2)
    flags = take_if(any(b.optional == "all" for b in blocks))
    spectra = take(n_spectra)
    held = take(len(blocks))
    priors = [take_if(b.prior) for b in blocks]
    prior_s = take_if(has_prior_s)
    outs = [take_if(b.out) for b in blocks]
    if with_spectra == "final":
        mine_out, other_out = take(2)
    elif with_spectra:
        (s_out,) = take(1)
    prior_held = [take_if(b.prior == "kept") for b in blocks]
    out_held = [take_if(b.out == "kept") for b in blocks]
    s_held = take_if(with_spectra)
    (sems,) = take(1)
    used = 0

    def move(source, target):
        nonlocal used
        copy = pltpu.make_async_copy(source, target, sems.at[used])
        copy.start()
        used += 1
        return copy

    moving = [
        move(priors[i].at[pl.ds(b.first, b.count)], prior_held[i]) if b.prior == "kept" else None
        for i, b in enumerate(blocks)
    ]
    moving_s = move(prior_s, s_held) if has_prior_s else None
    leaving = []

    def const(row):
        return consts[pl.ds(row, 1), pl.ds(0, 1)]

    scale, shift = const(0), const(1)
    row_labels = []
    for j in range(n_spectra):
        if spectra[j].shape[0] > rows:
            digits = spectra[j][pl.ds(rows, LABEL_ROWS), pl.ds(0, rows)].astype(jnp.float32)
            row_labels.append(digits[0:1] * 16384.0 + digits[1:2] * 128.0 + digits[2:3])
        else:
            row_labels.append(labels[:, pl.ds(j * rows, rows)])
    if has_prior_s:
        moving_s.wait()
    for i, block in enumerate(blocks):

        def work(i=i, block=block):
            where = pl.ds(block.first, block.count)
            glycans = held[i][where]
            targets = lax.broadcasted_iota(jnp.int32, (block.count, 1), 0).astype(jnp.float32)
            targets = targets + (const(row_of[i]) + float(block.first))
            total = None
            for j in range(block.first_spectra, n_spectra):
                here = spectra[j][pl.ds(0, rows)]
                logits = lax.dot_general(
                    glycans, here, (((1,), (1,)), ((), ())), preferred_element_type=jnp.float32
                )
                logits = scale * logits + shift
                positive = jnp.where(targets == row_labels[j], 1.0, 0.0)
                coef = jax.nn.sigmoid(logits) - positive
                masked = coef * const(KEEP_ROW) if block.optional == "spectra" else coef
                coef = coef.astype(jnp.bfloat16)
                if block.out:
                    part = jnp.dot(coef, here, preferred_element_type=jnp.float32)
                    total = part if total is None else total + part
                if with_spectra:
                    part = lax.dot_general(
                        masked.astype(jnp.bfloat16),
                        glycans,
                        (((0,), (0,)), ((), ())),
                        preferred_element_type=jnp.float32,
                    )
                    at = pl.ds(j * rows, rows)
                    if i > 0 or has_prior_s:
                        s_held[at] += part
                    else:
                        s_held[at] = part
            if block.prior == "kept":
                moving[i].wait()
                total = total + prior_held[i][...]
            elif block.prior:
                total = total + priors[i][where]
            if block.out == "kept":
                out_held[i][...] = total
                leaving.append(move(out_held[i], outs[i]))
            elif block.out == "total":
                outs[i][...] = total
            elif block.out == "scaled":
                outs[i][...] = scale * total
            elif block.out:
                outs[i][...] = (scale * total).astype(jnp.bfloat16)

        if block.optional == "all":
            pl.when(flags[i] != 0)(work)
        else:
            work()
    if with_spectra == "final":
        mine_out[...] = scale * s_held[pl.ds(0, rows)]
        other_out[...] = (scale * s_held[pl.ds(rows, rows)]).astype(jnp.bfloat16)
    elif with_spectra:
        leaving.append(move(s_held, s_out))
    for copy in leaving:
        copy.wait()


def in_vmem(array):
    return pltpu.with_memory_space_constraint(array, pltpu.VMEM)


def in_hbm(array):
    return pltpu.with_memory_space_constraint(array, pltpu.HBM)


def vmem_out(shape, kind):
    return pltpu.VMEM(shape, kind)


def hbm_out(shape, kind):
    return pltpu.HBM(shape, kind)


VMEM_SPEC = pl.BlockSpec(memory_space=pltpu.VMEM)
SMEM_SPEC = pl.BlockSpec(memory_space=pltpu.SMEM)
HBM_SPEC = pl.BlockSpec(memory_space=pltpu.HBM)
SMALL_COST = pl.CostEstimate(flops=1024, bytes_accessed=1024, transcendentals=0)


def params():
    return pltpu.CompilerParams(vmem_limit_bytes=VMEM_BYTES)


def pair_work(consts, spectra, labels, blocks, rows, with_spectra=False, prior_s=None):
    width = spectra[0].shape[1]
    all_rows = rows * len(spectra)
    shapes = tuple(b[0] for b in blocks)
    row_of = tuple(b[2] for b in blocks)
    plan = (len(spectra), shapes, with_spectra, prior_s is not None, rows, row_of)
    operands = [in_vmem(consts), in_vmem(labels)]
    in_specs = [VMEM_SPEC, VMEM_SPEC]
    if any(b.optional == "all" for b in shapes):
        operands.append(jnp.stack([jnp.int32(b[3]) for b in blocks]))
        in_specs.append(SMEM_SPEC)
    for array in list(spectra) + [b[1] for b in blocks]:
        operands.append(in_vmem(array))
        in_specs.append(VMEM_SPEC)
    for shape, _, _, _, prior in blocks:
        if shape.prior:
            operands.append(in_hbm(prior) if shape.prior == "kept" else in_vmem(prior))
            in_specs.append(HBM_SPEC if shape.prior == "kept" else VMEM_SPEC)
    if prior_s is not None:
        operands.append(in_hbm(prior_s))
        in_specs.append(HBM_SPEC)
    outs = []
    out_specs = []
    scratch = []
    for shape in shapes:
        if shape.prior == "kept":
            scratch.append(pltpu.VMEM((shape.count, width), jnp.float32))
    for shape in shapes:
        if shape.out == "kept":
            outs.append(hbm_out((shape.count, width), jnp.float32))
            out_specs.append(HBM_SPEC)
            scratch.append(pltpu.VMEM((shape.count, width), jnp.float32))
        elif shape.out:
            kind = jnp.bfloat16 if shape.out == "rounded" else jnp.float32
            outs.append(vmem_out((shape.count, width), kind))
            out_specs.append(VMEM_SPEC)
    if with_spectra == "final":
        outs.append(vmem_out((rows, width), jnp.float32))
        outs.append(vmem_out((rows, width), jnp.bfloat16))
        out_specs += [VMEM_SPEC, VMEM_SPEC]
    elif with_spectra:
        outs.append(hbm_out((all_rows, width), jnp.float32))
        out_specs.append(HBM_SPEC)
    if with_spectra:
        scratch.append(pltpu.VMEM((all_rows, width), jnp.float32))
    scratch.append(pltpu.SemaphoreType.DMA((2 * len(blocks) + 2,)))
    return pl.pallas_call(
        functools.partial(pair_body, plan),
        out_shape=outs,
        in_specs=in_specs,
        out_specs=out_specs,
        scratch_shapes=scratch,
        cost_estimate=SMALL_COST,
        compiler_params=params(),
    )(*operands)


def code_labels(labels, row_count, width):
    digits = jnp.stack([labels // 16384, labels // 128 % 128, labels % 128])
    spare = ((0, row_count - 3), (0, width - labels.shape[0]))
    return jnp.pad(digits.astype(jnp.bfloat16), spare)


def choose_body(flag, if_true, if_false, tail, out):
    rows = if_true.shape[0]

    @pl.when(flag[0] != 0)
    def _():
        out[pl.ds(0, rows)] = if_true[...]

    @pl.when(flag[0] == 0)
    def _():
        out[pl.ds(0, rows)] = if_false[...]

    out[pl.ds(rows, tail.shape[0])] = tail[...]


def choose(flag, if_true, if_false, tail):
    rows, width = if_true.shape
    return pl.pallas_call(
        choose_body,
        out_shape=vmem_out((rows + tail.shape[0], width), if_true.dtype),
        in_specs=[SMEM_SPEC] + [VMEM_SPEC] * 3,
        out_specs=VMEM_SPEC,
        cost_estimate=SMALL_COST,
        compiler_params=params(),
    )(jnp.int32(flag).reshape(1), in_vmem(if_true), in_vmem(if_false), in_vmem(tail))


def add_body(first, total, arrived, out):
    where = pl.ds(first, out.shape[0])
    out[...] = (total[where] + arrived[...].astype(jnp.float32)).astype(jnp.bfloat16)


def add_rounded(total, first, arrived):
    return pl.pallas_call(
        functools.partial(add_body, first),
        out_shape=vmem_out(arrived.shape, jnp.bfloat16),
        in_specs=[VMEM_SPEC] * 2,
        out_specs=VMEM_SPEC,
        cost_estimate=SMALL_COST,
        compiler_params=params(),
    )(in_vmem(total), in_vmem(arrived))


def finish_body(flag, mine_s, here_total, across_back, inside_a, inside_b, *rest):
    others, (spectra_out, glycans_out) = rest[:-2], rest[-2:]
    at = 0
    for other in others:
        where = pl.ds(at, other.shape[0])
        spectra_out[where] = (mine_s[where] + other[...].astype(jnp.float32)).astype(jnp.bfloat16)
        at += other.shape[0]

    @pl.when(flag[0] != 0)
    def _():
        glycans_out[pl.ds(0, inside_a.shape[0])] = inside_a[...]
        glycans_out[pl.ds(inside_a.shape[0], inside_b.shape[0])] = inside_b[...]

    @pl.when(flag[0] == 0)
    def _():
        total = here_total[...] + across_back[...].astype(jnp.float32)
        glycans_out[...] = total.astype(jnp.bfloat16)


def finish(flag, mine_s, here_total, across_back, inside_a, inside_b, others):
    arrays = [mine_s, here_total, across_back, inside_a, inside_b] + others
    out = jax.ShapeDtypeStruct(mine_s.shape, jnp.bfloat16)
    return pl.pallas_call(
        finish_body,
        out_shape=[out, out],
        in_specs=[SMEM_SPEC] + [VMEM_SPEC] * len(arrays),
        out_specs=[VMEM_SPEC, VMEM_SPEC],
        cost_estimate=SMALL_COST,
        compiler_params=params(),
    )(jnp.int32(flag).reshape(1), *[in_vmem(a) for a in arrays])


def along_line(spectra, glycans, labels, scale, shift):
    rows, width = spectra.shape
    first_part = rows // 2 + 16
    node_rows = rows * lax.axis_size("inner")
    position = lax.axis_index("blk")
    outer = (position == 0) | (position == LINE - 1)
    core_first = lax.axis_index("sub") * node_rows + lax.axis_index("inner") * rows
    lane_rows = lax.axis_size("sub") * node_rows

    def permute(block, pairs):
        return lax.ppermute(block, "blk", pairs)

    def first_of(block_position):
        return (block_position * lane_rows + core_first).astype(jnp.float32)

    sides = [(0, 1), (1, 0), (2, 3), (3, 2)]
    middle = [(1, 2), (2, 1), (0, 0), (3, 3)]
    here_at, side_at, across_at, far_at = 2, 3, 4, 5
    rows_of_consts = [
        scale,
        shift,
        first_of(position),
        first_of(position ^ 1),
        first_of(LINE - 1 - position),
        first_of((LINE - 1 - position) ^ 1),
        jnp.where(outer, 0.0, 1.0),
    ]
    index = lax.broadcasted_iota(jnp.int32, (8, 128), 0)
    consts = jnp.zeros((8, 128), jnp.float32)
    for i, value in enumerate(rows_of_consts):
        consts = jnp.where(index == i, value, consts)

    across = permute(glycans, middle)
    side = permute(glycans, sides)
    partner = swap_inner(spectra)
    own_labels = labels.reshape(1, rows)
    node_labels = jnp.concatenate([own_labels, swap_inner(own_labels)], axis=1)
    node_labels = node_labels.astype(jnp.float32)
    node = [spectra, partner]
    kept = Block(0, rows, "kept")
    here_g, own_s = pair_work(
        consts, node, node_labels, [(kept, glycans, here_at, 1, None)], rows, with_spectra=True
    )

    coded = code_labels(labels, LABEL_ROWS, width)
    side = after(side, here_g)
    far = permute(side, middle)
    across = after(across, side)
    mixed = permute(choose(outer, spectra, across, coded), sides)
    side_g, across_g, own_s = pair_work(
        consts,
        node,
        node_labels,
        [
            (kept, side, side_at, 1, None),
            (Block(0, rows, "kept", optional="spectra"), across, across_at, 1, None),
        ],
        rows,
        with_spectra=True,
        prior_s=own_s,
    )

    mixed, far = lax.optimization_barrier((mixed, far, own_s))[:2]
    mixed_other = swap_inner(mixed)
    last_out = permute(far, sides)
    (far_g,) = pair_work(
        consts,
        node + [mixed],
        node_labels,
        [(Block(0, rows, "total"), far, far_at, 1, None)],
        rows,
    )
    (far_a,) = pair_work(
        consts,
        [mixed_other],
        node_labels,
        [(Block(0, first_part, "rounded", "near"), far, far_at, 1, far_g)],
        rows,
    )
    back_a = permute(far_a, middle)
    ends = [mixed, mixed_other]
    far_b, across_out = pair_work(
        consts,
        ends,
        node_labels,
        [
            (Block(first_part, rows - first_part, "rounded", "near", first_spectra=1), after(far, far_a), far_at, 1, far_g),
            (Block(0, rows, "rounded", "kept"), across, across_at, 1, across_g),
        ],
        rows,
    )
    back_b = permute(far_b, middle)
    side_total, here_total = pair_work(
        consts,
        ends,
        node_labels,
        [
            (Block(0, rows, "scaled", "kept"), after(side, far_b), side_at, 1, side_g),
            (Block(0, rows, "scaled", "kept"), glycans, here_at, 1, here_g),
        ],
        rows,
    )
    total_a = add_rounded(side_total, 0, back_a)
    inside_a = permute(total_a, sides)
    across_back = permute(after(across_out, total_a), middle)
    total_b = add_rounded(side_total, first_part, after(back_b, total_a))
    inside_b = permute(total_b, sides)

    only_s = Block(0, rows, "", optional="all")
    mine_s, other_s = pair_work(
        consts,
        node,
        node_labels,
        [
            (only_s, after(far, total_b), far_at, ~outer, None),
            (only_s, mixed, far_at, outer, None),
            (only_s, last_out, across_at, outer, None),
        ],
        rows,
        with_spectra="final",
        prior_s=own_s,
    )
    piece = -(-rows // 48) * 16
    others = [swap_inner(other_s[at : at + piece]) for at in range(0, rows, piece)]
    return finish(outer, mine_s, here_total, across_back, inside_a, inside_b, others)


def local(
    mass_profile_vectors,
    sugar_tree_vectors,
    matching_glycan_rows,
    sharpness_factor,
    offset_shift_term,
):
    work = along_line if lax.axis_size("blk") == STEPS == LINE else around_ring
    return work(
        mass_profile_vectors,
        sugar_tree_vectors,
        matching_glycan_rows,
        sharpness_factor[0],
        offset_shift_term[0],
    )


def solution(mesh):
    placed = (
        P(("groups", "blk", "sub", "inner"), None),
        P(("groups", "blk", "sub", "inner"), None),
        P(("groups", "blk", "sub", "inner")),
        P(),
        P(),
    )
    return jax.shard_map(
        local,
        mesh=mesh,
        in_specs=placed,
        out_specs=(
            P(("groups", "blk", "sub", "inner"), None),
            P(("groups", "blk", "sub", "inner"), None),
        ),
        check_vma=False,
    )
```

```python
import dataclasses
import functools

import jax
import jax.numpy as jnp
from jax import lax
from jax.experimental import pallas as pl
from jax.experimental.pallas import tpu as pltpu
from jax.sharding import PartitionSpec as P

STEPS = 4
LINE = 4
LABEL_ROWS = 16
KEEP_ROW = 6
VMEM_BYTES = 20 * 1024 * 1024


def from_behind(block, axis, distance):
    devices = range(lax.axis_size(axis))
    route = [((i - distance) % len(devices), i) for i in devices]
    return lax.ppermute(block, axis, route)


def swap_inner(block):
    return from_behind(block, "inner", 1)


def after(value, *earlier):
    return lax.optimization_barrier((value,) + earlier)[0]


def coefficients(spectra, glycans, labels, first_target, scale, shift):
    logits = (
        scale
        * lax.dot_general(
            spectra, glycans, (((1,), (1,)), ((), ())), preferred_element_type=jnp.float32
        )
        + shift
    )
    targets = first_target + jnp.arange(glycans.shape[0], dtype=jnp.int32)
    positive = (labels[:, None] == targets[None, :]).astype(jnp.float32)
    return (jax.nn.sigmoid(logits) - positive).astype(jnp.bfloat16)


def around_ring(spectra, glycans, labels, scale, shift):
    rows_here = spectra.shape[0]
    node_rows = rows_here * lax.axis_size("inner")
    loop_count = lax.axis_size("blk")
    position = lax.axis_index("blk")
    core_first = lax.axis_index("sub") * node_rows + lax.axis_index("inner") * rows_here
    lane_rows = lax.axis_size("sub") * node_rows
    node_spectra = jnp.concatenate([spectra, swap_inner(spectra)])
    node_labels = jnp.concatenate([labels, swap_inner(labels)])
    spectrum_total = 0.0
    glycan_total = 0.0
    held = glycans
    for step in range(STEPS):
        if step > 0:
            held = from_behind(held, "blk", 1)
        first_target = (position - step) % loop_count * lane_rows + core_first
        coef = coefficients(node_spectra, held, node_labels, first_target, scale, shift)
        spectrum_total += jnp.dot(coef, held, preferred_element_type=jnp.float32)
        partial_value = scale * lax.dot_general(
            coef, node_spectra, (((0,), (0,)), ((), ())), preferred_element_type=jnp.float32
        )
        if step > 0:
            back = from_behind(partial_value.astype(jnp.bfloat16), "blk", -step)
            partial_value = back.astype(jnp.float32)
        glycan_total += partial_value
    other = swap_inner((scale * spectrum_total[rows_here:]).astype(jnp.bfloat16))
    spectrum_total = scale * spectrum_total[:rows_here] + other.astype(jnp.float32)
    return spectrum_total.astype(jnp.bfloat16), glycan_total.astype(jnp.bfloat16)


@dataclasses.dataclass(frozen=True)
class Block:
    first: int
    count: int
    out: str
    prior: str = ""
    optional: str = ""
    first_spectra: int = 0


@dataclasses.dataclass(frozen=True)
class Away:
    array: jax.Array


def pair_body(plan, *refs):
    blocks, with_spectra, has_prior_s, rows, row_of, away = plan
    n_spectra = len(away) - len(blocks)
    refs = list(refs)

    def take(count):
        taken = refs[:count]
        del refs[:count]
        return taken

    def take_if(condition):
        return take(1)[0] if condition else None

    consts, labels = take(2)
    flags = take_if(any(b.optional == "all" for b in blocks))
    spectra = take(n_spectra)
    held = take(len(blocks))
    priors = [take_if(b.prior) for b in blocks]
    prior_s = take_if(has_prior_s)
    outs = [take_if(b.out) for b in blocks]
    if with_spectra == "final":
        mine_out, other_out = take(2)
    elif with_spectra:
        (s_out,) = take(1)
    prior_held = [take_if(b.prior == "kept") for b in blocks]
    out_held = [take_if(b.out.startswith("kept")) for b in blocks]
    s_held = take_if(with_spectra)
    near = [take_if(flag) for flag in away]
    (sems,) = take(1)
    used = 0

    def move(source, target):
        nonlocal used
        copy = pltpu.make_async_copy(source, target, sems.at[used])
        copy.start()
        used += 1
        return copy

    arriving = [None] * len(away)
    for j in range(n_spectra):
        if away[j]:
            arriving[j] = move(spectra[j], near[j])
            spectra[j] = near[j]
    for i, b in enumerate(blocks):
        if away[n_spectra + i]:
            arriving[n_spectra + i] = move(held[i].at[pl.ds(b.first, b.count)], near[n_spectra + i])

    def arrive(at):
        if arriving[at] is not None:
            arriving[at].wait()
            arriving[at] = None

    moving = [
        move(priors[i].at[pl.ds(b.first, b.count)], prior_held[i]) if b.prior == "kept" else None
        for i, b in enumerate(blocks)
    ]
    moving_s = move(prior_s, s_held) if has_prior_s else None
    leaving = []

    def const(row):
        return consts[pl.ds(row, 1), pl.ds(0, 1)]

    scale, shift = const(0), const(1)
    row_labels = []
    plain = 0
    for j in range(n_spectra):
        if spectra[j].shape[0] > rows:
            digits = spectra[j][pl.ds(rows, LABEL_ROWS), pl.ds(0, rows)].astype(jnp.float32)
            row_labels.append(digits[0:1] * 16384.0 + digits[1:2] * 128.0 + digits[2:3])
        else:
            row_labels.append(labels[:, pl.ds(plain * rows, rows)])
            plain += 1
    if with_spectra == "final":
        for at in range(len(away)):
            arrive(at)
        moving_s.wait()
    for i, block in enumerate(blocks):

        def work(i=i, block=block):
            where = pl.ds(block.first, block.count)
            arrive(n_spectra + i)
            glycans = near[n_spectra + i][...] if away[n_spectra + i] else held[i][where]
            targets = lax.broadcasted_iota(jnp.int32, (block.count, 1), 0).astype(jnp.float32)
            targets = targets + (const(row_of[i]) + float(block.first))
            total = None
            for j in range(block.first_spectra, n_spectra):
                arrive(j)
                here = spectra[j][pl.ds(0, rows)]
                logits = lax.dot_general(
                    glycans, here, (((1,), (1,)), ((), ())), preferred_element_type=jnp.float32
                )
                logits = scale * logits + shift
                positive = jnp.where(targets == row_labels[j], 1.0, 0.0)
                coef = jax.nn.sigmoid(logits) - positive
                masked = coef * const(KEEP_ROW) if block.optional == "spectra" else coef
                coef = coef.astype(jnp.bfloat16)
                if block.out:
                    part = jnp.dot(coef, here, preferred_element_type=jnp.float32)
                    total = part if total is None else total + part
                if with_spectra:
                    part = lax.dot_general(
                        masked.astype(jnp.bfloat16),
                        glycans,
                        (((0,), (0,)), ((), ())),
                        preferred_element_type=jnp.float32,
                    )
                    at = pl.ds(j * rows, rows)
                    if i == 0 and j == 0 and with_spectra != "final" and has_prior_s:
                        moving_s.wait()
                    if i > 0 or has_prior_s:
                        s_held[at] += part
                    else:
                        s_held[at] = part
            if block.prior == "kept":
                moving[i].wait()
                total = total + prior_held[i][...]
            elif block.prior:
                total = total + priors[i][where]
            if block.out in ("kept", "kept scaled"):
                out_held[i][...] = scale * total if block.out == "kept scaled" else total
                leaving.append(move(out_held[i], outs[i]))
            elif block.out == "total":
                outs[i][...] = total
            elif block.out == "scaled":
                outs[i][...] = scale * total
            elif block.out:
                outs[i][...] = (scale * total).astype(jnp.bfloat16)

        if block.optional == "all":
            pl.when(flags[i] != 0)(work)
        else:
            work()
    if with_spectra == "final":
        mine_out[...] = scale * s_held[pl.ds(0, rows)]
        other_out[...] = (scale * s_held[pl.ds(rows, rows)]).astype(jnp.bfloat16)
    elif with_spectra:
        leaving.append(move(s_held, s_out))
    for copy in leaving:
        copy.wait()


def in_vmem(array):
    return pltpu.with_memory_space_constraint(array, pltpu.VMEM)


def in_hbm(array):
    return pltpu.with_memory_space_constraint(array, pltpu.HBM)


def vmem_out(shape, kind):
    return pltpu.VMEM(shape, kind)


def hbm_out(shape, kind):
    return pltpu.HBM(shape, kind)


VMEM_SPEC = pl.BlockSpec(memory_space=pltpu.VMEM)
SMEM_SPEC = pl.BlockSpec(memory_space=pltpu.SMEM)
HBM_SPEC = pl.BlockSpec(memory_space=pltpu.HBM)
SMALL_COST = pl.CostEstimate(flops=1024, bytes_accessed=1024, transcendentals=0)


def params():
    return pltpu.CompilerParams(vmem_limit_bytes=VMEM_BYTES)


def pair_work(
    consts, spectra, labels, blocks, rows, with_spectra=False, prior_s=None, cost=SMALL_COST
):
    placed = list(spectra) + [b[1] for b in blocks]
    away = tuple(isinstance(a, Away) for a in placed)
    placed = [a.array if isinstance(a, Away) else a for a in placed]
    width = placed[0].shape[1]
    all_rows = rows * len(spectra)
    shapes = tuple(b[0] for b in blocks)
    row_of = tuple(b[2] for b in blocks)
    plan = (shapes, with_spectra, prior_s is not None, rows, row_of, away)
    operands = [in_vmem(consts), in_vmem(labels)]
    in_specs = [VMEM_SPEC, VMEM_SPEC]
    if any(b.optional == "all" for b in shapes):
        operands.append(jnp.stack([jnp.int32(b[3]) for b in blocks]))
        in_specs.append(SMEM_SPEC)
    for array, flag in zip(placed, away):
        operands.append(in_hbm(array) if flag else in_vmem(array))
        in_specs.append(HBM_SPEC if flag else VMEM_SPEC)
    for shape, _, _, _, prior in blocks:
        if shape.prior:
            operands.append(in_hbm(prior) if shape.prior == "kept" else in_vmem(prior))
            in_specs.append(HBM_SPEC if shape.prior == "kept" else VMEM_SPEC)
    if prior_s is not None:
        operands.append(in_hbm(prior_s))
        in_specs.append(HBM_SPEC)
    outs = []
    out_specs = []
    scratch = []
    for shape in shapes:
        if shape.prior == "kept":
            scratch.append(pltpu.VMEM((shape.count, width), jnp.float32))
    for shape in shapes:
        if shape.out.startswith("kept"):
            outs.append(hbm_out((shape.count, width), jnp.float32))
            out_specs.append(HBM_SPEC)
            scratch.append(pltpu.VMEM((shape.count, width), jnp.float32))
        elif shape.out:
            kind = jnp.bfloat16 if shape.out == "rounded" else jnp.float32
            outs.append(vmem_out((shape.count, width), kind))
            out_specs.append(VMEM_SPEC)
    if with_spectra == "final":
        outs.append(vmem_out((rows, width), jnp.float32))
        outs.append(vmem_out((rows, width), jnp.bfloat16))
        out_specs += [VMEM_SPEC, VMEM_SPEC]
    elif with_spectra:
        outs.append(hbm_out((all_rows, width), jnp.float32))
        out_specs.append(HBM_SPEC)
    if with_spectra:
        scratch.append(pltpu.VMEM((all_rows, width), jnp.float32))
    counts = [rows] * len(spectra) + [shape.count for shape in shapes]
    scratch += [pltpu.VMEM((n, width), jnp.bfloat16) for n, flag in zip(counts, away) if flag]
    scratch.append(pltpu.SemaphoreType.DMA((len(away) + 2 * len(blocks) + 2,)))
    return pl.pallas_call(
        functools.partial(pair_body, plan),
        out_shape=outs,
        in_specs=in_specs,
        out_specs=out_specs,
        scratch_shapes=scratch,
        cost_estimate=cost,
        compiler_params=params(),
    )(*operands)


def code_labels(labels, row_count, width):
    digits = jnp.stack([labels // 16384, labels // 128 % 128, labels % 128])
    spare = ((0, row_count - 3), (0, width - labels.shape[0]))
    return jnp.pad(digits.astype(jnp.bfloat16), spare)


def choose_body(flag, if_true, if_false, tail, out, sem):
    rows = if_true.shape[0]

    @pl.when(flag[0] != 0)
    def _():
        copy = pltpu.make_async_copy(if_true, out.at[pl.ds(0, rows)], sem)
        copy.start()
        copy.wait()

    @pl.when(flag[0] == 0)
    def _():
        out[pl.ds(0, rows)] = if_false[...]

    out[pl.ds(rows, tail.shape[0])] = tail[...]


def choose(flag, if_true, if_false, tail):
    rows, width = if_true.shape
    return pl.pallas_call(
        choose_body,
        out_shape=vmem_out((rows + tail.shape[0], width), if_true.dtype),
        in_specs=[SMEM_SPEC, HBM_SPEC, VMEM_SPEC, VMEM_SPEC],
        out_specs=VMEM_SPEC,
        scratch_shapes=[pltpu.SemaphoreType.DMA],
        cost_estimate=SMALL_COST,
        compiler_params=params(),
    )(jnp.int32(flag).reshape(1), in_hbm(if_true), in_vmem(if_false), in_vmem(tail))


def add_body(total, arrived, out, *scratch):
    if scratch:
        near, sem = scratch
        copy = pltpu.make_async_copy(total, near, sem)
        copy.start()
        copy.wait()
        total = near
    out[...] = (total[...] + arrived[...].astype(jnp.float32)).astype(jnp.bfloat16)


def add_rounded(total, arrived):
    away = isinstance(total, Away)
    scratch = [pltpu.VMEM(arrived.shape, jnp.float32), pltpu.SemaphoreType.DMA] if away else []
    return pl.pallas_call(
        add_body,
        out_shape=vmem_out(arrived.shape, jnp.bfloat16),
        in_specs=[HBM_SPEC if away else VMEM_SPEC, VMEM_SPEC],
        out_specs=VMEM_SPEC,
        scratch_shapes=scratch,
        cost_estimate=SMALL_COST,
        compiler_params=params(),
    )(in_hbm(total.array) if away else in_vmem(total), in_vmem(arrived))


def finish_spectra_body(mine_s, *rest):
    others, out = rest[:-1], rest[-1]
    at = 0
    for other in others:
        where = pl.ds(at, other.shape[0])
        out[where] = (mine_s[where] + other[...].astype(jnp.float32)).astype(jnp.bfloat16)
        at += other.shape[0]


def finish_spectra(mine_s, others):
    return pl.pallas_call(
        finish_spectra_body,
        out_shape=jax.ShapeDtypeStruct(mine_s.shape, jnp.bfloat16),
        in_specs=[VMEM_SPEC] * (1 + len(others)),
        out_specs=VMEM_SPEC,
        cost_estimate=SMALL_COST,
        compiler_params=params(),
    )(*[in_vmem(a) for a in [mine_s] + others])


def finish_structures_body(flag, here_total, across_back, inside_a, inside_b, out):
    @pl.when(flag[0] != 0)
    def _():
        out[pl.ds(0, inside_a.shape[0])] = inside_a[...]
        out[pl.ds(inside_a.shape[0], inside_b.shape[0])] = inside_b[...]

    @pl.when(flag[0] == 0)
    def _():
        total = here_total[...] + across_back[...].astype(jnp.float32)
        out[...] = total.astype(jnp.bfloat16)


def finish_structures(flag, here_total, across_back, inside_a, inside_b):
    arrays = [here_total, across_back, inside_a, inside_b]
    return pl.pallas_call(
        finish_structures_body,
        out_shape=jax.ShapeDtypeStruct(here_total.shape, jnp.bfloat16),
        in_specs=[SMEM_SPEC] + [VMEM_SPEC] * len(arrays),
        out_specs=VMEM_SPEC,
        cost_estimate=SMALL_COST,
        compiler_params=params(),
    )(jnp.int32(flag).reshape(1), *[in_vmem(a) for a in arrays])


def along_line(spectra, glycans, labels, scale, shift):
    rows, width = spectra.shape
    first_part = rows // 2 + 16
    node_rows = rows * lax.axis_size("inner")
    position = lax.axis_index("blk")
    outer = (position == 0) | (position == LINE - 1)
    core_first = lax.axis_index("sub") * node_rows + lax.axis_index("inner") * rows
    lane_rows = lax.axis_size("sub") * node_rows

    def permute(block, pairs):
        return lax.ppermute(block, ("blk", "inner"), pairs)

    def first_of(block_position):
        return (block_position * lane_rows + core_first).astype(jnp.float32)

    n_inner = lax.axis_size("inner")
    last = LINE - 1
    sides = []
    middle = []
    for core in range(n_inner):
        for at in range(LINE):
            sides.append((at * n_inner + core, (at ^ 1) * n_inner + core))
        for at in range(1, last):
            middle.append((at * n_inner + core, (last - at) * n_inner + core))
        for at in (0, last):
            middle.append((at * n_inner + core, at * n_inner + (core + 1) % n_inner))
    here_at, side_at, across_at, far_at = 2, 3, 4, 5
    rows_of_consts = [
        scale,
        shift,
        first_of(position),
        first_of(position ^ 1),
        first_of(last - position),
        first_of((last - position) ^ 1),
        jnp.where(outer, 0.0, 1.0),
    ]
    index = lax.broadcasted_iota(jnp.int32, (8, 128), 0)
    consts = jnp.zeros((8, 128), jnp.float32)
    for i, value in enumerate(rows_of_consts):
        consts = jnp.where(index == i, value, consts)

    across = permute(glycans, middle)
    side = permute(glycans, sides)
    partner = swap_inner(spectra)
    own_labels = labels.reshape(1, rows)
    partner_labels = swap_inner(own_labels).astype(jnp.float32)
    own_labels = own_labels.astype(jnp.float32)
    node_labels = jnp.concatenate([own_labels, partner_labels], axis=1)
    other_first_labels = jnp.concatenate([partner_labels, own_labels], axis=1)
    node = [Away(spectra), partner]
    mine = Away(glycans)
    kept = Block(0, rows, "kept")
    here_g, own_s = pair_work(
        consts, node, node_labels, [(kept, mine, here_at, 1, None)], rows, with_spectra=True
    )

    coded = code_labels(labels, LABEL_ROWS, width)
    side = after(side, here_g)
    far = permute(side, middle)
    across = after(across, side)
    mixed = permute(choose(outer, spectra, across, coded), sides)
    side_g, across_g, own_s = pair_work(
        consts,
        node,
        node_labels,
        [
            (kept, Away(side), side_at, 1, None),
            (Block(0, rows, "kept", optional="spectra"), across, across_at, 1, None),
        ],
        rows,
        with_spectra=True,
        prior_s=own_s,
    )

    mixed, far = lax.optimization_barrier((mixed, far, own_s))[:2]
    mixed_other = swap_inner(mixed)
    last_out = permute(far, sides)
    (far_g,) = pair_work(
        consts,
        [mixed, partner, Away(spectra)],
        other_first_labels,
        [(Block(0, rows, "total"), far, far_at, 1, None)],
        rows,
    )
    (far_a,) = pair_work(
        consts,
        [mixed_other],
        node_labels,
        [(Block(0, first_part, "rounded", "near"), far, far_at, 1, far_g)],
        rows,
    )
    back_a = permute(far_a, middle)
    ends = [mixed, mixed_other]
    far_b, across_out = pair_work(
        consts,
        ends,
        node_labels,
        [
            (
                Block(first_part, rows - first_part, "rounded", "near", first_spectra=1),
                after(far, far_a),
                far_at,
                1,
                far_g,
            ),
            (Block(0, rows, "rounded", "kept"), across, across_at, 1, across_g),
        ],
        rows,
    )
    back_b = permute(far_b, middle)
    late_side = Away(after(side, far_b))
    side_total_a, side_total_b = pair_work(
        consts,
        ends,
        node_labels,
        [
            (Block(0, first_part, "scaled", "kept"), late_side, side_at, 1, side_g),
            (
                Block(first_part, rows - first_part, "kept scaled", "kept"),
                late_side,
                side_at,
                1,
                side_g,
            ),
        ],
        rows,
    )
    total_a = add_rounded(side_total_a, back_a)
    inside_a = permute(total_a, sides)
    across_back = permute(after(across_out, total_a), middle)
    total_b = add_rounded(Away(side_total_b), after(back_b, total_a))
    inside_b = permute(total_b, sides)

    only_s = Block(0, rows, "", optional="all")
    mine_s, other_s = pair_work(
        consts,
        node,
        node_labels,
        [
            (only_s, after(far, total_b), far_at, ~outer, None),
            (only_s, mixed, far_at, outer, None),
            (only_s, last_out, across_at, outer, None),
        ],
        rows,
        with_spectra="final",
        prior_s=own_s,
    )
    piece = -(-rows // 48) * 16
    others = [swap_inner(other_s[at : at + piece]) for at in range(0, rows, piece)]
    inside_a, late_mine = lax.optimization_barrier((inside_a, glycans))
    flops = 2 * 2 * 2 * rows * rows * width
    (here_total,) = pair_work(
        consts,
        ends,
        node_labels,
        [(Block(0, rows, "scaled", "kept"), Away(late_mine), here_at, 1, here_g)],
        rows,
        cost=pl.CostEstimate(flops=flops, bytes_accessed=8 * rows * width, transcendentals=0),
    )
    others[0] = after(others[0], inside_b, here_total)
    grad_spectra = finish_spectra(mine_s, others)
    across_back = after(across_back, grad_spectra)
    return grad_spectra, finish_structures(outer, here_total, across_back, inside_a, inside_b)


def local(
    mass_profile_vectors,
    sugar_tree_vectors,
    matching_glycan_rows,
    sharpness_factor,
    offset_shift_term,
):
    work = along_line if lax.axis_size("blk") == STEPS == LINE else around_ring
    return work(
        mass_profile_vectors,
        sugar_tree_vectors,
        matching_glycan_rows,
        sharpness_factor[0],
        offset_shift_term[0],
    )


def solution(mesh):
    placed = (
        P(("groups", "blk", "sub", "inner"), None),
        P(("groups", "blk", "sub", "inner"), None),
        P(("groups", "blk", "sub", "inner")),
        P(),
        P(),
    )
    return jax.shard_map(
        local,
        mesh=mesh,
        in_specs=placed,
        out_specs=(
            P(("groups", "blk", "sub", "inner"), None),
            P(("groups", "blk", "sub", "inner"), None),
        ),
        check_vma=False,
    )
```

```python
import dataclasses
import functools

import jax
import jax.numpy as jnp
from jax import lax
from jax.experimental import pallas as pl
from jax.experimental.pallas import tpu as pltpu
from jax.sharding import PartitionSpec as P

STEPS = 4
LINE = 4
LABEL_ROWS = 16
KEEP_ROW = 6
VMEM_BYTES = 20 * 1024 * 1024


def from_behind(block, axis, distance):
    devices = range(lax.axis_size(axis))
    route = [((i - distance) % len(devices), i) for i in devices]
    return lax.ppermute(block, axis, route)


def swap_inner(block):
    return from_behind(block, "inner", 1)


def after(value, *earlier):
    return lax.optimization_barrier((value,) + earlier)[0]


def coefficients(spectra, glycans, labels, first_target, scale, shift):
    logits = (
        scale
        * lax.dot_general(
            spectra, glycans, (((1,), (1,)), ((), ())), preferred_element_type=jnp.float32
        )
        + shift
    )
    targets = first_target + jnp.arange(glycans.shape[0], dtype=jnp.int32)
    positive = (labels[:, None] == targets[None, :]).astype(jnp.float32)
    return (jax.nn.sigmoid(logits) - positive).astype(jnp.bfloat16)


def around_ring(spectra, glycans, labels, scale, shift):
    rows_here = spectra.shape[0]
    node_rows = rows_here * lax.axis_size("inner")
    loop_count = lax.axis_size("blk")
    position = lax.axis_index("blk")
    core_first = lax.axis_index("sub") * node_rows + lax.axis_index("inner") * rows_here
    lane_rows = lax.axis_size("sub") * node_rows
    node_spectra = jnp.concatenate([spectra, swap_inner(spectra)])
    node_labels = jnp.concatenate([labels, swap_inner(labels)])
    spectrum_total = 0.0
    glycan_total = 0.0
    held = glycans
    for step in range(STEPS):
        if step > 0:
            held = from_behind(held, "blk", 1)
        first_target = (position - step) % loop_count * lane_rows + core_first
        coef = coefficients(node_spectra, held, node_labels, first_target, scale, shift)
        spectrum_total += jnp.dot(coef, held, preferred_element_type=jnp.float32)
        partial_value = scale * lax.dot_general(
            coef, node_spectra, (((0,), (0,)), ((), ())), preferred_element_type=jnp.float32
        )
        if step > 0:
            back = from_behind(partial_value.astype(jnp.bfloat16), "blk", -step)
            partial_value = back.astype(jnp.float32)
        glycan_total += partial_value
    other = swap_inner((scale * spectrum_total[rows_here:]).astype(jnp.bfloat16))
    spectrum_total = scale * spectrum_total[:rows_here] + other.astype(jnp.float32)
    return spectrum_total.astype(jnp.bfloat16), glycan_total.astype(jnp.bfloat16)


@dataclasses.dataclass(frozen=True)
class Away:
    array: jax.Array


@dataclasses.dataclass(frozen=True)
class Block:
    target: int
    uses: tuple
    out: str
    start: int = 0
    count: int = 0
    prior: str = ""
    optional: str = ""


@dataclasses.dataclass(frozen=True)
class Plan:
    blocks: tuple
    pieces: tuple
    node: bool
    ends: tuple
    gradient: str
    prior_s: bool
    rows: int


def pair_body(plan, *refs):
    refs = list(refs)
    blocks, rows = plan.blocks, plan.rows
    half = rows // 2

    def take(count):
        taken = refs[:count]
        del refs[:count]
        return taken

    def take_if(condition):
        return take(1)[0] if condition else None

    (consts,) = take(1)
    labels = take_if(plan.node)
    flags = take_if(any(b.optional == "all" for b in blocks))
    node_in = take(2) if plan.node else []
    ends_in = take(len(plan.ends))
    held_in = [take(len(p)) for p in plan.pieces]
    priors = [take_if(b.prior) for b in blocks]
    prior_s = take_if(plan.prior_s)
    outs = [take((b.out != "") + (b.out == "split")) for b in blocks]
    if plan.gradient == "final":
        mine_out, other_out = take(2)
    elif plan.gradient:
        (s_out,) = take(1)
    spectra = take_if(plan.node)
    ends = take_if(plan.ends)
    held = take(len(blocks))
    prior_held = [take_if(b.prior == "kept") for b in blocks]
    out_held = [take_if(b.out in ("kept", "split")) for b in blocks]
    s_held = take_if(plan.gradient)
    (sems,) = take(1)
    used = 0

    def move(source, target):
        nonlocal used
        copy = pltpu.make_async_copy(source, target, sems.at[used])
        copy.start()
        used += 1
        return copy

    moving_node = [move(ref, spectra.at[pl.ds(i * rows, rows)]) for i, ref in enumerate(node_in)]
    moving = []
    for i, block in enumerate(blocks):
        moves = []
        at = 0
        for ref, (count, away) in zip(held_in[i], plan.pieces[i]):
            if away:
                part = ref.at[pl.ds(block.start, count)]
                moves.append(move(part, held[i].at[pl.ds(at, count)]))
            at += count
        moving.append(moves)
    moving_prior = [
        move(priors[i], prior_held[i]) if b.prior == "kept" else None for i, b in enumerate(blocks)
    ]
    moving_s = move(prior_s, s_held) if plan.prior_s else None
    leaving = []

    def const(row):
        return consts[pl.ds(row, 1), pl.ds(0, 1)]

    scale, shift = const(0), const(1)
    if plan.ends:
        width = 2 * rows
        at = 0
        coded = []
        for ref, count in zip(ends_in, plan.ends):
            ending = at % rows + count > rows
            keep = count - LABEL_ROWS if ending else count
            ends[pl.ds(at, keep)] = ref[pl.ds(0, keep)]
            at += keep
            if ending:
                digits = ref[pl.ds(keep, LABEL_ROWS), pl.ds(0, width)].astype(jnp.float32)
                coded.append(digits[0:1] * 16384.0 + digits[1:2] * 128.0 + digits[2:3])
        lane = lax.broadcasted_iota(jnp.int32, (1, width), 1)
        end_labels = jnp.where(lane >= rows, coded[1], coded[0])

    def source(use):
        if use == "node":
            while moving_node:
                moving_node.pop(0).wait()
            return spectra[...], labels[...]
        return ends[...], end_labels

    if plan.gradient == "final":
        for copy in moving_node + [c for moves in moving for c in moves] + [moving_s]:
            copy.wait()
        moving_node, moving, moving_s = [], [[] for _ in blocks], None
    for i, block in enumerate(blocks):

        def work(i=i, block=block):
            nonlocal moving_s
            at = 0
            for ref, (count, away) in zip(held_in[i], plan.pieces[i]):
                if not away:
                    held[i][pl.ds(at, count)] = ref[pl.ds(block.start, count)]
                at += count
            for copy in moving[i]:
                copy.wait()
            glycans = held[i][...]
            targets = lax.broadcasted_iota(jnp.int32, (glycans.shape[0], 1), 0)
            targets = targets.astype(jnp.float32) + (const(block.target) + float(block.start))
            total = None
            for use in block.uses:
                here, row_labels = source(use)
                logits = lax.dot_general(
                    glycans, here, (((1,), (1,)), ((), ())), preferred_element_type=jnp.float32
                )
                logits = scale * logits + shift
                positive = jnp.where(targets == row_labels, 1.0, 0.0)
                coef = jax.nn.sigmoid(logits) - positive
                masked = coef * const(KEEP_ROW) if block.optional == "spectra" else coef
                coef = coef.astype(jnp.bfloat16)
                if block.out:
                    part = jnp.dot(coef, here, preferred_element_type=jnp.float32)
                    total = part if total is None else total + part
                if plan.gradient:
                    part = lax.dot_general(
                        masked.astype(jnp.bfloat16),
                        glycans,
                        (((0,), (0,)), ((), ())),
                        preferred_element_type=jnp.float32,
                    )
                    if moving_s is not None:
                        moving_s.wait()
                        moving_s = None
                    if i > 0 or plan.prior_s:
                        s_held[...] += part
                    else:
                        s_held[...] = part
            if block.prior == "kept":
                moving_prior[i].wait()
                total = total + prior_held[i][...]
            elif block.prior:
                total = total + priors[i][...]
            if block.out == "kept":
                out_held[i][...] = total
                leaving.append(move(out_held[i], outs[i][0]))
            elif block.out == "split":
                outs[i][0][...] = scale * total[:half]
                out_held[i][...] = scale * total[half:]
                leaving.append(move(out_held[i], outs[i][1]))
            elif block.out == "total":
                outs[i][0][...] = total
            elif block.out == "scaled":
                outs[i][0][...] = scale * total
            elif block.out:
                outs[i][0][...] = (scale * total).astype(jnp.bfloat16)

        if block.optional == "all":
            if block.prior == "kept":
                moving_prior[i].wait()
                moving_prior[i] = Waited()
                for copy in moving[i]:
                    copy.wait()
                moving[i] = []
            pl.when(flags[i] != 0)(work)
        else:
            work()
    if plan.gradient == "final":
        mine_out[...] = scale * s_held[pl.ds(0, rows)]
        other_out[...] = (scale * s_held[pl.ds(rows, rows)]).astype(jnp.bfloat16)
    elif plan.gradient:
        leaving.append(move(s_held, s_out))
    for copy in leaving:
        copy.wait()


class Waited:
    def wait(self):
        pass


def in_vmem(array):
    return pltpu.with_memory_space_constraint(array, pltpu.VMEM)


def in_hbm(array):
    return pltpu.with_memory_space_constraint(array, pltpu.HBM)


def vmem_out(shape, kind):
    return pltpu.VMEM(shape, kind)


def hbm_out(shape, kind):
    return pltpu.HBM(shape, kind)


VMEM_SPEC = pl.BlockSpec(memory_space=pltpu.VMEM)
SMEM_SPEC = pl.BlockSpec(memory_space=pltpu.SMEM)
HBM_SPEC = pl.BlockSpec(memory_space=pltpu.HBM)
SMALL_COST = pl.CostEstimate(flops=1024, bytes_accessed=1024, transcendentals=0)


def params():
    return pltpu.CompilerParams(vmem_limit_bytes=VMEM_BYTES)


def pair_work(consts, blocks, rows, labels=None, node=None, ends=None, gradient="", prior_s=None, cost=SMALL_COST):
    half = rows // 2
    shapes = tuple(b[0] for b in blocks)
    pieces = []
    arrays = []
    for shape, array, _, _ in blocks:
        parts = array if isinstance(array, tuple) else (array,)
        away = [isinstance(x, Away) for x in parts]
        parts = [x.array if flag else x for x, flag in zip(parts, away)]
        pieces.append(tuple((shape.count or x.shape[0], flag) for x, flag in zip(parts, away)))
        arrays += list(zip(parts, away))
    width = arrays[0][0].shape[1]
    ends = ends or ()
    end_rows = tuple(x.shape[0] for x in ends)
    plan = Plan(shapes, tuple(pieces), node is not None, end_rows, gradient, prior_s is not None, rows)

    operands = [in_vmem(consts)]
    in_specs = [VMEM_SPEC]

    def give(array, away):
        operands.append(in_hbm(array) if away else in_vmem(array))
        in_specs.append(HBM_SPEC if away else VMEM_SPEC)

    if node is not None:
        give(labels, False)
    if any(b.optional == "all" for b in shapes):
        operands.append(jnp.stack([jnp.int32(b[2]) for b in blocks]))
        in_specs.append(SMEM_SPEC)
    for array in node or ():
        give(array, True)
    for array in ends:
        give(array, False)
    for array, away in arrays:
        give(array, away)
    for shape, _, _, prior in blocks:
        if shape.prior:
            give(prior, shape.prior == "kept")
    if prior_s is not None:
        give(prior_s, True)

    counts = [sum(count for count, _ in p) for p in pieces]
    outs = []
    out_specs = []

    def get(shape, kind, away):
        outs.append((hbm_out if away else vmem_out)(shape, kind))
        out_specs.append(HBM_SPEC if away else VMEM_SPEC)

    for shape, count in zip(shapes, counts):
        if shape.out == "split":
            get((half, width), jnp.float32, False)
            get((half, width), jnp.float32, True)
        elif shape.out:
            kind = jnp.bfloat16 if shape.out == "rounded" else jnp.float32
            get((count, width), kind, shape.out == "kept")
    if gradient == "final":
        get((rows, width), jnp.float32, False)
        get((rows, width), jnp.bfloat16, False)
    elif gradient:
        get((2 * rows, width), jnp.float32, True)

    scratch = []
    if node is not None:
        scratch.append(pltpu.VMEM((2 * rows, width), jnp.bfloat16))
    if ends:
        scratch.append(pltpu.VMEM((2 * rows, width), jnp.bfloat16))
    scratch += [pltpu.VMEM((n, width), jnp.bfloat16) for n in counts]
    scratch += [pltpu.VMEM((n, width), jnp.float32) for n, b in zip(counts, shapes) if b.prior == "kept"]
    for n, b in zip(counts, shapes):
        if b.out in ("kept", "split"):
            scratch.append(pltpu.VMEM((n if b.out == "kept" else half, width), jnp.float32))
    if gradient:
        scratch.append(pltpu.VMEM((2 * rows, width), jnp.float32))
    scratch.append(pltpu.SemaphoreType.DMA((len(operands) + len(outs),)))
    return pl.pallas_call(
        functools.partial(pair_body, plan),
        out_shape=outs,
        in_specs=in_specs,
        out_specs=out_specs,
        scratch_shapes=scratch,
        cost_estimate=cost,
        compiler_params=params(),
    )(*operands)


def code_labels(labels, row_count, width):
    digits = jnp.stack([labels // 16384, labels // 128 % 128, labels % 128]).astype(jnp.bfloat16)
    digits = jnp.concatenate([digits, digits, digits], axis=1)
    return jnp.pad(digits, ((0, row_count - 3), (0, width - digits.shape[1])))


def add_body(total, arrived, out, *scratch):
    if scratch:
        near, sem = scratch
        copy = pltpu.make_async_copy(total, near, sem)
        copy.start()
        copy.wait()
        total = near
    out[...] = (total[...] + arrived[...].astype(jnp.float32)).astype(jnp.bfloat16)


def add_rounded(total, arrived):
    away = isinstance(total, Away)
    scratch = [pltpu.VMEM(arrived.shape, jnp.float32), pltpu.SemaphoreType.DMA] if away else []
    return pl.pallas_call(
        add_body,
        out_shape=vmem_out(arrived.shape, jnp.bfloat16),
        in_specs=[HBM_SPEC if away else VMEM_SPEC, VMEM_SPEC],
        out_specs=VMEM_SPEC,
        scratch_shapes=scratch,
        cost_estimate=SMALL_COST,
        compiler_params=params(),
    )(in_hbm(total.array) if away else in_vmem(total), in_vmem(arrived))


def finish_spectra_body(mine_s, *rest):
    others, out = rest[:-1], rest[-1]
    at = 0
    for other in others:
        where = pl.ds(at, other.shape[0])
        out[where] = (mine_s[where] + other[...].astype(jnp.float32)).astype(jnp.bfloat16)
        at += other.shape[0]


def finish_spectra(mine_s, others):
    return pl.pallas_call(
        finish_spectra_body,
        out_shape=jax.ShapeDtypeStruct(mine_s.shape, jnp.bfloat16),
        in_specs=[VMEM_SPEC] * (1 + len(others)),
        out_specs=VMEM_SPEC,
        cost_estimate=SMALL_COST,
        compiler_params=params(),
    )(*[in_vmem(a) for a in [mine_s] + others])


def finish_structures_body(flag, here_total, across_back, inside_a, inside_b, out):
    @pl.when(flag[0] != 0)
    def _():
        out[pl.ds(0, inside_a.shape[0])] = inside_a[...]
        out[pl.ds(inside_a.shape[0], inside_b.shape[0])] = inside_b[...]

    @pl.when(flag[0] == 0)
    def _():
        total = here_total[...] + across_back[...].astype(jnp.float32)
        out[...] = total.astype(jnp.bfloat16)


def finish_structures(flag, here_total, across_back, inside_a, inside_b):
    arrays = [here_total, across_back, inside_a, inside_b]
    return pl.pallas_call(
        finish_structures_body,
        out_shape=jax.ShapeDtypeStruct(here_total.shape, jnp.bfloat16),
        in_specs=[SMEM_SPEC] + [VMEM_SPEC] * len(arrays),
        out_specs=VMEM_SPEC,
        cost_estimate=SMALL_COST,
        compiler_params=params(),
    )(jnp.int32(flag).reshape(1), *[in_vmem(a) for a in arrays])


def along_line(spectra, glycans, labels, scale, shift):
    rows, width = spectra.shape
    half = rows // 2
    node_rows = rows * lax.axis_size("inner")
    position = lax.axis_index("blk")
    outer = (position == 0) | (position == LINE - 1)
    core_first = lax.axis_index("sub") * node_rows + lax.axis_index("inner") * rows
    lane_rows = lax.axis_size("sub") * node_rows

    def permute(block, pairs):
        return lax.ppermute(block, ("blk", "inner"), pairs)

    def first_of(block_position):
        return (block_position * lane_rows + core_first).astype(jnp.float32)

    n_inner = lax.axis_size("inner")
    last = LINE - 1
    sides = []
    middle = []
    inward = []
    for core in range(n_inner):
        inward += [(core, n_inner + core), (last * n_inner + core, (last - 1) * n_inner + core)]
        for at in range(LINE):
            sides.append((at * n_inner + core, (at ^ 1) * n_inner + core))
        for at in range(1, last):
            middle.append((at * n_inner + core, (last - at) * n_inner + core))
        for at in (0, last):
            middle.append((at * n_inner + core, at * n_inner + (core + 1) % n_inner))
    here_at, side_at, across_at, far_at = 2, 3, 4, 5
    rows_of_consts = [
        scale,
        shift,
        first_of(position),
        first_of(position ^ 1),
        first_of(last - position),
        first_of((last - position) ^ 1),
        jnp.where(outer, 0.0, 1.0),
    ]
    index = lax.broadcasted_iota(jnp.int32, (8, 128), 0)
    consts = jnp.zeros((8, 128), jnp.float32)
    for i, value in enumerate(rows_of_consts):
        consts = jnp.where(index == i, value, consts)

    def in_thirds(block):
        piece = -(-block.shape[0] // 48) * 16
        return tuple(swap_inner(block[at : at + piece]) for at in range(0, block.shape[0], piece))

    across = permute(glycans, middle)
    side = permute(glycans, sides)
    end_mine = permute(jnp.concatenate([spectra, code_labels(labels, LABEL_ROWS, width)]), inward)
    partner = swap_inner(spectra)
    own_labels = labels.reshape(1, rows)
    node_labels = jnp.concatenate([own_labels, swap_inner(own_labels)], axis=1)
    node_labels = node_labels.astype(jnp.float32)
    node = dict(node=(spectra, partner), labels=node_labels)
    here_g, own_s = pair_work(
        consts,
        [(Block(here_at, ("node",), "kept"), Away(glycans), 1, None)],
        rows,
        gradient="part",
        **node,
    )

    side = after(side, here_g)
    far = permute(side, middle)
    across = after(across, side)
    next_out = tuple(permute(across[at : at + half], sides) for at in (0, half))
    side_g, across_g, own_s = pair_work(
        consts,
        [
            (Block(side_at, ("node",), "kept"), Away(side), 1, None),
            (Block(across_at, ("node",), "kept", optional="spectra"), across, 1, None),
        ],
        rows,
        gradient="part",
        prior_s=own_s,
        **node,
    )
    end_mine = after(end_mine, own_s)
    ends = (end_mine,) + in_thirds(end_mine)

    far, *next_out = lax.optimization_barrier((far,) + next_out + (own_s,))[:3]
    last_out = permute(far, sides)
    (far_a,) = pair_work(
        consts,
        [(Block(far_at, ("node", "ends"), "rounded", 0, half), far, 1, None)],
        rows,
        ends=ends,
        **node,
    )
    back_a = permute(far_a, middle)
    far_b, across_out = pair_work(
        consts,
        [
            (
                Block(far_at, ("node", "ends"), "rounded", half, half),
                after(far, far_a),
                1,
                None,
            ),
            (Block(across_at, ("ends",), "rounded", prior="kept"), across, 1, across_g),
        ],
        rows,
        ends=ends,
        **node,
    )
    back_b = permute(far_b, middle)
    side_total_a, side_total_b = pair_work(
        consts,
        [
            (
                Block(side_at, ("ends",), "split", prior="kept"),
                Away(after(side, far_b)),
                1,
                side_g,
            )
        ],
        rows,
        ends=ends,
    )
    total_a = add_rounded(side_total_a, back_a)
    inside_a = permute(total_a, sides)
    across_back = permute(after(across_out, total_a), middle)
    total_b = add_rounded(Away(side_total_b), after(back_b, total_a))
    inside_b = permute(total_b, sides)

    def only_s(target):
        return Block(target, ("node",), "", optional="all")

    mine_s, other_s = pair_work(
        consts,
        [
            (only_s(far_at), after(far, total_b), ~outer, None),
            (only_s(far_at), tuple(next_out), outer, None),
            (only_s(across_at), last_out, outer, None),
        ],
        rows,
        gradient="final",
        prior_s=own_s,
        **node,
    )
    others = list(in_thirds(other_s))
    inside_a, late_mine = lax.optimization_barrier((inside_a, glycans))
    flops = 2 * 2 * 2 * rows * rows * width
    (here_total,) = pair_work(
        consts,
        [
            (
                Block(here_at, ("ends",), "scaled", prior="kept", optional="all"),
                Away(late_mine),
                ~outer,
                here_g,
            )
        ],
        rows,
        ends=ends,
        cost=pl.CostEstimate(flops=flops, bytes_accessed=8 * rows * width, transcendentals=0),
    )
    others[0] = after(others[0], inside_b, here_total)
    grad_spectra = finish_spectra(mine_s, others)
    across_back = after(across_back, grad_spectra)
    return grad_spectra, finish_structures(outer, here_total, across_back, inside_a, inside_b)


def local(
    mass_profile_vectors,
    sugar_tree_vectors,
    matching_glycan_rows,
    sharpness_factor,
    offset_shift_term,
):
    work = along_line if lax.axis_size("blk") == STEPS == LINE else around_ring
    return work(
        mass_profile_vectors,
        sugar_tree_vectors,
        matching_glycan_rows,
        sharpness_factor[0],
        offset_shift_term[0],
    )


def solution(mesh):
    placed = (
        P(("groups", "blk", "sub", "inner"), None),
        P(("groups", "blk", "sub", "inner"), None),
        P(("groups", "blk", "sub", "inner")),
        P(),
        P(),
    )
    return jax.shard_map(
        local,
        mesh=mesh,
        in_specs=placed,
        out_specs=(
            P(("groups", "blk", "sub", "inner"), None),
            P(("groups", "blk", "sub", "inner"), None),
        ),
        check_vma=False,
    )
```

```python
import dataclasses
import functools

import jax
import jax.numpy as jnp
from jax import lax
from jax.experimental import pallas as pl
from jax.experimental.pallas import tpu as pltpu
from jax.sharding import PartitionSpec as P

STEPS = 4
LINE = 4
LABEL_ROWS = 16
KEEP_ROW = 6
VMEM_BYTES = 20 * 1024 * 1024


def from_behind(block, axis, distance):
    devices = range(lax.axis_size(axis))
    route = [((i - distance) % len(devices), i) for i in devices]
    return lax.ppermute(block, axis, route)


def swap_inner(block):
    return from_behind(block, "inner", 1)


def after(value, *earlier):
    return lax.optimization_barrier((value,) + earlier)[0]


def coefficients(spectra, glycans, labels, first_target, scale, shift):
    logits = (
        scale
        * lax.dot_general(
            spectra, glycans, (((1,), (1,)), ((), ())), preferred_element_type=jnp.float32
        )
        + shift
    )
    targets = first_target + jnp.arange(glycans.shape[0], dtype=jnp.int32)
    positive = (labels[:, None] == targets[None, :]).astype(jnp.float32)
    return (jax.nn.sigmoid(logits) - positive).astype(jnp.bfloat16)


def around_ring(spectra, glycans, labels, scale, shift):
    rows_here = spectra.shape[0]
    node_rows = rows_here * lax.axis_size("inner")
    loop_count = lax.axis_size("blk")
    position = lax.axis_index("blk")
    core_first = lax.axis_index("sub") * node_rows + lax.axis_index("inner") * rows_here
    lane_rows = lax.axis_size("sub") * node_rows
    node_spectra = jnp.concatenate([spectra, swap_inner(spectra)])
    node_labels = jnp.concatenate([labels, swap_inner(labels)])
    spectrum_total = 0.0
    glycan_total = 0.0
    held = glycans
    for step in range(STEPS):
        if step > 0:
            held = from_behind(held, "blk", 1)
        first_target = (position - step) % loop_count * lane_rows + core_first
        coef = coefficients(node_spectra, held, node_labels, first_target, scale, shift)
        spectrum_total += jnp.dot(coef, held, preferred_element_type=jnp.float32)
        partial_value = scale * lax.dot_general(
            coef, node_spectra, (((0,), (0,)), ((), ())), preferred_element_type=jnp.float32
        )
        if step > 0:
            back = from_behind(partial_value.astype(jnp.bfloat16), "blk", -step)
            partial_value = back.astype(jnp.float32)
        glycan_total += partial_value
    other = swap_inner((scale * spectrum_total[rows_here:]).astype(jnp.bfloat16))
    spectrum_total = scale * spectrum_total[:rows_here] + other.astype(jnp.float32)
    return spectrum_total.astype(jnp.bfloat16), glycan_total.astype(jnp.bfloat16)


@dataclasses.dataclass(frozen=True)
class Away:
    array: jax.Array


@dataclasses.dataclass(frozen=True)
class Block:
    target: int
    uses: tuple
    out: str
    start: int = 0
    count: int = 0
    prior: str = ""
    optional: str = ""


@dataclasses.dataclass(frozen=True)
class Plan:
    blocks: tuple
    pieces: tuple
    node: bool
    ends: tuple
    gradient: str
    prior_s: bool
    rows: int


def pair_body(plan, *refs):
    refs = list(refs)
    blocks, rows = plan.blocks, plan.rows
    half = rows // 2

    def take(count):
        taken = refs[:count]
        del refs[:count]
        return taken

    def take_if(condition):
        return take(1)[0] if condition else None

    (consts,) = take(1)
    labels = take_if(plan.node)
    flags = take_if(any(b.optional == "all" for b in blocks))
    node_in = take(2) if plan.node else []
    ends_in = take(len(plan.ends))
    held_in = [take(len(p)) for p in plan.pieces]
    priors = [take_if(b.prior) for b in blocks]
    prior_s = take_if(plan.prior_s)
    outs = [take((b.out != "") + (b.out == "split")) for b in blocks]
    if plan.gradient == "final":
        mine_out, other_out = take(2)
    elif plan.gradient:
        (s_out,) = take(1)
    spectra = take_if(plan.node)
    ends = take_if(plan.ends)
    held = take(len(blocks))
    prior_held = [take_if(b.prior == "kept") for b in blocks]
    out_held = [take_if(b.out in ("kept", "split")) for b in blocks]
    s_held = take_if(plan.gradient)
    (sems,) = take(1)
    used = 0

    def move(source, target):
        nonlocal used
        copy = pltpu.make_async_copy(source, target, sems.at[used])
        copy.start()
        used += 1
        return copy

    moving_node = [move(ref, spectra.at[pl.ds(i * rows, rows)]) for i, ref in enumerate(node_in)]
    moving = []
    for i, block in enumerate(blocks):
        moves = []
        at = 0
        for ref, (count, away) in zip(held_in[i], plan.pieces[i]):
            if away:
                part = ref.at[pl.ds(block.start, count)]
                moves.append(move(part, held[i].at[pl.ds(at, count)]))
            at += count
        moving.append(moves)
    moving_prior = [
        move(priors[i], prior_held[i]) if b.prior == "kept" else None for i, b in enumerate(blocks)
    ]
    moving_s = move(prior_s, s_held) if plan.prior_s else None
    leaving = []

    def const(row):
        return consts[pl.ds(row, 1), pl.ds(0, 1)]

    scale, shift = const(0), const(1)
    if plan.ends:
        width = 2 * rows
        at = 0
        coded = []
        for ref, count in zip(ends_in, plan.ends):
            ending = at % rows + count > rows
            keep = count - LABEL_ROWS if ending else count
            ends[pl.ds(at, keep)] = ref[pl.ds(0, keep)]
            at += keep
            if ending:
                digits = ref[pl.ds(keep, LABEL_ROWS), pl.ds(0, width)].astype(jnp.float32)
                coded.append(digits[0:1] * 16384.0 + digits[1:2] * 128.0 + digits[2:3])
        lane = lax.broadcasted_iota(jnp.int32, (1, width), 1)
        end_labels = jnp.where(lane >= rows, coded[1], coded[0])

    def source(use):
        if use == "node":
            while moving_node:
                moving_node.pop(0).wait()
            return spectra[...], labels[...]
        return ends[...], end_labels

    if plan.gradient == "final":
        for copy in moving_node + [c for moves in moving for c in moves] + [moving_s]:
            copy.wait()
        moving_node, moving, moving_s = [], [[] for _ in blocks], None
    for i, block in enumerate(blocks):

        def work(i=i, block=block):
            nonlocal moving_s
            at = 0
            for ref, (count, away) in zip(held_in[i], plan.pieces[i]):
                if not away:
                    held[i][pl.ds(at, count)] = ref[pl.ds(block.start, count)]
                at += count
            for copy in moving[i]:
                copy.wait()
            glycans = held[i][...]
            targets = lax.broadcasted_iota(jnp.int32, (glycans.shape[0], 1), 0)
            targets = targets.astype(jnp.float32) + (const(block.target) + float(block.start))
            total = None
            for use in block.uses:
                here, row_labels = source(use)
                logits = lax.dot_general(
                    glycans, here, (((1,), (1,)), ((), ())), preferred_element_type=jnp.float32
                )
                logits = scale * logits + shift
                positive = jnp.where(targets == row_labels, 1.0, 0.0)
                coef = jax.nn.sigmoid(logits) - positive
                masked = coef * const(KEEP_ROW) if block.optional == "spectra" else coef
                coef = coef.astype(jnp.bfloat16)
                if block.out:
                    part = jnp.dot(coef, here, preferred_element_type=jnp.float32)
                    total = part if total is None else total + part
                if plan.gradient:
                    part = lax.dot_general(
                        masked.astype(jnp.bfloat16),
                        glycans,
                        (((0,), (0,)), ((), ())),
                        preferred_element_type=jnp.float32,
                    )
                    if moving_s is not None:
                        moving_s.wait()
                        moving_s = None
                    if i > 0 or plan.prior_s:
                        s_held[...] += part
                    else:
                        s_held[...] = part
            if block.prior == "kept":
                moving_prior[i].wait()
                total = total + prior_held[i][...]
            elif block.prior:
                total = total + priors[i][...]
            if block.out == "kept":
                out_held[i][...] = total
                leaving.append(move(out_held[i], outs[i][0]))
            elif block.out == "split":
                outs[i][0][...] = scale * total[:half]
                out_held[i][...] = scale * total[half:]
                leaving.append(move(out_held[i], outs[i][1]))
            elif block.out == "total":
                outs[i][0][...] = total
            elif block.out == "scaled":
                outs[i][0][...] = scale * total
            elif block.out:
                outs[i][0][...] = (scale * total).astype(jnp.bfloat16)

        if block.optional == "all":
            if block.prior == "kept":
                moving_prior[i].wait()
                moving_prior[i] = Waited()
                for copy in moving[i]:
                    copy.wait()
                moving[i] = []
            pl.when(flags[i] != 0)(work)
        else:
            work()
    if plan.gradient == "final":
        mine_out[...] = scale * s_held[pl.ds(0, rows)]
        other_out[...] = (scale * s_held[pl.ds(rows, rows)]).astype(jnp.bfloat16)
    elif plan.gradient:
        leaving.append(move(s_held, s_out))
    for copy in leaving:
        copy.wait()


class Waited:
    def wait(self):
        pass


def in_vmem(array):
    return pltpu.with_memory_space_constraint(array, pltpu.VMEM)


def in_hbm(array):
    return pltpu.with_memory_space_constraint(array, pltpu.HBM)


def vmem_out(shape, kind):
    return pltpu.VMEM(shape, kind)


def hbm_out(shape, kind):
    return pltpu.HBM(shape, kind)


VMEM_SPEC = pl.BlockSpec(memory_space=pltpu.VMEM)
SMEM_SPEC = pl.BlockSpec(memory_space=pltpu.SMEM)
HBM_SPEC = pl.BlockSpec(memory_space=pltpu.HBM)
SMALL_COST = pl.CostEstimate(flops=1024, bytes_accessed=1024, transcendentals=0)


def params():
    return pltpu.CompilerParams(vmem_limit_bytes=VMEM_BYTES)


def pair_work(consts, blocks, rows, labels=None, node=None, ends=None, gradient="", prior_s=None, cost=SMALL_COST):
    half = rows // 2
    shapes = tuple(b[0] for b in blocks)
    pieces = []
    arrays = []
    for shape, array, _, _ in blocks:
        parts = array if isinstance(array, tuple) else (array,)
        away = [isinstance(x, Away) for x in parts]
        parts = [x.array if flag else x for x, flag in zip(parts, away)]
        pieces.append(tuple((shape.count or x.shape[0], flag) for x, flag in zip(parts, away)))
        arrays += list(zip(parts, away))
    width = arrays[0][0].shape[1]
    ends = ends or ()
    end_rows = tuple(x.shape[0] for x in ends)
    plan = Plan(shapes, tuple(pieces), node is not None, end_rows, gradient, prior_s is not None, rows)

    operands = [in_vmem(consts)]
    in_specs = [VMEM_SPEC]

    def give(array, away):
        operands.append(in_hbm(array) if away else in_vmem(array))
        in_specs.append(HBM_SPEC if away else VMEM_SPEC)

    if node is not None:
        give(labels, False)
    if any(b.optional == "all" for b in shapes):
        operands.append(jnp.stack([jnp.int32(b[2]) for b in blocks]))
        in_specs.append(SMEM_SPEC)
    for array in node or ():
        give(array, True)
    for array in ends:
        give(array, False)
    for array, away in arrays:
        give(array, away)
    for shape, _, _, prior in blocks:
        if shape.prior:
            give(prior, shape.prior == "kept")
    if prior_s is not None:
        give(prior_s, True)

    counts = [sum(count for count, _ in p) for p in pieces]
    outs = []
    out_specs = []

    def get(shape, kind, away):
        outs.append((hbm_out if away else vmem_out)(shape, kind))
        out_specs.append(HBM_SPEC if away else VMEM_SPEC)

    for shape, count in zip(shapes, counts):
        if shape.out == "split":
            get((half, width), jnp.float32, False)
            get((half, width), jnp.float32, True)
        elif shape.out:
            kind = jnp.bfloat16 if shape.out == "rounded" else jnp.float32
            get((count, width), kind, shape.out == "kept")
    if gradient == "final":
        get((rows, width), jnp.float32, False)
        get((rows, width), jnp.bfloat16, False)
    elif gradient:
        get((2 * rows, width), jnp.float32, True)

    scratch = []
    if node is not None:
        scratch.append(pltpu.VMEM((2 * rows, width), jnp.bfloat16))
    if ends:
        scratch.append(pltpu.VMEM((2 * rows, width), jnp.bfloat16))
    scratch += [pltpu.VMEM((n, width), jnp.bfloat16) for n in counts]
    scratch += [pltpu.VMEM((n, width), jnp.float32) for n, b in zip(counts, shapes) if b.prior == "kept"]
    for n, b in zip(counts, shapes):
        if b.out in ("kept", "split"):
            scratch.append(pltpu.VMEM((n if b.out == "kept" else half, width), jnp.float32))
    if gradient:
        scratch.append(pltpu.VMEM((2 * rows, width), jnp.float32))
    scratch.append(pltpu.SemaphoreType.DMA((len(operands) + len(outs),)))
    return pl.pallas_call(
        functools.partial(pair_body, plan),
        out_shape=outs,
        in_specs=in_specs,
        out_specs=out_specs,
        scratch_shapes=scratch,
        cost_estimate=cost,
        compiler_params=params(),
    )(*operands)


def code_labels(labels, row_count, width):
    digits = jnp.stack([labels // 16384, labels // 128 % 128, labels % 128]).astype(jnp.bfloat16)
    digits = jnp.concatenate([digits, digits, digits], axis=1)
    return jnp.pad(digits, ((0, row_count - 3), (0, width - digits.shape[1])))


def add_body(total, arrived, out, *scratch):
    if scratch:
        near, sem = scratch
        copy = pltpu.make_async_copy(total, near, sem)
        copy.start()
        copy.wait()
        total = near
    out[...] = (total[...] + arrived[...].astype(jnp.float32)).astype(jnp.bfloat16)


def add_rounded(total, arrived):
    away = isinstance(total, Away)
    scratch = [pltpu.VMEM(arrived.shape, jnp.float32), pltpu.SemaphoreType.DMA] if away else []
    return pl.pallas_call(
        add_body,
        out_shape=vmem_out(arrived.shape, jnp.bfloat16),
        in_specs=[HBM_SPEC if away else VMEM_SPEC, VMEM_SPEC],
        out_specs=VMEM_SPEC,
        scratch_shapes=scratch,
        cost_estimate=SMALL_COST,
        compiler_params=params(),
    )(in_hbm(total.array) if away else in_vmem(total), in_vmem(arrived))


def finish_spectra_body(mine_s, *rest):
    others, out = rest[:-1], rest[-1]
    at = 0
    for other in others:
        where = pl.ds(at, other.shape[0])
        out[where] = (mine_s[where] + other[...].astype(jnp.float32)).astype(jnp.bfloat16)
        at += other.shape[0]


def finish_spectra(mine_s, others):
    return pl.pallas_call(
        finish_spectra_body,
        out_shape=jax.ShapeDtypeStruct(mine_s.shape, jnp.bfloat16),
        in_specs=[VMEM_SPEC] * (1 + len(others)),
        out_specs=VMEM_SPEC,
        cost_estimate=SMALL_COST,
        compiler_params=params(),
    )(*[in_vmem(a) for a in [mine_s] + others])


def finish_structures_body(flag, here_total, across_back, inside_a, inside_b, out):
    @pl.when(flag[0] != 0)
    def _():
        out[pl.ds(0, inside_a.shape[0])] = inside_a[...]
        out[pl.ds(inside_a.shape[0], inside_b.shape[0])] = inside_b[...]

    @pl.when(flag[0] == 0)
    def _():
        total = here_total[...] + across_back[...].astype(jnp.float32)
        out[...] = total.astype(jnp.bfloat16)


def finish_structures(flag, here_total, across_back, inside_a, inside_b):
    arrays = [here_total, across_back, inside_a, inside_b]
    return pl.pallas_call(
        finish_structures_body,
        out_shape=jax.ShapeDtypeStruct(here_total.shape, jnp.bfloat16),
        in_specs=[SMEM_SPEC] + [VMEM_SPEC] * len(arrays),
        out_specs=VMEM_SPEC,
        cost_estimate=SMALL_COST,
        compiler_params=params(),
    )(jnp.int32(flag).reshape(1), *[in_vmem(a) for a in arrays])


def along_line(spectra, glycans, labels, scale, shift):
    rows, width = spectra.shape
    half = rows // 2
    node_rows = rows * lax.axis_size("inner")
    position = lax.axis_index("blk")
    outer = (position == 0) | (position == LINE - 1)
    core_first = lax.axis_index("sub") * node_rows + lax.axis_index("inner") * rows
    lane_rows = lax.axis_size("sub") * node_rows

    def permute(block, pairs):
        return lax.ppermute(block, ("blk", "inner"), pairs)

    def first_of(block_position):
        return (block_position * lane_rows + core_first).astype(jnp.float32)

    n_inner = lax.axis_size("inner")
    last = LINE - 1
    sides = []
    middle = []
    inward = []
    outward = []
    for core in range(n_inner):
        inward += [(core, n_inner + core), (last * n_inner + core, (last - 1) * n_inner + core)]
        outward += [(n_inner + core, core), ((last - 1) * n_inner + core, last * n_inner + core)]
        for at in range(LINE):
            sides.append((at * n_inner + core, (at ^ 1) * n_inner + core))
        for at in range(1, last):
            middle.append((at * n_inner + core, (last - at) * n_inner + core))
        for at in (0, last):
            middle.append((at * n_inner + core, at * n_inner + (core + 1) % n_inner))
    here_at, side_at, across_at, far_at = 2, 3, 4, 5
    rows_of_consts = [
        scale,
        shift,
        first_of(position),
        first_of(position ^ 1),
        first_of(last - position),
        first_of((last - position) ^ 1),
        jnp.where(outer, 0.0, 1.0),
    ]
    index = lax.broadcasted_iota(jnp.int32, (8, 128), 0)
    consts = jnp.zeros((8, 128), jnp.float32)
    for i, value in enumerate(rows_of_consts):
        consts = jnp.where(index == i, value, consts)

    def in_thirds(block):
        piece = -(-block.shape[0] // 48) * 16
        return tuple(swap_inner(block[at : at + piece]) for at in range(0, block.shape[0], piece))

    across = permute(glycans, middle)
    side = permute(glycans, sides)
    end_mine = permute(jnp.concatenate([spectra, code_labels(labels, LABEL_ROWS, width)]), inward)
    partner = swap_inner(spectra)
    own_labels = labels.reshape(1, rows)
    node_labels = jnp.concatenate([own_labels, swap_inner(own_labels)], axis=1)
    node_labels = node_labels.astype(jnp.float32)
    node = dict(node=(spectra, partner), labels=node_labels)
    here_g, own_s = pair_work(
        consts,
        [(Block(here_at, ("node",), "kept"), Away(glycans), 1, None)],
        rows,
        gradient="part",
        **node,
    )

    side = after(side, here_g)
    far = permute(side, middle)
    across = after(across, side)
    next_out = tuple(permute(across[at : at + half], outward) for at in (0, half))
    side_g, across_g, own_s = pair_work(
        consts,
        [
            (Block(side_at, ("node",), "kept"), Away(side), 1, None),
            (Block(across_at, ("node",), "kept", optional="spectra"), across, 1, None),
        ],
        rows,
        gradient="part",
        prior_s=own_s,
        **node,
    )
    end_mine = after(end_mine, own_s)
    ends = (end_mine,) + in_thirds(end_mine)

    far, *next_out = lax.optimization_barrier((far,) + next_out + (own_s,))[:3]
    last_out = permute(far, sides)
    (far_a,) = pair_work(
        consts,
        [(Block(far_at, ("node", "ends"), "rounded", 0, half), far, 1, None)],
        rows,
        ends=ends,
        **node,
    )
    back_a = permute(far_a, middle)
    far_b, across_out = pair_work(
        consts,
        [
            (
                Block(far_at, ("node", "ends"), "rounded", half, half),
                after(far, far_a),
                1,
                None,
            ),
            (Block(across_at, ("ends",), "rounded", prior="kept"), across, 1, across_g),
        ],
        rows,
        ends=ends,
        **node,
    )
    back_b = permute(far_b, middle)
    side_total_a, side_total_b = pair_work(
        consts,
        [
            (
                Block(side_at, ("ends",), "split", prior="kept"),
                Away(after(side, far_b)),
                1,
                side_g,
            )
        ],
        rows,
        ends=ends,
    )
    total_a = add_rounded(side_total_a, back_a)
    inside_a = permute(total_a, sides)
    across_back = permute(after(across_out, total_a), middle)
    total_b = add_rounded(Away(side_total_b), after(back_b, total_a))
    inside_b = permute(total_b, sides)

    def only_s(target):
        return Block(target, ("node",), "", optional="all")

    mine_s, other_s = pair_work(
        consts,
        [
            (only_s(far_at), after(far, total_b), ~outer, None),
            (only_s(far_at), tuple(next_out), outer, None),
            (only_s(across_at), last_out, outer, None),
        ],
        rows,
        gradient="final",
        prior_s=own_s,
        **node,
    )
    others = list(in_thirds(other_s))
    inside_a, late_mine = lax.optimization_barrier((inside_a, glycans))
    flops = 2 * 2 * 2 * rows * rows * width
    (here_total,) = pair_work(
        consts,
        [
            (
                Block(here_at, ("ends",), "scaled", prior="kept", optional="all"),
                Away(late_mine),
                ~outer,
                here_g,
            )
        ],
        rows,
        ends=ends,
        cost=pl.CostEstimate(flops=flops, bytes_accessed=8 * rows * width, transcendentals=0),
    )
    others[0] = after(others[0], inside_b, here_total)
    grad_spectra = finish_spectra(mine_s, others)
    across_back = after(across_back, grad_spectra)
    return grad_spectra, finish_structures(outer, here_total, across_back, inside_a, inside_b)


def local(
    mass_profile_vectors,
    sugar_tree_vectors,
    matching_glycan_rows,
    sharpness_factor,
    offset_shift_term,
):
    work = along_line if lax.axis_size("blk") == STEPS == LINE else around_ring
    return work(
        mass_profile_vectors,
        sugar_tree_vectors,
        matching_glycan_rows,
        sharpness_factor[0],
        offset_shift_term[0],
    )


def solution(mesh):
    placed = (
        P(("groups", "blk", "sub", "inner"), None),
        P(("groups", "blk", "sub", "inner"), None),
        P(("groups", "blk", "sub", "inner")),
        P(),
        P(),
    )
    return jax.shard_map(
        local,
        mesh=mesh,
        in_specs=placed,
        out_specs=(
            P(("groups", "blk", "sub", "inner"), None),
            P(("groups", "blk", "sub", "inner"), None),
        ),
        check_vma=False,
    )
```

```python
import dataclasses
import functools

import jax
import jax.numpy as jnp
from jax import lax
from jax.experimental import pallas as pl
from jax.experimental.pallas import tpu as pltpu
from jax.sharding import PartitionSpec as P

STEPS = 4
LINE = 4
LABEL_ROWS = 16
KEEP_ROW = 6
VMEM_BYTES = 20 * 1024 * 1024


def from_behind(block, axis, distance):
    devices = range(lax.axis_size(axis))
    route = [((i - distance) % len(devices), i) for i in devices]
    return lax.ppermute(block, axis, route)


def swap_inner(block):
    return from_behind(block, "inner", 1)


def after(value, *earlier):
    return lax.optimization_barrier((value,) + earlier)[0]


def coefficients(spectra, glycans, labels, first_target, scale, shift):
    logits = (
        scale
        * lax.dot_general(
            spectra, glycans, (((1,), (1,)), ((), ())), preferred_element_type=jnp.float32
        )
        + shift
    )
    targets = first_target + jnp.arange(glycans.shape[0], dtype=jnp.int32)
    positive = (labels[:, None] == targets[None, :]).astype(jnp.float32)
    return (jax.nn.sigmoid(logits) - positive).astype(jnp.bfloat16)


def around_ring(spectra, glycans, labels, scale, shift):
    rows_here = spectra.shape[0]
    node_rows = rows_here * lax.axis_size("inner")
    loop_count = lax.axis_size("blk")
    position = lax.axis_index("blk")
    core_first = lax.axis_index("sub") * node_rows + lax.axis_index("inner") * rows_here
    lane_rows = lax.axis_size("sub") * node_rows
    node_spectra = jnp.concatenate([spectra, swap_inner(spectra)])
    node_labels = jnp.concatenate([labels, swap_inner(labels)])
    spectrum_total = 0.0
    glycan_total = 0.0
    held = glycans
    for step in range(STEPS):
        if step > 0:
            held = from_behind(held, "blk", 1)
        first_target = (position - step) % loop_count * lane_rows + core_first
        coef = coefficients(node_spectra, held, node_labels, first_target, scale, shift)
        spectrum_total += jnp.dot(coef, held, preferred_element_type=jnp.float32)
        partial_value = scale * lax.dot_general(
            coef, node_spectra, (((0,), (0,)), ((), ())), preferred_element_type=jnp.float32
        )
        if step > 0:
            back = from_behind(partial_value.astype(jnp.bfloat16), "blk", -step)
            partial_value = back.astype(jnp.float32)
        glycan_total += partial_value
    other = swap_inner((scale * spectrum_total[rows_here:]).astype(jnp.bfloat16))
    spectrum_total = scale * spectrum_total[:rows_here] + other.astype(jnp.float32)
    return spectrum_total.astype(jnp.bfloat16), glycan_total.astype(jnp.bfloat16)


@dataclasses.dataclass(frozen=True)
class Away:
    array: jax.Array


@dataclasses.dataclass(frozen=True)
class Block:
    target: int
    uses: tuple
    out: str
    start: int = 0
    count: int = 0
    prior: str = ""
    optional: str = ""


@dataclasses.dataclass(frozen=True)
class Plan:
    blocks: tuple
    pieces: tuple
    node: bool
    ends: tuple
    gradient: str
    prior_s: bool
    skips: bool
    rows: int


def pair_body(plan, *refs):
    if plan.skips:
        pl.when(refs[0][0] != 0)(functools.partial(pair_steps, plan, *refs[1:]))
    else:
        pair_steps(plan, *refs)


def pair_steps(plan, *refs):
    refs = list(refs)
    blocks, rows = plan.blocks, plan.rows
    half = rows // 2

    def take(count):
        taken = refs[:count]
        del refs[:count]
        return taken

    def take_if(condition):
        return take(1)[0] if condition else None

    (consts,) = take(1)
    labels = take_if(plan.node)
    flags = take_if(any(b.optional == "all" for b in blocks))
    node_in = take(2) if plan.node else []
    ends_in = take(len(plan.ends))
    held_in = [take(len(p)) for p in plan.pieces]
    priors = [take_if(b.prior) for b in blocks]
    prior_s = take_if(plan.prior_s)
    outs = [take((b.out != "") + (b.out == "split")) for b in blocks]
    if plan.gradient == "final":
        mine_out, other_out = take(2)
    elif plan.gradient:
        (s_out,) = take(1)
    spectra = take_if(plan.node)
    ends = take_if(plan.ends)
    held = take(len(blocks))
    prior_held = [take_if(b.prior == "kept") for b in blocks]
    out_held = [take_if(b.out in ("kept", "split")) for b in blocks]
    s_held = take_if(plan.gradient)
    (sems,) = take(1)
    used = 0

    def move(source, target):
        nonlocal used
        copy = pltpu.make_async_copy(source, target, sems.at[used])
        copy.start()
        used += 1
        return copy

    moving_node = [move(ref, spectra.at[pl.ds(i * rows, rows)]) for i, ref in enumerate(node_in)]
    moving = []
    for i, block in enumerate(blocks):
        moves = []
        at = 0
        for ref, (count, away) in zip(held_in[i], plan.pieces[i]):
            if away:
                part = ref.at[pl.ds(block.start, count)]
                moves.append(move(part, held[i].at[pl.ds(at, count)]))
            at += count
        moving.append(moves)
    moving_prior = [
        move(priors[i], prior_held[i]) if b.prior == "kept" else None for i, b in enumerate(blocks)
    ]
    moving_s = move(prior_s, s_held) if plan.prior_s else None
    leaving = []

    def const(row):
        return consts[pl.ds(row, 1), pl.ds(0, 1)]

    scale, shift = const(0), const(1)
    if plan.ends:
        width = 2 * rows
        at = 0
        coded = []
        for ref, count in zip(ends_in, plan.ends):
            ending = at % rows + count > rows
            keep = count - LABEL_ROWS if ending else count
            ends[pl.ds(at, keep)] = ref[pl.ds(0, keep)]
            at += keep
            if ending:
                digits = ref[pl.ds(keep, LABEL_ROWS), pl.ds(0, width)].astype(jnp.float32)
                coded.append(digits[0:1] * 16384.0 + digits[1:2] * 128.0 + digits[2:3])
        lane = lax.broadcasted_iota(jnp.int32, (1, width), 1)
        end_labels = jnp.where(lane >= rows, coded[1], coded[0])

    def source(use):
        if use == "node":
            while moving_node:
                moving_node.pop(0).wait()
            return spectra[...], labels[...]
        return ends[...], end_labels

    if plan.gradient == "final":
        for copy in moving_node + [c for moves in moving for c in moves] + [moving_s]:
            copy.wait()
        moving_node, moving, moving_s = [], [[] for _ in blocks], None
    for i, block in enumerate(blocks):

        def work(i=i, block=block):
            nonlocal moving_s
            at = 0
            for ref, (count, away) in zip(held_in[i], plan.pieces[i]):
                if not away:
                    held[i][pl.ds(at, count)] = ref[pl.ds(block.start, count)]
                at += count
            for copy in moving[i]:
                copy.wait()
            glycans = held[i][...]
            targets = lax.broadcasted_iota(jnp.int32, (glycans.shape[0], 1), 0)
            targets = targets.astype(jnp.float32) + (const(block.target) + float(block.start))
            total = None
            for use in block.uses:
                here, row_labels = source(use)
                logits = lax.dot_general(
                    glycans, here, (((1,), (1,)), ((), ())), preferred_element_type=jnp.float32
                )
                logits = scale * logits + shift
                positive = jnp.where(targets == row_labels, 1.0, 0.0)
                coef = jax.nn.sigmoid(logits) - positive
                masked = coef * const(KEEP_ROW) if block.optional == "spectra" else coef
                coef = coef.astype(jnp.bfloat16)
                if block.out:
                    part = jnp.dot(coef, here, preferred_element_type=jnp.float32)
                    total = part if total is None else total + part
                if plan.gradient:
                    part = lax.dot_general(
                        masked.astype(jnp.bfloat16),
                        glycans,
                        (((0,), (0,)), ((), ())),
                        preferred_element_type=jnp.float32,
                    )
                    if moving_s is not None:
                        moving_s.wait()
                        moving_s = None
                    if i > 0 or plan.prior_s:
                        s_held[...] += part
                    else:
                        s_held[...] = part
            if block.prior == "kept":
                moving_prior[i].wait()
                total = total + prior_held[i][...]
            elif block.prior:
                total = total + priors[i][...]
            if block.out == "kept":
                out_held[i][...] = total
                leaving.append(move(out_held[i], outs[i][0]))
            elif block.out == "split":
                outs[i][0][...] = scale * total[:half]
                out_held[i][...] = scale * total[half:]
                leaving.append(move(out_held[i], outs[i][1]))
            elif block.out == "total":
                outs[i][0][...] = total
            elif block.out == "scaled":
                outs[i][0][...] = scale * total
            elif block.out:
                outs[i][0][...] = (scale * total).astype(jnp.bfloat16)

        if block.optional == "all":
            pl.when(flags[i] != 0)(work)
        else:
            work()
    if plan.gradient == "final":
        mine_out[...] = scale * s_held[pl.ds(0, rows)]
        other_out[...] = (scale * s_held[pl.ds(rows, rows)]).astype(jnp.bfloat16)
    elif plan.gradient:
        leaving.append(move(s_held, s_out))
    for copy in leaving:
        copy.wait()


def in_vmem(array):
    return pltpu.with_memory_space_constraint(array, pltpu.VMEM)


def in_hbm(array):
    return pltpu.with_memory_space_constraint(array, pltpu.HBM)


def vmem_out(shape, kind):
    return pltpu.VMEM(shape, kind)


def hbm_out(shape, kind):
    return pltpu.HBM(shape, kind)


VMEM_SPEC = pl.BlockSpec(memory_space=pltpu.VMEM)
SMEM_SPEC = pl.BlockSpec(memory_space=pltpu.SMEM)
HBM_SPEC = pl.BlockSpec(memory_space=pltpu.HBM)
SMALL_COST = pl.CostEstimate(flops=1024, bytes_accessed=1024, transcendentals=0)


def params():
    return pltpu.CompilerParams(vmem_limit_bytes=VMEM_BYTES)


def pair_work(consts, blocks, rows, labels=None, node=None, ends=None, gradient="", prior_s=None, wanted=None, cost=SMALL_COST):
    half = rows // 2
    shapes = tuple(b[0] for b in blocks)
    pieces = []
    arrays = []
    for shape, array, _, _ in blocks:
        parts = array if isinstance(array, tuple) else (array,)
        away = [isinstance(x, Away) for x in parts]
        parts = [x.array if flag else x for x, flag in zip(parts, away)]
        pieces.append(tuple((shape.count or x.shape[0], flag) for x, flag in zip(parts, away)))
        arrays += list(zip(parts, away))
    width = arrays[0][0].shape[1]
    ends = ends or ()
    end_rows = tuple(x.shape[0] for x in ends)
    plan = Plan(
        shapes,
        tuple(pieces),
        node is not None,
        end_rows,
        gradient,
        prior_s is not None,
        wanted is not None,
        rows,
    )

    operands = []
    in_specs = []
    if wanted is not None:
        operands.append(jnp.int32(wanted).reshape(1))
        in_specs.append(SMEM_SPEC)

    def give(array, away):
        operands.append(in_hbm(array) if away else in_vmem(array))
        in_specs.append(HBM_SPEC if away else VMEM_SPEC)

    give(consts, False)
    if node is not None:
        give(labels, False)
    if any(b.optional == "all" for b in shapes):
        operands.append(jnp.stack([jnp.int32(b[2]) for b in blocks]))
        in_specs.append(SMEM_SPEC)
    for array in node or ():
        give(array, True)
    for array in ends:
        give(array, False)
    for array, away in arrays:
        give(array, away)
    for shape, _, _, prior in blocks:
        if shape.prior:
            give(prior, shape.prior == "kept")
    if prior_s is not None:
        give(prior_s, True)

    counts = [sum(count for count, _ in p) for p in pieces]
    outs = []
    out_specs = []

    def get(shape, kind, away):
        outs.append((hbm_out if away else vmem_out)(shape, kind))
        out_specs.append(HBM_SPEC if away else VMEM_SPEC)

    for shape, count in zip(shapes, counts):
        if shape.out == "split":
            get((half, width), jnp.float32, False)
            get((half, width), jnp.float32, True)
        elif shape.out:
            kind = jnp.bfloat16 if shape.out == "rounded" else jnp.float32
            get((count, width), kind, shape.out == "kept")
    if gradient == "final":
        get((rows, width), jnp.float32, False)
        get((rows, width), jnp.bfloat16, False)
    elif gradient:
        get((2 * rows, width), jnp.float32, True)

    scratch = []
    if node is not None:
        scratch.append(pltpu.VMEM((2 * rows, width), jnp.bfloat16))
    if ends:
        scratch.append(pltpu.VMEM((2 * rows, width), jnp.bfloat16))
    scratch += [pltpu.VMEM((n, width), jnp.bfloat16) for n in counts]
    scratch += [pltpu.VMEM((n, width), jnp.float32) for n, b in zip(counts, shapes) if b.prior == "kept"]
    for n, b in zip(counts, shapes):
        if b.out in ("kept", "split"):
            scratch.append(pltpu.VMEM((n if b.out == "kept" else half, width), jnp.float32))
    if gradient:
        scratch.append(pltpu.VMEM((2 * rows, width), jnp.float32))
    scratch.append(pltpu.SemaphoreType.DMA((len(operands) + len(outs),)))
    return pl.pallas_call(
        functools.partial(pair_body, plan),
        out_shape=outs,
        in_specs=in_specs,
        out_specs=out_specs,
        scratch_shapes=scratch,
        cost_estimate=cost,
        compiler_params=params(),
    )(*operands)


def code_labels(labels, row_count, width):
    digits = jnp.stack([labels // 16384, labels // 128 % 128, labels % 128]).astype(jnp.bfloat16)
    digits = jnp.concatenate([digits, digits, digits], axis=1)
    return jnp.pad(digits, ((0, row_count - 3), (0, width - digits.shape[1])))


def add_body(total, arrived, out, *scratch):
    if scratch:
        near, sem = scratch
        copy = pltpu.make_async_copy(total, near, sem)
        copy.start()
        copy.wait()
        total = near
    out[...] = (total[...] + arrived[...].astype(jnp.float32)).astype(jnp.bfloat16)


def add_rounded(total, arrived):
    away = isinstance(total, Away)
    scratch = [pltpu.VMEM(arrived.shape, jnp.float32), pltpu.SemaphoreType.DMA] if away else []
    return pl.pallas_call(
        add_body,
        out_shape=vmem_out(arrived.shape, jnp.bfloat16),
        in_specs=[HBM_SPEC if away else VMEM_SPEC, VMEM_SPEC],
        out_specs=VMEM_SPEC,
        scratch_shapes=scratch,
        cost_estimate=SMALL_COST,
        compiler_params=params(),
    )(in_hbm(total.array) if away else in_vmem(total), in_vmem(arrived))


def finish_spectra_body(mine_s, *rest):
    others, out = rest[:-1], rest[-1]
    at = 0
    for other in others:
        where = pl.ds(at, other.shape[0])
        out[where] = (mine_s[where] + other[...].astype(jnp.float32)).astype(jnp.bfloat16)
        at += other.shape[0]


def finish_spectra(mine_s, others):
    return pl.pallas_call(
        finish_spectra_body,
        out_shape=jax.ShapeDtypeStruct(mine_s.shape, jnp.bfloat16),
        in_specs=[VMEM_SPEC] * (1 + len(others)),
        out_specs=VMEM_SPEC,
        cost_estimate=SMALL_COST,
        compiler_params=params(),
    )(*[in_vmem(a) for a in [mine_s] + others])


def finish_structures_body(flag, here_total, across_back, inside_a, inside_b, out):
    @pl.when(flag[0] != 0)
    def _():
        out[pl.ds(0, inside_a.shape[0])] = inside_a[...]
        out[pl.ds(inside_a.shape[0], inside_b.shape[0])] = inside_b[...]

    @pl.when(flag[0] == 0)
    def _():
        total = here_total[...] + across_back[...].astype(jnp.float32)
        out[...] = total.astype(jnp.bfloat16)


def finish_structures(flag, here_total, across_back, inside_a, inside_b):
    arrays = [here_total, across_back, inside_a, inside_b]
    return pl.pallas_call(
        finish_structures_body,
        out_shape=jax.ShapeDtypeStruct(here_total.shape, jnp.bfloat16),
        in_specs=[SMEM_SPEC] + [VMEM_SPEC] * len(arrays),
        out_specs=VMEM_SPEC,
        cost_estimate=SMALL_COST,
        compiler_params=params(),
    )(jnp.int32(flag).reshape(1), *[in_vmem(a) for a in arrays])


def along_line(spectra, glycans, labels, scale, shift):
    rows, width = spectra.shape
    half = rows // 2
    node_rows = rows * lax.axis_size("inner")
    position = lax.axis_index("blk")
    outer = (position == 0) | (position == LINE - 1)
    core_first = lax.axis_index("sub") * node_rows + lax.axis_index("inner") * rows
    lane_rows = lax.axis_size("sub") * node_rows

    def permute(block, pairs):
        return lax.ppermute(block, ("blk", "inner"), pairs)

    def first_of(block_position):
        return (block_position * lane_rows + core_first).astype(jnp.float32)

    n_inner = lax.axis_size("inner")
    last = LINE - 1
    sides = []
    middle = []
    inward = []
    outward = []
    for core in range(n_inner):
        inward += [(core, n_inner + core), (last * n_inner + core, (last - 1) * n_inner + core)]
        outward += [(n_inner + core, core), ((last - 1) * n_inner + core, last * n_inner + core)]
        for at in range(LINE):
            sides.append((at * n_inner + core, (at ^ 1) * n_inner + core))
        for at in range(1, last):
            middle.append((at * n_inner + core, (last - at) * n_inner + core))
        for at in (0, last):
            middle.append((at * n_inner + core, at * n_inner + (core + 1) % n_inner))
    here_at, side_at, across_at, far_at = 2, 3, 4, 5
    rows_of_consts = [
        scale,
        shift,
        first_of(position),
        first_of(position ^ 1),
        first_of(last - position),
        first_of((last - position) ^ 1),
        jnp.where(outer, 0.0, 1.0),
    ]
    index = lax.broadcasted_iota(jnp.int32, (8, 128), 0)
    consts = jnp.zeros((8, 128), jnp.float32)
    for i, value in enumerate(rows_of_consts):
        consts = jnp.where(index == i, value, consts)

    def in_thirds(block):
        piece = -(-block.shape[0] // 48) * 16
        return tuple(swap_inner(block[at : at + piece]) for at in range(0, block.shape[0], piece))

    across = permute(glycans, middle)
    side = permute(glycans, sides)
    end_mine = permute(jnp.concatenate([spectra, code_labels(labels, LABEL_ROWS, width)]), inward)
    partner = swap_inner(spectra)
    own_labels = labels.reshape(1, rows)
    node_labels = jnp.concatenate([own_labels, swap_inner(own_labels)], axis=1)
    node_labels = node_labels.astype(jnp.float32)
    node = dict(node=(spectra, partner), labels=node_labels)
    here_g, own_s = pair_work(
        consts,
        [(Block(here_at, ("node",), "kept"), Away(glycans), 1, None)],
        rows,
        gradient="part",
        **node,
    )

    side = after(side, here_g)
    far = permute(side, middle)
    across = after(across, side)
    next_out = tuple(permute(across[at : at + half], outward) for at in (0, half))
    side_g, across_g, own_s = pair_work(
        consts,
        [
            (Block(side_at, ("node",), "kept"), Away(side), 1, None),
            (Block(across_at, ("node",), "kept", optional="spectra"), across, 1, None),
        ],
        rows,
        gradient="part",
        prior_s=own_s,
        **node,
    )
    end_mine = after(end_mine, own_s)
    ends = (end_mine,) + in_thirds(end_mine)

    far, *next_out = lax.optimization_barrier((far,) + next_out + (own_s,))[:3]
    (far_a,) = pair_work(
        consts,
        [(Block(far_at, ("node", "ends"), "rounded", 0, half), far, 1, None)],
        rows,
        wanted=~outer,
        ends=ends,
        **node,
    )
    back_a = permute(far_a, middle)
    last_out = permute(after(far, far_a), sides)
    far_b, across_out = pair_work(
        consts,
        [
            (
                Block(far_at, ("node", "ends"), "rounded", half, half),
                after(far, far_a),
                1,
                None,
            ),
            (Block(across_at, ("ends",), "rounded", prior="kept"), across, 1, across_g),
        ],
        rows,
        wanted=~outer,
        ends=ends,
        **node,
    )
    back_b = permute(far_b, middle)
    side_total_a, side_total_b = pair_work(
        consts,
        [
            (
                Block(side_at, ("ends",), "split", prior="kept"),
                Away(after(side, far_b)),
                1,
                side_g,
            )
        ],
        rows,
        wanted=~outer,
        ends=ends,
    )
    total_a = add_rounded(side_total_a, back_a)
    inside_a = permute(total_a, sides)
    across_back = permute(after(across_out, total_a), middle)
    total_b = add_rounded(Away(side_total_b), after(back_b, total_a))
    inside_b = permute(total_b, sides)

    def only_s(target):
        return Block(target, ("node",), "", optional="all")

    mine_s, other_s = pair_work(
        consts,
        [
            (only_s(far_at), after(far, total_b), ~outer, None),
            (only_s(far_at), tuple(next_out), outer, None),
            (only_s(across_at), last_out, outer, None),
        ],
        rows,
        gradient="final",
        prior_s=own_s,
        **node,
    )
    others = list(in_thirds(other_s))
    inside_a, late_mine = lax.optimization_barrier((inside_a, glycans))
    flops = 2 * 2 * 2 * rows * rows * width
    (here_total,) = pair_work(
        consts,
        [
            (
                Block(here_at, ("ends",), "scaled", prior="kept"),
                Away(late_mine),
                1,
                here_g,
            )
        ],
        rows,
        wanted=~outer,
        ends=ends,
        cost=pl.CostEstimate(flops=flops, bytes_accessed=8 * rows * width, transcendentals=0),
    )
    others[0] = after(others[0], inside_b, here_total)
    grad_spectra = finish_spectra(mine_s, others)
    across_back = after(across_back, grad_spectra)
    return grad_spectra, finish_structures(outer, here_total, across_back, inside_a, inside_b)


def local(
    mass_profile_vectors,
    sugar_tree_vectors,
    matching_glycan_rows,
    sharpness_factor,
    offset_shift_term,
):
    work = along_line if lax.axis_size("blk") == STEPS == LINE else around_ring
    return work(
        mass_profile_vectors,
        sugar_tree_vectors,
        matching_glycan_rows,
        sharpness_factor[0],
        offset_shift_term[0],
    )


def solution(mesh):
    placed = (
        P(("groups", "blk", "sub", "inner"), None),
        P(("groups", "blk", "sub", "inner"), None),
        P(("groups", "blk", "sub", "inner")),
        P(),
        P(),
    )
    return jax.shard_map(
        local,
        mesh=mesh,
        in_specs=placed,
        out_specs=(
            P(("groups", "blk", "sub", "inner"), None),
            P(("groups", "blk", "sub", "inner"), None),
        ),
        check_vma=False,
    )
```

```python
import dataclasses
import functools

import jax
import jax.numpy as jnp
from jax import lax
from jax.experimental import pallas as pl
from jax.experimental.pallas import tpu as pltpu
from jax.sharding import PartitionSpec as P

STEPS = 4
LINE = 4
LABEL_ROWS = 16
KEEP_ROW = 6
VMEM_BYTES = 20 * 1024 * 1024


def from_behind(block, axis, distance):
    devices = range(lax.axis_size(axis))
    route = [((i - distance) % len(devices), i) for i in devices]
    return lax.ppermute(block, axis, route)


def swap_inner(block):
    return from_behind(block, "inner", 1)


def after(value, *earlier):
    return lax.optimization_barrier((value,) + earlier)[0]


def coefficients(spectra, glycans, labels, first_target, scale, shift):
    logits = (
        scale
        * lax.dot_general(
            spectra, glycans, (((1,), (1,)), ((), ())), preferred_element_type=jnp.float32
        )
        + shift
    )
    targets = first_target + jnp.arange(glycans.shape[0], dtype=jnp.int32)
    positive = (labels[:, None] == targets[None, :]).astype(jnp.float32)
    return (jax.nn.sigmoid(logits) - positive).astype(jnp.bfloat16)


def around_ring(spectra, glycans, labels, scale, shift):
    rows_here = spectra.shape[0]
    node_rows = rows_here * lax.axis_size("inner")
    loop_count = lax.axis_size("blk")
    position = lax.axis_index("blk")
    core_first = lax.axis_index("sub") * node_rows + lax.axis_index("inner") * rows_here
    lane_rows = lax.axis_size("sub") * node_rows
    node_spectra = jnp.concatenate([spectra, swap_inner(spectra)])
    node_labels = jnp.concatenate([labels, swap_inner(labels)])
    spectrum_total = 0.0
    glycan_total = 0.0
    held = glycans
    for step in range(STEPS):
        if step > 0:
            held = from_behind(held, "blk", 1)
        first_target = (position - step) % loop_count * lane_rows + core_first
        coef = coefficients(node_spectra, held, node_labels, first_target, scale, shift)
        spectrum_total += jnp.dot(coef, held, preferred_element_type=jnp.float32)
        partial_value = scale * lax.dot_general(
            coef, node_spectra, (((0,), (0,)), ((), ())), preferred_element_type=jnp.float32
        )
        if step > 0:
            back = from_behind(partial_value.astype(jnp.bfloat16), "blk", -step)
            partial_value = back.astype(jnp.float32)
        glycan_total += partial_value
    other = swap_inner((scale * spectrum_total[rows_here:]).astype(jnp.bfloat16))
    spectrum_total = scale * spectrum_total[:rows_here] + other.astype(jnp.float32)
    return spectrum_total.astype(jnp.bfloat16), glycan_total.astype(jnp.bfloat16)


@dataclasses.dataclass(frozen=True)
class Away:
    array: jax.Array


@dataclasses.dataclass(frozen=True)
class Block:
    target: int
    uses: tuple
    out: str
    offset: int = 0
    cut: int = 0
    prior: str = ""
    optional: str = ""


@dataclasses.dataclass(frozen=True)
class Plan:
    blocks: tuple
    pieces: tuple
    node: bool
    ends: tuple
    gradient: str
    prior_s: bool
    skips: bool
    rows: int


def pair_body(plan, *refs):
    if plan.skips:
        pl.when(refs[0][0] != 0)(functools.partial(pair_steps, plan, *refs[1:]))
    else:
        pair_steps(plan, *refs)


def pair_steps(plan, *refs):
    refs = list(refs)
    blocks, rows = plan.blocks, plan.rows
    half = rows // 2

    def take(count):
        taken = refs[:count]
        del refs[:count]
        return taken

    def take_if(condition):
        return take(1)[0] if condition else None

    (consts,) = take(1)
    labels = take_if(plan.node)
    flags = take_if(any(b.optional == "all" for b in blocks))
    node_in = take(2) if plan.node else []
    ends_in = take(len(plan.ends))
    held_in = [take(len(p)) for p in plan.pieces]
    priors = [take_if(b.prior) for b in blocks]
    prior_s = take_if(plan.prior_s)
    outs = [take((b.out != "") + (b.out == "split")) for b in blocks]
    if plan.gradient == "final":
        mine_out, other_out = take(2)
    elif plan.gradient:
        (s_out,) = take(1)
    spectra = take_if(plan.node)
    ends = take_if(plan.ends)
    held = take(len(blocks))
    prior_held = [take_if(b.prior == "kept") for b in blocks]
    out_held = [take_if(b.out in ("kept", "split")) for b in blocks]
    s_held = take_if(plan.gradient)
    (sems,) = take(1)
    used = 0

    def move(source, target):
        nonlocal used
        copy = pltpu.make_async_copy(source, target, sems.at[used])
        copy.start()
        used += 1
        return copy

    moving_node = [move(ref, spectra.at[pl.ds(i * rows, rows)]) for i, ref in enumerate(node_in)]
    moving = []
    for i, block in enumerate(blocks):
        moves = []
        at = 0
        for ref, (count, away) in zip(held_in[i], plan.pieces[i]):
            if away:
                moves.append(move(ref, held[i].at[pl.ds(at, count)]))
            at += count
        moving.append(moves)
    moving_prior = [
        move(priors[i], prior_held[i]) if b.prior == "kept" else None for i, b in enumerate(blocks)
    ]
    moving_s = move(prior_s, s_held) if plan.prior_s else None
    leaving = []

    def const(row):
        return consts[pl.ds(row, 1), pl.ds(0, 1)]

    scale, shift = const(0), const(1)
    if plan.ends:
        width = 2 * rows
        at = 0
        coded = []
        for ref, count in zip(ends_in, plan.ends):
            ending = at % rows + count > rows
            keep = count - LABEL_ROWS if ending else count
            ends[pl.ds(at, keep)] = ref[pl.ds(0, keep)]
            at += keep
            if ending:
                digits = ref[pl.ds(keep, LABEL_ROWS), pl.ds(0, width)].astype(jnp.float32)
                coded.append(digits[0:1] * 16384.0 + digits[1:2] * 128.0 + digits[2:3])
        lane = lax.broadcasted_iota(jnp.int32, (1, width), 1)
        end_labels = jnp.where(lane >= rows, coded[1], coded[0])

    def source(use):
        if use == "node":
            while moving_node:
                moving_node.pop(0).wait()
            return spectra[...], labels[...]
        return ends[...], end_labels

    if plan.gradient == "final":
        for copy in moving_node + [c for moves in moving for c in moves] + [moving_s]:
            copy.wait()
        moving_node, moving, moving_s = [], [[] for _ in blocks], None
    for i, block in enumerate(blocks):

        def work(i=i, block=block):
            nonlocal moving_s
            at = 0
            for ref, (count, away) in zip(held_in[i], plan.pieces[i]):
                if not away:
                    held[i][pl.ds(at, count)] = ref[...]
                at += count
            for copy in moving[i]:
                copy.wait()
            glycans = held[i][...]
            targets = lax.broadcasted_iota(jnp.int32, (glycans.shape[0], 1), 0)
            targets = targets.astype(jnp.float32) + (const(block.target) + float(block.offset))
            total = None
            for use in block.uses:
                here, row_labels = source(use)
                logits = lax.dot_general(
                    glycans, here, (((1,), (1,)), ((), ())), preferred_element_type=jnp.float32
                )
                logits = scale * logits + shift
                positive = jnp.where(targets == row_labels, 1.0, 0.0)
                coef = jax.nn.sigmoid(logits) - positive
                masked = coef * const(KEEP_ROW) if block.optional == "spectra" else coef
                coef = coef.astype(jnp.bfloat16)
                if block.out:
                    part = jnp.dot(coef, here, preferred_element_type=jnp.float32)
                    total = part if total is None else total + part
                if plan.gradient:
                    part = lax.dot_general(
                        masked.astype(jnp.bfloat16),
                        glycans,
                        (((0,), (0,)), ((), ())),
                        preferred_element_type=jnp.float32,
                    )
                    if moving_s is not None:
                        moving_s.wait()
                        moving_s = None
                    if i > 0 or plan.prior_s:
                        s_held[...] += part
                    else:
                        s_held[...] = part
            if block.prior == "kept":
                moving_prior[i].wait()
                total = total + prior_held[i][...]
            elif block.prior:
                total = total + priors[i][...]
            if block.out == "kept":
                out_held[i][...] = total
                leaving.append(move(out_held[i], outs[i][0]))
            elif block.out == "split":
                cut = outs[i][0].shape[0]
                outs[i][0][...] = scale * total[:cut]
                out_held[i][...] = scale * total[cut:]
                leaving.append(move(out_held[i], outs[i][1]))
            elif block.out == "total":
                outs[i][0][...] = total
            elif block.out == "scaled":
                outs[i][0][...] = scale * total
            elif block.out:
                outs[i][0][...] = (scale * total).astype(jnp.bfloat16)

        if block.optional == "all":
            pl.when(flags[i] != 0)(work)
        else:
            work()
    if plan.gradient == "final":
        mine_out[...] = scale * s_held[pl.ds(0, rows)]
        other_out[...] = (scale * s_held[pl.ds(rows, rows)]).astype(jnp.bfloat16)
    elif plan.gradient:
        leaving.append(move(s_held, s_out))
    for copy in leaving:
        copy.wait()


def in_vmem(array):
    return pltpu.with_memory_space_constraint(array, pltpu.VMEM)


def in_hbm(array):
    return pltpu.with_memory_space_constraint(array, pltpu.HBM)


def vmem_out(shape, kind):
    return pltpu.VMEM(shape, kind)


def hbm_out(shape, kind):
    return pltpu.HBM(shape, kind)


VMEM_SPEC = pl.BlockSpec(memory_space=pltpu.VMEM)
SMEM_SPEC = pl.BlockSpec(memory_space=pltpu.SMEM)
HBM_SPEC = pl.BlockSpec(memory_space=pltpu.HBM)
SMALL_COST = pl.CostEstimate(flops=1024, bytes_accessed=1024, transcendentals=0)


def params():
    return pltpu.CompilerParams(vmem_limit_bytes=VMEM_BYTES)


def pair_work(consts, blocks, rows, labels=None, node=None, ends=None, gradient="", prior_s=None, wanted=None, cost=SMALL_COST):
    half = rows // 2
    shapes = tuple(b[0] for b in blocks)
    pieces = []
    arrays = []
    for shape, array, _, _ in blocks:
        parts = array if isinstance(array, tuple) else (array,)
        away = [isinstance(x, Away) for x in parts]
        parts = [x.array if flag else x for x, flag in zip(parts, away)]
        pieces.append(tuple((x.shape[0], flag) for x, flag in zip(parts, away)))
        arrays += list(zip(parts, away))
    width = arrays[0][0].shape[1]
    ends = ends or ()
    end_rows = tuple(x.shape[0] for x in ends)
    plan = Plan(
        shapes,
        tuple(pieces),
        node is not None,
        end_rows,
        gradient,
        prior_s is not None,
        wanted is not None,
        rows,
    )

    operands = []
    in_specs = []
    if wanted is not None:
        operands.append(jnp.int32(wanted).reshape(1))
        in_specs.append(SMEM_SPEC)

    def give(array, away):
        operands.append(in_hbm(array) if away else in_vmem(array))
        in_specs.append(HBM_SPEC if away else VMEM_SPEC)

    give(consts, False)
    if node is not None:
        give(labels, False)
    if any(b.optional == "all" for b in shapes):
        operands.append(jnp.stack([jnp.int32(b[2]) for b in blocks]))
        in_specs.append(SMEM_SPEC)
    for array in node or ():
        give(array, True)
    for array in ends:
        give(array, False)
    for array, away in arrays:
        give(array, away)
    for shape, _, _, prior in blocks:
        if shape.prior:
            give(prior, shape.prior == "kept")
    if prior_s is not None:
        give(prior_s, True)

    counts = [sum(count for count, _ in p) for p in pieces]
    outs = []
    out_specs = []

    def get(shape, kind, away):
        outs.append((hbm_out if away else vmem_out)(shape, kind))
        out_specs.append(HBM_SPEC if away else VMEM_SPEC)

    for shape, count in zip(shapes, counts):
        if shape.out == "split":
            get((shape.cut, width), jnp.float32, False)
            get((count - shape.cut, width), jnp.float32, True)
        elif shape.out:
            kind = jnp.bfloat16 if shape.out == "rounded" else jnp.float32
            get((count, width), kind, shape.out == "kept")
    if gradient == "final":
        get((rows, width), jnp.float32, False)
        get((rows, width), jnp.bfloat16, False)
    elif gradient:
        get((2 * rows, width), jnp.float32, True)

    scratch = []
    if node is not None:
        scratch.append(pltpu.VMEM((2 * rows, width), jnp.bfloat16))
    if ends:
        scratch.append(pltpu.VMEM((2 * rows, width), jnp.bfloat16))
    scratch += [pltpu.VMEM((n, width), jnp.bfloat16) for n in counts]
    scratch += [pltpu.VMEM((n, width), jnp.float32) for n, b in zip(counts, shapes) if b.prior == "kept"]
    for n, b in zip(counts, shapes):
        if b.out in ("kept", "split"):
            scratch.append(pltpu.VMEM((n - b.cut, width), jnp.float32))
    if gradient:
        scratch.append(pltpu.VMEM((2 * rows, width), jnp.float32))
    scratch.append(pltpu.SemaphoreType.DMA((len(operands) + len(outs),)))
    return pl.pallas_call(
        functools.partial(pair_body, plan),
        out_shape=outs,
        in_specs=in_specs,
        out_specs=out_specs,
        scratch_shapes=scratch,
        cost_estimate=cost,
        compiler_params=params(),
    )(*operands)


def code_labels(labels, row_count, width):
    digits = jnp.stack([labels // 16384, labels // 128 % 128, labels % 128]).astype(jnp.bfloat16)
    digits = jnp.concatenate([digits, digits, digits], axis=1)
    return jnp.pad(digits, ((0, row_count - 3), (0, width - digits.shape[1])))


def join_body(first, second, out):
    out[pl.ds(0, first.shape[0])] = first[...]
    out[pl.ds(first.shape[0], second.shape[0])] = second[...]


def join(first, second):
    rows = first.shape[0] + second.shape[0]
    return pl.pallas_call(
        join_body,
        out_shape=vmem_out((rows, first.shape[1]), first.dtype),
        in_specs=[VMEM_SPEC] * 2,
        out_specs=VMEM_SPEC,
        cost_estimate=SMALL_COST,
        compiler_params=params(),
    )(in_vmem(first), in_vmem(second))


def add_body(total, arrived, out, *scratch):
    if scratch:
        near, sem = scratch
        copy = pltpu.make_async_copy(total, near, sem)
        copy.start()
        copy.wait()
        total = near
    out[...] = (total[...] + arrived[...].astype(jnp.float32)).astype(jnp.bfloat16)


def add_rounded(total, arrived):
    away = isinstance(total, Away)
    scratch = [pltpu.VMEM(arrived.shape, jnp.float32), pltpu.SemaphoreType.DMA] if away else []
    return pl.pallas_call(
        add_body,
        out_shape=vmem_out(arrived.shape, jnp.bfloat16),
        in_specs=[HBM_SPEC if away else VMEM_SPEC, VMEM_SPEC],
        out_specs=VMEM_SPEC,
        scratch_shapes=scratch,
        cost_estimate=SMALL_COST,
        compiler_params=params(),
    )(in_hbm(total.array) if away else in_vmem(total), in_vmem(arrived))


def finish_spectra_body(mine_s, *rest):
    others, out = rest[:-1], rest[-1]
    at = 0
    for other in others:
        where = pl.ds(at, other.shape[0])
        out[where] = (mine_s[where] + other[...].astype(jnp.float32)).astype(jnp.bfloat16)
        at += other.shape[0]


def finish_spectra(mine_s, others):
    return pl.pallas_call(
        finish_spectra_body,
        out_shape=jax.ShapeDtypeStruct(mine_s.shape, jnp.bfloat16),
        in_specs=[VMEM_SPEC] * (1 + len(others)),
        out_specs=VMEM_SPEC,
        cost_estimate=SMALL_COST,
        compiler_params=params(),
    )(*[in_vmem(a) for a in [mine_s] + others])


def finish_structures_body(flag, here_total, across_back, inside_a, inside_b, out):
    @pl.when(flag[0] != 0)
    def _():
        out[pl.ds(0, inside_a.shape[0])] = inside_a[...]
        out[pl.ds(inside_a.shape[0], inside_b.shape[0])] = inside_b[...]

    @pl.when(flag[0] == 0)
    def _():
        total = here_total[...] + across_back[...].astype(jnp.float32)
        out[...] = total.astype(jnp.bfloat16)


def finish_structures(flag, here_total, across_back, inside_a, inside_b):
    arrays = [here_total, across_back, inside_a, inside_b]
    return pl.pallas_call(
        finish_structures_body,
        out_shape=jax.ShapeDtypeStruct(here_total.shape, jnp.bfloat16),
        in_specs=[SMEM_SPEC] + [VMEM_SPEC] * len(arrays),
        out_specs=VMEM_SPEC,
        cost_estimate=SMALL_COST,
        compiler_params=params(),
    )(jnp.int32(flag).reshape(1), *[in_vmem(a) for a in arrays])


def along_line(spectra, glycans, labels, scale, shift):
    rows, width = spectra.shape
    half = rows // 2
    node_rows = rows * lax.axis_size("inner")
    position = lax.axis_index("blk")
    outer = (position == 0) | (position == LINE - 1)
    core_first = lax.axis_index("sub") * node_rows + lax.axis_index("inner") * rows
    lane_rows = lax.axis_size("sub") * node_rows

    def permute(block, pairs):
        return lax.ppermute(block, ("blk", "inner"), pairs)

    def first_of(block_position):
        return (block_position * lane_rows + core_first).astype(jnp.float32)

    n_inner = lax.axis_size("inner")
    last = LINE - 1
    sides = []
    middle = []
    inward = []
    outward = []
    for core in range(n_inner):
        inward += [(core, n_inner + core), (last * n_inner + core, (last - 1) * n_inner + core)]
        outward += [(n_inner + core, core), ((last - 1) * n_inner + core, last * n_inner + core)]
        for at in range(LINE):
            sides.append((at * n_inner + core, (at ^ 1) * n_inner + core))
        for at in range(1, last):
            middle.append((at * n_inner + core, (last - at) * n_inner + core))
        for at in (0, last):
            middle.append((at * n_inner + core, at * n_inner + (core + 1) % n_inner))
    here_at, side_at, across_at, far_at = 2, 3, 4, 5
    rows_of_consts = [
        scale,
        shift,
        first_of(position),
        first_of(position ^ 1),
        first_of(last - position),
        first_of((last - position) ^ 1),
        jnp.where(outer, 0.0, 1.0),
    ]
    index = lax.broadcasted_iota(jnp.int32, (8, 128), 0)
    consts = jnp.zeros((8, 128), jnp.float32)
    for i, value in enumerate(rows_of_consts):
        consts = jnp.where(index == i, value, consts)

    def in_pieces(block, piece):
        return tuple(swap_inner(block[at : at + piece]) for at in range(0, block.shape[0], piece))

    across = permute(glycans, middle)
    cut_a = rows // 2 + 16
    side = permute(glycans, sides)
    coded = code_labels(labels, LABEL_ROWS, width)
    end_mine = permute(jnp.concatenate([spectra, coded]), inward)
    partner = swap_inner(spectra)
    own_labels = labels.reshape(1, rows)
    node_labels = jnp.concatenate([own_labels, swap_inner(own_labels)], axis=1)
    node_labels = node_labels.astype(jnp.float32)
    node = dict(node=(spectra, partner), labels=node_labels)
    here_g, own_s = pair_work(
        consts,
        [(Block(here_at, ("node",), "kept"), Away(glycans), 1, None)],
        rows,
        gradient="part",
        **node,
    )

    side = after(side, here_g)
    far_a = permute(side[:cut_a], middle)
    far_b = permute(side[cut_a:], middle)
    across = after(across, side)
    cut = rows // 2
    next_out = (permute(across[:cut], outward), permute(across[cut:], outward))
    side_g, across_g, own_s = pair_work(
        consts,
        [
            (Block(side_at, ("node",), "kept"), Away(side), 1, None),
            (Block(across_at, ("node",), "kept", optional="spectra"), across, 1, None),
        ],
        rows,
        gradient="part",
        prior_s=own_s,
        **node,
    )
    far_a = after(far_a, own_s)
    (far_g,) = pair_work(
        consts,
        [(Block(far_at, ("node",), "total"), far_a, 1, None)],
        rows,
        wanted=~outer,
        **node,
    )
    end_mine = after(end_mine, own_s)
    piece = -(-rows // 48) * 16
    ends = (end_mine,) + in_pieces(end_mine, piece)

    far_a, *next_out = lax.optimization_barrier((far_a,) + next_out + (far_g,))[:3]
    (far_a_out,) = pair_work(
        consts,
        [(Block(far_at, ("ends",), "rounded", prior="near"), far_a, 1, far_g)],
        rows,
        wanted=~outer,
        ends=ends,
    )
    back_a = permute(far_a_out, middle)
    far_b = after(far_b, far_a_out)
    far = join(far_a, far_b)
    last_out = permute(far, sides)
    far_b_out, across_out = pair_work(
        consts,
        [
            (Block(far_at, ("node", "ends"), "rounded", cut_a), far_b, 1, None),
            (Block(across_at, ("ends",), "rounded", prior="kept"), across, 1, across_g),
        ],
        rows,
        wanted=~outer,
        ends=ends,
        **node,
    )
    back_b = permute(far_b_out, middle)
    late_side = Away(after(side, far_b_out))
    side_total_a, side_total_b = pair_work(
        consts,
        [(Block(side_at, ("ends",), "split", cut=cut_a, prior="kept"), late_side, 1, side_g)],
        rows,
        wanted=~outer,
        ends=ends,
    )
    total_a = add_rounded(side_total_a, back_a)
    inside_a = permute(total_a, sides)
    across_back = permute(after(across_out, total_a), middle)
    total_b = add_rounded(Away(side_total_b), after(back_b, total_a))
    inside_b = permute(total_b, sides)

    def only_s(target):
        return Block(target, ("node",), "", optional="all")

    mine_s, other_s = pair_work(
        consts,
        [
            (only_s(far_at), after(far, total_b), ~outer, None),
            (only_s(far_at), tuple(next_out), outer, None),
            (only_s(across_at), last_out, outer, None),
        ],
        rows,
        gradient="final",
        prior_s=own_s,
        **node,
    )
    others = list(in_pieces(other_s, piece))
    inside_a, late_mine = lax.optimization_barrier((inside_a, glycans))
    flops = 2 * 2 * 2 * rows * rows * width
    (here_total,) = pair_work(
        consts,
        [(Block(here_at, ("ends",), "scaled", prior="kept"), Away(late_mine), 1, here_g)],
        rows,
        wanted=~outer,
        ends=ends,
        cost=pl.CostEstimate(flops=flops, bytes_accessed=8 * rows * width, transcendentals=0),
    )
    others[0] = after(others[0], here_total)
    grad_spectra = finish_spectra(mine_s, others)
    across_back = after(across_back, grad_spectra)
    return grad_spectra, finish_structures(outer, here_total, across_back, inside_a, inside_b)


def local(
    mass_profile_vectors,
    sugar_tree_vectors,
    matching_glycan_rows,
    sharpness_factor,
    offset_shift_term,
):
    work = along_line if lax.axis_size("blk") == STEPS == LINE else around_ring
    return work(
        mass_profile_vectors,
        sugar_tree_vectors,
        matching_glycan_rows,
        sharpness_factor[0],
        offset_shift_term[0],
    )


def solution(mesh):
    placed = (
        P(("groups", "blk", "sub", "inner"), None),
        P(("groups", "blk", "sub", "inner"), None),
        P(("groups", "blk", "sub", "inner")),
        P(),
        P(),
    )
    return jax.shard_map(
        local,
        mesh=mesh,
        in_specs=placed,
        out_specs=(
            P(("groups", "blk", "sub", "inner"), None),
            P(("groups", "blk", "sub", "inner"), None),
        ),
        check_vma=False,
    )
```

```python
import dataclasses
import functools

import jax
import jax.numpy as jnp
from jax import lax
from jax.experimental import pallas as pl
from jax.experimental.pallas import tpu as pltpu
from jax.sharding import PartitionSpec as P

STEPS = 4
LINE = 4
LABEL_ROWS = 16
FAR_ROW, KEEP_ROW, LAST_ROW = 5, 6, 7
VMEM_BYTES = 20 * 1024 * 1024


def from_behind(block, axis, distance):
    devices = range(lax.axis_size(axis))
    route = [((i - distance) % len(devices), i) for i in devices]
    return lax.ppermute(block, axis, route)


def swap_inner(block):
    return from_behind(block, "inner", 1)


def after(value, *earlier):
    return lax.optimization_barrier((value,) + earlier)[0]


def coefficients(spectra, glycans, labels, first_target, scale, shift):
    logits = (
        scale
        * lax.dot_general(
            spectra, glycans, (((1,), (1,)), ((), ())), preferred_element_type=jnp.float32
        )
        + shift
    )
    targets = first_target + jnp.arange(glycans.shape[0], dtype=jnp.int32)
    positive = (labels[:, None] == targets[None, :]).astype(jnp.float32)
    return (jax.nn.sigmoid(logits) - positive).astype(jnp.bfloat16)


def around_ring(spectra, glycans, labels, scale, shift):
    rows_here = spectra.shape[0]
    node_rows = rows_here * lax.axis_size("inner")
    loop_count = lax.axis_size("blk")
    position = lax.axis_index("blk")
    core_first = lax.axis_index("sub") * node_rows + lax.axis_index("inner") * rows_here
    lane_rows = lax.axis_size("sub") * node_rows
    node_spectra = jnp.concatenate([spectra, swap_inner(spectra)])
    node_labels = jnp.concatenate([labels, swap_inner(labels)])
    spectrum_total = 0.0
    glycan_total = 0.0
    held = glycans
    for step in range(STEPS):
        if step > 0:
            held = from_behind(held, "blk", 1)
        first_target = (position - step) % loop_count * lane_rows + core_first
        coef = coefficients(node_spectra, held, node_labels, first_target, scale, shift)
        spectrum_total += jnp.dot(coef, held, preferred_element_type=jnp.float32)
        partial_value = scale * lax.dot_general(
            coef, node_spectra, (((0,), (0,)), ((), ())), preferred_element_type=jnp.float32
        )
        if step > 0:
            back = from_behind(partial_value.astype(jnp.bfloat16), "blk", -step)
            partial_value = back.astype(jnp.float32)
        glycan_total += partial_value
    other = swap_inner((scale * spectrum_total[rows_here:]).astype(jnp.bfloat16))
    spectrum_total = scale * spectrum_total[:rows_here] + other.astype(jnp.float32)
    return spectrum_total.astype(jnp.bfloat16), glycan_total.astype(jnp.bfloat16)


@dataclasses.dataclass(frozen=True)
class Away:
    array: jax.Array


@dataclasses.dataclass(frozen=True)
class Block:
    target: int
    uses: tuple
    out: str
    offset: int = 0
    cut: int = 0
    prior: str = ""
    coef: str = ""


@dataclasses.dataclass(frozen=True)
class Plan:
    blocks: tuple
    pieces: tuple
    node: bool
    ends: tuple
    skips: bool
    rows: int


def pair_body(plan, *refs):
    if plan.skips:
        pl.when(refs[0][0] != 0)(functools.partial(pair_steps, plan, *refs[1:]))
    else:
        pair_steps(plan, *refs)


def pair_steps(plan, *refs):
    refs = list(refs)
    blocks, rows = plan.blocks, plan.rows

    def take(count):
        taken = refs[:count]
        del refs[:count]
        return taken

    def take_if(condition):
        return take(1)[0] if condition else None

    (consts,) = take(1)
    labels = take_if(plan.node)
    node_in = take(2) if plan.node else []
    ends_in = take(len(plan.ends))
    held_in = [take(len(p)) for p in plan.pieces]
    priors = [take_if(b.prior) for b in blocks]
    outs = [take((b.out != "") + (b.out == "split")) for b in blocks]
    coef_outs = [take_if(b.coef) for b in blocks]
    spectra = take_if(plan.node)
    ends = take_if(plan.ends)
    held = take(len(blocks))
    prior_held = [take_if(b.prior == "kept") for b in blocks]
    out_held = [take_if(b.out in ("kept", "kept scaled", "split")) for b in blocks]
    coef_held = [take_if(b.coef) for b in blocks]
    (sems,) = take(1)
    used = 0

    def move(source, target):
        nonlocal used
        copy = pltpu.make_async_copy(source, target, sems.at[used])
        copy.start()
        used += 1
        return copy

    moving_node = [move(ref, spectra.at[pl.ds(i * rows, rows)]) for i, ref in enumerate(node_in)]
    moving = []
    for i, block in enumerate(blocks):
        moves = []
        at = 0
        for ref, (count, away) in zip(held_in[i], plan.pieces[i]):
            if away:
                moves.append(move(ref, held[i].at[pl.ds(at, count)]))
            at += count
        moving.append(moves)
    moving_prior = [
        move(priors[i], prior_held[i]) if b.prior == "kept" else None for i, b in enumerate(blocks)
    ]
    leaving = []

    def const(row):
        return consts[pl.ds(row, 1), pl.ds(0, 1)]

    scale, shift = const(0), const(1)
    if plan.ends:
        width = 2 * rows
        at = 0
        coded = []
        for ref, count in zip(ends_in, plan.ends):
            ending = at % rows + count > rows
            keep = count - LABEL_ROWS if ending else count
            ends[pl.ds(at, keep)] = ref[pl.ds(0, keep)]
            at += keep
            if ending:
                digits = ref[pl.ds(keep, LABEL_ROWS), pl.ds(0, width)].astype(jnp.float32)
                coded.append(digits[0:1] * 16384.0 + digits[1:2] * 128.0 + digits[2:3])
        lane = lax.broadcasted_iota(jnp.int32, (1, width), 1)
        end_labels = jnp.where(lane >= rows, coded[1], coded[0])

    def source(use):
        if use == "node":
            while moving_node:
                moving_node.pop(0).wait()
            return spectra[...], labels[...]
        return ends[...], end_labels

    for i, block in enumerate(blocks):

        def work(i=i, block=block):
            at = 0
            for ref, (count, away) in zip(held_in[i], plan.pieces[i]):
                if not away:
                    held[i][pl.ds(at, count)] = ref[...]
                at += count
            for copy in moving[i]:
                copy.wait()
            glycans = held[i][...]
            targets = lax.broadcasted_iota(jnp.int32, (glycans.shape[0], 1), 0)
            targets = targets.astype(jnp.float32) + (const(block.target) + float(block.offset))
            total = None
            for use in block.uses:
                here, row_labels = source(use)
                logits = lax.dot_general(
                    glycans, here, (((1,), (1,)), ((), ())), preferred_element_type=jnp.float32
                )
                logits = scale * logits + shift
                positive = jnp.where(targets == row_labels, 1.0, 0.0)
                coef = jax.nn.sigmoid(logits) - positive
                coef = coef.astype(jnp.bfloat16)
                if block.out:
                    part = jnp.dot(coef, here, preferred_element_type=jnp.float32)
                    total = part if total is None else total + part
                if block.coef and use == "node":
                    kept = coef * const(KEEP_ROW).astype(jnp.bfloat16) if block.coef == "masked" else coef
                    coef_held[i][...] = kept
                    leaving.append(move(coef_held[i], coef_outs[i]))
            if block.prior == "kept":
                moving_prior[i].wait()
                total = total + prior_held[i][...]
            elif block.prior:
                total = total + priors[i][...]
            if block.out.startswith("kept"):
                out_held[i][...] = scale * total if block.out == "kept scaled" else total
                leaving.append(move(out_held[i], outs[i][0]))
            elif block.out == "split":
                cut = outs[i][0].shape[0]
                outs[i][0][...] = scale * total[:cut]
                out_held[i][...] = scale * total[cut:]
                leaving.append(move(out_held[i], outs[i][1]))
            elif block.out == "total":
                outs[i][0][...] = total
            elif block.out:
                outs[i][0][...] = (scale * total).astype(jnp.bfloat16)

        work()
    for copy in leaving:
        copy.wait()


def in_vmem(array):
    return pltpu.with_memory_space_constraint(array, pltpu.VMEM)


def in_hbm(array):
    return pltpu.with_memory_space_constraint(array, pltpu.HBM)


def vmem_out(shape, kind):
    return pltpu.VMEM(shape, kind)


def hbm_out(shape, kind):
    return pltpu.HBM(shape, kind)


VMEM_SPEC = pl.BlockSpec(memory_space=pltpu.VMEM)
SMEM_SPEC = pl.BlockSpec(memory_space=pltpu.SMEM)
HBM_SPEC = pl.BlockSpec(memory_space=pltpu.HBM)
SMALL_COST = pl.CostEstimate(flops=1024, bytes_accessed=1024, transcendentals=0)


def params():
    return pltpu.CompilerParams(vmem_limit_bytes=VMEM_BYTES)


def pair_work(consts, blocks, rows, labels=None, node=None, ends=None, wanted=None):
    shapes = tuple(b[0] for b in blocks)
    pieces = []
    arrays = []
    for shape, array, _ in blocks:
        parts = array if isinstance(array, tuple) else (array,)
        away = [isinstance(x, Away) for x in parts]
        parts = [x.array if flag else x for x, flag in zip(parts, away)]
        pieces.append(tuple((x.shape[0], flag) for x, flag in zip(parts, away)))
        arrays += list(zip(parts, away))
    width = arrays[0][0].shape[1]
    ends = ends or ()
    end_rows = tuple(x.shape[0] for x in ends)
    plan = Plan(
        shapes,
        tuple(pieces),
        node is not None,
        end_rows,
        wanted is not None,
        rows,
    )

    operands = []
    in_specs = []
    if wanted is not None:
        operands.append(jnp.int32(wanted).reshape(1))
        in_specs.append(SMEM_SPEC)

    def give(array, away):
        operands.append(in_hbm(array) if away else in_vmem(array))
        in_specs.append(HBM_SPEC if away else VMEM_SPEC)

    give(consts, False)
    if node is not None:
        give(labels, False)
    for array in node or ():
        give(array, True)
    for array in ends:
        give(array, False)
    for array, away in arrays:
        give(array, away)
    for shape, _, prior in blocks:
        if shape.prior:
            give(prior, shape.prior == "kept")

    counts = [sum(count for count, _ in p) for p in pieces]
    outs = []
    out_specs = []

    def get(shape, kind, away):
        outs.append((hbm_out if away else vmem_out)(shape, kind))
        out_specs.append(HBM_SPEC if away else VMEM_SPEC)

    for shape, count in zip(shapes, counts):
        if shape.out == "split":
            get((shape.cut, width), jnp.float32, False)
            get((count - shape.cut, width), jnp.float32, True)
        elif shape.out:
            kind = jnp.bfloat16 if shape.out == "rounded" else jnp.float32
            get((count, width), kind, shape.out.startswith("kept"))
    for shape, count in zip(shapes, counts):
        if shape.coef:
            get((count, 2 * rows), jnp.bfloat16, True)

    scratch = []
    if node is not None:
        scratch.append(pltpu.VMEM((2 * rows, width), jnp.bfloat16))
    if ends:
        scratch.append(pltpu.VMEM((2 * rows, width), jnp.bfloat16))
    scratch += [pltpu.VMEM((n, width), jnp.bfloat16) for n in counts]
    scratch += [pltpu.VMEM((n, width), jnp.float32) for n, b in zip(counts, shapes) if b.prior == "kept"]
    for n, b in zip(counts, shapes):
        if b.out in ("kept", "kept scaled", "split"):
            scratch.append(pltpu.VMEM((n - b.cut, width), jnp.float32))
    scratch += [pltpu.VMEM((n, 2 * rows), jnp.bfloat16) for n, b in zip(counts, shapes) if b.coef]
    scratch.append(pltpu.SemaphoreType.DMA((len(operands) + len(outs),)))
    return pl.pallas_call(
        functools.partial(pair_body, plan),
        out_shape=outs,
        in_specs=in_specs,
        out_specs=out_specs,
        scratch_shapes=scratch,
        cost_estimate=SMALL_COST,
        compiler_params=params(),
    )(*operands)


def code_labels(labels, row_count, width):
    digits = jnp.stack([labels // 16384, labels // 128 % 128, labels % 128]).astype(jnp.bfloat16)
    digits = jnp.concatenate([digits, digits, digits], axis=1)
    return jnp.pad(digits, ((0, row_count - 3), (0, width - digits.shape[1])))


def spectra_body(plan, outer, consts, labels, s_mine, s_other, coef_here, coef_side, coef_across, here, side, across, *rest):
    rows, n_next, n_far = plan
    nexts, rest = rest[:n_next], rest[n_next:]
    fars, rest = rest[:n_far], rest[n_far:]
    last, mine_out, other_out, spectra, coefs, held, sems = rest
    used = 0

    def move(source, target):
        nonlocal used
        copy = pltpu.make_async_copy(source, target, sems.at[used])
        copy.start()
        used += 1
        return copy

    def fill(parts, target, at):
        moves = []
        for part in parts:
            moves.append(move(part, target.at[pl.ds(at, part.shape[0])]))
            at += part.shape[0]
        return moves

    moves = fill([s_mine, s_other], spectra, 0) + fill([coef_here, coef_side], coefs, 0)
    moves += fill([here, side], held, 0)

    @pl.when(outer[0] == 0)
    def _():
        for copy in fill([across] + list(fars), held, 2 * rows) + fill([coef_across], coefs, 2 * rows):
            copy.wait()

    @pl.when(outer[0] != 0)
    def _():
        for copy in fill(list(nexts) + [last], held, 2 * rows):
            copy.wait()

    for copy in moves:
        copy.wait()
    scale, shift = consts[0:1, 0:1], consts[1:2, 0:1]

    def work_out(first, target_row):
        logits = lax.dot_general(
            held[pl.ds(first, rows)],
            spectra[...],
            (((1,), (1,)), ((), ())),
            preferred_element_type=jnp.float32,
        )
        logits = scale * logits + shift
        targets = lax.broadcasted_iota(jnp.int32, (rows, 1), 0).astype(jnp.float32)
        targets = targets + consts[target_row : target_row + 1, 0:1]
        positive = jnp.where(targets == labels[...], 1.0, 0.0)
        coefs[pl.ds(first, rows)] = (jax.nn.sigmoid(logits) - positive).astype(jnp.bfloat16)

    @pl.when(outer[0] != 0)
    def _():
        work_out(2 * rows, FAR_ROW)

    work_out(3 * rows, LAST_ROW)
    for i, out in enumerate((mine_out, other_out)):
        total = lax.dot_general(
            coefs[:, i * rows : (i + 1) * rows],
            held[...],
            (((0,), (0,)), ((), ())),
            preferred_element_type=jnp.float32,
        )
        out[...] = (scale * total).astype(out.dtype)


def spectra_work(outer, consts, labels, node, coefs, here, side, across, nexts, fars, last):
    rows, width = here.shape
    arrays = list(node) + list(coefs) + [here, side, across] + list(nexts) + list(fars) + [last]
    plan = (rows, len(nexts), len(fars))
    return pl.pallas_call(
        functools.partial(spectra_body, plan),
        out_shape=[vmem_out((rows, width), jnp.float32), vmem_out((rows, width), jnp.bfloat16)],
        in_specs=[SMEM_SPEC, VMEM_SPEC, VMEM_SPEC] + [HBM_SPEC] * len(arrays),
        out_specs=[VMEM_SPEC] * 2,
        scratch_shapes=[
            pltpu.VMEM((2 * rows, width), jnp.bfloat16),
            pltpu.VMEM((4 * rows, 2 * rows), jnp.bfloat16),
            pltpu.VMEM((4 * rows, width), jnp.bfloat16),
            pltpu.SemaphoreType.DMA((len(arrays),)),
        ],
        cost_estimate=SMALL_COST,
        compiler_params=params(),
    )(
        jnp.int32(outer).reshape(1),
        in_vmem(consts),
        in_vmem(labels),
        *[in_hbm(a) for a in arrays],
    )


def split_body(whole, *parts):
    at = 0
    for part in parts:
        part[...] = whole[pl.ds(at, part.shape[0])]
        at += part.shape[0]


def split(whole, counts):
    return pl.pallas_call(
        split_body,
        out_shape=[vmem_out((n, whole.shape[1]), whole.dtype) for n in counts],
        in_specs=[VMEM_SPEC],
        out_specs=[VMEM_SPEC] * len(counts),
        cost_estimate=SMALL_COST,
        compiler_params=params(),
    )(in_vmem(whole))


def join_body(first, second, out):
    out[pl.ds(0, first.shape[0])] = first[...]
    out[pl.ds(first.shape[0], second.shape[0])] = second[...]


def join(first, second):
    rows = first.shape[0] + second.shape[0]
    return pl.pallas_call(
        join_body,
        out_shape=vmem_out((rows, first.shape[1]), first.dtype),
        in_specs=[VMEM_SPEC] * 2,
        out_specs=VMEM_SPEC,
        cost_estimate=SMALL_COST,
        compiler_params=params(),
    )(in_vmem(first), in_vmem(second))


def add_body(total, arrived, out, *scratch):
    if scratch:
        near, sem = scratch
        copy = pltpu.make_async_copy(total, near, sem)
        copy.start()
        copy.wait()
        total = near
    out[...] = (total[...] + arrived[...].astype(jnp.float32)).astype(jnp.bfloat16)


def add_rounded(total, arrived):
    away = isinstance(total, Away)
    scratch = [pltpu.VMEM(arrived.shape, jnp.float32), pltpu.SemaphoreType.DMA] if away else []
    return pl.pallas_call(
        add_body,
        out_shape=vmem_out(arrived.shape, jnp.bfloat16),
        in_specs=[HBM_SPEC if away else VMEM_SPEC, VMEM_SPEC],
        out_specs=VMEM_SPEC,
        scratch_shapes=scratch,
        cost_estimate=SMALL_COST,
        compiler_params=params(),
    )(in_hbm(total.array) if away else in_vmem(total), in_vmem(arrived))


def finish_spectra_body(mine_s, away, *rest):
    others, (out, near, sem) = rest[:-3], rest[-3:]
    copy = pltpu.make_async_copy(away, near, sem)
    copy.start()
    at = 0
    for other in others:
        where = pl.ds(at, other.shape[0])
        out[where] = (mine_s[where] + other[...].astype(jnp.float32)).astype(jnp.bfloat16)
        at += other.shape[0]
    copy.wait()


def finish_spectra(mine_s, others, away):
    return pl.pallas_call(
        finish_spectra_body,
        out_shape=[
            jax.ShapeDtypeStruct(mine_s.shape, jnp.bfloat16),
            vmem_out(away.shape, away.dtype),
        ],
        in_specs=[VMEM_SPEC, HBM_SPEC] + [VMEM_SPEC] * len(others),
        out_specs=[VMEM_SPEC] * 2,
        scratch_shapes=[pltpu.SemaphoreType.DMA],
        cost_estimate=SMALL_COST,
        compiler_params=params(),
    )(in_vmem(mine_s), in_hbm(away), *[in_vmem(a) for a in others])


def finish_structures_body(flag, here_total, across_back, inside_a, inside_b, out):
    @pl.when(flag[0] != 0)
    def _():
        out[pl.ds(0, inside_a.shape[0])] = inside_a[...]
        out[pl.ds(inside_a.shape[0], inside_b.shape[0])] = inside_b[...]

    @pl.when(flag[0] == 0)
    def _():
        total = here_total[...] + across_back[...].astype(jnp.float32)
        out[...] = total.astype(jnp.bfloat16)


def finish_structures(flag, here_total, across_back, inside_a, inside_b):
    arrays = [here_total, across_back, inside_a, inside_b]
    return pl.pallas_call(
        finish_structures_body,
        out_shape=jax.ShapeDtypeStruct(here_total.shape, jnp.bfloat16),
        in_specs=[SMEM_SPEC] + [VMEM_SPEC] * len(arrays),
        out_specs=VMEM_SPEC,
        cost_estimate=SMALL_COST,
        compiler_params=params(),
    )(jnp.int32(flag).reshape(1), *[in_vmem(a) for a in arrays])


def along_line(spectra, glycans, labels, scale, shift):
    rows, width = spectra.shape
    node_rows = rows * lax.axis_size("inner")
    position = lax.axis_index("blk")
    outer = (position == 0) | (position == LINE - 1)
    core_first = lax.axis_index("sub") * node_rows + lax.axis_index("inner") * rows
    lane_rows = lax.axis_size("sub") * node_rows

    def permute(block, pairs):
        return lax.ppermute(block, ("blk", "inner"), pairs)

    def first_of(block_position):
        return (block_position * lane_rows + core_first).astype(jnp.float32)

    n_inner = lax.axis_size("inner")
    last = LINE - 1
    sides = []
    middle = []
    inward = []
    outward = []
    for core in range(n_inner):
        inward += [(core, n_inner + core), (last * n_inner + core, (last - 1) * n_inner + core)]
        outward += [(n_inner + core, core), ((last - 1) * n_inner + core, last * n_inner + core)]
        for at in range(LINE):
            sides.append((at * n_inner + core, (at ^ 1) * n_inner + core))
        for at in range(1, last):
            middle.append((at * n_inner + core, (last - at) * n_inner + core))
        for at in (0, last):
            middle.append((at * n_inner + core, at * n_inner + (core + 1) % n_inner))
    here_at, side_at, across_at, far_at = 2, 3, 4, FAR_ROW
    rows_of_consts = [
        scale,
        shift,
        first_of(position),
        first_of(position ^ 1),
        first_of(last - position),
        first_of((last - position) ^ 1),
        jnp.where(outer, 0.0, 1.0),
        first_of(jnp.where(outer, last - position, (last - position) ^ 1)),
    ]
    index = lax.broadcasted_iota(jnp.int32, (8, 128), 0)
    consts = jnp.zeros((8, 128), jnp.float32)
    for i, value in enumerate(rows_of_consts):
        consts = jnp.where(index == i, value, consts)

    cut = rows // 2
    half = rows // 2
    across = permute(glycans, middle)
    side = permute(glycans, sides)
    coded = code_labels(labels, LABEL_ROWS, width)
    end_mine = permute(jnp.concatenate([spectra, coded]), inward)
    partner = swap_inner(spectra)
    own_labels = labels.reshape(1, rows)
    node_labels = jnp.concatenate([own_labels, swap_inner(own_labels)], axis=1)
    node_labels = node_labels.astype(jnp.float32)
    node = dict(node=(spectra, partner), labels=node_labels)
    here_g, here_c = pair_work(
        consts, [(Block(here_at, ("node",), "kept", coef="all"), Away(glycans), None)], rows, **node
    )

    side = after(side, here_g)
    far_a, far_b = [permute(x, middle) for x in split(side, (cut, rows - cut))]
    across = after(across, here_g)
    next_out = permute(across, outward)
    side_g, across_g, side_c, across_c = pair_work(
        consts,
        [
            (Block(side_at, ("node",), "kept", coef="all"), Away(side), None),
            (Block(across_at, ("node",), "kept", coef="masked"), across, None),
        ],
        rows,
        **node,
    )
    end_mine = after(end_mine, across_g)
    piece = -(-rows // 48) * 16
    ends = (end_mine,) + tuple(swap_inner(x) for x in split(end_mine, (piece,) * 3))
    far_a = after(far_a, across_g)
    (far_g,) = pair_work(
        consts, [(Block(far_at, ("node",), "total"), far_a, None)], rows, wanted=~outer, **node
    )

    far_a, next_out = lax.optimization_barrier((far_a, next_out, far_g))[:2]
    (far_a_out,) = pair_work(
        consts,
        [(Block(far_at, ("ends",), "rounded", prior="near"), far_a, far_g)],
        rows,
        wanted=~outer,
        ends=ends,
    )
    back_a = permute(far_a_out, middle)
    last_out = permute(join(after(far_a, far_a_out), far_b), sides)
    far_b = after(far_b, far_a_out)
    far_b_out, across_out = pair_work(
        consts,
        [
            (Block(far_at, ("node", "ends"), "rounded", cut), far_b, None),
            (Block(across_at, ("ends",), "rounded", prior="kept"), across, across_g),
        ],
        rows,
        wanted=~outer,
        ends=ends,
        **node,
    )
    back_b = permute(far_b_out, middle)
    late_side = Away(after(side, far_b_out))
    side_total_a, side_total_b = pair_work(
        consts,
        [(Block(side_at, ("ends",), "split", cut=cut, prior="kept"), late_side, side_g)],
        rows,
        wanted=~outer,
        ends=ends,
    )
    total_a = add_rounded(side_total_a, back_a)
    inside_a = permute(total_a, sides)
    across_back = permute(after(across_out, total_a), middle)
    (here_total,) = pair_work(
        consts,
        [(Block(here_at, ("ends",), "kept scaled", prior="kept"), Away(after(glycans, total_a)), here_g)],
        rows,
        wanted=~outer,
        ends=ends,
    )
    total_b = add_rounded(Away(side_total_b), after(back_b, here_total))
    inside_b = permute(total_b, sides)

    mine_s, other_s = spectra_work(
        outer,
        consts,
        node_labels,
        (spectra, partner),
        (here_c, side_c, across_c),
        after(glycans, total_b),
        side,
        across,
        (next_out,),
        (far_a, far_b),
        last_out,
    )
    others = [swap_inner(x) for x in split(other_s, (piece, piece, rows - 2 * piece))]
    others[0] = after(others[0], inside_a)
    grad_spectra, here_total = finish_spectra(mine_s, others, here_total)
    across_back = after(across_back, grad_spectra)
    return grad_spectra, finish_structures(outer, here_total, across_back, inside_a, inside_b)


def local(
    mass_profile_vectors,
    sugar_tree_vectors,
    matching_glycan_rows,
    sharpness_factor,
    offset_shift_term,
):
    work = along_line if lax.axis_size("blk") == STEPS == LINE else around_ring
    return work(
        mass_profile_vectors,
        sugar_tree_vectors,
        matching_glycan_rows,
        sharpness_factor[0],
        offset_shift_term[0],
    )


def solution(mesh):
    placed = (
        P(("groups", "blk", "sub", "inner"), None),
        P(("groups", "blk", "sub", "inner"), None),
        P(("groups", "blk", "sub", "inner")),
        P(),
        P(),
    )
    return jax.shard_map(
        local,
        mesh=mesh,
        in_specs=placed,
        out_specs=(
            P(("groups", "blk", "sub", "inner"), None),
            P(("groups", "blk", "sub", "inner"), None),
        ),
        check_vma=False,
    )
```

```python
import dataclasses
import functools

import jax
import jax.numpy as jnp
from jax import lax
from jax.experimental import pallas as pl
from jax.experimental.pallas import tpu as pltpu
from jax.sharding import PartitionSpec as P

STEPS = 4
LINE = 4
LABEL_ROWS = 16
FAR_ROW, KEEP_ROW, LAST_ROW = 5, 6, 7
VMEM_BYTES = 20 * 1024 * 1024


def from_behind(block, axis, distance):
    devices = range(lax.axis_size(axis))
    route = [((i - distance) % len(devices), i) for i in devices]
    return lax.ppermute(block, axis, route)


def swap_inner(block):
    return from_behind(block, "inner", 1)


def after(value, *earlier):
    return lax.optimization_barrier((value,) + earlier)[0]


def coefficients(spectra, glycans, labels, first_target, scale, shift):
    logits = (
        scale
        * lax.dot_general(
            spectra, glycans, (((1,), (1,)), ((), ())), preferred_element_type=jnp.float32
        )
        + shift
    )
    targets = first_target + jnp.arange(glycans.shape[0], dtype=jnp.int32)
    positive = (labels[:, None] == targets[None, :]).astype(jnp.float32)
    return (jax.nn.sigmoid(logits) - positive).astype(jnp.bfloat16)


def around_ring(spectra, glycans, labels, scale, shift):
    rows_here = spectra.shape[0]
    node_rows = rows_here * lax.axis_size("inner")
    loop_count = lax.axis_size("blk")
    position = lax.axis_index("blk")
    core_first = lax.axis_index("sub") * node_rows + lax.axis_index("inner") * rows_here
    lane_rows = lax.axis_size("sub") * node_rows
    node_spectra = jnp.concatenate([spectra, swap_inner(spectra)])
    node_labels = jnp.concatenate([labels, swap_inner(labels)])
    spectrum_total = 0.0
    glycan_total = 0.0
    held = glycans
    for step in range(STEPS):
        if step > 0:
            held = from_behind(held, "blk", 1)
        first_target = (position - step) % loop_count * lane_rows + core_first
        coef = coefficients(node_spectra, held, node_labels, first_target, scale, shift)
        spectrum_total += jnp.dot(coef, held, preferred_element_type=jnp.float32)
        partial_value = scale * lax.dot_general(
            coef, node_spectra, (((0,), (0,)), ((), ())), preferred_element_type=jnp.float32
        )
        if step > 0:
            back = from_behind(partial_value.astype(jnp.bfloat16), "blk", -step)
            partial_value = back.astype(jnp.float32)
        glycan_total += partial_value
    other = swap_inner((scale * spectrum_total[rows_here:]).astype(jnp.bfloat16))
    spectrum_total = scale * spectrum_total[:rows_here] + other.astype(jnp.float32)
    return spectrum_total.astype(jnp.bfloat16), glycan_total.astype(jnp.bfloat16)


@dataclasses.dataclass(frozen=True)
class Away:
    array: jax.Array


@dataclasses.dataclass(frozen=True)
class Block:
    target: int
    uses: tuple
    out: str
    offset: int = 0
    cut: int = 0
    prior: str = ""
    coef: str = ""


@dataclasses.dataclass(frozen=True)
class Plan:
    blocks: tuple
    pieces: tuple
    node: bool
    ends: tuple
    skips: bool
    rows: int


def pair_body(plan, *refs):
    if plan.skips:
        pl.when(refs[0][0] != 0)(functools.partial(pair_steps, plan, *refs[1:]))
    else:
        pair_steps(plan, *refs)


def pair_steps(plan, *refs):
    refs = list(refs)
    blocks, rows = plan.blocks, plan.rows

    def take(count):
        taken = refs[:count]
        del refs[:count]
        return taken

    def take_if(condition):
        return take(1)[0] if condition else None

    (consts,) = take(1)
    labels = take_if(plan.node)
    node_in = take(2) if plan.node else []
    ends_in = take(len(plan.ends))
    held_in = [take(len(p)) for p in plan.pieces]
    priors = [take_if(b.prior) for b in blocks]
    outs = [take((b.out != "") + (b.out == "split")) for b in blocks]
    coef_outs = [take_if(b.coef) for b in blocks]
    spectra = take_if(plan.node)
    ends = take_if(plan.ends)
    held = take(len(blocks))
    prior_held = [take_if(b.prior == "kept") for b in blocks]
    out_held = [take_if(b.out in ("kept", "kept scaled", "split")) for b in blocks]
    coef_held = [take_if(b.coef) for b in blocks]
    (sems,) = take(1)
    used = 0

    def move(source, target):
        nonlocal used
        copy = pltpu.make_async_copy(source, target, sems.at[used])
        copy.start()
        used += 1
        return copy

    moving_node = [move(ref, spectra.at[pl.ds(i * rows, rows)]) for i, ref in enumerate(node_in)]
    moving = []
    for i, block in enumerate(blocks):
        moves = []
        at = 0
        for ref, (count, away) in zip(held_in[i], plan.pieces[i]):
            if away:
                moves.append(move(ref, held[i].at[pl.ds(at, count)]))
            at += count
        moving.append(moves)
    moving_prior = [
        move(priors[i], prior_held[i]) if b.prior == "kept" else None for i, b in enumerate(blocks)
    ]
    leaving = []

    def const(row):
        return consts[pl.ds(row, 1), pl.ds(0, 1)]

    scale, shift = const(0), const(1)
    if plan.ends:
        width = 2 * rows
        at = 0
        coded = []
        for ref, count in zip(ends_in, plan.ends):
            ending = at % rows + count > rows
            keep = count - LABEL_ROWS if ending else count
            ends[pl.ds(at, keep)] = ref[pl.ds(0, keep)]
            at += keep
            if ending:
                digits = ref[pl.ds(keep, LABEL_ROWS), pl.ds(0, width)].astype(jnp.float32)
                coded.append(digits[0:1] * 16384.0 + digits[1:2] * 128.0 + digits[2:3])
        lane = lax.broadcasted_iota(jnp.int32, (1, width), 1)
        end_labels = jnp.where(lane >= rows, coded[1], coded[0])

    def source(use):
        if use == "node":
            while moving_node:
                moving_node.pop(0).wait()
            return spectra[...], labels[...]
        return ends[...], end_labels

    for i, block in enumerate(blocks):

        def work(i=i, block=block):
            at = 0
            for ref, (count, away) in zip(held_in[i], plan.pieces[i]):
                if not away:
                    held[i][pl.ds(at, count)] = ref[...]
                at += count
            for copy in moving[i]:
                copy.wait()
            glycans = held[i][...]
            targets = lax.broadcasted_iota(jnp.int32, (glycans.shape[0], 1), 0)
            targets = targets.astype(jnp.float32) + (const(block.target) + float(block.offset))
            total = None
            for use in block.uses:
                here, row_labels = source(use)
                logits = lax.dot_general(
                    glycans, here, (((1,), (1,)), ((), ())), preferred_element_type=jnp.float32
                )
                logits = scale * logits + shift
                positive = jnp.where(targets == row_labels, 1.0, 0.0)
                coef = jax.nn.sigmoid(logits) - positive
                coef = coef.astype(jnp.bfloat16)
                if block.out:
                    part = jnp.dot(coef, here, preferred_element_type=jnp.float32)
                    total = part if total is None else total + part
                if block.coef and use == "node":
                    kept = coef * const(KEEP_ROW).astype(jnp.bfloat16) if block.coef == "masked" else coef
                    coef_held[i][...] = kept
                    leaving.append(move(coef_held[i], coef_outs[i]))
            if block.prior == "kept":
                moving_prior[i].wait()
                total = total + prior_held[i][...]
            elif block.prior:
                total = total + priors[i][...]
            if block.out.startswith("kept"):
                out_held[i][...] = scale * total if block.out == "kept scaled" else total
                leaving.append(move(out_held[i], outs[i][0]))
            elif block.out == "split":
                cut = outs[i][0].shape[0]
                outs[i][0][...] = scale * total[:cut]
                out_held[i][...] = scale * total[cut:]
                leaving.append(move(out_held[i], outs[i][1]))
            elif block.out == "total":
                outs[i][0][...] = total
            elif block.out:
                outs[i][0][...] = (scale * total).astype(jnp.bfloat16)

        work()
    for copy in leaving:
        copy.wait()


def in_vmem(array):
    return pltpu.with_memory_space_constraint(array, pltpu.VMEM)


def in_hbm(array):
    return pltpu.with_memory_space_constraint(array, pltpu.HBM)


def vmem_out(shape, kind):
    return pltpu.VMEM(shape, kind)


def hbm_out(shape, kind):
    return pltpu.HBM(shape, kind)


VMEM_SPEC = pl.BlockSpec(memory_space=pltpu.VMEM)
SMEM_SPEC = pl.BlockSpec(memory_space=pltpu.SMEM)
HBM_SPEC = pl.BlockSpec(memory_space=pltpu.HBM)
SMALL_COST = pl.CostEstimate(flops=1024, bytes_accessed=1024, transcendentals=0)


def params():
    return pltpu.CompilerParams(vmem_limit_bytes=VMEM_BYTES)


def pair_work(consts, blocks, rows, labels=None, node=None, ends=None, wanted=None):
    shapes = tuple(b[0] for b in blocks)
    pieces = []
    arrays = []
    for shape, array, _ in blocks:
        parts = array if isinstance(array, tuple) else (array,)
        away = [isinstance(x, Away) for x in parts]
        parts = [x.array if flag else x for x, flag in zip(parts, away)]
        pieces.append(tuple((x.shape[0], flag) for x, flag in zip(parts, away)))
        arrays += list(zip(parts, away))
    width = arrays[0][0].shape[1]
    ends = ends or ()
    end_rows = tuple(x.shape[0] for x in ends)
    plan = Plan(
        shapes,
        tuple(pieces),
        node is not None,
        end_rows,
        wanted is not None,
        rows,
    )

    operands = []
    in_specs = []
    if wanted is not None:
        operands.append(jnp.int32(wanted).reshape(1))
        in_specs.append(SMEM_SPEC)

    def give(array, away):
        operands.append(in_hbm(array) if away else in_vmem(array))
        in_specs.append(HBM_SPEC if away else VMEM_SPEC)

    give(consts, False)
    if node is not None:
        give(labels, False)
    for array in node or ():
        give(array, True)
    for array in ends:
        give(array, False)
    for array, away in arrays:
        give(array, away)
    for shape, _, prior in blocks:
        if shape.prior:
            give(prior, shape.prior == "kept")

    counts = [sum(count for count, _ in p) for p in pieces]
    outs = []
    out_specs = []

    def get(shape, kind, away):
        outs.append((hbm_out if away else vmem_out)(shape, kind))
        out_specs.append(HBM_SPEC if away else VMEM_SPEC)

    for shape, count in zip(shapes, counts):
        if shape.out == "split":
            get((shape.cut, width), jnp.float32, False)
            get((count - shape.cut, width), jnp.float32, True)
        elif shape.out:
            kind = jnp.bfloat16 if shape.out == "rounded" else jnp.float32
            get((count, width), kind, shape.out.startswith("kept"))
    for shape, count in zip(shapes, counts):
        if shape.coef:
            get((count, 2 * rows), jnp.bfloat16, True)

    scratch = []
    if node is not None:
        scratch.append(pltpu.VMEM((2 * rows, width), jnp.bfloat16))
    if ends:
        scratch.append(pltpu.VMEM((2 * rows, width), jnp.bfloat16))
    scratch += [pltpu.VMEM((n, width), jnp.bfloat16) for n in counts]
    scratch += [pltpu.VMEM((n, width), jnp.float32) for n, b in zip(counts, shapes) if b.prior == "kept"]
    for n, b in zip(counts, shapes):
        if b.out in ("kept", "kept scaled", "split"):
            scratch.append(pltpu.VMEM((n - b.cut, width), jnp.float32))
    scratch += [pltpu.VMEM((n, 2 * rows), jnp.bfloat16) for n, b in zip(counts, shapes) if b.coef]
    scratch.append(pltpu.SemaphoreType.DMA((len(operands) + len(outs),)))
    return pl.pallas_call(
        functools.partial(pair_body, plan),
        out_shape=outs,
        in_specs=in_specs,
        out_specs=out_specs,
        scratch_shapes=scratch,
        cost_estimate=SMALL_COST,
        compiler_params=params(),
    )(*operands)


def code_labels(labels, row_count, width):
    digits = jnp.stack([labels // 16384, labels // 128 % 128, labels % 128]).astype(jnp.bfloat16)
    digits = jnp.concatenate([digits, digits, digits], axis=1)
    return jnp.pad(digits, ((0, row_count - 3), (0, width - digits.shape[1])))


def spectra_body(plan, outer, consts, labels, s_mine, s_other, coef_here, coef_side, coef_across, here, side, across, *rest):
    rows, n_next, n_far = plan
    nexts, rest = rest[:n_next], rest[n_next:]
    fars, rest = rest[:n_far], rest[n_far:]
    last, mine_out, other_out, spectra, coefs, held, sems = rest
    used = 0

    def move(source, target):
        nonlocal used
        copy = pltpu.make_async_copy(source, target, sems.at[used])
        copy.start()
        used += 1
        return copy

    def fill(parts, target, at):
        moves = []
        for part in parts:
            moves.append(move(part, target.at[pl.ds(at, part.shape[0])]))
            at += part.shape[0]
        return moves

    moves = fill([s_mine, s_other], spectra, 0) + fill([coef_here, coef_side], coefs, 0)
    moves += fill([here, side], held, 0)

    @pl.when(outer[0] == 0)
    def _():
        for copy in fill([across] + list(fars), held, 2 * rows) + fill([coef_across], coefs, 2 * rows):
            copy.wait()

    @pl.when(outer[0] != 0)
    def _():
        for copy in fill(list(nexts) + [last], held, 2 * rows):
            copy.wait()

    for copy in moves:
        copy.wait()
    scale, shift = consts[0:1, 0:1], consts[1:2, 0:1]

    def work_out(first, target_row):
        logits = lax.dot_general(
            held[pl.ds(first, rows)],
            spectra[...],
            (((1,), (1,)), ((), ())),
            preferred_element_type=jnp.float32,
        )
        logits = scale * logits + shift
        targets = lax.broadcasted_iota(jnp.int32, (rows, 1), 0).astype(jnp.float32)
        targets = targets + consts[target_row : target_row + 1, 0:1]
        positive = jnp.where(targets == labels[...], 1.0, 0.0)
        coefs[pl.ds(first, rows)] = (jax.nn.sigmoid(logits) - positive).astype(jnp.bfloat16)

    @pl.when(outer[0] != 0)
    def _():
        work_out(2 * rows, FAR_ROW)

    work_out(3 * rows, LAST_ROW)
    for i, out in enumerate((mine_out, other_out)):
        total = lax.dot_general(
            coefs[:, i * rows : (i + 1) * rows],
            held[...],
            (((0,), (0,)), ((), ())),
            preferred_element_type=jnp.float32,
        )
        out[...] = (scale * total).astype(out.dtype)


def spectra_work(outer, consts, labels, node, coefs, here, side, across, nexts, fars, last):
    rows, width = here.shape
    arrays = list(node) + list(coefs) + [here, side, across] + list(nexts) + list(fars) + [last]
    plan = (rows, len(nexts), len(fars))
    return pl.pallas_call(
        functools.partial(spectra_body, plan),
        out_shape=[vmem_out((rows, width), jnp.float32), vmem_out((rows, width), jnp.bfloat16)],
        in_specs=[SMEM_SPEC, VMEM_SPEC, VMEM_SPEC] + [HBM_SPEC] * len(arrays),
        out_specs=[VMEM_SPEC] * 2,
        scratch_shapes=[
            pltpu.VMEM((2 * rows, width), jnp.bfloat16),
            pltpu.VMEM((4 * rows, 2 * rows), jnp.bfloat16),
            pltpu.VMEM((4 * rows, width), jnp.bfloat16),
            pltpu.SemaphoreType.DMA((len(arrays),)),
        ],
        cost_estimate=SMALL_COST,
        compiler_params=params(),
    )(
        jnp.int32(outer).reshape(1),
        in_vmem(consts),
        in_vmem(labels),
        *[in_hbm(a) for a in arrays],
    )


def split_body(whole, *parts):
    at = 0
    for part in parts:
        part[...] = whole[pl.ds(at, part.shape[0])]
        at += part.shape[0]


def split(whole, counts):
    return pl.pallas_call(
        split_body,
        out_shape=[vmem_out((n, whole.shape[1]), whole.dtype) for n in counts],
        in_specs=[VMEM_SPEC],
        out_specs=[VMEM_SPEC] * len(counts),
        cost_estimate=SMALL_COST,
        compiler_params=params(),
    )(in_vmem(whole))


def join_body(first, second, out):
    out[pl.ds(0, first.shape[0])] = first[...]
    out[pl.ds(first.shape[0], second.shape[0])] = second[...]


def join(first, second):
    rows = first.shape[0] + second.shape[0]
    return pl.pallas_call(
        join_body,
        out_shape=vmem_out((rows, first.shape[1]), first.dtype),
        in_specs=[VMEM_SPEC] * 2,
        out_specs=VMEM_SPEC,
        cost_estimate=SMALL_COST,
        compiler_params=params(),
    )(in_vmem(first), in_vmem(second))


def add_body(total, arrived, out, *scratch):
    if scratch:
        near, sem = scratch
        copy = pltpu.make_async_copy(total, near, sem)
        copy.start()
        copy.wait()
        total = near
    out[...] = (total[...] + arrived[...].astype(jnp.float32)).astype(jnp.bfloat16)


def add_rounded(total, arrived):
    away = isinstance(total, Away)
    scratch = [pltpu.VMEM(arrived.shape, jnp.float32), pltpu.SemaphoreType.DMA] if away else []
    return pl.pallas_call(
        add_body,
        out_shape=vmem_out(arrived.shape, jnp.bfloat16),
        in_specs=[HBM_SPEC if away else VMEM_SPEC, VMEM_SPEC],
        out_specs=VMEM_SPEC,
        scratch_shapes=scratch,
        cost_estimate=SMALL_COST,
        compiler_params=params(),
    )(in_hbm(total.array) if away else in_vmem(total), in_vmem(arrived))


def finish_spectra_body(mine_s, away, inside, *rest):
    others, (out, near, inside_near, sem) = rest[:-4], rest[-4:]
    copy = pltpu.make_async_copy(away, near, sem)
    copy.start()
    at = 0
    for other in others:
        where = pl.ds(at, other.shape[0])
        out[where] = (mine_s[where] + other[...].astype(jnp.float32)).astype(jnp.bfloat16)
        at += other.shape[0]
    inside_near[...] = inside[...]
    copy.wait()


def finish_spectra(mine_s, others, away, inside):
    return pl.pallas_call(
        finish_spectra_body,
        out_shape=[
            jax.ShapeDtypeStruct(mine_s.shape, jnp.bfloat16),
            vmem_out(away.shape, away.dtype),
            vmem_out(inside.shape, inside.dtype),
        ],
        in_specs=[VMEM_SPEC, HBM_SPEC] + [VMEM_SPEC] * (1 + len(others)),
        out_specs=[VMEM_SPEC] * 3,
        scratch_shapes=[pltpu.SemaphoreType.DMA],
        cost_estimate=SMALL_COST,
        compiler_params=params(),
    )(in_vmem(mine_s), in_hbm(away), *[in_vmem(a) for a in [inside] + others])


def finish_structures_body(flag, here_total, across_back, inside_a, inside_b, out):
    @pl.when(flag[0] != 0)
    def _():
        out[pl.ds(0, inside_a.shape[0])] = inside_a[...]
        out[pl.ds(inside_a.shape[0], inside_b.shape[0])] = inside_b[...]

    @pl.when(flag[0] == 0)
    def _():
        total = here_total[...] + across_back[...].astype(jnp.float32)
        out[...] = total.astype(jnp.bfloat16)


def finish_structures(flag, here_total, across_back, inside_a, inside_b):
    arrays = [here_total, across_back, inside_a, inside_b]
    return pl.pallas_call(
        finish_structures_body,
        out_shape=jax.ShapeDtypeStruct(here_total.shape, jnp.bfloat16),
        in_specs=[SMEM_SPEC] + [VMEM_SPEC] * len(arrays),
        out_specs=VMEM_SPEC,
        cost_estimate=SMALL_COST,
        compiler_params=params(),
    )(jnp.int32(flag).reshape(1), *[in_vmem(a) for a in arrays])


def along_line(spectra, glycans, labels, scale, shift):
    rows, width = spectra.shape
    node_rows = rows * lax.axis_size("inner")
    position = lax.axis_index("blk")
    outer = (position == 0) | (position == LINE - 1)
    core_first = lax.axis_index("sub") * node_rows + lax.axis_index("inner") * rows
    lane_rows = lax.axis_size("sub") * node_rows

    def permute(block, pairs):
        return lax.ppermute(block, ("blk", "inner"), pairs)

    def first_of(block_position):
        return (block_position * lane_rows + core_first).astype(jnp.float32)

    n_inner = lax.axis_size("inner")
    last = LINE - 1
    sides = []
    middle = []
    inward = []
    outward = []
    for core in range(n_inner):
        inward += [(core, n_inner + core), (last * n_inner + core, (last - 1) * n_inner + core)]
        outward += [(n_inner + core, core), ((last - 1) * n_inner + core, last * n_inner + core)]
        for at in range(LINE):
            sides.append((at * n_inner + core, (at ^ 1) * n_inner + core))
        for at in range(1, last):
            middle.append((at * n_inner + core, (last - at) * n_inner + core))
        for at in (0, last):
            middle.append((at * n_inner + core, at * n_inner + (core + 1) % n_inner))
    here_at, side_at, across_at, far_at = 2, 3, 4, FAR_ROW
    rows_of_consts = [
        scale,
        shift,
        first_of(position),
        first_of(position ^ 1),
        first_of(last - position),
        first_of((last - position) ^ 1),
        jnp.where(outer, 0.0, 1.0),
        first_of(jnp.where(outer, last - position, (last - position) ^ 1)),
    ]
    index = lax.broadcasted_iota(jnp.int32, (8, 128), 0)
    consts = jnp.zeros((8, 128), jnp.float32)
    for i, value in enumerate(rows_of_consts):
        consts = jnp.where(index == i, value, consts)

    cut = rows // 2
    half = rows // 2
    across = permute(glycans, middle)
    side = permute(glycans, sides)
    coded = code_labels(labels, LABEL_ROWS, width)
    end_mine = permute(jnp.concatenate([spectra, coded]), inward)
    partner = swap_inner(spectra)
    own_labels = labels.reshape(1, rows)
    node_labels = jnp.concatenate([own_labels, swap_inner(own_labels)], axis=1)
    node_labels = node_labels.astype(jnp.float32)
    node = dict(node=(spectra, partner), labels=node_labels)
    here_g, here_c = pair_work(
        consts, [(Block(here_at, ("node",), "kept", coef="all"), Away(glycans), None)], rows, **node
    )

    side = after(side, here_g)
    far_a, far_b = [permute(x, middle) for x in split(side, (cut, rows - cut))]
    across = after(across, here_g)
    next_out = permute(across, outward)
    side_g, across_g, side_c, across_c = pair_work(
        consts,
        [
            (Block(side_at, ("node",), "kept", coef="all"), Away(side), None),
            (Block(across_at, ("node",), "kept", coef="masked"), Away(across), None),
        ],
        rows,
        **node,
    )
    far_a = after(far_a, across_g)
    (far_g,) = pair_work(
        consts, [(Block(far_at, ("node",), "total"), far_a, None)], rows, wanted=~outer, **node
    )
    end_mine = after(end_mine, far_g)
    piece = -(-rows // 48) * 16
    ends = (end_mine,) + tuple(swap_inner(x) for x in split(end_mine, (piece,) * 3))

    far_a, next_out = lax.optimization_barrier((far_a, next_out, far_g))[:2]
    (far_a_out,) = pair_work(
        consts,
        [(Block(far_at, ("ends",), "rounded", prior="near"), far_a, far_g)],
        rows,
        wanted=~outer,
        ends=ends,
    )
    back_a = permute(far_a_out, middle)
    last_out = permute(join(after(far_a, far_a_out), far_b), sides)
    far_b = after(far_b, far_a_out)
    far_b_out, across_out = pair_work(
        consts,
        [
            (Block(far_at, ("node", "ends"), "rounded", cut), far_b, None),
            (Block(across_at, ("ends",), "rounded", prior="kept"), Away(across), across_g),
        ],
        rows,
        wanted=~outer,
        ends=ends,
        **node,
    )
    back_b = permute(far_b_out, middle)
    late_side = Away(after(side, far_b_out))
    side_total_a, side_total_b = pair_work(
        consts,
        [(Block(side_at, ("ends",), "split", cut=cut, prior="kept"), late_side, side_g)],
        rows,
        wanted=~outer,
        ends=ends,
    )
    total_a = add_rounded(side_total_a, back_a)
    inside_a = permute(total_a, sides)
    across_back = permute(after(across_out, total_a), middle)
    (here_total,) = pair_work(
        consts,
        [(Block(here_at, ("ends",), "kept scaled", prior="kept"), Away(after(glycans, total_a)), here_g)],
        rows,
        wanted=~outer,
        ends=ends,
    )
    total_b = add_rounded(Away(side_total_b), after(back_b, here_total))
    inside_b = permute(total_b, sides)

    mine_s, other_s = spectra_work(
        outer,
        consts,
        node_labels,
        (spectra, partner),
        (here_c, side_c, across_c),
        after(glycans, total_b),
        side,
        across,
        (next_out,),
        (far_a, far_b),
        last_out,
    )
    others = [swap_inner(x) for x in split(other_s, (piece, piece, rows - 2 * piece))]
    grad_spectra, here_total, inside_a = finish_spectra(mine_s, others, here_total, inside_a)
    across_back = after(across_back, grad_spectra)
    return grad_spectra, finish_structures(outer, here_total, across_back, inside_a, inside_b)


def local(
    mass_profile_vectors,
    sugar_tree_vectors,
    matching_glycan_rows,
    sharpness_factor,
    offset_shift_term,
):
    work = along_line if lax.axis_size("blk") == STEPS == LINE else around_ring
    return work(
        mass_profile_vectors,
        sugar_tree_vectors,
        matching_glycan_rows,
        sharpness_factor[0],
        offset_shift_term[0],
    )


def solution(mesh):
    placed = (
        P(("groups", "blk", "sub", "inner"), None),
        P(("groups", "blk", "sub", "inner"), None),
        P(("groups", "blk", "sub", "inner")),
        P(),
        P(),
    )
    return jax.shard_map(
        local,
        mesh=mesh,
        in_specs=placed,
        out_specs=(
            P(("groups", "blk", "sub", "inner"), None),
            P(("groups", "blk", "sub", "inner"), None),
        ),
        check_vma=False,
    )
```

```python
import dataclasses
import functools

import jax
import jax.numpy as jnp
from jax import lax
from jax.experimental import pallas as pl
from jax.experimental.pallas import tpu as pltpu
from jax.sharding import PartitionSpec as P

STEPS = 4
LINE = 4
LABEL_ROWS = 16
FAR_ROW, KEEP_ROW, LAST_ROW = 5, 6, 7
VMEM_BYTES = 20 * 1024 * 1024


def from_behind(block, axis, distance):
    devices = range(lax.axis_size(axis))
    route = [((i - distance) % len(devices), i) for i in devices]
    return lax.ppermute(block, axis, route)


def swap_inner(block):
    return from_behind(block, "inner", 1)


def after(value, *earlier):
    return lax.optimization_barrier((value,) + earlier)[0]


def coefficients(spectra, glycans, labels, first_target, scale, shift):
    logits = (
        scale
        * lax.dot_general(
            spectra, glycans, (((1,), (1,)), ((), ())), preferred_element_type=jnp.float32
        )
        + shift
    )
    targets = first_target + jnp.arange(glycans.shape[0], dtype=jnp.int32)
    positive = (labels[:, None] == targets[None, :]).astype(jnp.float32)
    return (jax.nn.sigmoid(logits) - positive).astype(jnp.bfloat16)


def around_ring(spectra, glycans, labels, scale, shift):
    rows_here = spectra.shape[0]
    node_rows = rows_here * lax.axis_size("inner")
    loop_count = lax.axis_size("blk")
    position = lax.axis_index("blk")
    core_first = lax.axis_index("sub") * node_rows + lax.axis_index("inner") * rows_here
    lane_rows = lax.axis_size("sub") * node_rows
    node_spectra = jnp.concatenate([spectra, swap_inner(spectra)])
    node_labels = jnp.concatenate([labels, swap_inner(labels)])
    spectrum_total = 0.0
    glycan_total = 0.0
    held = glycans
    for step in range(STEPS):
        if step > 0:
            held = from_behind(held, "blk", 1)
        first_target = (position - step) % loop_count * lane_rows + core_first
        coef = coefficients(node_spectra, held, node_labels, first_target, scale, shift)
        spectrum_total += jnp.dot(coef, held, preferred_element_type=jnp.float32)
        partial_value = scale * lax.dot_general(
            coef, node_spectra, (((0,), (0,)), ((), ())), preferred_element_type=jnp.float32
        )
        if step > 0:
            back = from_behind(partial_value.astype(jnp.bfloat16), "blk", -step)
            partial_value = back.astype(jnp.float32)
        glycan_total += partial_value
    other = swap_inner((scale * spectrum_total[rows_here:]).astype(jnp.bfloat16))
    spectrum_total = scale * spectrum_total[:rows_here] + other.astype(jnp.float32)
    return spectrum_total.astype(jnp.bfloat16), glycan_total.astype(jnp.bfloat16)


@dataclasses.dataclass(frozen=True)
class Away:
    array: jax.Array


@dataclasses.dataclass(frozen=True)
class Block:
    target: int
    uses: tuple
    out: str
    offset: int = 0
    cut: int = 0
    prior: str = ""
    coef: str = ""


@dataclasses.dataclass(frozen=True)
class Plan:
    blocks: tuple
    pieces: tuple
    node: bool
    ends: tuple
    skips: bool
    rows: int


def pair_body(plan, *refs):
    if plan.skips:
        pl.when(refs[0][0] != 0)(functools.partial(pair_steps, plan, *refs[1:]))
    else:
        pair_steps(plan, *refs)


def pair_steps(plan, *refs):
    refs = list(refs)
    blocks, rows = plan.blocks, plan.rows

    def take(count):
        taken = refs[:count]
        del refs[:count]
        return taken

    def take_if(condition):
        return take(1)[0] if condition else None

    (consts,) = take(1)
    labels = take_if(plan.node)
    node_in = take(2) if plan.node else []
    ends_in = take(len(plan.ends))
    held_in = [take(len(p)) for p in plan.pieces]
    priors = [take_if(b.prior) for b in blocks]
    outs = [take((b.out != "") + (b.out == "split")) for b in blocks]
    coef_outs = [take_if(b.coef) for b in blocks]
    spectra = take_if(plan.node)
    ends = take_if(plan.ends)
    held = take(len(blocks))
    prior_held = [take_if(b.prior == "kept") for b in blocks]
    out_held = [take_if(b.out in ("kept", "kept scaled", "split")) for b in blocks]
    coef_held = [take_if(b.coef) for b in blocks]
    (sems,) = take(1)
    used = 0

    def move(source, target):
        nonlocal used
        copy = pltpu.make_async_copy(source, target, sems.at[used])
        copy.start()
        used += 1
        return copy

    moving_node = [move(ref, spectra.at[pl.ds(i * rows, rows)]) for i, ref in enumerate(node_in)]
    moving = []
    for i, block in enumerate(blocks):
        moves = []
        at = 0
        for ref, (count, away) in zip(held_in[i], plan.pieces[i]):
            if away:
                moves.append(move(ref, held[i].at[pl.ds(at, count)]))
            at += count
        moving.append(moves)
    moving_prior = [
        move(priors[i], prior_held[i]) if b.prior == "kept" else None for i, b in enumerate(blocks)
    ]
    leaving = []

    def const(row):
        return consts[pl.ds(row, 1), pl.ds(0, 1)]

    scale, shift = const(0), const(1)
    if plan.ends:
        width = 2 * rows
        at = 0
        coded = []
        for ref, count in zip(ends_in, plan.ends):
            ending = at % rows + count > rows
            keep = count - LABEL_ROWS if ending else count
            ends[pl.ds(at, keep)] = ref[pl.ds(0, keep)]
            at += keep
            if ending:
                digits = ref[pl.ds(keep, LABEL_ROWS), pl.ds(0, width)].astype(jnp.float32)
                coded.append(digits[0:1] * 16384.0 + digits[1:2] * 128.0 + digits[2:3])
        lane = lax.broadcasted_iota(jnp.int32, (1, width), 1)
        end_labels = jnp.where(lane >= rows, coded[1], coded[0])

    def source(use):
        if use == "node":
            while moving_node:
                moving_node.pop(0).wait()
            return spectra[...], labels[...]
        return ends[...], end_labels

    for i, block in enumerate(blocks):

        def work(i=i, block=block):
            at = 0
            for ref, (count, away) in zip(held_in[i], plan.pieces[i]):
                if not away:
                    held[i][pl.ds(at, count)] = ref[...]
                at += count
            for copy in moving[i]:
                copy.wait()
            glycans = held[i][...]
            targets = lax.broadcasted_iota(jnp.int32, (glycans.shape[0], 1), 0)
            targets = targets.astype(jnp.float32) + (const(block.target) + float(block.offset))
            total = None
            for use in block.uses:
                here, row_labels = source(use)
                logits = lax.dot_general(
                    glycans, here, (((1,), (1,)), ((), ())), preferred_element_type=jnp.float32
                )
                logits = scale * logits + shift
                positive = jnp.where(targets == row_labels, 1.0, 0.0)
                coef = jax.nn.sigmoid(logits) - positive
                coef = coef.astype(jnp.bfloat16)
                if block.out:
                    part = jnp.dot(coef, here, preferred_element_type=jnp.float32)
                    total = part if total is None else total + part
                if block.coef and use == "node":
                    kept = coef * const(KEEP_ROW).astype(jnp.bfloat16) if block.coef == "masked" else coef
                    coef_held[i][...] = kept
                    leaving.append(move(coef_held[i], coef_outs[i]))
            if block.prior == "kept":
                moving_prior[i].wait()
                total = total + prior_held[i][...]
            elif block.prior:
                total = total + priors[i][...]
            if block.out.startswith("kept"):
                out_held[i][...] = scale * total if block.out == "kept scaled" else total
                leaving.append(move(out_held[i], outs[i][0]))
            elif block.out == "split":
                cut = outs[i][0].shape[0]
                outs[i][0][...] = scale * total[:cut]
                out_held[i][...] = scale * total[cut:]
                leaving.append(move(out_held[i], outs[i][1]))
            elif block.out == "total":
                outs[i][0][...] = total
            elif block.out:
                outs[i][0][...] = (scale * total).astype(jnp.bfloat16)

        work()
    for copy in leaving:
        copy.wait()


def in_vmem(array):
    return pltpu.with_memory_space_constraint(array, pltpu.VMEM)


def in_hbm(array):
    return pltpu.with_memory_space_constraint(array, pltpu.HBM)


def vmem_out(shape, kind):
    return pltpu.VMEM(shape, kind)


def hbm_out(shape, kind):
    return pltpu.HBM(shape, kind)


VMEM_SPEC = pl.BlockSpec(memory_space=pltpu.VMEM)
SMEM_SPEC = pl.BlockSpec(memory_space=pltpu.SMEM)
HBM_SPEC = pl.BlockSpec(memory_space=pltpu.HBM)
SMALL_COST = pl.CostEstimate(flops=1024, bytes_accessed=1024, transcendentals=0)


def params():
    return pltpu.CompilerParams(vmem_limit_bytes=VMEM_BYTES)


def pair_work(consts, blocks, rows, labels=None, node=None, ends=None, wanted=None):
    shapes = tuple(b[0] for b in blocks)
    pieces = []
    arrays = []
    for shape, array, _ in blocks:
        parts = array if isinstance(array, tuple) else (array,)
        away = [isinstance(x, Away) for x in parts]
        parts = [x.array if flag else x for x, flag in zip(parts, away)]
        pieces.append(tuple((x.shape[0], flag) for x, flag in zip(parts, away)))
        arrays += list(zip(parts, away))
    width = arrays[0][0].shape[1]
    ends = ends or ()
    end_rows = tuple(x.shape[0] for x in ends)
    plan = Plan(
        shapes,
        tuple(pieces),
        node is not None,
        end_rows,
        wanted is not None,
        rows,
    )

    operands = []
    in_specs = []
    if wanted is not None:
        operands.append(jnp.int32(wanted).reshape(1))
        in_specs.append(SMEM_SPEC)

    def give(array, away):
        operands.append(in_hbm(array) if away else in_vmem(array))
        in_specs.append(HBM_SPEC if away else VMEM_SPEC)

    give(consts, False)
    if node is not None:
        give(labels, False)
    for array in node or ():
        give(array, True)
    for array in ends:
        give(array, False)
    for array, away in arrays:
        give(array, away)
    for shape, _, prior in blocks:
        if shape.prior:
            give(prior, shape.prior == "kept")

    counts = [sum(count for count, _ in p) for p in pieces]
    outs = []
    out_specs = []

    def get(shape, kind, away):
        outs.append((hbm_out if away else vmem_out)(shape, kind))
        out_specs.append(HBM_SPEC if away else VMEM_SPEC)

    for shape, count in zip(shapes, counts):
        if shape.out == "split":
            get((shape.cut, width), jnp.float32, False)
            get((count - shape.cut, width), jnp.float32, True)
        elif shape.out:
            kind = jnp.bfloat16 if shape.out == "rounded" else jnp.float32
            get((count, width), kind, shape.out.startswith("kept"))
    for shape, count in zip(shapes, counts):
        if shape.coef:
            get((count, 2 * rows), jnp.bfloat16, True)

    scratch = []
    if node is not None:
        scratch.append(pltpu.VMEM((2 * rows, width), jnp.bfloat16))
    if ends:
        scratch.append(pltpu.VMEM((2 * rows, width), jnp.bfloat16))
    scratch += [pltpu.VMEM((n, width), jnp.bfloat16) for n in counts]
    scratch += [pltpu.VMEM((n, width), jnp.float32) for n, b in zip(counts, shapes) if b.prior == "kept"]
    for n, b in zip(counts, shapes):
        if b.out in ("kept", "kept scaled", "split"):
            scratch.append(pltpu.VMEM((n - b.cut, width), jnp.float32))
    scratch += [pltpu.VMEM((n, 2 * rows), jnp.bfloat16) for n, b in zip(counts, shapes) if b.coef]
    scratch.append(pltpu.SemaphoreType.DMA((len(operands) + len(outs),)))
    return pl.pallas_call(
        functools.partial(pair_body, plan),
        out_shape=outs,
        in_specs=in_specs,
        out_specs=out_specs,
        scratch_shapes=scratch,
        cost_estimate=SMALL_COST,
        compiler_params=params(),
    )(*operands)


def code_labels(labels, row_count, width):
    digits = jnp.stack([labels // 16384, labels // 128 % 128, labels % 128]).astype(jnp.bfloat16)
    digits = jnp.concatenate([digits, digits, digits], axis=1)
    return jnp.pad(digits, ((0, row_count - 3), (0, width - digits.shape[1])))


def spectra_body(plan, outer, consts, labels, s_mine, s_other, coef_here, coef_side, coef_across, here, side, across, *rest):
    rows, n_next, n_far, n_last = plan
    nexts, rest = rest[:n_next], rest[n_next:]
    fars, rest = rest[:n_far], rest[n_far:]
    lasts, rest = rest[:n_last], rest[n_last:]
    mine_out, other_out, spectra, coefs, held, sems = rest
    used = 0

    def move(source, target):
        nonlocal used
        copy = pltpu.make_async_copy(source, target, sems.at[used])
        copy.start()
        used += 1
        return copy

    def fill(parts, target, at):
        moves = []
        for part in parts:
            moves.append(move(part, target.at[pl.ds(at, part.shape[0])]))
            at += part.shape[0]
        return moves

    moves = fill([s_mine, s_other], spectra, 0) + fill([coef_here, coef_side], coefs, 0)
    moves += fill([here, side], held, 0)

    @pl.when(outer[0] == 0)
    def _():
        for copy in fill([across] + list(fars), held, 2 * rows) + fill([coef_across], coefs, 2 * rows):
            copy.wait()

    @pl.when(outer[0] != 0)
    def _():
        for copy in fill(list(nexts) + list(lasts), held, 2 * rows):
            copy.wait()

    for copy in moves:
        copy.wait()
    scale, shift = consts[0:1, 0:1], consts[1:2, 0:1]

    def work_out(first, target_row):
        logits = lax.dot_general(
            held[pl.ds(first, rows)],
            spectra[...],
            (((1,), (1,)), ((), ())),
            preferred_element_type=jnp.float32,
        )
        logits = scale * logits + shift
        targets = lax.broadcasted_iota(jnp.int32, (rows, 1), 0).astype(jnp.float32)
        targets = targets + consts[target_row : target_row + 1, 0:1]
        positive = jnp.where(targets == labels[...], 1.0, 0.0)
        coefs[pl.ds(first, rows)] = (jax.nn.sigmoid(logits) - positive).astype(jnp.bfloat16)

    @pl.when(outer[0] != 0)
    def _():
        work_out(2 * rows, FAR_ROW)

    work_out(3 * rows, LAST_ROW)
    for i, out in enumerate((mine_out, other_out)):
        total = lax.dot_general(
            coefs[:, i * rows : (i + 1) * rows],
            held[...],
            (((0,), (0,)), ((), ())),
            preferred_element_type=jnp.float32,
        )
        out[...] = (scale * total).astype(out.dtype)


def spectra_work(outer, consts, labels, node, coefs, here, side, across, nexts, fars, lasts):
    rows, width = here.shape
    arrays = list(node) + list(coefs) + [here, side, across] + list(nexts) + list(fars) + list(lasts)
    plan = (rows, len(nexts), len(fars), len(lasts))
    return pl.pallas_call(
        functools.partial(spectra_body, plan),
        out_shape=[vmem_out((rows, width), jnp.float32), vmem_out((rows, width), jnp.bfloat16)],
        in_specs=[SMEM_SPEC, VMEM_SPEC, VMEM_SPEC] + [HBM_SPEC] * len(arrays),
        out_specs=[VMEM_SPEC] * 2,
        scratch_shapes=[
            pltpu.VMEM((2 * rows, width), jnp.bfloat16),
            pltpu.VMEM((4 * rows, 2 * rows), jnp.bfloat16),
            pltpu.VMEM((4 * rows, width), jnp.bfloat16),
            pltpu.SemaphoreType.DMA((len(arrays),)),
        ],
        cost_estimate=SMALL_COST,
        compiler_params=params(),
    )(
        jnp.int32(outer).reshape(1),
        in_vmem(consts),
        in_vmem(labels),
        *[in_hbm(a) for a in arrays],
    )


def split_body(whole, *parts):
    at = 0
    for part in parts:
        part[...] = whole[pl.ds(at, part.shape[0])]
        at += part.shape[0]


def split(whole, counts):
    return pl.pallas_call(
        split_body,
        out_shape=[vmem_out((n, whole.shape[1]), whole.dtype) for n in counts],
        in_specs=[VMEM_SPEC],
        out_specs=[VMEM_SPEC] * len(counts),
        cost_estimate=SMALL_COST,
        compiler_params=params(),
    )(in_vmem(whole))


def add_body(total, arrived, out, *scratch):
    if scratch:
        near, sem = scratch
        copy = pltpu.make_async_copy(total, near, sem)
        copy.start()
        copy.wait()
        total = near
    out[...] = (total[...] + arrived[...].astype(jnp.float32)).astype(jnp.bfloat16)


def add_rounded(total, arrived):
    away = isinstance(total, Away)
    scratch = [pltpu.VMEM(arrived.shape, jnp.float32), pltpu.SemaphoreType.DMA] if away else []
    return pl.pallas_call(
        add_body,
        out_shape=vmem_out(arrived.shape, jnp.bfloat16),
        in_specs=[HBM_SPEC if away else VMEM_SPEC, VMEM_SPEC],
        out_specs=VMEM_SPEC,
        scratch_shapes=scratch,
        cost_estimate=SMALL_COST,
        compiler_params=params(),
    )(in_hbm(total.array) if away else in_vmem(total), in_vmem(arrived))


def finish_spectra_body(mine_s, away, inside, *rest):
    others, (out, near, inside_near, sem) = rest[:-4], rest[-4:]
    copy = pltpu.make_async_copy(away, near, sem)
    copy.start()
    at = 0
    for other in others:
        where = pl.ds(at, other.shape[0])
        out[where] = (mine_s[where] + other[...].astype(jnp.float32)).astype(jnp.bfloat16)
        at += other.shape[0]
    inside_near[...] = inside[...]
    copy.wait()


def finish_spectra(mine_s, others, away, inside):
    return pl.pallas_call(
        finish_spectra_body,
        out_shape=[
            jax.ShapeDtypeStruct(mine_s.shape, jnp.bfloat16),
            vmem_out(away.shape, away.dtype),
            vmem_out(inside.shape, inside.dtype),
        ],
        in_specs=[VMEM_SPEC, HBM_SPEC] + [VMEM_SPEC] * (1 + len(others)),
        out_specs=[VMEM_SPEC] * 3,
        scratch_shapes=[pltpu.SemaphoreType.DMA],
        cost_estimate=SMALL_COST,
        compiler_params=params(),
    )(in_vmem(mine_s), in_hbm(away), *[in_vmem(a) for a in [inside] + others])


def finish_structures_body(flag, here_total, across_back, inside_a, inside_b, out):
    @pl.when(flag[0] != 0)
    def _():
        out[pl.ds(0, inside_a.shape[0])] = inside_a[...]
        out[pl.ds(inside_a.shape[0], inside_b.shape[0])] = inside_b[...]

    @pl.when(flag[0] == 0)
    def _():
        total = here_total[...] + across_back[...].astype(jnp.float32)
        out[...] = total.astype(jnp.bfloat16)


def finish_structures(flag, here_total, across_back, inside_a, inside_b):
    arrays = [here_total, across_back, inside_a, inside_b]
    return pl.pallas_call(
        finish_structures_body,
        out_shape=jax.ShapeDtypeStruct(here_total.shape, jnp.bfloat16),
        in_specs=[SMEM_SPEC] + [VMEM_SPEC] * len(arrays),
        out_specs=VMEM_SPEC,
        cost_estimate=SMALL_COST,
        compiler_params=params(),
    )(jnp.int32(flag).reshape(1), *[in_vmem(a) for a in arrays])


def along_line(spectra, glycans, labels, scale, shift):
    rows, width = spectra.shape
    node_rows = rows * lax.axis_size("inner")
    position = lax.axis_index("blk")
    outer = (position == 0) | (position == LINE - 1)
    core_first = lax.axis_index("sub") * node_rows + lax.axis_index("inner") * rows
    lane_rows = lax.axis_size("sub") * node_rows

    def permute(block, pairs):
        return lax.ppermute(block, ("blk", "inner"), pairs)

    def first_of(block_position):
        return (block_position * lane_rows + core_first).astype(jnp.float32)

    n_inner = lax.axis_size("inner")
    last = LINE - 1
    sides = []
    middle = []
    inward = []
    outward = []
    for core in range(n_inner):
        inward += [(core, n_inner + core), (last * n_inner + core, (last - 1) * n_inner + core)]
        outward += [(n_inner + core, core), ((last - 1) * n_inner + core, last * n_inner + core)]
        for at in range(LINE):
            sides.append((at * n_inner + core, (at ^ 1) * n_inner + core))
        for at in range(1, last):
            middle.append((at * n_inner + core, (last - at) * n_inner + core))
        for at in (0, last):
            middle.append((at * n_inner + core, at * n_inner + (core + 1) % n_inner))
    here_at, side_at, across_at, far_at = 2, 3, 4, FAR_ROW
    rows_of_consts = [
        scale,
        shift,
        first_of(position),
        first_of(position ^ 1),
        first_of(last - position),
        first_of((last - position) ^ 1),
        jnp.where(outer, 0.0, 1.0),
        first_of(jnp.where(outer, last - position, (last - position) ^ 1)),
    ]
    index = lax.broadcasted_iota(jnp.int32, (8, 128), 0)
    consts = jnp.zeros((8, 128), jnp.float32)
    for i, value in enumerate(rows_of_consts):
        consts = jnp.where(index == i, value, consts)

    cut = 2 * rows // 5
    half = rows // 2
    across = permute(glycans, middle)
    side = permute(glycans, sides)
    coded = code_labels(labels, LABEL_ROWS, width)
    end_mine = permute(jnp.concatenate([spectra, coded]), inward)
    partner = swap_inner(spectra)
    own_labels = labels.reshape(1, rows)
    node_labels = jnp.concatenate([own_labels, swap_inner(own_labels)], axis=1)
    node_labels = node_labels.astype(jnp.float32)
    node = dict(node=(spectra, partner), labels=node_labels)
    here_g, here_c = pair_work(
        consts, [(Block(here_at, ("node",), "kept", coef="all"), Away(glycans), None)], rows, **node
    )

    side = after(side, here_g)
    far_a, far_b = [permute(x, middle) for x in split(side, (cut, rows - cut))]
    across = after(across, here_g)
    next_out = permute(across, outward)
    side_g, across_g, side_c, across_c = pair_work(
        consts,
        [
            (Block(side_at, ("node",), "kept", coef="all"), Away(side), None),
            (Block(across_at, ("node",), "kept", coef="masked"), Away(across), None),
        ],
        rows,
        **node,
    )
    far_a = after(far_a, across_g)
    last_a = permute(far_a, sides)
    (far_g,) = pair_work(
        consts, [(Block(far_at, ("node",), "total"), far_a, None)], rows, wanted=~outer, **node
    )
    end_mine = after(end_mine, far_g)
    piece = -(-rows // 48) * 16
    two = (half + LABEL_ROWS, half)
    ends = (end_mine,) + tuple(swap_inner(x) for x in split(end_mine, two))

    far_a, far_b, next_out = lax.optimization_barrier((far_a, far_b, next_out, far_g))[:3]
    (far_a_out,) = pair_work(
        consts,
        [(Block(far_at, ("ends",), "rounded", prior="near"), far_a, far_g)],
        rows,
        wanted=~outer,
        ends=ends,
    )
    back_a = permute(far_a_out, middle)
    far_b = after(far_b, far_a_out)
    last_b = permute(far_b, sides)
    (far_b_out,) = pair_work(
        consts,
        [(Block(far_at, ("node", "ends"), "rounded", cut), far_b, None)],
        rows,
        wanted=~outer,
        ends=ends,
        **node,
    )
    back_b = permute(far_b_out, middle)
    (across_out,) = pair_work(
        consts,
        [
            (
                Block(across_at, ("ends",), "rounded", prior="kept"),
                Away(after(across, far_b_out)),
                across_g,
            )
        ],
        rows,
        wanted=~outer,
        ends=ends,
    )
    late_side, last_a = lax.optimization_barrier((side, last_a, across_out))[:2]
    late_side = Away(late_side)
    side_total_a, side_total_b = pair_work(
        consts,
        [(Block(side_at, ("ends",), "split", cut=cut, prior="kept"), late_side, side_g)],
        rows,
        wanted=~outer,
        ends=ends,
    )
    total_a = add_rounded(side_total_a, back_a)
    inside_a = permute(total_a, sides)
    across_back = permute(after(across_out, total_a), middle)
    (here_total,) = pair_work(
        consts,
        [(Block(here_at, ("ends",), "kept scaled", prior="kept"), Away(after(glycans, total_a)), here_g)],
        rows,
        wanted=~outer,
        ends=ends,
    )
    back_b, last_b = lax.optimization_barrier((back_b, last_b, here_total))[:2]
    total_b = add_rounded(Away(side_total_b), back_b)
    inside_b = permute(total_b, sides)

    mine_s, other_s = spectra_work(
        outer,
        consts,
        node_labels,
        (spectra, partner),
        (here_c, side_c, across_c),
        after(glycans, total_b),
        side,
        across,
        (next_out,),
        (far_a, far_b),
        (last_a, last_b),
    )
    others = [swap_inner(x) for x in split(other_s, (piece, piece, rows - 2 * piece))]
    grad_spectra, here_total, inside_a = finish_spectra(mine_s, others, here_total, inside_a)
    across_back = after(across_back, grad_spectra)
    return grad_spectra, finish_structures(outer, here_total, across_back, inside_a, inside_b)


def local(
    mass_profile_vectors,
    sugar_tree_vectors,
    matching_glycan_rows,
    sharpness_factor,
    offset_shift_term,
):
    work = along_line if lax.axis_size("blk") == STEPS == LINE else around_ring
    return work(
        mass_profile_vectors,
        sugar_tree_vectors,
        matching_glycan_rows,
        sharpness_factor[0],
        offset_shift_term[0],
    )


def solution(mesh):
    placed = (
        P(("groups", "blk", "sub", "inner"), None),
        P(("groups", "blk", "sub", "inner"), None),
        P(("groups", "blk", "sub", "inner")),
        P(),
        P(),
    )
    return jax.shard_map(
        local,
        mesh=mesh,
        in_specs=placed,
        out_specs=(
            P(("groups", "blk", "sub", "inner"), None),
            P(("groups", "blk", "sub", "inner"), None),
        ),
        check_vma=False,
    )
```

```python
import dataclasses
import functools

import jax
import jax.numpy as jnp
from jax import lax
from jax.experimental import pallas as pl
from jax.experimental.pallas import tpu as pltpu
from jax.sharding import PartitionSpec as P

STEPS = 4
LINE = 4
LABEL_ROWS = 16
FAR_ROW, KEEP_ROW, LAST_ROW = 5, 6, 7
VMEM_BYTES = 20 * 1024 * 1024


def from_behind(block, axis, distance):
    devices = range(lax.axis_size(axis))
    route = [((i - distance) % len(devices), i) for i in devices]
    return lax.ppermute(block, axis, route)


def swap_inner(block):
    return from_behind(block, "inner", 1)


def after(value, *earlier):
    return lax.optimization_barrier((value,) + earlier)[0]


def coefficients(spectra, glycans, labels, first_target, scale, shift):
    logits = (
        scale
        * lax.dot_general(
            spectra, glycans, (((1,), (1,)), ((), ())), preferred_element_type=jnp.float32
        )
        + shift
    )
    targets = first_target + jnp.arange(glycans.shape[0], dtype=jnp.int32)
    positive = (labels[:, None] == targets[None, :]).astype(jnp.float32)
    return (jax.nn.sigmoid(logits) - positive).astype(jnp.bfloat16)


def around_ring(spectra, glycans, labels, scale, shift):
    rows_here = spectra.shape[0]
    node_rows = rows_here * lax.axis_size("inner")
    loop_count = lax.axis_size("blk")
    position = lax.axis_index("blk")
    core_first = lax.axis_index("sub") * node_rows + lax.axis_index("inner") * rows_here
    lane_rows = lax.axis_size("sub") * node_rows
    node_spectra = jnp.concatenate([spectra, swap_inner(spectra)])
    node_labels = jnp.concatenate([labels, swap_inner(labels)])
    spectrum_total = 0.0
    glycan_total = 0.0
    held = glycans
    for step in range(STEPS):
        if step > 0:
            held = from_behind(held, "blk", 1)
        first_target = (position - step) % loop_count * lane_rows + core_first
        coef = coefficients(node_spectra, held, node_labels, first_target, scale, shift)
        spectrum_total += jnp.dot(coef, held, preferred_element_type=jnp.float32)
        partial_value = scale * lax.dot_general(
            coef, node_spectra, (((0,), (0,)), ((), ())), preferred_element_type=jnp.float32
        )
        if step > 0:
            back = from_behind(partial_value.astype(jnp.bfloat16), "blk", -step)
            partial_value = back.astype(jnp.float32)
        glycan_total += partial_value
    other = swap_inner((scale * spectrum_total[rows_here:]).astype(jnp.bfloat16))
    spectrum_total = scale * spectrum_total[:rows_here] + other.astype(jnp.float32)
    return spectrum_total.astype(jnp.bfloat16), glycan_total.astype(jnp.bfloat16)


@dataclasses.dataclass(frozen=True)
class Away:
    array: jax.Array


@dataclasses.dataclass(frozen=True)
class Block:
    target: int
    uses: tuple
    out: str
    offset: int = 0
    cut: int = 0
    prior: str = ""
    coef: str = ""


@dataclasses.dataclass(frozen=True)
class Plan:
    blocks: tuple
    pieces: tuple
    node: bool
    ends: tuple
    skips: bool
    rows: int


def pair_body(plan, *refs):
    if plan.skips:
        pl.when(refs[0][0] != 0)(functools.partial(pair_steps, plan, *refs[1:]))
    else:
        pair_steps(plan, *refs)


def pair_steps(plan, *refs):
    refs = list(refs)
    blocks, rows = plan.blocks, plan.rows

    def take(count):
        taken = refs[:count]
        del refs[:count]
        return taken

    def take_if(condition):
        return take(1)[0] if condition else None

    (consts,) = take(1)
    labels = take_if(plan.node)
    node_in = take(2) if plan.node else []
    ends_in = take(len(plan.ends))
    held_in = [take(len(p)) for p in plan.pieces]
    priors = [take_if(b.prior) for b in blocks]
    outs = [take((b.out != "") + (b.out == "split")) for b in blocks]
    coef_outs = [take_if(b.coef) for b in blocks]
    spectra = take_if(plan.node)
    ends = take_if(plan.ends)
    held = take(len(blocks))
    prior_held = [take_if(b.prior == "kept") for b in blocks]
    out_held = [take_if(b.out in ("kept", "split")) for b in blocks]
    coef_held = [take_if(b.coef) for b in blocks]
    (sems,) = take(1)
    used = 0

    def move(source, target):
        nonlocal used
        copy = pltpu.make_async_copy(source, target, sems.at[used])
        copy.start()
        used += 1
        return copy

    moving_node = [move(ref, spectra.at[pl.ds(i * rows, rows)]) for i, ref in enumerate(node_in)]
    moving = []
    for i, block in enumerate(blocks):
        moves = []
        at = 0
        for ref, (count, away) in zip(held_in[i], plan.pieces[i]):
            if away:
                moves.append(move(ref, held[i].at[pl.ds(at, count)]))
            at += count
        moving.append(moves)
    moving_prior = [
        move(priors[i], prior_held[i]) if b.prior == "kept" else None for i, b in enumerate(blocks)
    ]
    leaving = []

    def const(row):
        return consts[pl.ds(row, 1), pl.ds(0, 1)]

    scale, shift = const(0), const(1)
    if plan.ends:
        width = 2 * rows
        at = 0
        coded = []
        for ref, count in zip(ends_in, plan.ends):
            ending = at % rows + count > rows
            keep = count - LABEL_ROWS if ending else count
            ends[pl.ds(at, keep)] = ref[pl.ds(0, keep)]
            at += keep
            if ending:
                digits = ref[pl.ds(keep, LABEL_ROWS), pl.ds(0, width)].astype(jnp.float32)
                coded.append(digits[0:1] * 16384.0 + digits[1:2] * 128.0 + digits[2:3])
        lane = lax.broadcasted_iota(jnp.int32, (1, width), 1)
        end_labels = jnp.where(lane >= rows, coded[1], coded[0])

    def source(use):
        if use == "node":
            while moving_node:
                moving_node.pop(0).wait()
            return spectra[...], labels[...]
        return ends[...], end_labels

    for i, block in enumerate(blocks):

        def work(i=i, block=block):
            at = 0
            for ref, (count, away) in zip(held_in[i], plan.pieces[i]):
                if not away:
                    held[i][pl.ds(at, count)] = ref[...]
                at += count
            for copy in moving[i]:
                copy.wait()
            glycans = held[i][...]
            targets = lax.broadcasted_iota(jnp.int32, (glycans.shape[0], 1), 0)
            targets = targets.astype(jnp.float32) + (const(block.target) + float(block.offset))
            total = None
            for use in block.uses:
                here, row_labels = source(use)
                logits = lax.dot_general(
                    glycans, here, (((1,), (1,)), ((), ())), preferred_element_type=jnp.float32
                )
                logits = scale * logits + shift
                positive = jnp.where(targets == row_labels, 1.0, 0.0)
                coef = jax.nn.sigmoid(logits) - positive
                coef = coef.astype(jnp.bfloat16)
                if block.out:
                    part = jnp.dot(coef, here, preferred_element_type=jnp.float32)
                    total = part if total is None else total + part
                if block.coef and use == "node":
                    kept = coef * const(KEEP_ROW).astype(jnp.bfloat16) if block.coef == "masked" else coef
                    coef_held[i][...] = kept
                    leaving.append(move(coef_held[i], coef_outs[i]))
            if block.prior == "kept":
                moving_prior[i].wait()
                total = total + prior_held[i][...]
            elif block.prior:
                total = total + priors[i][...]
            if block.out == "kept":
                out_held[i][...] = total
                leaving.append(move(out_held[i], outs[i][0]))
            elif block.out == "split":
                cut = outs[i][0].shape[0]
                outs[i][0][...] = scale * total[:cut]
                out_held[i][...] = scale * total[cut:]
                leaving.append(move(out_held[i], outs[i][1]))
            elif block.out == "total":
                outs[i][0][...] = total
            elif block.out == "scaled":
                outs[i][0][...] = scale * total
            elif block.out:
                outs[i][0][...] = (scale * total).astype(jnp.bfloat16)

        work()
    for copy in leaving:
        copy.wait()


def in_vmem(array):
    return pltpu.with_memory_space_constraint(array, pltpu.VMEM)


def in_hbm(array):
    return pltpu.with_memory_space_constraint(array, pltpu.HBM)


def vmem_out(shape, kind):
    return pltpu.VMEM(shape, kind)


def hbm_out(shape, kind):
    return pltpu.HBM(shape, kind)


VMEM_SPEC = pl.BlockSpec(memory_space=pltpu.VMEM)
SMEM_SPEC = pl.BlockSpec(memory_space=pltpu.SMEM)
HBM_SPEC = pl.BlockSpec(memory_space=pltpu.HBM)
SMALL_COST = pl.CostEstimate(flops=1024, bytes_accessed=1024, transcendentals=0)


def params():
    return pltpu.CompilerParams(vmem_limit_bytes=VMEM_BYTES)


def pair_work(consts, blocks, rows, labels=None, node=None, ends=None, wanted=None):
    shapes = tuple(b[0] for b in blocks)
    pieces = []
    arrays = []
    for shape, array, _ in blocks:
        parts = array if isinstance(array, tuple) else (array,)
        away = [isinstance(x, Away) for x in parts]
        parts = [x.array if flag else x for x, flag in zip(parts, away)]
        pieces.append(tuple((x.shape[0], flag) for x, flag in zip(parts, away)))
        arrays += list(zip(parts, away))
    width = arrays[0][0].shape[1]
    ends = ends or ()
    end_rows = tuple(x.shape[0] for x in ends)
    plan = Plan(
        shapes,
        tuple(pieces),
        node is not None,
        end_rows,
        wanted is not None,
        rows,
    )

    operands = []
    in_specs = []
    if wanted is not None:
        operands.append(jnp.int32(wanted).reshape(1))
        in_specs.append(SMEM_SPEC)

    def give(array, away):
        operands.append(in_hbm(array) if away else in_vmem(array))
        in_specs.append(HBM_SPEC if away else VMEM_SPEC)

    give(consts, False)
    if node is not None:
        give(labels, False)
    for array in node or ():
        give(array, True)
    for array in ends:
        give(array, False)
    for array, away in arrays:
        give(array, away)
    for shape, _, prior in blocks:
        if shape.prior:
            give(prior, shape.prior == "kept")

    counts = [sum(count for count, _ in p) for p in pieces]
    outs = []
    out_specs = []

    def get(shape, kind, away):
        outs.append((hbm_out if away else vmem_out)(shape, kind))
        out_specs.append(HBM_SPEC if away else VMEM_SPEC)

    for shape, count in zip(shapes, counts):
        if shape.out == "split":
            get((shape.cut, width), jnp.float32, False)
            get((count - shape.cut, width), jnp.float32, True)
        elif shape.out:
            kind = jnp.bfloat16 if shape.out == "rounded" else jnp.float32
            get((count, width), kind, shape.out == "kept")
    for shape, count in zip(shapes, counts):
        if shape.coef:
            get((count, 2 * rows), jnp.bfloat16, True)

    scratch = []
    if node is not None:
        scratch.append(pltpu.VMEM((2 * rows, width), jnp.bfloat16))
    if ends:
        scratch.append(pltpu.VMEM((2 * rows, width), jnp.bfloat16))
    scratch += [pltpu.VMEM((n, width), jnp.bfloat16) for n in counts]
    scratch += [pltpu.VMEM((n, width), jnp.float32) for n, b in zip(counts, shapes) if b.prior == "kept"]
    for n, b in zip(counts, shapes):
        if b.out in ("kept", "split"):
            scratch.append(pltpu.VMEM((n - b.cut, width), jnp.float32))
    scratch += [pltpu.VMEM((n, 2 * rows), jnp.bfloat16) for n, b in zip(counts, shapes) if b.coef]
    scratch.append(pltpu.SemaphoreType.DMA((len(operands) + len(outs),)))
    return pl.pallas_call(
        functools.partial(pair_body, plan),
        out_shape=outs,
        in_specs=in_specs,
        out_specs=out_specs,
        scratch_shapes=scratch,
        cost_estimate=SMALL_COST,
        compiler_params=params(),
    )(*operands)


def code_labels(labels, row_count, width):
    digits = jnp.stack([labels // 16384, labels // 128 % 128, labels % 128]).astype(jnp.bfloat16)
    digits = jnp.concatenate([digits, digits, digits], axis=1)
    return jnp.pad(digits, ((0, row_count - 3), (0, width - digits.shape[1])))


def spectra_body(plan, outer, consts, labels, s_mine, s_other, coef_here, coef_side, coef_across, here, side, across, *rest):
    rows, n_next, n_far, n_last = plan
    nexts, rest = rest[:n_next], rest[n_next:]
    fars, rest = rest[:n_far], rest[n_far:]
    lasts, rest = rest[:n_last], rest[n_last:]
    mine_out, other_out, spectra, coefs, held, sems = rest
    used = 0

    def move(source, target):
        nonlocal used
        copy = pltpu.make_async_copy(source, target, sems.at[used])
        copy.start()
        used += 1
        return copy

    def fill(parts, target, at):
        moves = []
        for part in parts:
            moves.append(move(part, target.at[pl.ds(at, part.shape[0])]))
            at += part.shape[0]
        return moves

    moves = fill([s_mine, s_other], spectra, 0) + fill([coef_here, coef_side], coefs, 0)
    moves += fill([here, side], held, 0)

    @pl.when(outer[0] == 0)
    def _():
        for copy in fill([across] + list(fars), held, 2 * rows) + fill([coef_across], coefs, 2 * rows):
            copy.wait()

    @pl.when(outer[0] != 0)
    def _():
        for copy in fill(list(nexts) + list(lasts), held, 2 * rows):
            copy.wait()

    for copy in moves:
        copy.wait()
    scale, shift = consts[0:1, 0:1], consts[1:2, 0:1]

    def work_out(first, target_row):
        logits = lax.dot_general(
            held[pl.ds(first, rows)],
            spectra[...],
            (((1,), (1,)), ((), ())),
            preferred_element_type=jnp.float32,
        )
        logits = scale * logits + shift
        targets = lax.broadcasted_iota(jnp.int32, (rows, 1), 0).astype(jnp.float32)
        targets = targets + consts[target_row : target_row + 1, 0:1]
        positive = jnp.where(targets == labels[...], 1.0, 0.0)
        coefs[pl.ds(first, rows)] = (jax.nn.sigmoid(logits) - positive).astype(jnp.bfloat16)

    @pl.when(outer[0] != 0)
    def _():
        work_out(2 * rows, FAR_ROW)

    work_out(3 * rows, LAST_ROW)
    for i, out in enumerate((mine_out, other_out)):
        total = lax.dot_general(
            coefs[:, i * rows : (i + 1) * rows],
            held[...],
            (((0,), (0,)), ((), ())),
            preferred_element_type=jnp.float32,
        )
        out[...] = (scale * total).astype(out.dtype)


def spectra_work(outer, consts, labels, node, coefs, here, side, across, nexts, fars, lasts):
    rows, width = here.shape
    arrays = list(node) + list(coefs) + [here, side, across] + list(nexts) + list(fars) + list(lasts)
    plan = (rows, len(nexts), len(fars), len(lasts))
    return pl.pallas_call(
        functools.partial(spectra_body, plan),
        out_shape=[vmem_out((rows, width), jnp.float32), vmem_out((rows, width), jnp.bfloat16)],
        in_specs=[SMEM_SPEC, VMEM_SPEC, VMEM_SPEC] + [HBM_SPEC] * len(arrays),
        out_specs=[VMEM_SPEC] * 2,
        scratch_shapes=[
            pltpu.VMEM((2 * rows, width), jnp.bfloat16),
            pltpu.VMEM((4 * rows, 2 * rows), jnp.bfloat16),
            pltpu.VMEM((4 * rows, width), jnp.bfloat16),
            pltpu.SemaphoreType.DMA((len(arrays),)),
        ],
        cost_estimate=SMALL_COST,
        compiler_params=params(),
    )(
        jnp.int32(outer).reshape(1),
        in_vmem(consts),
        in_vmem(labels),
        *[in_hbm(a) for a in arrays],
    )


def split_body(whole, *parts):
    at = 0
    for part in parts:
        part[...] = whole[pl.ds(at, part.shape[0])]
        at += part.shape[0]


def split(whole, counts):
    return pl.pallas_call(
        split_body,
        out_shape=[vmem_out((n, whole.shape[1]), whole.dtype) for n in counts],
        in_specs=[VMEM_SPEC],
        out_specs=[VMEM_SPEC] * len(counts),
        cost_estimate=SMALL_COST,
        compiler_params=params(),
    )(in_vmem(whole))


def add_body(total, arrived, out, *scratch):
    if scratch:
        near, sem = scratch
        copy = pltpu.make_async_copy(total, near, sem)
        copy.start()
        copy.wait()
        total = near
    out[...] = (total[...] + arrived[...].astype(jnp.float32)).astype(jnp.bfloat16)


def add_rounded(total, arrived):
    away = isinstance(total, Away)
    scratch = [pltpu.VMEM(arrived.shape, jnp.float32), pltpu.SemaphoreType.DMA] if away else []
    return pl.pallas_call(
        add_body,
        out_shape=vmem_out(arrived.shape, jnp.bfloat16),
        in_specs=[HBM_SPEC if away else VMEM_SPEC, VMEM_SPEC],
        out_specs=VMEM_SPEC,
        scratch_shapes=scratch,
        cost_estimate=SMALL_COST,
        compiler_params=params(),
    )(in_hbm(total.array) if away else in_vmem(total), in_vmem(arrived))


def finish_spectra_body(mine_s, inside, *rest):
    others, (out, near) = rest[:-2], rest[-2:]
    at = 0
    for other in others:
        where = pl.ds(at, other.shape[0])
        out[where] = (mine_s[where] + other[...].astype(jnp.float32)).astype(jnp.bfloat16)
        at += other.shape[0]
    near[...] = inside[...]


def finish_spectra(mine_s, others, inside):
    return pl.pallas_call(
        finish_spectra_body,
        out_shape=[
            jax.ShapeDtypeStruct(mine_s.shape, jnp.bfloat16),
            vmem_out(inside.shape, inside.dtype),
        ],
        in_specs=[VMEM_SPEC] * (2 + len(others)),
        out_specs=[VMEM_SPEC] * 2,
        cost_estimate=SMALL_COST,
        compiler_params=params(),
    )(*[in_vmem(a) for a in [mine_s, inside] + others])


def finish_structures_body(flag, here_total, across_back, inside_a, inside_b, out):
    @pl.when(flag[0] != 0)
    def _():
        out[pl.ds(0, inside_a.shape[0])] = inside_a[...]
        out[pl.ds(inside_a.shape[0], inside_b.shape[0])] = inside_b[...]

    @pl.when(flag[0] == 0)
    def _():
        total = here_total[...] + across_back[...].astype(jnp.float32)
        out[...] = total.astype(jnp.bfloat16)


def finish_structures(flag, here_total, across_back, inside_a, inside_b):
    arrays = [here_total, across_back, inside_a, inside_b]
    return pl.pallas_call(
        finish_structures_body,
        out_shape=jax.ShapeDtypeStruct(here_total.shape, jnp.bfloat16),
        in_specs=[SMEM_SPEC] + [VMEM_SPEC] * len(arrays),
        out_specs=VMEM_SPEC,
        cost_estimate=SMALL_COST,
        compiler_params=params(),
    )(jnp.int32(flag).reshape(1), *[in_vmem(a) for a in arrays])


def along_line(spectra, glycans, labels, scale, shift):
    rows, width = spectra.shape
    node_rows = rows * lax.axis_size("inner")
    position = lax.axis_index("blk")
    outer = (position == 0) | (position == LINE - 1)
    core_first = lax.axis_index("sub") * node_rows + lax.axis_index("inner") * rows
    lane_rows = lax.axis_size("sub") * node_rows

    def permute(block, pairs):
        return lax.ppermute(block, ("blk", "inner"), pairs)

    def first_of(block_position):
        return (block_position * lane_rows + core_first).astype(jnp.float32)

    n_inner = lax.axis_size("inner")
    last = LINE - 1
    sides = []
    middle = []
    inward = []
    outward = []
    for core in range(n_inner):
        inward += [(core, n_inner + core), (last * n_inner + core, (last - 1) * n_inner + core)]
        outward += [(n_inner + core, core), ((last - 1) * n_inner + core, last * n_inner + core)]
        for at in range(LINE):
            sides.append((at * n_inner + core, (at ^ 1) * n_inner + core))
        for at in range(1, last):
            middle.append((at * n_inner + core, (last - at) * n_inner + core))
        for at in (0, last):
            middle.append((at * n_inner + core, at * n_inner + (core + 1) % n_inner))
    here_at, side_at, across_at, far_at = 2, 3, 4, FAR_ROW
    rows_of_consts = [
        scale,
        shift,
        first_of(position),
        first_of(position ^ 1),
        first_of(last - position),
        first_of((last - position) ^ 1),
        jnp.where(outer, 0.0, 1.0),
        first_of(jnp.where(outer, last - position, (last - position) ^ 1)),
    ]
    index = lax.broadcasted_iota(jnp.int32, (8, 128), 0)
    consts = jnp.zeros((8, 128), jnp.float32)
    for i, value in enumerate(rows_of_consts):
        consts = jnp.where(index == i, value, consts)

    cut = 2 * rows // 5
    half = rows // 2
    across = permute(glycans, middle)
    side = permute(glycans, sides)
    coded = code_labels(labels, LABEL_ROWS, width)
    end_mine = permute(jnp.concatenate([spectra, coded]), inward)
    partner = swap_inner(spectra)
    own_labels = labels.reshape(1, rows)
    node_labels = jnp.concatenate([own_labels, swap_inner(own_labels)], axis=1)
    node_labels = node_labels.astype(jnp.float32)
    node = dict(node=(spectra, partner), labels=node_labels)
    here_g, here_c = pair_work(
        consts, [(Block(here_at, ("node",), "kept", coef="all"), Away(glycans), None)], rows, **node
    )

    side = after(side, here_g)
    far_a, far_b = [permute(x, middle) for x in split(side, (cut, rows - cut))]
    across = after(across, here_g)
    next_out = permute(across, outward)
    side_g, across_g, side_c, across_c = pair_work(
        consts,
        [
            (Block(side_at, ("node",), "kept", coef="all"), Away(side), None),
            (Block(across_at, ("node",), "kept", coef="masked"), Away(across), None),
        ],
        rows,
        **node,
    )
    far_a = after(far_a, across_g)
    last_a = permute(far_a, sides)
    (far_g,) = pair_work(
        consts, [(Block(far_at, ("node",), "total"), far_a, None)], rows, wanted=~outer, **node
    )
    end_mine = after(end_mine, far_g)
    piece = -(-rows // 48) * 16
    two = (half + LABEL_ROWS, half)
    ends = (end_mine,) + tuple(swap_inner(x) for x in split(end_mine, two))

    far_a, far_b, next_out = lax.optimization_barrier((far_a, far_b, next_out, far_g))[:3]
    (far_a_out,) = pair_work(
        consts,
        [(Block(far_at, ("ends",), "rounded", prior="near"), far_a, far_g)],
        rows,
        wanted=~outer,
        ends=ends,
    )
    back_a = permute(far_a_out, middle)
    far_b = after(far_b, far_a_out)
    last_b = permute(far_b, sides)
    (far_b_out,) = pair_work(
        consts,
        [(Block(far_at, ("node", "ends"), "rounded", cut), far_b, None)],
        rows,
        wanted=~outer,
        ends=ends,
        **node,
    )
    back_b = permute(far_b_out, middle)
    (across_out,) = pair_work(
        consts,
        [
            (
                Block(across_at, ("ends",), "rounded", prior="kept"),
                Away(after(across, far_b_out)),
                across_g,
            )
        ],
        rows,
        wanted=~outer,
        ends=ends,
    )
    late_side, last_a = lax.optimization_barrier((side, last_a, across_out))[:2]
    late_side = Away(late_side)
    side_total_a, side_total_b = pair_work(
        consts,
        [(Block(side_at, ("ends",), "split", cut=cut, prior="kept"), late_side, side_g)],
        rows,
        wanted=~outer,
        ends=ends,
    )
    total_a = add_rounded(side_total_a, back_a)
    inside_a = permute(total_a, sides)
    across_back = permute(after(across_out, total_a), middle)
    back_b, last_b = lax.optimization_barrier((back_b, last_b, total_a))[:2]
    total_b = add_rounded(Away(side_total_b), back_b)
    inside_b = permute(total_b, sides)

    mine_s, other_s = spectra_work(
        outer,
        consts,
        node_labels,
        (spectra, partner),
        (here_c, side_c, across_c),
        after(glycans, total_b),
        side,
        across,
        (next_out,),
        (far_a, far_b),
        (last_a, last_b),
    )
    others = [swap_inner(x) for x in split(other_s, (piece, piece, rows - 2 * piece))]
    late, inside_a = lax.optimization_barrier((glycans, inside_a, mine_s))[:2]
    (here_total,) = pair_work(
        consts,
        [(Block(here_at, ("ends",), "scaled", prior="kept"), Away(late), here_g)],
        rows,
        wanted=~outer,
        ends=ends,
    )
    others[0] = after(others[0], here_total)
    grad_spectra, inside_a = finish_spectra(mine_s, others, inside_a)
    across_back = after(across_back, grad_spectra)
    return grad_spectra, finish_structures(outer, here_total, across_back, inside_a, inside_b)


def local(
    mass_profile_vectors,
    sugar_tree_vectors,
    matching_glycan_rows,
    sharpness_factor,
    offset_shift_term,
):
    work = along_line if lax.axis_size("blk") == STEPS == LINE else around_ring
    return work(
        mass_profile_vectors,
        sugar_tree_vectors,
        matching_glycan_rows,
        sharpness_factor[0],
        offset_shift_term[0],
    )


def solution(mesh):
    placed = (
        P(("groups", "blk", "sub", "inner"), None),
        P(("groups", "blk", "sub", "inner"), None),
        P(("groups", "blk", "sub", "inner")),
        P(),
        P(),
    )
    return jax.shard_map(
        local,
        mesh=mesh,
        in_specs=placed,
        out_specs=(
            P(("groups", "blk", "sub", "inner"), None),
            P(("groups", "blk", "sub", "inner"), None),
        ),
        check_vma=False,
    )
```

```python
import dataclasses
import functools

import jax
import jax.numpy as jnp
from jax import lax
from jax.experimental import pallas as pl
from jax.experimental.pallas import tpu as pltpu
from jax.sharding import PartitionSpec as P

STEPS = 4
LINE = 4
LABEL_ROWS = 16
FAR_ROW, KEEP_ROW, LAST_ROW = 5, 6, 7
VMEM_BYTES = 10 * 1024 * 1024


def from_behind(block, axis, distance):
    devices = range(lax.axis_size(axis))
    route = [((i - distance) % len(devices), i) for i in devices]
    return lax.ppermute(block, axis, route)


def swap_inner(block):
    return from_behind(block, "inner", 1)


def after(value, *earlier):
    return lax.optimization_barrier((value,) + earlier)[0]


def coefficients(spectra, glycans, labels, first_target, scale, shift):
    logits = (
        scale
        * lax.dot_general(
            spectra, glycans, (((1,), (1,)), ((), ())), preferred_element_type=jnp.float32
        )
        + shift
    )
    targets = first_target + jnp.arange(glycans.shape[0], dtype=jnp.int32)
    positive = (labels[:, None] == targets[None, :]).astype(jnp.float32)
    return (jax.nn.sigmoid(logits) - positive).astype(jnp.bfloat16)


def around_ring(spectra, glycans, labels, scale, shift):
    rows_here = spectra.shape[0]
    node_rows = rows_here * lax.axis_size("inner")
    loop_count = lax.axis_size("blk")
    position = lax.axis_index("blk")
    core_first = lax.axis_index("sub") * node_rows + lax.axis_index("inner") * rows_here
    lane_rows = lax.axis_size("sub") * node_rows
    node_spectra = jnp.concatenate([spectra, swap_inner(spectra)])
    node_labels = jnp.concatenate([labels, swap_inner(labels)])
    spectrum_total = 0.0
    glycan_total = 0.0
    held = glycans
    for step in range(STEPS):
        if step > 0:
            held = from_behind(held, "blk", 1)
        first_target = (position - step) % loop_count * lane_rows + core_first
        coef = coefficients(node_spectra, held, node_labels, first_target, scale, shift)
        spectrum_total += jnp.dot(coef, held, preferred_element_type=jnp.float32)
        partial_value = scale * lax.dot_general(
            coef, node_spectra, (((0,), (0,)), ((), ())), preferred_element_type=jnp.float32
        )
        if step > 0:
            back = from_behind(partial_value.astype(jnp.bfloat16), "blk", -step)
            partial_value = back.astype(jnp.float32)
        glycan_total += partial_value
    other = swap_inner((scale * spectrum_total[rows_here:]).astype(jnp.bfloat16))
    spectrum_total = scale * spectrum_total[:rows_here] + other.astype(jnp.float32)
    return spectrum_total.astype(jnp.bfloat16), glycan_total.astype(jnp.bfloat16)


@dataclasses.dataclass(frozen=True)
class Away:
    array: jax.Array


@dataclasses.dataclass(frozen=True)
class Block:
    target: int
    uses: tuple
    out: str
    offset: int = 0
    cut: int = 0
    prior: str = ""
    coef: str = ""


@dataclasses.dataclass(frozen=True)
class Plan:
    blocks: tuple
    pieces: tuple
    node: bool
    ends: tuple
    skips: bool
    rows: int


def pair_body(plan, *refs):
    if plan.skips:
        pl.when(refs[0][0] != 0)(functools.partial(pair_steps, plan, *refs[1:]))
    else:
        pair_steps(plan, *refs)


def pair_steps(plan, *refs):
    refs = list(refs)
    blocks, rows = plan.blocks, plan.rows

    def take(count):
        taken = refs[:count]
        del refs[:count]
        return taken

    def take_if(condition):
        return take(1)[0] if condition else None

    (consts,) = take(1)
    labels = take_if(plan.node)
    node_in = take(2) if plan.node else []
    ends_in = take(len(plan.ends))
    held_in = [take(len(p)) for p in plan.pieces]
    priors = [take_if(b.prior) for b in blocks]
    outs = [take((b.out != "") + (b.out == "split")) for b in blocks]
    coef_outs = [take_if(b.coef) for b in blocks]
    spectra = take_if(plan.node)
    ends = take_if(plan.ends)
    held = take(len(blocks))
    prior_held = [take_if(b.prior == "kept") for b in blocks]
    out_held = [take_if(b.out in ("kept", "split")) for b in blocks]
    coef_held = [take_if(b.coef) for b in blocks]
    (sems,) = take(1)
    used = 0

    def move(source, target):
        nonlocal used
        copy = pltpu.make_async_copy(source, target, sems.at[used])
        copy.start()
        used += 1
        return copy

    moving_node = [move(ref, spectra.at[pl.ds(i * rows, rows)]) for i, ref in enumerate(node_in)]
    moving = []
    for i, block in enumerate(blocks):
        moves = []
        at = 0
        for ref, (count, away) in zip(held_in[i], plan.pieces[i]):
            if away:
                moves.append(move(ref, held[i].at[pl.ds(at, count)]))
            at += count
        moving.append(moves)
    moving_prior = [
        move(priors[i], prior_held[i]) if b.prior == "kept" else None for i, b in enumerate(blocks)
    ]
    leaving = []

    def const(row):
        return consts[pl.ds(row, 1), pl.ds(0, 1)]

    scale, shift = const(0), const(1)
    if plan.ends:
        width = 2 * rows
        at = 0
        coded = []
        for ref, count in zip(ends_in, plan.ends):
            ending = at % rows + count > rows
            keep = count - LABEL_ROWS if ending else count
            ends[pl.ds(at, keep)] = ref[pl.ds(0, keep)]
            at += keep
            if ending:
                digits = ref[pl.ds(keep, LABEL_ROWS), pl.ds(0, width)].astype(jnp.float32)
                coded.append(digits[0:1] * 16384.0 + digits[1:2] * 128.0 + digits[2:3])
        lane = lax.broadcasted_iota(jnp.int32, (1, width), 1)
        end_labels = jnp.where(lane >= rows, coded[1], coded[0])

    def source(use):
        if use == "node":
            while moving_node:
                moving_node.pop(0).wait()
            return spectra[...], labels[...]
        return ends[...], end_labels

    for i, block in enumerate(blocks):

        def work(i=i, block=block):
            at = 0
            for ref, (count, away) in zip(held_in[i], plan.pieces[i]):
                if not away:
                    held[i][pl.ds(at, count)] = ref[...]
                at += count
            for copy in moving[i]:
                copy.wait()
            glycans = held[i][...]
            targets = lax.broadcasted_iota(jnp.int32, (glycans.shape[0], 1), 0)
            targets = targets.astype(jnp.float32) + (const(block.target) + float(block.offset))
            total = None
            for use in block.uses:
                here, row_labels = source(use)
                logits = lax.dot_general(
                    glycans, here, (((1,), (1,)), ((), ())), preferred_element_type=jnp.float32
                )
                logits = scale * logits + shift
                positive = jnp.where(targets == row_labels, 1.0, 0.0)
                coef = jax.nn.sigmoid(logits) - positive
                coef = coef.astype(jnp.bfloat16)
                if block.out:
                    part = jnp.dot(coef, here, preferred_element_type=jnp.float32)
                    total = part if total is None else total + part
                if block.coef and use == "node":
                    kept = coef * const(KEEP_ROW).astype(jnp.bfloat16) if block.coef == "masked" else coef
                    coef_held[i][...] = kept
                    leaving.append(move(coef_held[i], coef_outs[i]))
            if block.prior == "kept":
                moving_prior[i].wait()
                total = total + prior_held[i][...]
            elif block.prior:
                total = total + priors[i][...]
            if block.out == "kept":
                out_held[i][...] = total
                leaving.append(move(out_held[i], outs[i][0]))
            elif block.out == "split":
                cut = outs[i][0].shape[0]
                outs[i][0][...] = scale * total[:cut]
                out_held[i][...] = scale * total[cut:]
                leaving.append(move(out_held[i], outs[i][1]))
            elif block.out == "total":
                outs[i][0][...] = total
            elif block.out == "scaled":
                outs[i][0][...] = scale * total
            elif block.out:
                outs[i][0][...] = (scale * total).astype(jnp.bfloat16)

        work()
    for copy in leaving:
        copy.wait()


def in_vmem(array):
    return pltpu.with_memory_space_constraint(array, pltpu.VMEM)


def in_hbm(array):
    return pltpu.with_memory_space_constraint(array, pltpu.HBM)


def vmem_out(shape, kind):
    return pltpu.VMEM(shape, kind)


def hbm_out(shape, kind):
    return pltpu.HBM(shape, kind)


VMEM_SPEC = pl.BlockSpec(memory_space=pltpu.VMEM)
SMEM_SPEC = pl.BlockSpec(memory_space=pltpu.SMEM)
HBM_SPEC = pl.BlockSpec(memory_space=pltpu.HBM)
SMALL_COST = pl.CostEstimate(flops=1024, bytes_accessed=1024, transcendentals=0)


def params():
    return pltpu.CompilerParams(vmem_limit_bytes=VMEM_BYTES)


def pair_work(consts, blocks, rows, labels=None, node=None, ends=None, wanted=None):
    shapes = tuple(b[0] for b in blocks)
    pieces = []
    arrays = []
    for shape, array, _ in blocks:
        parts = array if isinstance(array, tuple) else (array,)
        away = [isinstance(x, Away) for x in parts]
        parts = [x.array if flag else x for x, flag in zip(parts, away)]
        pieces.append(tuple((x.shape[0], flag) for x, flag in zip(parts, away)))
        arrays += list(zip(parts, away))
    width = arrays[0][0].shape[1]
    ends = ends or ()
    end_rows = tuple(x.shape[0] for x in ends)
    plan = Plan(
        shapes,
        tuple(pieces),
        node is not None,
        end_rows,
        wanted is not None,
        rows,
    )

    operands = []
    in_specs = []
    if wanted is not None:
        operands.append(jnp.int32(wanted).reshape(1))
        in_specs.append(SMEM_SPEC)

    def give(array, away):
        operands.append(in_hbm(array) if away else in_vmem(array))
        in_specs.append(HBM_SPEC if away else VMEM_SPEC)

    give(consts, False)
    if node is not None:
        give(labels, False)
    for array in node or ():
        give(array, True)
    for array in ends:
        give(array, False)
    for array, away in arrays:
        give(array, away)
    for shape, _, prior in blocks:
        if shape.prior:
            give(prior, shape.prior == "kept")

    counts = [sum(count for count, _ in p) for p in pieces]
    outs = []
    out_specs = []

    def get(shape, kind, away):
        outs.append((hbm_out if away else vmem_out)(shape, kind))
        out_specs.append(HBM_SPEC if away else VMEM_SPEC)

    for shape, count in zip(shapes, counts):
        if shape.out == "split":
            get((shape.cut, width), jnp.float32, False)
            get((count - shape.cut, width), jnp.float32, True)
        elif shape.out:
            kind = jnp.bfloat16 if shape.out == "rounded" else jnp.float32
            get((count, width), kind, shape.out == "kept")
    for shape, count in zip(shapes, counts):
        if shape.coef:
            get((count, 2 * rows), jnp.bfloat16, True)

    scratch = []
    if node is not None:
        scratch.append(pltpu.VMEM((2 * rows, width), jnp.bfloat16))
    if ends:
        scratch.append(pltpu.VMEM((2 * rows, width), jnp.bfloat16))
    scratch += [pltpu.VMEM((n, width), jnp.bfloat16) for n in counts]
    scratch += [pltpu.VMEM((n, width), jnp.float32) for n, b in zip(counts, shapes) if b.prior == "kept"]
    for n, b in zip(counts, shapes):
        if b.out in ("kept", "split"):
            scratch.append(pltpu.VMEM((n - b.cut, width), jnp.float32))
    scratch += [pltpu.VMEM((n, 2 * rows), jnp.bfloat16) for n, b in zip(counts, shapes) if b.coef]
    scratch.append(pltpu.SemaphoreType.DMA((len(operands) + len(outs),)))
    return pl.pallas_call(
        functools.partial(pair_body, plan),
        out_shape=outs,
        in_specs=in_specs,
        out_specs=out_specs,
        scratch_shapes=scratch,
        cost_estimate=SMALL_COST,
        compiler_params=params(),
    )(*operands)


def code_labels(labels, row_count, width):
    digits = jnp.stack([labels // 16384, labels // 128 % 128, labels % 128]).astype(jnp.bfloat16)
    digits = jnp.concatenate([digits, digits, digits], axis=1)
    return jnp.pad(digits, ((0, row_count - 3), (0, width - digits.shape[1])))


def spectra_body(plan, outer, consts, labels, s_mine, s_other, coef_here, coef_side, coef_across, here, side, across, *rest):
    rows, n_next, n_far, n_last = plan
    nexts, rest = rest[:n_next], rest[n_next:]
    fars, rest = rest[:n_far], rest[n_far:]
    lasts, rest = rest[:n_last], rest[n_last:]
    mine_out, other_out, spectra, coefs, held, sems = rest
    used = 0

    def move(source, target):
        nonlocal used
        copy = pltpu.make_async_copy(source, target, sems.at[used])
        copy.start()
        used += 1
        return copy

    def fill(parts, target, at):
        moves = []
        for part in parts:
            moves.append(move(part, target.at[pl.ds(at, part.shape[0])]))
            at += part.shape[0]
        return moves

    moves = fill([s_mine, s_other], spectra, 0) + fill([coef_here, coef_side], coefs, 0)
    moves += fill([here, side], held, 0)

    @pl.when(outer[0] == 0)
    def _():
        for copy in fill([across] + list(fars), held, 2 * rows) + fill([coef_across], coefs, 2 * rows):
            copy.wait()

    @pl.when(outer[0] != 0)
    def _():
        for copy in fill(list(nexts) + list(lasts), held, 2 * rows):
            copy.wait()

    for copy in moves:
        copy.wait()
    scale, shift = consts[0:1, 0:1], consts[1:2, 0:1]

    def work_out(first, target_row):
        logits = lax.dot_general(
            held[pl.ds(first, rows)],
            spectra[...],
            (((1,), (1,)), ((), ())),
            preferred_element_type=jnp.float32,
        )
        logits = scale * logits + shift
        targets = lax.broadcasted_iota(jnp.int32, (rows, 1), 0).astype(jnp.float32)
        targets = targets + consts[target_row : target_row + 1, 0:1]
        positive = jnp.where(targets == labels[...], 1.0, 0.0)
        coefs[pl.ds(first, rows)] = (jax.nn.sigmoid(logits) - positive).astype(jnp.bfloat16)

    @pl.when(outer[0] != 0)
    def _():
        work_out(2 * rows, FAR_ROW)

    work_out(3 * rows, LAST_ROW)
    for i, out in enumerate((mine_out, other_out)):
        total = lax.dot_general(
            coefs[:, i * rows : (i + 1) * rows],
            held[...],
            (((0,), (0,)), ((), ())),
            preferred_element_type=jnp.float32,
        )
        out[...] = (scale * total).astype(out.dtype)


def spectra_work(outer, consts, labels, node, coefs, here, side, across, nexts, fars, lasts):
    rows, width = here.shape
    arrays = list(node) + list(coefs) + [here, side, across] + list(nexts) + list(fars) + list(lasts)
    plan = (rows, len(nexts), len(fars), len(lasts))
    return pl.pallas_call(
        functools.partial(spectra_body, plan),
        out_shape=[vmem_out((rows, width), jnp.float32), vmem_out((rows, width), jnp.bfloat16)],
        in_specs=[SMEM_SPEC, VMEM_SPEC, VMEM_SPEC] + [HBM_SPEC] * len(arrays),
        out_specs=[VMEM_SPEC] * 2,
        scratch_shapes=[
            pltpu.VMEM((2 * rows, width), jnp.bfloat16),
            pltpu.VMEM((4 * rows, 2 * rows), jnp.bfloat16),
            pltpu.VMEM((4 * rows, width), jnp.bfloat16),
            pltpu.SemaphoreType.DMA((len(arrays),)),
        ],
        cost_estimate=SMALL_COST,
        compiler_params=params(),
    )(
        jnp.int32(outer).reshape(1),
        in_vmem(consts),
        in_vmem(labels),
        *[in_hbm(a) for a in arrays],
    )


def split_body(whole, *parts):
    at = 0
    for part in parts:
        part[...] = whole[pl.ds(at, part.shape[0])]
        at += part.shape[0]


def split(whole, counts):
    return pl.pallas_call(
        split_body,
        out_shape=[vmem_out((n, whole.shape[1]), whole.dtype) for n in counts],
        in_specs=[VMEM_SPEC],
        out_specs=[VMEM_SPEC] * len(counts),
        cost_estimate=SMALL_COST,
        compiler_params=params(),
    )(in_vmem(whole))


def add_body(total, arrived, out, *scratch):
    if scratch:
        near, sem = scratch
        copy = pltpu.make_async_copy(total, near, sem)
        copy.start()
        copy.wait()
        total = near
    out[...] = (total[...] + arrived[...].astype(jnp.float32)).astype(jnp.bfloat16)


def add_rounded(total, arrived):
    away = isinstance(total, Away)
    scratch = [pltpu.VMEM(arrived.shape, jnp.float32), pltpu.SemaphoreType.DMA] if away else []
    return pl.pallas_call(
        add_body,
        out_shape=vmem_out(arrived.shape, jnp.bfloat16),
        in_specs=[HBM_SPEC if away else VMEM_SPEC, VMEM_SPEC],
        out_specs=VMEM_SPEC,
        scratch_shapes=scratch,
        cost_estimate=SMALL_COST,
        compiler_params=params(),
    )(in_hbm(total.array) if away else in_vmem(total), in_vmem(arrived))


def finish_spectra_body(mine_s, inside, *rest):
    others, (out, near) = rest[:-2], rest[-2:]
    at = 0
    for other in others:
        where = pl.ds(at, other.shape[0])
        out[where] = (mine_s[where] + other[...].astype(jnp.float32)).astype(jnp.bfloat16)
        at += other.shape[0]
    near[...] = inside[...]


def finish_spectra(mine_s, others, inside):
    return pl.pallas_call(
        finish_spectra_body,
        out_shape=[
            jax.ShapeDtypeStruct(mine_s.shape, jnp.bfloat16),
            vmem_out(inside.shape, inside.dtype),
        ],
        in_specs=[VMEM_SPEC] * (2 + len(others)),
        out_specs=[VMEM_SPEC] * 2,
        cost_estimate=SMALL_COST,
        compiler_params=params(),
    )(*[in_vmem(a) for a in [mine_s, inside] + others])


def finish_structures_body(flag, here_total, across_back, inside_a, inside_b, out):
    @pl.when(flag[0] != 0)
    def _():
        out[pl.ds(0, inside_a.shape[0])] = inside_a[...]
        out[pl.ds(inside_a.shape[0], inside_b.shape[0])] = inside_b[...]

    @pl.when(flag[0] == 0)
    def _():
        total = here_total[...] + across_back[...].astype(jnp.float32)
        out[...] = total.astype(jnp.bfloat16)


def finish_structures(flag, here_total, across_back, inside_a, inside_b):
    arrays = [here_total, across_back, inside_a, inside_b]
    return pl.pallas_call(
        finish_structures_body,
        out_shape=jax.ShapeDtypeStruct(here_total.shape, jnp.bfloat16),
        in_specs=[SMEM_SPEC] + [VMEM_SPEC] * len(arrays),
        out_specs=VMEM_SPEC,
        cost_estimate=SMALL_COST,
        compiler_params=params(),
    )(jnp.int32(flag).reshape(1), *[in_vmem(a) for a in arrays])


def along_line(spectra, glycans, labels, scale, shift):
    rows, width = spectra.shape
    node_rows = rows * lax.axis_size("inner")
    position = lax.axis_index("blk")
    outer = (position == 0) | (position == LINE - 1)
    core_first = lax.axis_index("sub") * node_rows + lax.axis_index("inner") * rows
    lane_rows = lax.axis_size("sub") * node_rows

    def permute(block, pairs):
        return lax.ppermute(block, ("blk", "inner"), pairs)

    def first_of(block_position):
        return (block_position * lane_rows + core_first).astype(jnp.float32)

    n_inner = lax.axis_size("inner")
    last = LINE - 1
    sides = []
    middle = []
    inward = []
    outward = []
    for core in range(n_inner):
        inward += [(core, n_inner + core), (last * n_inner + core, (last - 1) * n_inner + core)]
        outward += [(n_inner + core, core), ((last - 1) * n_inner + core, last * n_inner + core)]
        for at in range(LINE):
            sides.append((at * n_inner + core, (at ^ 1) * n_inner + core))
        for at in range(1, last):
            middle.append((at * n_inner + core, (last - at) * n_inner + core))
        for at in (0, last):
            middle.append((at * n_inner + core, at * n_inner + (core + 1) % n_inner))
    here_at, side_at, across_at, far_at = 2, 3, 4, FAR_ROW
    rows_of_consts = [
        scale,
        shift,
        first_of(position),
        first_of(position ^ 1),
        first_of(last - position),
        first_of((last - position) ^ 1),
        jnp.where(outer, 0.0, 1.0),
        first_of(jnp.where(outer, last - position, (last - position) ^ 1)),
    ]
    index = lax.broadcasted_iota(jnp.int32, (8, 128), 0)
    consts = jnp.zeros((8, 128), jnp.float32)
    for i, value in enumerate(rows_of_consts):
        consts = jnp.where(index == i, value, consts)

    cut = 2 * rows // 5
    half = rows // 2
    across = permute(glycans, middle)
    side = permute(glycans, sides)
    coded = code_labels(labels, LABEL_ROWS, width)
    end_mine = permute(jnp.concatenate([spectra, coded]), inward)
    partner = swap_inner(spectra)
    own_labels = labels.reshape(1, rows)
    node_labels = jnp.concatenate([own_labels, swap_inner(own_labels)], axis=1)
    node_labels = node_labels.astype(jnp.float32)
    node = dict(node=(spectra, partner), labels=node_labels)
    here_g, here_c = pair_work(
        consts, [(Block(here_at, ("node",), "kept", coef="all"), Away(glycans), None)], rows, **node
    )

    side = after(side, here_g)
    far_a, far_b = [permute(x, middle) for x in split(side, (cut, rows - cut))]
    across = after(across, here_g)
    next_out = permute(across, outward)
    side_g, across_g, side_c, across_c = pair_work(
        consts,
        [
            (Block(side_at, ("node",), "kept", coef="all"), Away(side), None),
            (Block(across_at, ("node",), "kept", coef="masked"), Away(across), None),
        ],
        rows,
        **node,
    )
    far_a = after(far_a, across_g)
    last_a = permute(far_a, sides)
    (far_g,) = pair_work(
        consts, [(Block(far_at, ("node",), "total"), far_a, None)], rows, wanted=~outer, **node
    )
    end_mine = after(end_mine, far_g)
    piece = -(-rows // 48) * 16
    two = (half + LABEL_ROWS, half)
    ends = (end_mine,) + tuple(swap_inner(x) for x in split(end_mine, two))

    far_a, far_b, next_out = lax.optimization_barrier((far_a, far_b, next_out, far_g))[:3]
    (far_a_out,) = pair_work(
        consts,
        [(Block(far_at, ("ends",), "rounded", prior="near"), far_a, far_g)],
        rows,
        wanted=~outer,
        ends=ends,
    )
    back_a = permute(far_a_out, middle)
    far_b = after(far_b, far_a_out)
    last_b = permute(far_b, sides)
    (far_b_out,) = pair_work(
        consts,
        [(Block(far_at, ("node", "ends"), "rounded", cut), far_b, None)],
        rows,
        wanted=~outer,
        ends=ends,
        **node,
    )
    back_b = permute(far_b_out, middle)
    (across_out,) = pair_work(
        consts,
        [
            (
                Block(across_at, ("ends",), "rounded", prior="kept"),
                Away(after(across, far_b_out)),
                across_g,
            )
        ],
        rows,
        wanted=~outer,
        ends=ends,
    )
    late_side, last_a = lax.optimization_barrier((side, last_a, across_out))[:2]
    late_side = Away(late_side)
    side_total_a, side_total_b = pair_work(
        consts,
        [(Block(side_at, ("ends",), "split", cut=cut, prior="kept"), late_side, side_g)],
        rows,
        wanted=~outer,
        ends=ends,
    )
    total_a = add_rounded(side_total_a, back_a)
    inside_a = permute(total_a, sides)
    across_back = permute(after(across_out, total_a), middle)
    back_b, last_b = lax.optimization_barrier((back_b, last_b, total_a))[:2]
    total_b = add_rounded(Away(side_total_b), back_b)
    inside_b = permute(total_b, sides)

    mine_s, other_s = spectra_work(
        outer,
        consts,
        node_labels,
        (spectra, partner),
        (here_c, side_c, across_c),
        after(glycans, total_b),
        side,
        across,
        (next_out,),
        (far_a, far_b),
        (last_a, last_b),
    )
    others = [swap_inner(x) for x in split(other_s, (piece, piece, rows - 2 * piece))]
    late, inside_a = lax.optimization_barrier((glycans, inside_a, mine_s))[:2]
    (here_total,) = pair_work(
        consts,
        [(Block(here_at, ("ends",), "scaled", prior="kept"), Away(late), here_g)],
        rows,
        wanted=~outer,
        ends=ends,
    )
    others[0] = after(others[0], here_total)
    grad_spectra, inside_a = finish_spectra(mine_s, others, inside_a)
    across_back = after(across_back, grad_spectra)
    return grad_spectra, finish_structures(outer, here_total, across_back, inside_a, inside_b)


def local(
    mass_profile_vectors,
    sugar_tree_vectors,
    matching_glycan_rows,
    sharpness_factor,
    offset_shift_term,
):
    work = along_line if lax.axis_size("blk") == STEPS == LINE else around_ring
    return work(
        mass_profile_vectors,
        sugar_tree_vectors,
        matching_glycan_rows,
        sharpness_factor[0],
        offset_shift_term[0],
    )


def solution(mesh):
    placed = (
        P(("groups", "blk", "sub", "inner"), None),
        P(("groups", "blk", "sub", "inner"), None),
        P(("groups", "blk", "sub", "inner")),
        P(),
        P(),
    )
    return jax.shard_map(
        local,
        mesh=mesh,
        in_specs=placed,
        out_specs=(
            P(("groups", "blk", "sub", "inner"), None),
            P(("groups", "blk", "sub", "inner"), None),
        ),
        check_vma=False,
    )
```

```python
import dataclasses
import functools

import jax
import jax.numpy as jnp
from jax import lax
from jax.experimental import pallas as pl
from jax.experimental.pallas import tpu as pltpu
from jax.sharding import PartitionSpec as P

STEPS = 4
LINE = 4
LABEL_ROWS = 16
FAR_ROW, KEEP_ROW, LAST_ROW = 5, 6, 7
VMEM_BYTES = 10 * 1024 * 1024


def from_behind(block, axis, distance):
    devices = range(lax.axis_size(axis))
    route = [((i - distance) % len(devices), i) for i in devices]
    return lax.ppermute(block, axis, route)


def swap_inner(block):
    return from_behind(block, "inner", 1)


def after(value, *earlier):
    return lax.optimization_barrier((value,) + earlier)[0]


def coefficients(spectra, glycans, labels, first_target, scale, shift):
    logits = (
        scale
        * lax.dot_general(
            spectra, glycans, (((1,), (1,)), ((), ())), preferred_element_type=jnp.float32
        )
        + shift
    )
    targets = first_target + jnp.arange(glycans.shape[0], dtype=jnp.int32)
    positive = (labels[:, None] == targets[None, :]).astype(jnp.float32)
    return (jax.nn.sigmoid(logits) - positive).astype(jnp.bfloat16)


def around_ring(spectra, glycans, labels, scale, shift):
    rows_here = spectra.shape[0]
    node_rows = rows_here * lax.axis_size("inner")
    loop_count = lax.axis_size("blk")
    position = lax.axis_index("blk")
    core_first = lax.axis_index("sub") * node_rows + lax.axis_index("inner") * rows_here
    lane_rows = lax.axis_size("sub") * node_rows
    node_spectra = jnp.concatenate([spectra, swap_inner(spectra)])
    node_labels = jnp.concatenate([labels, swap_inner(labels)])
    spectrum_total = 0.0
    glycan_total = 0.0
    held = glycans
    for step in range(STEPS):
        if step > 0:
            held = from_behind(held, "blk", 1)
        first_target = (position - step) % loop_count * lane_rows + core_first
        coef = coefficients(node_spectra, held, node_labels, first_target, scale, shift)
        spectrum_total += jnp.dot(coef, held, preferred_element_type=jnp.float32)
        partial_value = scale * lax.dot_general(
            coef, node_spectra, (((0,), (0,)), ((), ())), preferred_element_type=jnp.float32
        )
        if step > 0:
            back = from_behind(partial_value.astype(jnp.bfloat16), "blk", -step)
            partial_value = back.astype(jnp.float32)
        glycan_total += partial_value
    other = swap_inner((scale * spectrum_total[rows_here:]).astype(jnp.bfloat16))
    spectrum_total = scale * spectrum_total[:rows_here] + other.astype(jnp.float32)
    return spectrum_total.astype(jnp.bfloat16), glycan_total.astype(jnp.bfloat16)


@dataclasses.dataclass(frozen=True)
class Away:
    array: jax.Array


@dataclasses.dataclass(frozen=True)
class Block:
    target: int
    uses: tuple
    out: str
    offset: int = 0
    cut: int = 0
    prior: str = ""
    coef: str = ""


@dataclasses.dataclass(frozen=True)
class Plan:
    blocks: tuple
    pieces: tuple
    node: bool
    ends: tuple
    skips: bool
    rows: int


def pair_body(plan, *refs):
    if plan.skips:
        pl.when(refs[0][0] != 0)(functools.partial(pair_steps, plan, *refs[1:]))
    else:
        pair_steps(plan, *refs)


def pair_steps(plan, *refs):
    refs = list(refs)
    blocks, rows = plan.blocks, plan.rows

    def take(count):
        taken = refs[:count]
        del refs[:count]
        return taken

    def take_if(condition):
        return take(1)[0] if condition else None

    (consts,) = take(1)
    labels = take_if(plan.node)
    node_in = take(2) if plan.node else []
    ends_in = take(len(plan.ends))
    held_in = [take(len(p)) for p in plan.pieces]
    priors = [take_if(b.prior) for b in blocks]
    outs = [take((b.out != "") + (b.out == "split")) for b in blocks]
    coef_outs = [take_if(b.coef) for b in blocks]
    spectra = take_if(plan.node)
    ends = take_if(plan.ends)
    held = take(len(blocks))
    prior_held = [take_if(b.prior == "kept") for b in blocks]
    out_held = [take_if(b.out in ("kept", "split")) for b in blocks]
    coef_held = [take_if(b.coef) for b in blocks]
    (sems,) = take(1)
    used = 0

    def move(source, target):
        nonlocal used
        copy = pltpu.make_async_copy(source, target, sems.at[used])
        copy.start()
        used += 1
        return copy

    moving_node = [move(ref, spectra.at[pl.ds(i * rows, rows)]) for i, ref in enumerate(node_in)]
    moving = []
    for i, block in enumerate(blocks):
        moves = []
        at = 0
        for ref, (count, away) in zip(held_in[i], plan.pieces[i]):
            if away:
                moves.append(move(ref, held[i].at[pl.ds(at, count)]))
            at += count
        moving.append(moves)
    moving_prior = [
        move(priors[i], prior_held[i]) if b.prior == "kept" else None for i, b in enumerate(blocks)
    ]
    leaving = []

    def const(row):
        return consts[pl.ds(row, 1), pl.ds(0, 1)]

    scale, shift = const(0), const(1)
    if plan.ends:
        width = 2 * rows
        at = 0
        coded = []
        for ref, count in zip(ends_in, plan.ends):
            ending = at % rows + count > rows
            keep = count - LABEL_ROWS if ending else count
            ends[pl.ds(at, keep)] = ref[pl.ds(0, keep)]
            at += keep
            if ending:
                digits = ref[pl.ds(keep, LABEL_ROWS), pl.ds(0, width)].astype(jnp.float32)
                coded.append(digits[0:1] * 16384.0 + digits[1:2] * 128.0 + digits[2:3])
        lane = lax.broadcasted_iota(jnp.int32, (1, width), 1)
        end_labels = jnp.where(lane >= rows, coded[1], coded[0])

    def source(use):
        if use == "node":
            while moving_node:
                moving_node.pop(0).wait()
            return spectra[...], labels[...]
        return ends[...], end_labels

    for i, block in enumerate(blocks):

        def work(i=i, block=block):
            at = 0
            for ref, (count, away) in zip(held_in[i], plan.pieces[i]):
                if not away:
                    held[i][pl.ds(at, count)] = ref[...]
                at += count
            for copy in moving[i]:
                copy.wait()
            glycans = held[i][...]
            targets = lax.broadcasted_iota(jnp.int32, (glycans.shape[0], 1), 0)
            targets = targets.astype(jnp.float32) + (const(block.target) + float(block.offset))
            total = None
            for use in block.uses:
                here, row_labels = source(use)
                logits = lax.dot_general(
                    glycans, here, (((1,), (1,)), ((), ())), preferred_element_type=jnp.float32
                )
                logits = scale * logits + shift
                positive = jnp.where(targets == row_labels, 1.0, 0.0)
                coef = jax.nn.sigmoid(logits) - positive
                coef = coef.astype(jnp.bfloat16)
                if block.out:
                    part = jnp.dot(coef, here, preferred_element_type=jnp.float32)
                    total = part if total is None else total + part
                if block.coef and use == "node":
                    kept = coef * const(KEEP_ROW).astype(jnp.bfloat16) if block.coef == "masked" else coef
                    coef_held[i][...] = kept
                    leaving.append(move(coef_held[i], coef_outs[i]))
            if block.prior == "kept":
                moving_prior[i].wait()
                total = total + prior_held[i][...]
            elif block.prior:
                total = total + priors[i][...]
            if block.out == "kept":
                out_held[i][...] = total
                leaving.append(move(out_held[i], outs[i][0]))
            elif block.out == "split":
                cut = outs[i][0].shape[0]
                outs[i][0][...] = scale * total[:cut]
                out_held[i][...] = scale * total[cut:]
                leaving.append(move(out_held[i], outs[i][1]))
            elif block.out == "total":
                outs[i][0][...] = total
            elif block.out == "scaled":
                outs[i][0][...] = scale * total
            elif block.out:
                outs[i][0][...] = (scale * total).astype(jnp.bfloat16)

        work()
    for copy in leaving:
        copy.wait()


def in_vmem(array):
    return pltpu.with_memory_space_constraint(array, pltpu.VMEM)


def in_hbm(array):
    return pltpu.with_memory_space_constraint(array, pltpu.HBM)


def vmem_out(shape, kind):
    return pltpu.VMEM(shape, kind)


def hbm_out(shape, kind):
    return pltpu.HBM(shape, kind)


VMEM_SPEC = pl.BlockSpec(memory_space=pltpu.VMEM)
SMEM_SPEC = pl.BlockSpec(memory_space=pltpu.SMEM)
HBM_SPEC = pl.BlockSpec(memory_space=pltpu.HBM)
SMALL_COST = pl.CostEstimate(flops=1024, bytes_accessed=1024, transcendentals=0)


def params():
    return pltpu.CompilerParams(vmem_limit_bytes=VMEM_BYTES)


def pair_work(consts, blocks, rows, labels=None, node=None, ends=None, wanted=None):
    shapes = tuple(b[0] for b in blocks)
    pieces = []
    arrays = []
    for shape, array, _ in blocks:
        parts = array if isinstance(array, tuple) else (array,)
        away = [isinstance(x, Away) for x in parts]
        parts = [x.array if flag else x for x, flag in zip(parts, away)]
        pieces.append(tuple((x.shape[0], flag) for x, flag in zip(parts, away)))
        arrays += list(zip(parts, away))
    width = arrays[0][0].shape[1]
    ends = ends or ()
    end_rows = tuple(x.shape[0] for x in ends)
    plan = Plan(
        shapes,
        tuple(pieces),
        node is not None,
        end_rows,
        wanted is not None,
        rows,
    )

    operands = []
    in_specs = []
    if wanted is not None:
        operands.append(jnp.int32(wanted).reshape(1))
        in_specs.append(SMEM_SPEC)

    def give(array, away):
        operands.append(in_hbm(array) if away else in_vmem(array))
        in_specs.append(HBM_SPEC if away else VMEM_SPEC)

    give(consts, False)
    if node is not None:
        give(labels, False)
    for array in node or ():
        give(array, True)
    for array in ends:
        give(array, False)
    for array, away in arrays:
        give(array, away)
    for shape, _, prior in blocks:
        if shape.prior:
            give(prior, shape.prior == "kept")

    counts = [sum(count for count, _ in p) for p in pieces]
    outs = []
    out_specs = []

    def get(shape, kind, away):
        outs.append((hbm_out if away else vmem_out)(shape, kind))
        out_specs.append(HBM_SPEC if away else VMEM_SPEC)

    for shape, count in zip(shapes, counts):
        if shape.out == "split":
            get((shape.cut, width), jnp.float32, False)
            get((count - shape.cut, width), jnp.float32, True)
        elif shape.out:
            kind = jnp.bfloat16 if shape.out == "rounded" else jnp.float32
            get((count, width), kind, shape.out == "kept")
    for shape, count in zip(shapes, counts):
        if shape.coef:
            get((count, 2 * rows), jnp.bfloat16, True)

    scratch = []
    if node is not None:
        scratch.append(pltpu.VMEM((2 * rows, width), jnp.bfloat16))
    if ends:
        scratch.append(pltpu.VMEM((2 * rows, width), jnp.bfloat16))
    scratch += [pltpu.VMEM((n, width), jnp.bfloat16) for n in counts]
    scratch += [pltpu.VMEM((n, width), jnp.float32) for n, b in zip(counts, shapes) if b.prior == "kept"]
    for n, b in zip(counts, shapes):
        if b.out in ("kept", "split"):
            scratch.append(pltpu.VMEM((n - b.cut, width), jnp.float32))
    scratch += [pltpu.VMEM((n, 2 * rows), jnp.bfloat16) for n, b in zip(counts, shapes) if b.coef]
    scratch.append(pltpu.SemaphoreType.DMA((len(operands) + len(outs),)))
    return pl.pallas_call(
        functools.partial(pair_body, plan),
        out_shape=outs,
        in_specs=in_specs,
        out_specs=out_specs,
        scratch_shapes=scratch,
        cost_estimate=SMALL_COST,
        compiler_params=params(),
    )(*operands)


def code_labels(labels, row_count, width):
    digits = jnp.stack([labels // 16384, labels // 128 % 128, labels % 128]).astype(jnp.bfloat16)
    digits = jnp.concatenate([digits, digits, digits], axis=1)
    return jnp.pad(digits, ((0, row_count - 3), (0, width - digits.shape[1])))


def spectra_body(plan, outer, consts, labels, s_mine, s_other, coef_here, coef_side, coef_across, here, side, across, *rest):
    rows, n_next, n_far, n_last = plan
    nexts, rest = rest[:n_next], rest[n_next:]
    fars, rest = rest[:n_far], rest[n_far:]
    lasts, rest = rest[:n_last], rest[n_last:]
    mine_out, other_out, spectra, coefs, held, sems = rest
    used = 0

    def move(source, target):
        nonlocal used
        copy = pltpu.make_async_copy(source, target, sems.at[used])
        copy.start()
        used += 1
        return copy

    def fill(parts, target, at):
        moves = []
        for part in parts:
            moves.append(move(part, target.at[pl.ds(at, part.shape[0])]))
            at += part.shape[0]
        return moves

    moves = fill([s_mine, s_other], spectra, 0) + fill([coef_here, coef_side], coefs, 0)
    moves += fill([here, side], held, 0)

    @pl.when(outer[0] == 0)
    def _():
        for copy in fill([across] + list(fars), held, 2 * rows) + fill([coef_across], coefs, 2 * rows):
            copy.wait()

    @pl.when(outer[0] != 0)
    def _():
        for copy in fill(list(nexts) + list(lasts), held, 2 * rows):
            copy.wait()

    for copy in moves:
        copy.wait()
    scale, shift = consts[0:1, 0:1], consts[1:2, 0:1]

    def work_out(first, target_row):
        logits = lax.dot_general(
            held[pl.ds(first, rows)],
            spectra[...],
            (((1,), (1,)), ((), ())),
            preferred_element_type=jnp.float32,
        )
        logits = scale * logits + shift
        targets = lax.broadcasted_iota(jnp.int32, (rows, 1), 0).astype(jnp.float32)
        targets = targets + consts[target_row : target_row + 1, 0:1]
        positive = jnp.where(targets == labels[...], 1.0, 0.0)
        coefs[pl.ds(first, rows)] = (jax.nn.sigmoid(logits) - positive).astype(jnp.bfloat16)

    @pl.when(outer[0] != 0)
    def _():
        work_out(2 * rows, FAR_ROW)

    work_out(3 * rows, LAST_ROW)
    for i, out in enumerate((mine_out, other_out)):
        total = lax.dot_general(
            coefs[:, i * rows : (i + 1) * rows],
            held[...],
            (((0,), (0,)), ((), ())),
            preferred_element_type=jnp.float32,
        )
        out[...] = (scale * total).astype(out.dtype)


def spectra_work(outer, consts, labels, node, coefs, here, side, across, nexts, fars, lasts):
    rows, width = here.shape
    arrays = list(node) + list(coefs) + [here, side, across] + list(nexts) + list(fars) + list(lasts)
    plan = (rows, len(nexts), len(fars), len(lasts))
    return pl.pallas_call(
        functools.partial(spectra_body, plan),
        out_shape=[vmem_out((rows, width), jnp.float32), vmem_out((rows, width), jnp.bfloat16)],
        in_specs=[SMEM_SPEC, VMEM_SPEC, VMEM_SPEC] + [HBM_SPEC] * len(arrays),
        out_specs=[VMEM_SPEC] * 2,
        scratch_shapes=[
            pltpu.VMEM((2 * rows, width), jnp.bfloat16),
            pltpu.VMEM((4 * rows, 2 * rows), jnp.bfloat16),
            pltpu.VMEM((4 * rows, width), jnp.bfloat16),
            pltpu.SemaphoreType.DMA((len(arrays),)),
        ],
        cost_estimate=SMALL_COST,
        compiler_params=params(),
    )(
        jnp.int32(outer).reshape(1),
        in_vmem(consts),
        in_vmem(labels),
        *[in_hbm(a) for a in arrays],
    )


def split_body(whole, *parts):
    at = 0
    for part in parts:
        part[...] = whole[pl.ds(at, part.shape[0])]
        at += part.shape[0]


def split(whole, counts):
    return pl.pallas_call(
        split_body,
        out_shape=[vmem_out((n, whole.shape[1]), whole.dtype) for n in counts],
        in_specs=[VMEM_SPEC],
        out_specs=[VMEM_SPEC] * len(counts),
        cost_estimate=SMALL_COST,
        compiler_params=params(),
    )(in_vmem(whole))


def add_body(total, arrived, out, *scratch):
    if scratch:
        near, sem = scratch
        copy = pltpu.make_async_copy(total, near, sem)
        copy.start()
        copy.wait()
        total = near
    out[...] = (total[...] + arrived[...].astype(jnp.float32)).astype(jnp.bfloat16)


def add_rounded(total, arrived):
    away = isinstance(total, Away)
    scratch = [pltpu.VMEM(arrived.shape, jnp.float32), pltpu.SemaphoreType.DMA] if away else []
    return pl.pallas_call(
        add_body,
        out_shape=vmem_out(arrived.shape, jnp.bfloat16),
        in_specs=[HBM_SPEC if away else VMEM_SPEC, VMEM_SPEC],
        out_specs=VMEM_SPEC,
        scratch_shapes=scratch,
        cost_estimate=SMALL_COST,
        compiler_params=params(),
    )(in_hbm(total.array) if away else in_vmem(total), in_vmem(arrived))


def finish_spectra_body(mine_s, *rest):
    others, out = rest[:-1], rest[-1]
    at = 0
    for other in others:
        where = pl.ds(at, other.shape[0])
        out[where] = (mine_s[where] + other[...].astype(jnp.float32)).astype(jnp.bfloat16)
        at += other.shape[0]


def finish_spectra(mine_s, others):
    return pl.pallas_call(
        finish_spectra_body,
        out_shape=jax.ShapeDtypeStruct(mine_s.shape, jnp.bfloat16),
        in_specs=[VMEM_SPEC] * (1 + len(others)),
        out_specs=VMEM_SPEC,
        cost_estimate=SMALL_COST,
        compiler_params=params(),
    )(*[in_vmem(a) for a in [mine_s] + others])


def finish_structures_body(flag, here_total, across_back, inside_a, inside_b, out, held, sems):
    cut = inside_a.shape[0]

    @pl.when(flag[0] != 0)
    def _():
        first = pltpu.make_async_copy(inside_a, out.at[pl.ds(0, cut)], sems.at[0])
        second = pltpu.make_async_copy(inside_b, out.at[pl.ds(cut, inside_b.shape[0])], sems.at[1])
        first.start()
        second.start()
        first.wait()
        second.wait()

    @pl.when(flag[0] == 0)
    def _():
        total = here_total[...] + across_back[...].astype(jnp.float32)
        held[...] = total.astype(jnp.bfloat16)
        copy = pltpu.make_async_copy(held, out, sems.at[0])
        copy.start()
        copy.wait()


def finish_structures(flag, here_total, across_back, inside_a, inside_b):
    shape = here_total.shape
    return pl.pallas_call(
        finish_structures_body,
        out_shape=jax.ShapeDtypeStruct(shape, jnp.bfloat16),
        in_specs=[SMEM_SPEC, VMEM_SPEC, VMEM_SPEC, HBM_SPEC, HBM_SPEC],
        out_specs=HBM_SPEC,
        scratch_shapes=[pltpu.VMEM(shape, jnp.bfloat16), pltpu.SemaphoreType.DMA((2,))],
        cost_estimate=SMALL_COST,
        compiler_params=params(),
    )(
        jnp.int32(flag).reshape(1),
        in_vmem(here_total),
        in_vmem(across_back),
        in_hbm(inside_a),
        in_hbm(inside_b),
    )


def along_line(spectra, glycans, labels, scale, shift):
    rows, width = spectra.shape
    node_rows = rows * lax.axis_size("inner")
    position = lax.axis_index("blk")
    outer = (position == 0) | (position == LINE - 1)
    core_first = lax.axis_index("sub") * node_rows + lax.axis_index("inner") * rows
    lane_rows = lax.axis_size("sub") * node_rows

    def permute(block, pairs):
        return lax.ppermute(block, ("blk", "inner"), pairs)

    def first_of(block_position):
        return (block_position * lane_rows + core_first).astype(jnp.float32)

    n_inner = lax.axis_size("inner")
    last = LINE - 1
    sides = []
    middle = []
    inward = []
    outward = []
    for core in range(n_inner):
        inward += [(core, n_inner + core), (last * n_inner + core, (last - 1) * n_inner + core)]
        outward += [(n_inner + core, core), ((last - 1) * n_inner + core, last * n_inner + core)]
        for at in range(LINE):
            sides.append((at * n_inner + core, (at ^ 1) * n_inner + core))
        for at in range(1, last):
            middle.append((at * n_inner + core, (last - at) * n_inner + core))
        for at in (0, last):
            middle.append((at * n_inner + core, at * n_inner + (core + 1) % n_inner))
    here_at, side_at, across_at, far_at = 2, 3, 4, FAR_ROW
    rows_of_consts = [
        scale,
        shift,
        first_of(position),
        first_of(position ^ 1),
        first_of(last - position),
        first_of((last - position) ^ 1),
        jnp.where(outer, 0.0, 1.0),
        first_of(jnp.where(outer, last - position, (last - position) ^ 1)),
    ]
    index = lax.broadcasted_iota(jnp.int32, (8, 128), 0)
    consts = jnp.zeros((8, 128), jnp.float32)
    for i, value in enumerate(rows_of_consts):
        consts = jnp.where(index == i, value, consts)

    cut = 2 * rows // 5
    half = rows // 2
    across = permute(glycans, middle)
    side = permute(glycans, sides)
    coded = code_labels(labels, LABEL_ROWS, width)
    end_mine = permute(jnp.concatenate([spectra, coded]), inward)
    partner = swap_inner(spectra)
    own_labels = labels.reshape(1, rows)
    node_labels = jnp.concatenate([own_labels, swap_inner(own_labels)], axis=1)
    node_labels = node_labels.astype(jnp.float32)
    node = dict(node=(spectra, partner), labels=node_labels)
    here_g, here_c = pair_work(
        consts, [(Block(here_at, ("node",), "kept", coef="all"), Away(glycans), None)], rows, **node
    )

    side = after(side, here_g)
    far_a, far_b = [permute(x, middle) for x in split(side, (cut, rows - cut))]
    across = after(across, here_g)
    next_out = permute(across, outward)
    side_g, across_g, side_c, across_c = pair_work(
        consts,
        [
            (Block(side_at, ("node",), "kept", coef="all"), Away(side), None),
            (Block(across_at, ("node",), "kept", coef="masked"), Away(across), None),
        ],
        rows,
        **node,
    )
    far_a = after(far_a, across_g)
    last_a = permute(far_a, sides)
    (far_g,) = pair_work(
        consts, [(Block(far_at, ("node",), "total"), far_a, None)], rows, wanted=~outer, **node
    )
    end_mine = after(end_mine, far_g)
    piece = -(-rows // 48) * 16
    two = (half + LABEL_ROWS, half)
    ends = (end_mine,) + tuple(swap_inner(x) for x in split(end_mine, two))

    far_a, far_b, next_out = lax.optimization_barrier((far_a, far_b, next_out, far_g))[:3]
    (far_a_out,) = pair_work(
        consts,
        [(Block(far_at, ("ends",), "rounded", prior="near"), far_a, far_g)],
        rows,
        wanted=~outer,
        ends=ends,
    )
    back_a = permute(far_a_out, middle)
    far_b = after(far_b, far_a_out)
    last_b = permute(far_b, sides)
    (far_b_out,) = pair_work(
        consts,
        [(Block(far_at, ("node", "ends"), "rounded", cut), far_b, None)],
        rows,
        wanted=~outer,
        ends=ends,
        **node,
    )
    back_b = permute(far_b_out, middle)
    (across_out,) = pair_work(
        consts,
        [
            (
                Block(across_at, ("ends",), "rounded", prior="kept"),
                Away(after(across, far_b_out)),
                across_g,
            )
        ],
        rows,
        wanted=~outer,
        ends=ends,
    )
    late_side, last_a = lax.optimization_barrier((side, last_a, across_out))[:2]
    late_side = Away(late_side)
    side_total_a, side_total_b = pair_work(
        consts,
        [(Block(side_at, ("ends",), "split", cut=cut, prior="kept"), late_side, side_g)],
        rows,
        wanted=~outer,
        ends=ends,
    )
    total_a = add_rounded(side_total_a, back_a)
    inside_a = permute(total_a, sides)
    across_back = permute(after(across_out, total_a), middle)
    back_b, last_b = lax.optimization_barrier((back_b, last_b, total_a))[:2]
    total_b = add_rounded(Away(side_total_b), back_b)
    inside_b = permute(total_b, sides)

    mine_s, other_s = spectra_work(
        outer,
        consts,
        node_labels,
        (spectra, partner),
        (here_c, side_c, across_c),
        after(glycans, total_b),
        side,
        across,
        (next_out,),
        (far_a, far_b),
        (last_a, last_b),
    )
    others = [swap_inner(x) for x in split(other_s, (piece, piece, rows - 2 * piece))]
    late, inside_a = lax.optimization_barrier((glycans, inside_a, mine_s))[:2]
    (here_total,) = pair_work(
        consts,
        [(Block(here_at, ("ends",), "scaled", prior="kept"), Away(late), here_g)],
        rows,
        wanted=~outer,
        ends=ends,
    )
    others[0] = after(others[0], here_total)
    grad_spectra = finish_spectra(mine_s, others)
    across_back = after(across_back, grad_spectra)
    return grad_spectra, finish_structures(outer, here_total, across_back, inside_a, inside_b)


def local(
    mass_profile_vectors,
    sugar_tree_vectors,
    matching_glycan_rows,
    sharpness_factor,
    offset_shift_term,
):
    work = along_line if lax.axis_size("blk") == STEPS == LINE else around_ring
    return work(
        mass_profile_vectors,
        sugar_tree_vectors,
        matching_glycan_rows,
        sharpness_factor[0],
        offset_shift_term[0],
    )


def solution(mesh):
    placed = (
        P(("groups", "blk", "sub", "inner"), None),
        P(("groups", "blk", "sub", "inner"), None),
        P(("groups", "blk", "sub", "inner")),
        P(),
        P(),
    )
    return jax.shard_map(
        local,
        mesh=mesh,
        in_specs=placed,
        out_specs=(
            P(("groups", "blk", "sub", "inner"), None),
            P(("groups", "blk", "sub", "inner"), None),
        ),
        check_vma=False,
    )
```

```python
import dataclasses
import functools

import jax
import jax.numpy as jnp
from jax import lax
from jax.experimental import pallas as pl
from jax.experimental.pallas import tpu as pltpu
from jax.sharding import PartitionSpec as P

STEPS = 4
LINE = 4
LABEL_ROWS = 16
FAR_ROW, KEEP_ROW, LAST_ROW = 5, 6, 7
VMEM_BYTES = 10 * 1024 * 1024


def from_behind(block, axis, distance):
    devices = range(lax.axis_size(axis))
    route = [((i - distance) % len(devices), i) for i in devices]
    return lax.ppermute(block, axis, route)


def swap_inner(block):
    return from_behind(block, "inner", 1)


def after(value, *earlier):
    return lax.optimization_barrier((value,) + earlier)[0]


def coefficients(spectra, glycans, labels, first_target, scale, shift):
    logits = (
        scale
        * lax.dot_general(
            spectra, glycans, (((1,), (1,)), ((), ())), preferred_element_type=jnp.float32
        )
        + shift
    )
    targets = first_target + jnp.arange(glycans.shape[0], dtype=jnp.int32)
    positive = (labels[:, None] == targets[None, :]).astype(jnp.float32)
    return (jax.nn.sigmoid(logits) - positive).astype(jnp.bfloat16)


def around_ring(spectra, glycans, labels, scale, shift):
    rows_here = spectra.shape[0]
    node_rows = rows_here * lax.axis_size("inner")
    loop_count = lax.axis_size("blk")
    position = lax.axis_index("blk")
    core_first = lax.axis_index("sub") * node_rows + lax.axis_index("inner") * rows_here
    lane_rows = lax.axis_size("sub") * node_rows
    node_spectra = jnp.concatenate([spectra, swap_inner(spectra)])
    node_labels = jnp.concatenate([labels, swap_inner(labels)])
    spectrum_total = 0.0
    glycan_total = 0.0
    held = glycans
    for step in range(STEPS):
        if step > 0:
            held = from_behind(held, "blk", 1)
        first_target = (position - step) % loop_count * lane_rows + core_first
        coef = coefficients(node_spectra, held, node_labels, first_target, scale, shift)
        spectrum_total += jnp.dot(coef, held, preferred_element_type=jnp.float32)
        partial_value = scale * lax.dot_general(
            coef, node_spectra, (((0,), (0,)), ((), ())), preferred_element_type=jnp.float32
        )
        if step > 0:
            back = from_behind(partial_value.astype(jnp.bfloat16), "blk", -step)
            partial_value = back.astype(jnp.float32)
        glycan_total += partial_value
    other = swap_inner((scale * spectrum_total[rows_here:]).astype(jnp.bfloat16))
    spectrum_total = scale * spectrum_total[:rows_here] + other.astype(jnp.float32)
    return spectrum_total.astype(jnp.bfloat16), glycan_total.astype(jnp.bfloat16)


@dataclasses.dataclass(frozen=True)
class Away:
    array: jax.Array


@dataclasses.dataclass(frozen=True)
class Block:
    target: int
    uses: tuple
    out: str
    offset: int = 0
    cut: int = 0
    prior: str = ""
    coef: str = ""


@dataclasses.dataclass(frozen=True)
class Plan:
    blocks: tuple
    pieces: tuple
    node: bool
    ends: tuple
    skips: bool
    rows: int


def pair_body(plan, *refs):
    if plan.skips:
        pl.when(refs[0][0] != 0)(functools.partial(pair_steps, plan, *refs[1:]))
    else:
        pair_steps(plan, *refs)


def pair_steps(plan, *refs):
    refs = list(refs)
    blocks, rows = plan.blocks, plan.rows

    def take(count):
        taken = refs[:count]
        del refs[:count]
        return taken

    def take_if(condition):
        return take(1)[0] if condition else None

    (consts,) = take(1)
    labels = take_if(plan.node)
    node_in = take(2) if plan.node else []
    ends_in = take(len(plan.ends))
    held_in = [take(len(p)) for p in plan.pieces]
    priors = [take_if(b.prior) for b in blocks]
    outs = [take((b.out != "") + (b.out == "split")) for b in blocks]
    coef_outs = [take_if(b.coef) for b in blocks]
    spectra = take_if(plan.node)
    ends = take_if(plan.ends)
    held = take(len(blocks))
    prior_held = [take_if(b.prior == "kept") for b in blocks]
    out_held = [take_if(b.out in ("kept", "split")) for b in blocks]
    coef_held = [take_if(b.coef) for b in blocks]
    (sems,) = take(1)
    used = 0

    def move(source, target):
        nonlocal used
        copy = pltpu.make_async_copy(source, target, sems.at[used])
        copy.start()
        used += 1
        return copy

    moving_node = [move(ref, spectra.at[pl.ds(i * rows, rows)]) for i, ref in enumerate(node_in)]
    moving = []
    for i, block in enumerate(blocks):
        moves = []
        at = 0
        for ref, (count, away) in zip(held_in[i], plan.pieces[i]):
            if away:
                moves.append(move(ref, held[i].at[pl.ds(at, count)]))
            at += count
        moving.append(moves)
    moving_prior = [
        move(priors[i], prior_held[i]) if b.prior == "kept" else None for i, b in enumerate(blocks)
    ]
    leaving = []

    def const(row):
        return consts[pl.ds(row, 1), pl.ds(0, 1)]

    scale, shift = const(0), const(1)
    if plan.ends:
        width = 2 * rows
        at = 0
        coded = []
        for ref, count in zip(ends_in, plan.ends):
            ending = at % rows + count > rows
            keep = count - LABEL_ROWS if ending else count
            ends[pl.ds(at, keep)] = ref[pl.ds(0, keep)]
            at += keep
            if ending:
                digits = ref[pl.ds(keep, LABEL_ROWS), pl.ds(0, width)].astype(jnp.float32)
                coded.append(digits[0:1] * 16384.0 + digits[1:2] * 128.0 + digits[2:3])
        lane = lax.broadcasted_iota(jnp.int32, (1, width), 1)
        end_labels = jnp.where(lane >= rows, coded[1], coded[0])

    def source(use):
        if use == "node":
            while moving_node:
                moving_node.pop(0).wait()
            return spectra[...], labels[...]
        return ends[...], end_labels

    for i, block in enumerate(blocks):

        def work(i=i, block=block):
            at = 0
            for ref, (count, away) in zip(held_in[i], plan.pieces[i]):
                if not away:
                    held[i][pl.ds(at, count)] = ref[...]
                at += count
            for copy in moving[i]:
                copy.wait()
            glycans = held[i][...]
            targets = lax.broadcasted_iota(jnp.int32, (glycans.shape[0], 1), 0)
            targets = targets.astype(jnp.float32) + (const(block.target) + float(block.offset))
            total = None
            for use in block.uses:
                here, row_labels = source(use)
                logits = lax.dot_general(
                    glycans, here, (((1,), (1,)), ((), ())), preferred_element_type=jnp.float32
                )
                logits = scale * logits + shift
                positive = jnp.where(targets == row_labels, 1.0, 0.0)
                coef = jax.nn.sigmoid(logits) - positive
                coef = coef.astype(jnp.bfloat16)
                if block.out:
                    part = jnp.dot(coef, here, preferred_element_type=jnp.float32)
                    total = part if total is None else total + part
                if block.coef and use == "node":
                    kept = coef * const(KEEP_ROW).astype(jnp.bfloat16) if block.coef == "masked" else coef
                    coef_held[i][...] = kept
                    leaving.append(move(coef_held[i], coef_outs[i]))
            if block.prior == "kept":
                moving_prior[i].wait()
                total = total + prior_held[i][...]
            elif block.prior:
                total = total + priors[i][...]
            if block.out == "kept":
                out_held[i][...] = total
                leaving.append(move(out_held[i], outs[i][0]))
            elif block.out == "split":
                cut = outs[i][0].shape[0]
                outs[i][0][...] = scale * total[:cut]
                out_held[i][...] = scale * total[cut:]
                leaving.append(move(out_held[i], outs[i][1]))
            elif block.out == "total":
                outs[i][0][...] = total
            elif block.out == "scaled":
                outs[i][0][...] = scale * total
            elif block.out:
                outs[i][0][...] = (scale * total).astype(jnp.bfloat16)

        work()
    for copy in leaving:
        copy.wait()


def in_vmem(array):
    return pltpu.with_memory_space_constraint(array, pltpu.VMEM)


def in_hbm(array):
    return pltpu.with_memory_space_constraint(array, pltpu.HBM)


def vmem_out(shape, kind):
    return pltpu.VMEM(shape, kind)


def hbm_out(shape, kind):
    return pltpu.HBM(shape, kind)


VMEM_SPEC = pl.BlockSpec(memory_space=pltpu.VMEM)
SMEM_SPEC = pl.BlockSpec(memory_space=pltpu.SMEM)
HBM_SPEC = pl.BlockSpec(memory_space=pltpu.HBM)
SMALL_COST = pl.CostEstimate(flops=1024, bytes_accessed=1024, transcendentals=0)


def params():
    return pltpu.CompilerParams(vmem_limit_bytes=VMEM_BYTES)


def pair_work(consts, blocks, rows, labels=None, node=None, ends=None, wanted=None):
    shapes = tuple(b[0] for b in blocks)
    pieces = []
    arrays = []
    for shape, array, _ in blocks:
        parts = array if isinstance(array, tuple) else (array,)
        away = [isinstance(x, Away) for x in parts]
        parts = [x.array if flag else x for x, flag in zip(parts, away)]
        pieces.append(tuple((x.shape[0], flag) for x, flag in zip(parts, away)))
        arrays += list(zip(parts, away))
    width = arrays[0][0].shape[1]
    ends = ends or ()
    end_rows = tuple(x.shape[0] for x in ends)
    plan = Plan(
        shapes,
        tuple(pieces),
        node is not None,
        end_rows,
        wanted is not None,
        rows,
    )

    operands = []
    in_specs = []
    if wanted is not None:
        operands.append(jnp.int32(wanted).reshape(1))
        in_specs.append(SMEM_SPEC)

    def give(array, away):
        operands.append(in_hbm(array) if away else in_vmem(array))
        in_specs.append(HBM_SPEC if away else VMEM_SPEC)

    give(consts, False)
    if node is not None:
        give(labels, False)
    for array in node or ():
        give(array, True)
    for array in ends:
        give(array, False)
    for array, away in arrays:
        give(array, away)
    for shape, _, prior in blocks:
        if shape.prior:
            give(prior, shape.prior == "kept")

    counts = [sum(count for count, _ in p) for p in pieces]
    outs = []
    out_specs = []

    def get(shape, kind, away):
        outs.append((hbm_out if away else vmem_out)(shape, kind))
        out_specs.append(HBM_SPEC if away else VMEM_SPEC)

    for shape, count in zip(shapes, counts):
        if shape.out == "split":
            get((shape.cut, width), jnp.float32, False)
            get((count - shape.cut, width), jnp.float32, True)
        elif shape.out:
            kind = jnp.bfloat16 if shape.out == "rounded" else jnp.float32
            get((count, width), kind, shape.out == "kept")
    for shape, count in zip(shapes, counts):
        if shape.coef:
            get((count, 2 * rows), jnp.bfloat16, True)

    scratch = []
    if node is not None:
        scratch.append(pltpu.VMEM((2 * rows, width), jnp.bfloat16))
    if ends:
        scratch.append(pltpu.VMEM((2 * rows, width), jnp.bfloat16))
    scratch += [pltpu.VMEM((n, width), jnp.bfloat16) for n in counts]
    scratch += [pltpu.VMEM((n, width), jnp.float32) for n, b in zip(counts, shapes) if b.prior == "kept"]
    for n, b in zip(counts, shapes):
        if b.out in ("kept", "split"):
            scratch.append(pltpu.VMEM((n - b.cut, width), jnp.float32))
    scratch += [pltpu.VMEM((n, 2 * rows), jnp.bfloat16) for n, b in zip(counts, shapes) if b.coef]
    scratch.append(pltpu.SemaphoreType.DMA((len(operands) + len(outs),)))
    return pl.pallas_call(
        functools.partial(pair_body, plan),
        out_shape=outs,
        in_specs=in_specs,
        out_specs=out_specs,
        scratch_shapes=scratch,
        cost_estimate=SMALL_COST,
        compiler_params=params(),
    )(*operands)


def code_labels(labels, row_count, width):
    digits = jnp.stack([labels // 16384, labels // 128 % 128, labels % 128]).astype(jnp.bfloat16)
    digits = jnp.concatenate([digits, digits, digits], axis=1)
    return jnp.pad(digits, ((0, row_count - 3), (0, width - digits.shape[1])))


def spectra_body(plan, outer, consts, labels, s_mine, s_other, coef_here, coef_side, coef_across, here, side, across, *rest):
    rows, n_next, n_far, n_last = plan
    nexts, rest = rest[:n_next], rest[n_next:]
    fars, rest = rest[:n_far], rest[n_far:]
    lasts, rest = rest[:n_last], rest[n_last:]
    mine_out, other_out, spectra, coefs, held, sems = rest
    used = 0

    def move(source, target):
        nonlocal used
        copy = pltpu.make_async_copy(source, target, sems.at[used])
        copy.start()
        used += 1
        return copy

    def fill(parts, target, at):
        moves = []
        for part in parts:
            moves.append(move(part, target.at[pl.ds(at, part.shape[0])]))
            at += part.shape[0]
        return moves

    moves = fill([s_mine, s_other], spectra, 0) + fill([coef_here, coef_side], coefs, 0)
    moves += fill([here, side], held, 0)

    @pl.when(outer[0] == 0)
    def _():
        for copy in fill([across] + list(fars), held, 2 * rows) + fill([coef_across], coefs, 2 * rows):
            copy.wait()

    @pl.when(outer[0] != 0)
    def _():
        for copy in fill(list(nexts) + list(lasts), held, 2 * rows):
            copy.wait()

    for copy in moves:
        copy.wait()
    scale, shift = consts[0:1, 0:1], consts[1:2, 0:1]

    def work_out(first, target_row):
        logits = lax.dot_general(
            held[pl.ds(first, rows)],
            spectra[...],
            (((1,), (1,)), ((), ())),
            preferred_element_type=jnp.float32,
        )
        logits = scale * logits + shift
        targets = lax.broadcasted_iota(jnp.int32, (rows, 1), 0).astype(jnp.float32)
        targets = targets + consts[target_row : target_row + 1, 0:1]
        positive = jnp.where(targets == labels[...], 1.0, 0.0)
        coefs[pl.ds(first, rows)] = (jax.nn.sigmoid(logits) - positive).astype(jnp.bfloat16)

    @pl.when(outer[0] != 0)
    def _():
        work_out(2 * rows, FAR_ROW)

    work_out(3 * rows, LAST_ROW)
    for i, out in enumerate((mine_out, other_out)):
        total = lax.dot_general(
            coefs[:, i * rows : (i + 1) * rows],
            held[...],
            (((0,), (0,)), ((), ())),
            preferred_element_type=jnp.float32,
        )
        out[...] = (scale * total).astype(out.dtype)


def spectra_work(outer, consts, labels, node, coefs, here, side, across, nexts, fars, lasts):
    rows, width = here.shape
    arrays = list(node) + list(coefs) + [here, side, across] + list(nexts) + list(fars) + list(lasts)
    plan = (rows, len(nexts), len(fars), len(lasts))
    return pl.pallas_call(
        functools.partial(spectra_body, plan),
        out_shape=[vmem_out((rows, width), jnp.float32), vmem_out((rows, width), jnp.bfloat16)],
        in_specs=[SMEM_SPEC, VMEM_SPEC, VMEM_SPEC] + [HBM_SPEC] * len(arrays),
        out_specs=[VMEM_SPEC] * 2,
        scratch_shapes=[
            pltpu.VMEM((2 * rows, width), jnp.bfloat16),
            pltpu.VMEM((4 * rows, 2 * rows), jnp.bfloat16),
            pltpu.VMEM((4 * rows, width), jnp.bfloat16),
            pltpu.SemaphoreType.DMA((len(arrays),)),
        ],
        cost_estimate=SMALL_COST,
        compiler_params=params(),
    )(
        jnp.int32(outer).reshape(1),
        in_vmem(consts),
        in_vmem(labels),
        *[in_hbm(a) for a in arrays],
    )


def split_body(whole, *parts):
    at = 0
    for part in parts:
        part[...] = whole[pl.ds(at, part.shape[0])]
        at += part.shape[0]


def split(whole, counts):
    return pl.pallas_call(
        split_body,
        out_shape=[vmem_out((n, whole.shape[1]), whole.dtype) for n in counts],
        in_specs=[VMEM_SPEC],
        out_specs=[VMEM_SPEC] * len(counts),
        cost_estimate=SMALL_COST,
        compiler_params=params(),
    )(in_vmem(whole))


def add_body(total, arrived, out, *scratch):
    if scratch:
        near, sem = scratch
        copy = pltpu.make_async_copy(total, near, sem)
        copy.start()
        copy.wait()
        total = near
    out[...] = (total[...] + arrived[...].astype(jnp.float32)).astype(jnp.bfloat16)


def add_rounded(total, arrived):
    away = isinstance(total, Away)
    scratch = [pltpu.VMEM(arrived.shape, jnp.float32), pltpu.SemaphoreType.DMA] if away else []
    return pl.pallas_call(
        add_body,
        out_shape=vmem_out(arrived.shape, jnp.bfloat16),
        in_specs=[HBM_SPEC if away else VMEM_SPEC, VMEM_SPEC],
        out_specs=VMEM_SPEC,
        scratch_shapes=scratch,
        cost_estimate=SMALL_COST,
        compiler_params=params(),
    )(in_hbm(total.array) if away else in_vmem(total), in_vmem(arrived))


def finish_spectra_body(mine_s, *rest):
    others, out = rest[:-1], rest[-1]
    at = 0
    for other in others:
        where = pl.ds(at, other.shape[0])
        out[where] = (mine_s[where] + other[...].astype(jnp.float32)).astype(jnp.bfloat16)
        at += other.shape[0]


def finish_spectra(mine_s, others):
    return pl.pallas_call(
        finish_spectra_body,
        out_shape=jax.ShapeDtypeStruct(mine_s.shape, jnp.bfloat16),
        in_specs=[VMEM_SPEC] * (1 + len(others)),
        out_specs=VMEM_SPEC,
        cost_estimate=SMALL_COST,
        compiler_params=params(),
    )(*[in_vmem(a) for a in [mine_s] + others])


def finish_structures_body(flag, here_total, across_back, inside_a, inside_b, out, held, sems):
    cut = inside_a.shape[0]

    @pl.when(flag[0] != 0)
    def _():
        first = pltpu.make_async_copy(inside_a, held.at[pl.ds(0, cut)], sems.at[0])
        rest = pl.ds(cut, inside_b.shape[0])
        second = pltpu.make_async_copy(inside_b, held.at[rest], sems.at[1])
        first.start()
        second.start()
        first.wait()
        second.wait()

    @pl.when(flag[0] == 0)
    def _():
        total = here_total[...] + across_back[...].astype(jnp.float32)
        held[...] = total.astype(jnp.bfloat16)

    copy = pltpu.make_async_copy(held, out, sems.at[0])
    copy.start()
    copy.wait()


def finish_structures(flag, here_total, across_back, inside_a, inside_b):
    shape = here_total.shape
    return pl.pallas_call(
        finish_structures_body,
        out_shape=jax.ShapeDtypeStruct(shape, jnp.bfloat16),
        in_specs=[SMEM_SPEC, VMEM_SPEC, VMEM_SPEC, HBM_SPEC, HBM_SPEC],
        out_specs=HBM_SPEC,
        scratch_shapes=[pltpu.VMEM(shape, jnp.bfloat16), pltpu.SemaphoreType.DMA((2,))],
        cost_estimate=SMALL_COST,
        compiler_params=params(),
    )(
        jnp.int32(flag).reshape(1),
        in_vmem(here_total),
        in_vmem(across_back),
        in_hbm(inside_a),
        in_hbm(inside_b),
    )


def along_line(spectra, glycans, labels, scale, shift):
    rows, width = spectra.shape
    node_rows = rows * lax.axis_size("inner")
    position = lax.axis_index("blk")
    outer = (position == 0) | (position == LINE - 1)
    core_first = lax.axis_index("sub") * node_rows + lax.axis_index("inner") * rows
    lane_rows = lax.axis_size("sub") * node_rows

    def permute(block, pairs):
        return lax.ppermute(block, ("blk", "inner"), pairs)

    def first_of(block_position):
        return (block_position * lane_rows + core_first).astype(jnp.float32)

    n_inner = lax.axis_size("inner")
    last = LINE - 1
    sides = []
    middle = []
    inward = []
    outward = []
    for core in range(n_inner):
        inward += [(core, n_inner + core), (last * n_inner + core, (last - 1) * n_inner + core)]
        outward += [(n_inner + core, core), ((last - 1) * n_inner + core, last * n_inner + core)]
        for at in range(LINE):
            sides.append((at * n_inner + core, (at ^ 1) * n_inner + core))
        for at in range(1, last):
            middle.append((at * n_inner + core, (last - at) * n_inner + core))
        for at in (0, last):
            middle.append((at * n_inner + core, at * n_inner + (core + 1) % n_inner))
    here_at, side_at, across_at, far_at = 2, 3, 4, FAR_ROW
    rows_of_consts = [
        scale,
        shift,
        first_of(position),
        first_of(position ^ 1),
        first_of(last - position),
        first_of((last - position) ^ 1),
        jnp.where(outer, 0.0, 1.0),
        first_of(jnp.where(outer, last - position, (last - position) ^ 1)),
    ]
    index = lax.broadcasted_iota(jnp.int32, (8, 128), 0)
    consts = jnp.zeros((8, 128), jnp.float32)
    for i, value in enumerate(rows_of_consts):
        consts = jnp.where(index == i, value, consts)

    cut = 2 * rows // 5
    half = rows // 2
    across = permute(glycans, middle)
    side = permute(glycans, sides)
    coded = code_labels(labels, LABEL_ROWS, width)
    end_mine = permute(jnp.concatenate([spectra, coded]), inward)
    partner = swap_inner(spectra)
    own_labels = labels.reshape(1, rows)
    node_labels = jnp.concatenate([own_labels, swap_inner(own_labels)], axis=1)
    node_labels = node_labels.astype(jnp.float32)
    node = dict(node=(spectra, partner), labels=node_labels)
    here_g, here_c = pair_work(
        consts, [(Block(here_at, ("node",), "kept", coef="all"), Away(glycans), None)], rows, **node
    )

    side = after(side, here_g)
    far_a, far_b = [permute(x, middle) for x in split(side, (cut, rows - cut))]
    across = after(across, here_g)
    next_out = permute(across, outward)
    side_g, across_g, side_c, across_c = pair_work(
        consts,
        [
            (Block(side_at, ("node",), "kept", coef="all"), Away(side), None),
            (Block(across_at, ("node",), "kept", coef="masked"), Away(across), None),
        ],
        rows,
        **node,
    )
    far_a = after(far_a, across_g)
    last_a = permute(far_a, sides)
    (far_g,) = pair_work(
        consts, [(Block(far_at, ("node",), "total"), far_a, None)], rows, wanted=~outer, **node
    )
    end_mine = after(end_mine, far_g)
    piece = -(-rows // 48) * 16
    two = (half + LABEL_ROWS, half)
    ends = (end_mine,) + tuple(swap_inner(x) for x in split(end_mine, two))

    far_a, far_b, next_out = lax.optimization_barrier((far_a, far_b, next_out, far_g))[:3]
    (far_a_out,) = pair_work(
        consts,
        [(Block(far_at, ("ends",), "rounded", prior="near"), far_a, far_g)],
        rows,
        wanted=~outer,
        ends=ends,
    )
    back_a = permute(far_a_out, middle)
    far_b = after(far_b, far_a_out)
    last_b = permute(far_b, sides)
    (far_b_out,) = pair_work(
        consts,
        [(Block(far_at, ("node", "ends"), "rounded", cut), far_b, None)],
        rows,
        wanted=~outer,
        ends=ends,
        **node,
    )
    back_b = permute(far_b_out, middle)
    (across_out,) = pair_work(
        consts,
        [
            (
                Block(across_at, ("ends",), "rounded", prior="kept"),
                Away(after(across, far_b_out)),
                across_g,
            )
        ],
        rows,
        wanted=~outer,
        ends=ends,
    )
    late_side, last_a = lax.optimization_barrier((side, last_a, across_out))[:2]
    late_side = Away(late_side)
    side_total_a, side_total_b = pair_work(
        consts,
        [(Block(side_at, ("ends",), "split", cut=cut, prior="kept"), late_side, side_g)],
        rows,
        wanted=~outer,
        ends=ends,
    )
    total_a = add_rounded(side_total_a, back_a)
    inside_a = permute(total_a, sides)
    across_back = permute(after(across_out, total_a), middle)
    back_b, last_b = lax.optimization_barrier((back_b, last_b, total_a))[:2]
    total_b = add_rounded(Away(side_total_b), back_b)
    inside_b = permute(total_b, sides)

    mine_s, other_s = spectra_work(
        outer,
        consts,
        node_labels,
        (spectra, partner),
        (here_c, side_c, across_c),
        after(glycans, total_b),
        side,
        across,
        (next_out,),
        (far_a, far_b),
        (last_a, last_b),
    )
    others = [swap_inner(x) for x in split(other_s, (piece, piece, rows - 2 * piece))]
    late, inside_a = lax.optimization_barrier((glycans, inside_a, mine_s))[:2]
    (here_total,) = pair_work(
        consts,
        [(Block(here_at, ("ends",), "scaled", prior="kept"), Away(late), here_g)],
        rows,
        wanted=~outer,
        ends=ends,
    )
    others[0] = after(others[0], here_total)
    grad_spectra = finish_spectra(mine_s, others)
    across_back = after(across_back, grad_spectra)
    return grad_spectra, finish_structures(outer, here_total, across_back, inside_a, inside_b)


def local(
    mass_profile_vectors,
    sugar_tree_vectors,
    matching_glycan_rows,
    sharpness_factor,
    offset_shift_term,
):
    work = along_line if lax.axis_size("blk") == STEPS == LINE else around_ring
    return work(
        mass_profile_vectors,
        sugar_tree_vectors,
        matching_glycan_rows,
        sharpness_factor[0],
        offset_shift_term[0],
    )


def solution(mesh):
    placed = (
        P(("groups", "blk", "sub", "inner"), None),
        P(("groups", "blk", "sub", "inner"), None),
        P(("groups", "blk", "sub", "inner")),
        P(),
        P(),
    )
    return jax.shard_map(
        local,
        mesh=mesh,
        in_specs=placed,
        out_specs=(
            P(("groups", "blk", "sub", "inner"), None),
            P(("groups", "blk", "sub", "inner"), None),
        ),
        check_vma=False,
    )
```

```python
import dataclasses
import functools

import jax
import jax.numpy as jnp
from jax import lax
from jax.experimental import pallas as pl
from jax.experimental.pallas import tpu as pltpu
from jax.sharding import PartitionSpec as P

STEPS = 4
LINE = 4
LABEL_ROWS = 16
FAR_ROW, KEEP_ROW, LAST_ROW = 5, 6, 7
VMEM_BYTES = 20 * 1024 * 1024


def from_behind(block, axis, distance):
    devices = range(lax.axis_size(axis))
    route = [((i - distance) % len(devices), i) for i in devices]
    return lax.ppermute(block, axis, route)


def swap_inner(block):
    return from_behind(block, "inner", 1)


def after(value, *earlier):
    return lax.optimization_barrier((value,) + earlier)[0]


def coefficients(spectra, glycans, labels, first_target, scale, shift):
    logits = (
        scale
        * lax.dot_general(
            spectra, glycans, (((1,), (1,)), ((), ())), preferred_element_type=jnp.float32
        )
        + shift
    )
    targets = first_target + jnp.arange(glycans.shape[0], dtype=jnp.int32)
    positive = (labels[:, None] == targets[None, :]).astype(jnp.float32)
    return (jax.nn.sigmoid(logits) - positive).astype(jnp.bfloat16)


def around_ring(spectra, glycans, labels, scale, shift):
    rows_here = spectra.shape[0]
    node_rows = rows_here * lax.axis_size("inner")
    loop_count = lax.axis_size("blk")
    position = lax.axis_index("blk")
    core_first = lax.axis_index("sub") * node_rows + lax.axis_index("inner") * rows_here
    lane_rows = lax.axis_size("sub") * node_rows
    node_spectra = jnp.concatenate([spectra, swap_inner(spectra)])
    node_labels = jnp.concatenate([labels, swap_inner(labels)])
    spectrum_total = 0.0
    glycan_total = 0.0
    held = glycans
    for step in range(STEPS):
        if step > 0:
            held = from_behind(held, "blk", 1)
        first_target = (position - step) % loop_count * lane_rows + core_first
        coef = coefficients(node_spectra, held, node_labels, first_target, scale, shift)
        spectrum_total += jnp.dot(coef, held, preferred_element_type=jnp.float32)
        partial_value = scale * lax.dot_general(
            coef, node_spectra, (((0,), (0,)), ((), ())), preferred_element_type=jnp.float32
        )
        if step > 0:
            back = from_behind(partial_value.astype(jnp.bfloat16), "blk", -step)
            partial_value = back.astype(jnp.float32)
        glycan_total += partial_value
    other = swap_inner((scale * spectrum_total[rows_here:]).astype(jnp.bfloat16))
    spectrum_total = scale * spectrum_total[:rows_here] + other.astype(jnp.float32)
    return spectrum_total.astype(jnp.bfloat16), glycan_total.astype(jnp.bfloat16)


@dataclasses.dataclass(frozen=True)
class Away:
    array: jax.Array


@dataclasses.dataclass(frozen=True)
class Block:
    target: int
    uses: tuple
    out: str
    offset: int = 0
    cut: int = 0
    prior: str = ""
    coef: str = ""


@dataclasses.dataclass(frozen=True)
class Plan:
    blocks: tuple
    pieces: tuple
    node: bool
    ends: tuple
    skips: bool
    rows: int


def pair_body(plan, *refs):
    if plan.skips:
        pl.when(refs[0][0] != 0)(functools.partial(pair_steps, plan, *refs[1:]))
    else:
        pair_steps(plan, *refs)


def pair_steps(plan, *refs):
    refs = list(refs)
    blocks, rows = plan.blocks, plan.rows

    def take(count):
        taken = refs[:count]
        del refs[:count]
        return taken

    def take_if(condition):
        return take(1)[0] if condition else None

    (consts,) = take(1)
    labels = take_if(plan.node)
    node_in = take(2) if plan.node else []
    ends_in = take(len(plan.ends))
    held_in = [take(len(p)) for p in plan.pieces]
    priors = [take_if(b.prior) for b in blocks]
    outs = [take((b.out != "") + (b.out == "split")) for b in blocks]
    coef_outs = [take_if(b.coef) for b in blocks]
    spectra = take_if(plan.node)
    ends = take_if(plan.ends)
    held = take(len(blocks))
    prior_held = [take_if(b.prior == "kept") for b in blocks]
    out_held = [take_if(b.out in ("kept", "kept scaled", "split")) for b in blocks]
    coef_held = [take_if(b.coef) for b in blocks]
    (sems,) = take(1)
    used = 0

    def move(source, target):
        nonlocal used
        copy = pltpu.make_async_copy(source, target, sems.at[used])
        copy.start()
        used += 1
        return copy

    moving_node = [move(ref, spectra.at[pl.ds(i * rows, rows)]) for i, ref in enumerate(node_in)]
    moving = []
    for i, block in enumerate(blocks):
        moves = []
        at = 0
        for ref, (count, away) in zip(held_in[i], plan.pieces[i]):
            if away:
                moves.append(move(ref, held[i].at[pl.ds(at, count)]))
            at += count
        moving.append(moves)
    moving_prior = [
        move(priors[i], prior_held[i]) if b.prior == "kept" else None for i, b in enumerate(blocks)
    ]
    leaving = []

    def const(row):
        return consts[pl.ds(row, 1), pl.ds(0, 1)]

    scale, shift = const(0), const(1)
    if plan.ends:
        width = 2 * rows
        at = 0
        coded = []
        for ref, count in zip(ends_in, plan.ends):
            ending = at % rows + count > rows
            keep = count - LABEL_ROWS if ending else count
            ends[pl.ds(at, keep)] = ref[pl.ds(0, keep)]
            at += keep
            if ending:
                digits = ref[pl.ds(keep, LABEL_ROWS), pl.ds(0, width)].astype(jnp.float32)
                coded.append(digits[0:1] * 16384.0 + digits[1:2] * 128.0 + digits[2:3])
        lane = lax.broadcasted_iota(jnp.int32, (1, width), 1)
        end_labels = jnp.where(lane >= rows, coded[1], coded[0])

    def source(use):
        if use == "node":
            while moving_node:
                moving_node.pop(0).wait()
            return spectra[...], labels[...]
        return ends[...], end_labels

    for i, block in enumerate(blocks):

        def work(i=i, block=block):
            at = 0
            for ref, (count, away) in zip(held_in[i], plan.pieces[i]):
                if not away:
                    held[i][pl.ds(at, count)] = ref[...]
                at += count
            for copy in moving[i]:
                copy.wait()
            glycans = held[i][...]
            targets = lax.broadcasted_iota(jnp.int32, (glycans.shape[0], 1), 0)
            targets = targets.astype(jnp.float32) + (const(block.target) + float(block.offset))
            total = None
            for use in block.uses:
                here, row_labels = source(use)
                logits = lax.dot_general(
                    glycans, here, (((1,), (1,)), ((), ())), preferred_element_type=jnp.float32
                )
                logits = scale * logits + shift
                positive = jnp.where(targets == row_labels, 1.0, 0.0)
                coef = jax.nn.sigmoid(logits) - positive
                coef = coef.astype(jnp.bfloat16)
                if block.out:
                    part = jnp.dot(coef, here, preferred_element_type=jnp.float32)
                    total = part if total is None else total + part
                if block.coef and use == "node":
                    kept = coef * const(KEEP_ROW).astype(jnp.bfloat16) if block.coef == "masked" else coef
                    coef_held[i][...] = kept
                    leaving.append(move(coef_held[i], coef_outs[i]))
            if block.prior == "kept":
                moving_prior[i].wait()
                total = total + prior_held[i][...]
            elif block.prior:
                total = total + priors[i][...]
            if block.out.startswith("kept"):
                out_held[i][...] = scale * total if block.out == "kept scaled" else total
                leaving.append(move(out_held[i], outs[i][0]))
            elif block.out == "split":
                cut = outs[i][0].shape[0]
                outs[i][0][...] = scale * total[:cut]
                out_held[i][...] = scale * total[cut:]
                leaving.append(move(out_held[i], outs[i][1]))
            elif block.out == "total":
                outs[i][0][...] = total
            elif block.out:
                outs[i][0][...] = (scale * total).astype(jnp.bfloat16)

        work()
    for copy in leaving:
        copy.wait()


def in_vmem(array):
    return pltpu.with_memory_space_constraint(array, pltpu.VMEM)


def in_hbm(array):
    return pltpu.with_memory_space_constraint(array, pltpu.HBM)


def vmem_out(shape, kind):
    return pltpu.VMEM(shape, kind)


def hbm_out(shape, kind):
    return pltpu.HBM(shape, kind)


VMEM_SPEC = pl.BlockSpec(memory_space=pltpu.VMEM)
SMEM_SPEC = pl.BlockSpec(memory_space=pltpu.SMEM)
HBM_SPEC = pl.BlockSpec(memory_space=pltpu.HBM)
SMALL_COST = pl.CostEstimate(flops=1024, bytes_accessed=1024, transcendentals=0)


def params():
    return pltpu.CompilerParams(vmem_limit_bytes=VMEM_BYTES)


def pair_work(consts, blocks, rows, labels=None, node=None, ends=None, wanted=None):
    shapes = tuple(b[0] for b in blocks)
    pieces = []
    arrays = []
    for shape, array, _ in blocks:
        parts = array if isinstance(array, tuple) else (array,)
        away = [isinstance(x, Away) for x in parts]
        parts = [x.array if flag else x for x, flag in zip(parts, away)]
        pieces.append(tuple((x.shape[0], flag) for x, flag in zip(parts, away)))
        arrays += list(zip(parts, away))
    width = arrays[0][0].shape[1]
    ends = ends or ()
    end_rows = tuple(x.shape[0] for x in ends)
    plan = Plan(
        shapes,
        tuple(pieces),
        node is not None,
        end_rows,
        wanted is not None,
        rows,
    )

    operands = []
    in_specs = []
    if wanted is not None:
        operands.append(jnp.int32(wanted).reshape(1))
        in_specs.append(SMEM_SPEC)

    def give(array, away):
        operands.append(in_hbm(array) if away else in_vmem(array))
        in_specs.append(HBM_SPEC if away else VMEM_SPEC)

    give(consts, False)
    if node is not None:
        give(labels, False)
    for array in node or ():
        give(array, True)
    for array in ends:
        give(array, False)
    for array, away in arrays:
        give(array, away)
    for shape, _, prior in blocks:
        if shape.prior:
            give(prior, shape.prior == "kept")

    counts = [sum(count for count, _ in p) for p in pieces]
    outs = []
    out_specs = []

    def get(shape, kind, away):
        outs.append((hbm_out if away else vmem_out)(shape, kind))
        out_specs.append(HBM_SPEC if away else VMEM_SPEC)

    for shape, count in zip(shapes, counts):
        if shape.out == "split":
            get((shape.cut, width), jnp.float32, False)
            get((count - shape.cut, width), jnp.float32, True)
        elif shape.out:
            kind = jnp.bfloat16 if shape.out == "rounded" else jnp.float32
            get((count, width), kind, shape.out.startswith("kept"))
    for shape, count in zip(shapes, counts):
        if shape.coef:
            get((count, 2 * rows), jnp.bfloat16, True)

    scratch = []
    if node is not None:
        scratch.append(pltpu.VMEM((2 * rows, width), jnp.bfloat16))
    if ends:
        scratch.append(pltpu.VMEM((2 * rows, width), jnp.bfloat16))
    scratch += [pltpu.VMEM((n, width), jnp.bfloat16) for n in counts]
    scratch += [pltpu.VMEM((n, width), jnp.float32) for n, b in zip(counts, shapes) if b.prior == "kept"]
    for n, b in zip(counts, shapes):
        if b.out in ("kept", "kept scaled", "split"):
            scratch.append(pltpu.VMEM((n - b.cut, width), jnp.float32))
    scratch += [pltpu.VMEM((n, 2 * rows), jnp.bfloat16) for n, b in zip(counts, shapes) if b.coef]
    scratch.append(pltpu.SemaphoreType.DMA((len(operands) + len(outs),)))
    return pl.pallas_call(
        functools.partial(pair_body, plan),
        out_shape=outs,
        in_specs=in_specs,
        out_specs=out_specs,
        scratch_shapes=scratch,
        cost_estimate=SMALL_COST,
        compiler_params=params(),
    )(*operands)


def code_labels(labels, row_count, width):
    digits = jnp.stack([labels // 16384, labels // 128 % 128, labels % 128]).astype(jnp.bfloat16)
    digits = jnp.concatenate([digits, digits, digits], axis=1)
    return jnp.pad(digits, ((0, row_count - 3), (0, width - digits.shape[1])))


def spectra_body(plan, outer, consts, labels, s_mine, s_other, coef_here, coef_side, coef_across, here, side, across, *rest):
    rows, n_next, n_far, n_last = plan
    nexts, rest = rest[:n_next], rest[n_next:]
    fars, rest = rest[:n_far], rest[n_far:]
    lasts, rest = rest[:n_last], rest[n_last:]
    mine_out, other_out, spectra, coefs, held, sems = rest
    used = 0

    def move(source, target):
        nonlocal used
        copy = pltpu.make_async_copy(source, target, sems.at[used])
        copy.start()
        used += 1
        return copy

    def fill(parts, target, at):
        moves = []
        for part in parts:
            moves.append(move(part, target.at[pl.ds(at, part.shape[0])]))
            at += part.shape[0]
        return moves

    moves = fill([s_mine, s_other], spectra, 0) + fill([coef_here, coef_side], coefs, 0)
    moves += fill([here, side], held, 0)

    @pl.when(outer[0] == 0)
    def _():
        for copy in fill([across] + list(fars), held, 2 * rows) + fill([coef_across], coefs, 2 * rows):
            copy.wait()

    @pl.when(outer[0] != 0)
    def _():
        for copy in fill(list(nexts) + list(lasts), held, 2 * rows):
            copy.wait()

    for copy in moves:
        copy.wait()
    scale, shift = consts[0:1, 0:1], consts[1:2, 0:1]

    def work_out(first, target_row):
        logits = lax.dot_general(
            held[pl.ds(first, rows)],
            spectra[...],
            (((1,), (1,)), ((), ())),
            preferred_element_type=jnp.float32,
        )
        logits = scale * logits + shift
        targets = lax.broadcasted_iota(jnp.int32, (rows, 1), 0).astype(jnp.float32)
        targets = targets + consts[target_row : target_row + 1, 0:1]
        positive = jnp.where(targets == labels[...], 1.0, 0.0)
        coefs[pl.ds(first, rows)] = (jax.nn.sigmoid(logits) - positive).astype(jnp.bfloat16)

    @pl.when(outer[0] != 0)
    def _():
        work_out(2 * rows, FAR_ROW)

    work_out(3 * rows, LAST_ROW)
    for i, out in enumerate((mine_out, other_out)):
        total = lax.dot_general(
            coefs[:, i * rows : (i + 1) * rows],
            held[...],
            (((0,), (0,)), ((), ())),
            preferred_element_type=jnp.float32,
        )
        out[...] = (scale * total).astype(out.dtype)


def spectra_work(outer, consts, labels, node, coefs, here, side, across, nexts, fars, lasts):
    rows, width = here.shape
    arrays = list(node) + list(coefs) + [here, side, across] + list(nexts) + list(fars) + list(lasts)
    plan = (rows, len(nexts), len(fars), len(lasts))
    return pl.pallas_call(
        functools.partial(spectra_body, plan),
        out_shape=[vmem_out((rows, width), jnp.float32), vmem_out((rows, width), jnp.bfloat16)],
        in_specs=[SMEM_SPEC, VMEM_SPEC, VMEM_SPEC] + [HBM_SPEC] * len(arrays),
        out_specs=[VMEM_SPEC] * 2,
        scratch_shapes=[
            pltpu.VMEM((2 * rows, width), jnp.bfloat16),
            pltpu.VMEM((4 * rows, 2 * rows), jnp.bfloat16),
            pltpu.VMEM((4 * rows, width), jnp.bfloat16),
            pltpu.SemaphoreType.DMA((len(arrays),)),
        ],
        cost_estimate=SMALL_COST,
        compiler_params=params(),
    )(
        jnp.int32(outer).reshape(1),
        in_vmem(consts),
        in_vmem(labels),
        *[in_hbm(a) for a in arrays],
    )


def split_body(whole, *parts):
    at = 0
    for part in parts:
        part[...] = whole[pl.ds(at, part.shape[0])]
        at += part.shape[0]


def split(whole, counts):
    return pl.pallas_call(
        split_body,
        out_shape=[vmem_out((n, whole.shape[1]), whole.dtype) for n in counts],
        in_specs=[VMEM_SPEC],
        out_specs=[VMEM_SPEC] * len(counts),
        cost_estimate=SMALL_COST,
        compiler_params=params(),
    )(in_vmem(whole))


def add_body(total, arrived, out, *scratch):
    if scratch:
        near, sem = scratch
        copy = pltpu.make_async_copy(total, near, sem)
        copy.start()
        copy.wait()
        total = near
    out[...] = (total[...] + arrived[...].astype(jnp.float32)).astype(jnp.bfloat16)


def add_rounded(total, arrived):
    away = isinstance(total, Away)
    scratch = [pltpu.VMEM(arrived.shape, jnp.float32), pltpu.SemaphoreType.DMA] if away else []
    return pl.pallas_call(
        add_body,
        out_shape=vmem_out(arrived.shape, jnp.bfloat16),
        in_specs=[HBM_SPEC if away else VMEM_SPEC, VMEM_SPEC],
        out_specs=VMEM_SPEC,
        scratch_shapes=scratch,
        cost_estimate=SMALL_COST,
        compiler_params=params(),
    )(in_hbm(total.array) if away else in_vmem(total), in_vmem(arrived))


def finish_spectra_body(mine_s, inside, *rest):
    others, (out, near) = rest[:-2], rest[-2:]
    at = 0
    for other in others:
        where = pl.ds(at, other.shape[0])
        out[where] = (mine_s[where] + other[...].astype(jnp.float32)).astype(jnp.bfloat16)
        at += other.shape[0]
    near[...] = inside[...]


def finish_spectra(mine_s, others, inside):
    return pl.pallas_call(
        finish_spectra_body,
        out_shape=[
            jax.ShapeDtypeStruct(mine_s.shape, jnp.bfloat16),
            vmem_out(inside.shape, inside.dtype),
        ],
        in_specs=[VMEM_SPEC] * (2 + len(others)),
        out_specs=[VMEM_SPEC] * 2,
        cost_estimate=SMALL_COST,
        compiler_params=params(),
    )(*[in_vmem(a) for a in [mine_s, inside] + others])


def bring_body(wanted, away, near, sem):
    @pl.when(wanted[0] != 0)
    def _():
        copy = pltpu.make_async_copy(away, near, sem)
        copy.start()
        copy.wait()


def bring(wanted, away):
    return pl.pallas_call(
        bring_body,
        out_shape=vmem_out(away.shape, away.dtype),
        in_specs=[SMEM_SPEC, HBM_SPEC],
        out_specs=VMEM_SPEC,
        scratch_shapes=[pltpu.SemaphoreType.DMA],
        cost_estimate=SMALL_COST,
        compiler_params=params(),
    )(jnp.int32(wanted).reshape(1), in_hbm(away))


def finish_structures_body(flag, here_total, across_back, inside_a, inside_b, out):
    @pl.when(flag[0] != 0)
    def _():
        out[pl.ds(0, inside_a.shape[0])] = inside_a[...]
        out[pl.ds(inside_a.shape[0], inside_b.shape[0])] = inside_b[...]

    @pl.when(flag[0] == 0)
    def _():
        total = here_total[...] + across_back[...].astype(jnp.float32)
        out[...] = total.astype(jnp.bfloat16)


def finish_structures(flag, here_total, across_back, inside_a, inside_b):
    arrays = [here_total, across_back, inside_a, inside_b]
    return pl.pallas_call(
        finish_structures_body,
        out_shape=jax.ShapeDtypeStruct(here_total.shape, jnp.bfloat16),
        in_specs=[SMEM_SPEC] + [VMEM_SPEC] * len(arrays),
        out_specs=VMEM_SPEC,
        cost_estimate=SMALL_COST,
        compiler_params=params(),
    )(jnp.int32(flag).reshape(1), *[in_vmem(a) for a in arrays])


def along_line(spectra, glycans, labels, scale, shift):
    rows, width = spectra.shape
    node_rows = rows * lax.axis_size("inner")
    position = lax.axis_index("blk")
    outer = (position == 0) | (position == LINE - 1)
    core_first = lax.axis_index("sub") * node_rows + lax.axis_index("inner") * rows
    lane_rows = lax.axis_size("sub") * node_rows

    def permute(block, pairs):
        return lax.ppermute(block, ("blk", "inner"), pairs)

    def first_of(block_position):
        return (block_position * lane_rows + core_first).astype(jnp.float32)

    n_inner = lax.axis_size("inner")
    last = LINE - 1
    sides = []
    middle = []
    inward = []
    outward = []
    for core in range(n_inner):
        inward += [(core, n_inner + core), (last * n_inner + core, (last - 1) * n_inner + core)]
        outward += [(n_inner + core, core), ((last - 1) * n_inner + core, last * n_inner + core)]
        for at in range(LINE):
            sides.append((at * n_inner + core, (at ^ 1) * n_inner + core))
        for at in range(1, last):
            middle.append((at * n_inner + core, (last - at) * n_inner + core))
        for at in (0, last):
            middle.append((at * n_inner + core, at * n_inner + (core + 1) % n_inner))
    here_at, side_at, across_at, far_at = 2, 3, 4, FAR_ROW
    rows_of_consts = [
        scale,
        shift,
        first_of(position),
        first_of(position ^ 1),
        first_of(last - position),
        first_of((last - position) ^ 1),
        jnp.where(outer, 0.0, 1.0),
        first_of(jnp.where(outer, last - position, (last - position) ^ 1)),
    ]
    index = lax.broadcasted_iota(jnp.int32, (8, 128), 0)
    consts = jnp.zeros((8, 128), jnp.float32)
    for i, value in enumerate(rows_of_consts):
        consts = jnp.where(index == i, value, consts)

    cut = 2 * rows // 5
    half = rows // 2
    across = permute(glycans, middle)
    side = permute(glycans, sides)
    coded = code_labels(labels, LABEL_ROWS, width)
    end_mine = permute(jnp.concatenate([spectra, coded]), inward)
    partner = swap_inner(spectra)
    own_labels = labels.reshape(1, rows)
    node_labels = jnp.concatenate([own_labels, swap_inner(own_labels)], axis=1)
    node_labels = node_labels.astype(jnp.float32)
    node = dict(node=(spectra, partner), labels=node_labels)
    here_g, here_c = pair_work(
        consts, [(Block(here_at, ("node",), "kept", coef="all"), Away(glycans), None)], rows, **node
    )

    side = after(side, here_g)
    far_a, far_b = [permute(x, middle) for x in split(side, (cut, rows - cut))]
    across = after(across, here_g)
    next_out = permute(across, outward)
    side_g, across_g, side_c, across_c = pair_work(
        consts,
        [
            (Block(side_at, ("node",), "kept", coef="all"), Away(side), None),
            (Block(across_at, ("node",), "kept", coef="masked"), Away(across), None),
        ],
        rows,
        **node,
    )
    far_a = after(far_a, across_g)
    last_a = permute(far_a, sides)
    (far_g,) = pair_work(
        consts, [(Block(far_at, ("node",), "total"), far_a, None)], rows, wanted=~outer, **node
    )
    end_mine = after(end_mine, far_g)
    piece = -(-rows // 48) * 16
    two = (half + LABEL_ROWS, half)
    ends = (end_mine,) + tuple(swap_inner(x) for x in split(end_mine, two))

    far_a, far_b, next_out = lax.optimization_barrier((far_a, far_b, next_out, far_g))[:3]
    (far_a_out,) = pair_work(
        consts,
        [(Block(far_at, ("ends",), "rounded", prior="near"), far_a, far_g)],
        rows,
        wanted=~outer,
        ends=ends,
    )
    back_a = permute(far_a_out, middle)
    far_b = after(far_b, far_a_out)
    last_b = permute(far_b, sides)
    (far_b_out,) = pair_work(
        consts,
        [(Block(far_at, ("node", "ends"), "rounded", cut), far_b, None)],
        rows,
        wanted=~outer,
        ends=ends,
        **node,
    )
    back_b = permute(far_b_out, middle)
    (across_out,) = pair_work(
        consts,
        [
            (
                Block(across_at, ("ends",), "rounded", prior="kept"),
                Away(after(across, far_b_out)),
                across_g,
            )
        ],
        rows,
        wanted=~outer,
        ends=ends,
    )
    late_side, last_a = lax.optimization_barrier((side, last_a, across_out))[:2]
    late_side = Away(late_side)
    side_total_a, side_total_b = pair_work(
        consts,
        [(Block(side_at, ("ends",), "split", cut=cut, prior="kept"), late_side, side_g)],
        rows,
        wanted=~outer,
        ends=ends,
    )
    total_a = add_rounded(side_total_a, back_a)
    inside_a = permute(total_a, sides)
    across_back = permute(after(across_out, total_a), middle)
    (here_total,) = pair_work(
        consts,
        [(Block(here_at, ("ends",), "kept scaled", prior="kept"), Away(after(glycans, total_a)), here_g)],
        rows,
        wanted=~outer,
        ends=ends,
    )
    back_b, last_b = lax.optimization_barrier((back_b, last_b, here_total))[:2]
    total_b = add_rounded(Away(side_total_b), back_b)
    inside_b = permute(total_b, sides)

    mine_s, other_s = spectra_work(
        outer,
        consts,
        node_labels,
        (spectra, partner),
        (here_c, side_c, across_c),
        after(glycans, total_b),
        side,
        across,
        (next_out,),
        (far_a, far_b),
        (last_a, last_b),
    )
    others = [swap_inner(x) for x in split(other_s, (piece, piece, rows - 2 * piece))]
    grad_spectra, inside_a = finish_spectra(mine_s, others, inside_a)
    here_total = bring(~outer, after(here_total, grad_spectra))
    across_back = after(across_back, here_total)
    return grad_spectra, finish_structures(outer, here_total, across_back, inside_a, inside_b)


def local(
    mass_profile_vectors,
    sugar_tree_vectors,
    matching_glycan_rows,
    sharpness_factor,
    offset_shift_term,
):
    work = along_line if lax.axis_size("blk") == STEPS == LINE else around_ring
    return work(
        mass_profile_vectors,
        sugar_tree_vectors,
        matching_glycan_rows,
        sharpness_factor[0],
        offset_shift_term[0],
    )


def solution(mesh):
    placed = (
        P(("groups", "blk", "sub", "inner"), None),
        P(("groups", "blk", "sub", "inner"), None),
        P(("groups", "blk", "sub", "inner")),
        P(),
        P(),
    )
    return jax.shard_map(
        local,
        mesh=mesh,
        in_specs=placed,
        out_specs=(
            P(("groups", "blk", "sub", "inner"), None),
            P(("groups", "blk", "sub", "inner"), None),
        ),
        check_vma=False,
    )
```

```python
import dataclasses
import functools

import jax
import jax.numpy as jnp
from jax import lax
from jax.experimental import pallas as pl
from jax.experimental.pallas import tpu as pltpu
from jax.sharding import PartitionSpec as P

STEPS = 4
LINE = 4
LABEL_ROWS = 16
FAR_ROW, KEEP_ROW, LAST_ROW = 5, 6, 7
VMEM_BYTES = 20 * 1024 * 1024


def from_behind(block, axis, distance):
    devices = range(lax.axis_size(axis))
    route = [((i - distance) % len(devices), i) for i in devices]
    return lax.ppermute(block, axis, route)


def swap_inner(block):
    return from_behind(block, "inner", 1)


def after(value, *earlier):
    return lax.optimization_barrier((value,) + earlier)[0]


def coefficients(spectra, glycans, labels, first_target, scale, shift):
    logits = (
        scale
        * lax.dot_general(
            spectra, glycans, (((1,), (1,)), ((), ())), preferred_element_type=jnp.float32
        )
        + shift
    )
    targets = first_target + jnp.arange(glycans.shape[0], dtype=jnp.int32)
    positive = (labels[:, None] == targets[None, :]).astype(jnp.float32)
    return (jax.nn.sigmoid(logits) - positive).astype(jnp.bfloat16)


def around_ring(spectra, glycans, labels, scale, shift):
    rows_here = spectra.shape[0]
    node_rows = rows_here * lax.axis_size("inner")
    loop_count = lax.axis_size("blk")
    position = lax.axis_index("blk")
    core_first = lax.axis_index("sub") * node_rows + lax.axis_index("inner") * rows_here
    lane_rows = lax.axis_size("sub") * node_rows
    node_spectra = jnp.concatenate([spectra, swap_inner(spectra)])
    node_labels = jnp.concatenate([labels, swap_inner(labels)])
    spectrum_total = 0.0
    glycan_total = 0.0
    held = glycans
    for step in range(STEPS):
        if step > 0:
            held = from_behind(held, "blk", 1)
        first_target = (position - step) % loop_count * lane_rows + core_first
        coef = coefficients(node_spectra, held, node_labels, first_target, scale, shift)
        spectrum_total += jnp.dot(coef, held, preferred_element_type=jnp.float32)
        partial_value = scale * lax.dot_general(
            coef, node_spectra, (((0,), (0,)), ((), ())), preferred_element_type=jnp.float32
        )
        if step > 0:
            back = from_behind(partial_value.astype(jnp.bfloat16), "blk", -step)
            partial_value = back.astype(jnp.float32)
        glycan_total += partial_value
    other = swap_inner((scale * spectrum_total[rows_here:]).astype(jnp.bfloat16))
    spectrum_total = scale * spectrum_total[:rows_here] + other.astype(jnp.float32)
    return spectrum_total.astype(jnp.bfloat16), glycan_total.astype(jnp.bfloat16)


@dataclasses.dataclass(frozen=True)
class Away:
    array: jax.Array


@dataclasses.dataclass(frozen=True)
class Block:
    target: int
    uses: tuple
    out: str
    offset: int = 0
    cut: int = 0
    prior: str = ""
    coef: str = ""


@dataclasses.dataclass(frozen=True)
class Plan:
    blocks: tuple
    pieces: tuple
    node: bool
    ends: tuple
    skips: bool
    rows: int


def pair_body(plan, *refs):
    if plan.skips:
        pl.when(refs[0][0] != 0)(functools.partial(pair_steps, plan, *refs[1:]))
    else:
        pair_steps(plan, *refs)


def pair_steps(plan, *refs):
    refs = list(refs)
    blocks, rows = plan.blocks, plan.rows

    def take(count):
        taken = refs[:count]
        del refs[:count]
        return taken

    def take_if(condition):
        return take(1)[0] if condition else None

    (consts,) = take(1)
    labels = take_if(plan.node)
    node_in = take(2) if plan.node else []
    ends_in = take(len(plan.ends))
    held_in = [take(len(p)) for p in plan.pieces]
    priors = [take_if(b.prior) for b in blocks]
    outs = [take((b.out != "") + (b.out == "split")) for b in blocks]
    coef_outs = [take_if(b.coef) for b in blocks]
    spectra = take_if(plan.node)
    ends = take_if(plan.ends)
    held = take(len(blocks))
    prior_held = [take_if(b.prior == "kept") for b in blocks]
    out_held = [take_if(b.out in ("kept", "kept scaled", "split")) for b in blocks]
    coef_held = [take_if(b.coef) for b in blocks]
    (sems,) = take(1)
    used = 0

    def move(source, target):
        nonlocal used
        copy = pltpu.make_async_copy(source, target, sems.at[used])
        copy.start()
        used += 1
        return copy

    moving_node = [move(ref, spectra.at[pl.ds(i * rows, rows)]) for i, ref in enumerate(node_in)]
    moving = []
    for i, block in enumerate(blocks):
        moves = []
        at = 0
        for ref, (count, away) in zip(held_in[i], plan.pieces[i]):
            if away:
                moves.append(move(ref, held[i].at[pl.ds(at, count)]))
            at += count
        moving.append(moves)
    moving_prior = [
        move(priors[i], prior_held[i]) if b.prior == "kept" else None for i, b in enumerate(blocks)
    ]
    leaving = []

    def const(row):
        return consts[pl.ds(row, 1), pl.ds(0, 1)]

    scale, shift = const(0), const(1)
    if plan.ends:
        width = 2 * rows
        at = 0
        coded = []
        for ref, count in zip(ends_in, plan.ends):
            ending = at % rows + count > rows
            keep = count - LABEL_ROWS if ending else count
            ends[pl.ds(at, keep)] = ref[pl.ds(0, keep)]
            at += keep
            if ending:
                digits = ref[pl.ds(keep, LABEL_ROWS), pl.ds(0, width)].astype(jnp.float32)
                coded.append(digits[0:1] * 16384.0 + digits[1:2] * 128.0 + digits[2:3])
        lane = lax.broadcasted_iota(jnp.int32, (1, width), 1)
        end_labels = jnp.where(lane >= rows, coded[1], coded[0])

    def source(use):
        if use == "node":
            while moving_node:
                moving_node.pop(0).wait()
            return spectra[...], labels[...]
        return ends[...], end_labels

    for i, block in enumerate(blocks):

        def work(i=i, block=block):
            at = 0
            for ref, (count, away) in zip(held_in[i], plan.pieces[i]):
                if not away:
                    held[i][pl.ds(at, count)] = ref[...]
                at += count
            for copy in moving[i]:
                copy.wait()
            glycans = held[i][...]
            targets = lax.broadcasted_iota(jnp.int32, (glycans.shape[0], 1), 0)
            targets = targets.astype(jnp.float32) + (const(block.target) + float(block.offset))
            total = None
            for use in block.uses:
                here, row_labels = source(use)
                logits = lax.dot_general(
                    glycans, here, (((1,), (1,)), ((), ())), preferred_element_type=jnp.float32
                )
                logits = scale * logits + shift
                positive = jnp.where(targets == row_labels, 1.0, 0.0)
                coef = jax.nn.sigmoid(logits) - positive
                coef = coef.astype(jnp.bfloat16)
                if block.out:
                    part = jnp.dot(coef, here, preferred_element_type=jnp.float32)
                    total = part if total is None else total + part
                if block.coef and use == "node":
                    kept = coef * const(KEEP_ROW).astype(jnp.bfloat16) if block.coef == "masked" else coef
                    coef_held[i][...] = kept
                    leaving.append(move(coef_held[i], coef_outs[i]))
            if block.prior == "kept":
                moving_prior[i].wait()
                total = total + prior_held[i][...]
            elif block.prior:
                total = total + priors[i][...]
            if block.out.startswith("kept"):
                out_held[i][...] = scale * total if block.out == "kept scaled" else total
                leaving.append(move(out_held[i], outs[i][0]))
            elif block.out == "split":
                cut = outs[i][0].shape[0]
                outs[i][0][...] = scale * total[:cut]
                out_held[i][...] = scale * total[cut:]
                leaving.append(move(out_held[i], outs[i][1]))
            elif block.out == "total":
                outs[i][0][...] = total
            elif block.out:
                outs[i][0][...] = (scale * total).astype(jnp.bfloat16)

        work()
    for copy in leaving:
        copy.wait()


def in_vmem(array):
    return pltpu.with_memory_space_constraint(array, pltpu.VMEM)


def in_hbm(array):
    return pltpu.with_memory_space_constraint(array, pltpu.HBM)


def vmem_out(shape, kind):
    return pltpu.VMEM(shape, kind)


def hbm_out(shape, kind):
    return pltpu.HBM(shape, kind)


VMEM_SPEC = pl.BlockSpec(memory_space=pltpu.VMEM)
SMEM_SPEC = pl.BlockSpec(memory_space=pltpu.SMEM)
HBM_SPEC = pl.BlockSpec(memory_space=pltpu.HBM)
SMALL_COST = pl.CostEstimate(flops=1024, bytes_accessed=1024, transcendentals=0)


def params():
    return pltpu.CompilerParams(vmem_limit_bytes=VMEM_BYTES)


def pair_work(consts, blocks, rows, labels=None, node=None, ends=None, wanted=None):
    shapes = tuple(b[0] for b in blocks)
    pieces = []
    arrays = []
    for shape, array, _ in blocks:
        parts = array if isinstance(array, tuple) else (array,)
        away = [isinstance(x, Away) for x in parts]
        parts = [x.array if flag else x for x, flag in zip(parts, away)]
        pieces.append(tuple((x.shape[0], flag) for x, flag in zip(parts, away)))
        arrays += list(zip(parts, away))
    width = arrays[0][0].shape[1]
    ends = ends or ()
    end_rows = tuple(x.shape[0] for x in ends)
    plan = Plan(
        shapes,
        tuple(pieces),
        node is not None,
        end_rows,
        wanted is not None,
        rows,
    )

    operands = []
    in_specs = []
    if wanted is not None:
        operands.append(jnp.int32(wanted).reshape(1))
        in_specs.append(SMEM_SPEC)

    def give(array, away):
        operands.append(in_hbm(array) if away else in_vmem(array))
        in_specs.append(HBM_SPEC if away else VMEM_SPEC)

    give(consts, False)
    if node is not None:
        give(labels, False)
    for array in node or ():
        give(array, True)
    for array in ends:
        give(array, False)
    for array, away in arrays:
        give(array, away)
    for shape, _, prior in blocks:
        if shape.prior:
            give(prior, shape.prior == "kept")

    counts = [sum(count for count, _ in p) for p in pieces]
    outs = []
    out_specs = []

    def get(shape, kind, away):
        outs.append((hbm_out if away else vmem_out)(shape, kind))
        out_specs.append(HBM_SPEC if away else VMEM_SPEC)

    for shape, count in zip(shapes, counts):
        if shape.out == "split":
            get((shape.cut, width), jnp.float32, False)
            get((count - shape.cut, width), jnp.float32, True)
        elif shape.out:
            kind = jnp.bfloat16 if shape.out == "rounded" else jnp.float32
            get((count, width), kind, shape.out.startswith("kept"))
    for shape, count in zip(shapes, counts):
        if shape.coef:
            get((count, 2 * rows), jnp.bfloat16, True)

    scratch = []
    if node is not None:
        scratch.append(pltpu.VMEM((2 * rows, width), jnp.bfloat16))
    if ends:
        scratch.append(pltpu.VMEM((2 * rows, width), jnp.bfloat16))
    scratch += [pltpu.VMEM((n, width), jnp.bfloat16) for n in counts]
    scratch += [pltpu.VMEM((n, width), jnp.float32) for n, b in zip(counts, shapes) if b.prior == "kept"]
    for n, b in zip(counts, shapes):
        if b.out in ("kept", "kept scaled", "split"):
            scratch.append(pltpu.VMEM((n - b.cut, width), jnp.float32))
    scratch += [pltpu.VMEM((n, 2 * rows), jnp.bfloat16) for n, b in zip(counts, shapes) if b.coef]
    scratch.append(pltpu.SemaphoreType.DMA((len(operands) + len(outs),)))
    return pl.pallas_call(
        functools.partial(pair_body, plan),
        out_shape=outs,
        in_specs=in_specs,
        out_specs=out_specs,
        scratch_shapes=scratch,
        cost_estimate=SMALL_COST,
        compiler_params=params(),
    )(*operands)


def code_labels(labels, row_count, width):
    digits = jnp.stack([labels // 16384, labels // 128 % 128, labels % 128]).astype(jnp.bfloat16)
    digits = jnp.concatenate([digits, digits, digits], axis=1)
    return jnp.pad(digits, ((0, row_count - 3), (0, width - digits.shape[1])))


def spectra_body(plan, outer, consts, labels, s_mine, s_other, coef_here, coef_side, coef_across, here, side, across, *rest):
    rows, n_next, n_far, n_last = plan
    nexts, rest = rest[:n_next], rest[n_next:]
    fars, rest = rest[:n_far], rest[n_far:]
    lasts, rest = rest[:n_last], rest[n_last:]
    mine_out, other_out, spectra, coefs, held, sems = rest
    used = 0

    def move(source, target):
        nonlocal used
        copy = pltpu.make_async_copy(source, target, sems.at[used])
        copy.start()
        used += 1
        return copy

    def fill(parts, target, at):
        moves = []
        for part in parts:
            moves.append(move(part, target.at[pl.ds(at, part.shape[0])]))
            at += part.shape[0]
        return moves

    moves = fill([s_mine, s_other], spectra, 0) + fill([coef_here, coef_side], coefs, 0)
    moves += fill([here, side], held, 0)

    @pl.when(outer[0] == 0)
    def _():
        for copy in fill([across] + list(fars), held, 2 * rows) + fill([coef_across], coefs, 2 * rows):
            copy.wait()

    @pl.when(outer[0] != 0)
    def _():
        for copy in fill(list(nexts) + list(lasts), held, 2 * rows):
            copy.wait()

    for copy in moves[:2]:
        copy.wait()
    scale, shift = consts[0:1, 0:1], consts[1:2, 0:1]

    def work_out(first, target_row):
        logits = lax.dot_general(
            held[pl.ds(first, rows)],
            spectra[...],
            (((1,), (1,)), ((), ())),
            preferred_element_type=jnp.float32,
        )
        logits = scale * logits + shift
        targets = lax.broadcasted_iota(jnp.int32, (rows, 1), 0).astype(jnp.float32)
        targets = targets + consts[target_row : target_row + 1, 0:1]
        positive = jnp.where(targets == labels[...], 1.0, 0.0)
        coefs[pl.ds(first, rows)] = (jax.nn.sigmoid(logits) - positive).astype(jnp.bfloat16)

    @pl.when(outer[0] != 0)
    def _():
        work_out(2 * rows, FAR_ROW)

    work_out(3 * rows, LAST_ROW)
    for copy in moves[2:]:
        copy.wait()
    for i, out in enumerate((mine_out, other_out)):
        total = lax.dot_general(
            coefs[:, i * rows : (i + 1) * rows],
            held[...],
            (((0,), (0,)), ((), ())),
            preferred_element_type=jnp.float32,
        )
        out[...] = (scale * total).astype(out.dtype)


def spectra_work(outer, consts, labels, node, coefs, here, side, across, nexts, fars, lasts):
    rows, width = here.shape
    arrays = list(node) + list(coefs) + [here, side, across] + list(nexts) + list(fars) + list(lasts)
    plan = (rows, len(nexts), len(fars), len(lasts))
    return pl.pallas_call(
        functools.partial(spectra_body, plan),
        out_shape=[vmem_out((rows, width), jnp.float32), vmem_out((rows, width), jnp.bfloat16)],
        in_specs=[SMEM_SPEC, VMEM_SPEC, VMEM_SPEC] + [HBM_SPEC] * len(arrays),
        out_specs=[VMEM_SPEC] * 2,
        scratch_shapes=[
            pltpu.VMEM((2 * rows, width), jnp.bfloat16),
            pltpu.VMEM((4 * rows, 2 * rows), jnp.bfloat16),
            pltpu.VMEM((4 * rows, width), jnp.bfloat16),
            pltpu.SemaphoreType.DMA((len(arrays),)),
        ],
        cost_estimate=SMALL_COST,
        compiler_params=params(),
    )(
        jnp.int32(outer).reshape(1),
        in_vmem(consts),
        in_vmem(labels),
        *[in_hbm(a) for a in arrays],
    )


def split_body(whole, *parts):
    at = 0
    for part in parts:
        part[...] = whole[pl.ds(at, part.shape[0])]
        at += part.shape[0]


def split(whole, counts):
    return pl.pallas_call(
        split_body,
        out_shape=[vmem_out((n, whole.shape[1]), whole.dtype) for n in counts],
        in_specs=[VMEM_SPEC],
        out_specs=[VMEM_SPEC] * len(counts),
        cost_estimate=SMALL_COST,
        compiler_params=params(),
    )(in_vmem(whole))


def add_body(total, arrived, out, *scratch):
    if scratch:
        near, sem = scratch
        copy = pltpu.make_async_copy(total, near, sem)
        copy.start()
        copy.wait()
        total = near
    out[...] = (total[...] + arrived[...].astype(jnp.float32)).astype(jnp.bfloat16)


def add_rounded(total, arrived):
    away = isinstance(total, Away)
    scratch = [pltpu.VMEM(arrived.shape, jnp.float32), pltpu.SemaphoreType.DMA] if away else []
    return pl.pallas_call(
        add_body,
        out_shape=vmem_out(arrived.shape, jnp.bfloat16),
        in_specs=[HBM_SPEC if away else VMEM_SPEC, VMEM_SPEC],
        out_specs=VMEM_SPEC,
        scratch_shapes=scratch,
        cost_estimate=SMALL_COST,
        compiler_params=params(),
    )(in_hbm(total.array) if away else in_vmem(total), in_vmem(arrived))


def finish_spectra_body(mine_s, inside, *rest):
    others, (out, near) = rest[:-2], rest[-2:]
    at = 0
    for other in others:
        where = pl.ds(at, other.shape[0])
        out[where] = (mine_s[where] + other[...].astype(jnp.float32)).astype(jnp.bfloat16)
        at += other.shape[0]
    near[...] = inside[...]


def finish_spectra(mine_s, others, inside):
    return pl.pallas_call(
        finish_spectra_body,
        out_shape=[
            jax.ShapeDtypeStruct(mine_s.shape, jnp.bfloat16),
            vmem_out(inside.shape, inside.dtype),
        ],
        in_specs=[VMEM_SPEC] * (2 + len(others)),
        out_specs=[VMEM_SPEC] * 2,
        cost_estimate=SMALL_COST,
        compiler_params=params(),
    )(*[in_vmem(a) for a in [mine_s, inside] + others])


def bring_body(wanted, away, near, sem):
    @pl.when(wanted[0] != 0)
    def _():
        copy = pltpu.make_async_copy(away, near, sem)
        copy.start()
        copy.wait()


def bring(wanted, away):
    return pl.pallas_call(
        bring_body,
        out_shape=vmem_out(away.shape, away.dtype),
        in_specs=[SMEM_SPEC, HBM_SPEC],
        out_specs=VMEM_SPEC,
        scratch_shapes=[pltpu.SemaphoreType.DMA],
        cost_estimate=SMALL_COST,
        compiler_params=params(),
    )(jnp.int32(wanted).reshape(1), in_hbm(away))


def finish_structures_body(flag, here_total, across_back, inside_a, inside_b, out):
    @pl.when(flag[0] != 0)
    def _():
        out[pl.ds(0, inside_a.shape[0])] = inside_a[...]
        out[pl.ds(inside_a.shape[0], inside_b.shape[0])] = inside_b[...]

    @pl.when(flag[0] == 0)
    def _():
        total = here_total[...] + across_back[...].astype(jnp.float32)
        out[...] = total.astype(jnp.bfloat16)


def finish_structures(flag, here_total, across_back, inside_a, inside_b):
    arrays = [here_total, across_back, inside_a, inside_b]
    return pl.pallas_call(
        finish_structures_body,
        out_shape=jax.ShapeDtypeStruct(here_total.shape, jnp.bfloat16),
        in_specs=[SMEM_SPEC] + [VMEM_SPEC] * len(arrays),
        out_specs=VMEM_SPEC,
        cost_estimate=SMALL_COST,
        compiler_params=params(),
    )(jnp.int32(flag).reshape(1), *[in_vmem(a) for a in arrays])


def along_line(spectra, glycans, labels, scale, shift):
    rows, width = spectra.shape
    node_rows = rows * lax.axis_size("inner")
    position = lax.axis_index("blk")
    outer = (position == 0) | (position == LINE - 1)
    core_first = lax.axis_index("sub") * node_rows + lax.axis_index("inner") * rows
    lane_rows = lax.axis_size("sub") * node_rows

    def permute(block, pairs):
        return lax.ppermute(block, ("blk", "inner"), pairs)

    def first_of(block_position):
        return (block_position * lane_rows + core_first).astype(jnp.float32)

    n_inner = lax.axis_size("inner")
    last = LINE - 1
    sides = []
    middle = []
    inward = []
    outward = []
    for core in range(n_inner):
        inward += [(core, n_inner + core), (last * n_inner + core, (last - 1) * n_inner + core)]
        outward += [(n_inner + core, core), ((last - 1) * n_inner + core, last * n_inner + core)]
        for at in range(LINE):
            sides.append((at * n_inner + core, (at ^ 1) * n_inner + core))
        for at in range(1, last):
            middle.append((at * n_inner + core, (last - at) * n_inner + core))
        for at in (0, last):
            middle.append((at * n_inner + core, at * n_inner + (core + 1) % n_inner))
    here_at, side_at, across_at, far_at = 2, 3, 4, FAR_ROW
    rows_of_consts = [
        scale,
        shift,
        first_of(position),
        first_of(position ^ 1),
        first_of(last - position),
        first_of((last - position) ^ 1),
        jnp.where(outer, 0.0, 1.0),
        first_of(jnp.where(outer, last - position, (last - position) ^ 1)),
    ]
    index = lax.broadcasted_iota(jnp.int32, (8, 128), 0)
    consts = jnp.zeros((8, 128), jnp.float32)
    for i, value in enumerate(rows_of_consts):
        consts = jnp.where(index == i, value, consts)

    cut = 2 * rows // 5
    half = rows // 2
    across = permute(glycans, middle)
    side = permute(glycans, sides)
    coded = code_labels(labels, LABEL_ROWS, width)
    end_mine = permute(jnp.concatenate([spectra, coded]), inward)
    partner = swap_inner(spectra)
    own_labels = labels.reshape(1, rows)
    node_labels = jnp.concatenate([own_labels, swap_inner(own_labels)], axis=1)
    node_labels = node_labels.astype(jnp.float32)
    node = dict(node=(spectra, partner), labels=node_labels)
    here_g, here_c = pair_work(
        consts, [(Block(here_at, ("node",), "kept", coef="all"), Away(glycans), None)], rows, **node
    )

    side = after(side, here_g)
    far_a, far_b = [permute(x, middle) for x in split(side, (cut, rows - cut))]
    across = after(across, here_g)
    next_out = permute(across, outward)
    side_g, across_g, side_c, across_c = pair_work(
        consts,
        [
            (Block(side_at, ("node",), "kept", coef="all"), Away(side), None),
            (Block(across_at, ("node",), "kept", coef="masked"), Away(across), None),
        ],
        rows,
        **node,
    )
    far_a = after(far_a, across_g)
    last_a = permute(far_a, sides)
    (far_g,) = pair_work(
        consts, [(Block(far_at, ("node",), "total"), far_a, None)], rows, wanted=~outer, **node
    )
    end_mine = after(end_mine, far_g)
    piece = -(-rows // 48) * 16
    two = (half + LABEL_ROWS, half)
    ends = (end_mine,) + tuple(swap_inner(x) for x in split(end_mine, two))

    far_a, far_b, next_out = lax.optimization_barrier((far_a, far_b, next_out, far_g))[:3]
    (far_a_out,) = pair_work(
        consts,
        [(Block(far_at, ("ends",), "rounded", prior="near"), far_a, far_g)],
        rows,
        wanted=~outer,
        ends=ends,
    )
    back_a = permute(far_a_out, middle)
    far_b = after(far_b, far_a_out)
    last_b = permute(far_b, sides)
    (far_b_out,) = pair_work(
        consts,
        [(Block(far_at, ("node", "ends"), "rounded", cut), far_b, None)],
        rows,
        wanted=~outer,
        ends=ends,
        **node,
    )
    back_b = permute(far_b_out, middle)
    (across_out,) = pair_work(
        consts,
        [
            (
                Block(across_at, ("ends",), "rounded", prior="kept"),
                Away(after(across, far_b_out)),
                across_g,
            )
        ],
        rows,
        wanted=~outer,
        ends=ends,
    )
    late_side, last_a = lax.optimization_barrier((side, last_a, across_out))[:2]
    late_side = Away(late_side)
    side_total_a, side_total_b = pair_work(
        consts,
        [(Block(side_at, ("ends",), "split", cut=cut, prior="kept"), late_side, side_g)],
        rows,
        wanted=~outer,
        ends=ends,
    )
    total_a = add_rounded(side_total_a, back_a)
    inside_a = permute(total_a, sides)
    across_back = permute(after(across_out, total_a), middle)
    (here_total,) = pair_work(
        consts,
        [(Block(here_at, ("ends",), "kept scaled", prior="kept"), Away(after(glycans, total_a)), here_g)],
        rows,
        wanted=~outer,
        ends=ends,
    )
    back_b, last_b = lax.optimization_barrier((back_b, last_b, here_total))[:2]
    total_b = add_rounded(Away(side_total_b), back_b)
    inside_b = permute(total_b, sides)

    mine_s, other_s = spectra_work(
        outer,
        consts,
        node_labels,
        (spectra, partner),
        (here_c, side_c, across_c),
        after(glycans, total_b),
        side,
        across,
        (next_out,),
        (far_a, far_b),
        (last_a, last_b),
    )
    others = [swap_inner(x) for x in split(other_s, (piece, piece, rows - 2 * piece))]
    grad_spectra, inside_a = finish_spectra(mine_s, others, inside_a)
    here_total = bring(~outer, after(here_total, grad_spectra))
    across_back = after(across_back, here_total)
    return grad_spectra, finish_structures(outer, here_total, across_back, inside_a, inside_b)


def local(
    mass_profile_vectors,
    sugar_tree_vectors,
    matching_glycan_rows,
    sharpness_factor,
    offset_shift_term,
):
    work = along_line if lax.axis_size("blk") == STEPS == LINE else around_ring
    return work(
        mass_profile_vectors,
        sugar_tree_vectors,
        matching_glycan_rows,
        sharpness_factor[0],
        offset_shift_term[0],
    )


def solution(mesh):
    placed = (
        P(("groups", "blk", "sub", "inner"), None),
        P(("groups", "blk", "sub", "inner"), None),
        P(("groups", "blk", "sub", "inner")),
        P(),
        P(),
    )
    return jax.shard_map(
        local,
        mesh=mesh,
        in_specs=placed,
        out_specs=(
            P(("groups", "blk", "sub", "inner"), None),
            P(("groups", "blk", "sub", "inner"), None),
        ),
        check_vma=False,
    )
```
